32 devices in a mesh: dp: 8 (over y, x, core), head: 4 (over z).
Axes of the slice: x: 2, y: 2, z: 4, core: 2. Of those that a mesh axis runs over, the one named last changes fastest.
Arguments:
- frames: bfloat16 [16384, 512], P(('dp', 'head')), may hold values from -6 to 6
- out_grad: bfloat16 [16384, 512], P(('dp', 'head')), may hold values from -6 to 6
- bucket_len: int32 [8], P('dp'), may hold values from 256 to 1024, as said below
- batch_count: int32 [8], P('dp'), may hold values from 1 to 8, as said below
- utt_lengths: int32 [8, 8], P('dp'), may hold values from 0 to 1024, as said below
- owner_slots: int32 [48], replicated, may hold values from 0 to 47, as said below
- masters: float32 [4, 48, 512, 64], P('head', 'dp'), as said below
- first_moment: float32 [4, 48, 512, 64], P('head', 'dp'), may hold values from -6 to 6
- second_moment: float32 [4, 48, 512, 64], P('head', 'dp'), may hold values from 19.33312 to 77.66016
- left_basis: float32 [4, 48, 512, 512], P('head', 'dp'), as said below
- right_basis: float32 [4, 48, 64, 64], P('head', 'dp'), as said below
- norm_params: float32 [10, 512], replicated, as said below
- norm_first: float32 [10, 512], replicated, may hold values from -40 to 40
- norm_second: float32 [10, 512], replicated, may hold values from 216.2688 to 861.7984
- conv_params: float32 [512, 34], P('head'), as said below
- conv_first: float32 [512, 34], P('head'), may hold values from -32 to 32
- conv_second: float32 [512, 34], P('head'), may hold values from 137.6256 to 552.1408
Outputs:
- layer_out: bfloat16 [16384, 512], P(('dp', 'head'))
- frames_grad: float32 [16384, 512], P(('dp', 'head'))
- new_masters: float32 [4, 48, 512, 64], P('head', 'dp')
- new_first: float32 [4, 48, 512, 64], P('head', 'dp')
- new_second: float32 [4, 48, 512, 64], P('head', 'dp')
- norm_grads: float32 [10, 512], replicated
- new_norms: float32 [10, 512], replicated
- norm_first_new: float32 [10, 512], replicated
- norm_second_new: float32 [10, 512], replicated
- new_conv: float32 [512, 34], P('head')
- conv_first_new: float32 [512, 34], P('head')
- conv_second_new: float32 [512, 34], P('head')
The draws below stay inside these ranges and needn't reach their ends.
Inputs may be any that keep to these rules, and one draw needn't show every extreme that they name: `bucket_len`: each group's bucket length is 256, 512 or 1024; in every draw some group has 1024 and some group has 256. `batch_count`: A group with bucket length L holds between half of 2048/L (rounded up) and 2048/L utterances; in every draw some group with bucket 1024 holds 2 and some group with bucket 1024/4 holds 8. `utt_lengths`: for a group with bucket length L and B utterances, slots 0 .. B-1 hold lengths above L/2 and at most L, slot 0 exactly L, the other slots 0. `owner_slots`: A permutation of 0 .. 47; a slot whose entry is 46 or more holds no block. `masters`: weight blocks in their slots. `left_basis`: left bases, one a slot. `right_basis`: right bases, one a slot. `norm_params`: rows 0 to 4 gains, rows 5 to 9 biases. `conv_params`: columns 0 .. 31 taps, then gain and bias.
All inputs are finite; a program needn't handle non-finite values.
Results may differ from the reference program's by a relative error of at most 0.015.
The reference program's roundings to bfloat16 on the way count: a program that leaves them out, or rounds other values in their place, can miss the bound.
Values may be sent and summed in bfloat16 or wider, within the bound.
A program may use at most 192 MiB of HBM per device.

```python
import math
import jax
import jax.numpy as jnp
from jax import lax

D = 512
HEADS = 8
HD = 64
KERNEL = 32
BLOCKW = 64
STEP = 10
LONGEST = 1024
TOK_DEV = 2048
NG = 8
TOKENS = 16384
MAXU = 8
NHG = 4
FFH = 512
CH = 128
NC = 26
NR = 20
NBLK = 46
SLOTS = 48


def bucket_plan(key):
    bucket_level = jax.random.randint(jax.random.fold_in(key, 21), (NG,), 0, 3)
    forced = jax.random.randint(jax.random.fold_in(key, 22), (), 0, NG)
    forced_short = (forced + 1) % NG
    group_ids = jnp.arange(NG)
    bucket_level = jnp.where(group_ids == forced, 2, bucket_level)
    bucket_level = jnp.where(group_ids == forced_short, 0, bucket_level)
    length = jnp.where(bucket_level == 0, LONGEST // 4, jnp.where(bucket_level == 1, LONGEST // 2, LONGEST)).astype(jnp.int32)
    capacity = TOK_DEV // length
    lowest = (capacity + 1) // 2
    raw_batch = jax.random.randint(jax.random.fold_in(key, 23), (NG,), 0, 1 << 20)
    batch_size = lowest + raw_batch % (capacity - lowest + 1)
    full_group = (group_ids == forced) | (group_ids == forced_short)
    batch_size = jnp.where(full_group, capacity, batch_size).astype(jnp.int32)
    half_len = length[:, None] // 2
    raw_len = jax.random.randint(jax.random.fold_in(key, 24), (NG, MAXU), 0, 1 << 20)
    lengths = half_len + 1 + raw_len % half_len
    slot_index = jnp.arange(MAXU)[None, :]
    lengths = jnp.where(slot_index == 0, length[:, None], lengths)
    lengths = jnp.where(slot_index < batch_size[:, None], lengths, 0).astype(jnp.int32)
    return (length, batch_size, lengths)


def slot_order(key):
    return jax.random.permutation(jax.random.fold_in(key, 7), SLOTS).astype(jnp.int32)


def draw_bucket_len(key, part):
    return bucket_plan(key)[0]


def draw_batch_count(key, part):
    return bucket_plan(key)[1]


def draw_utt_lengths(key, part):
    return bucket_plan(key)[2]


def draw_owner_slots(key, part):
    return slot_order(key)


def draw_masters(key, part):
    order = slot_order(key)
    noise = jax.random.normal(jax.random.fold_in(key, 31), (NHG, SLOTS, D, BLOCKW), jnp.float32)
    col_start = order * BLOCKW
    row_start = (order - NC) * BLOCKW
    attn_query = (order < NC) & (col_start >= 2 * FFH) & (col_start < 2 * FFH + 2 * CH)
    attn_output = (order >= NC) & (order < NBLK) & (row_start >= 2 * FFH) & (row_start < 2 * FFH + CH)
    factor = jnp.where(attn_output, 2.5, jnp.where(attn_query, 1.5, 1.0)).astype(jnp.float32)
    return noise * factor[None, :, None, None] * D ** (-0.5)


def draw_left_basis(key, part):
    noise = jax.random.normal(jax.random.fold_in(key, 41), (NHG, SLOTS, D, D), jnp.float32)
    return noise * (0.5 * D ** (-0.5)) + jnp.eye(D, dtype=jnp.float32)


def draw_right_basis(key, part):
    noise = jax.random.normal(jax.random.fold_in(key, 43), (NHG, SLOTS, BLOCKW, BLOCKW), jnp.float32)
    return noise * (0.5 * BLOCKW ** (-0.5)) + jnp.eye(BLOCKW, dtype=jnp.float32)


def draw_norm_params(key, part):
    noise = jax.random.normal(jax.random.fold_in(key, 51), (10, D), jnp.float32)
    row_ids = jnp.arange(10)[:, None]
    return jnp.where(row_ids < 5, 1.0 + 0.1 * noise, 0.2 * noise)


def draw_conv_params(key, part):
    noise = jax.random.normal(jax.random.fold_in(key, 61), (D, KERNEL + 2), jnp.float32)
    col_ids = jnp.arange(KERNEL + 2)[None, :]
    return jnp.where(col_ids < KERNEL, noise * KERNEL ** (-0.5), jnp.where(col_ids == KERNEL, 1.0 + 0.1 * noise, 0.2 * noise))


def steps_of(stream_key, extent, split, least, high):
    def one(axis_at, parts):
        draws = jax.random.uniform(jax.random.fold_in(jax.random.fold_in(stream_key, 6), axis_at), (parts,), jnp.float32, least / len(split), high / len(split))
        return jnp.repeat(jnp.exp(draws), extent[axis_at] // parts).reshape((-1,) + (1,) * (len(extent) - axis_at - 1))

    factor_of = one(*split[0])
    for cut in split[1:]:
        factor_of = factor_of * one(*cut)
    return factor_of


def centred(rng, shape, spread, reach, cuts=(), held_as=jnp.bfloat16):
    values = jax.random.normal(rng, shape, jnp.float32) * spread
    if len(cuts) > 0:
        values = steps_of(rng, shape, cuts, -0.22, 0.18) * values
    return jnp.clip(values, min=-reach, max=reach).astype(held_as)


def setup_inputs(seed: int = 0) -> dict:
    splits = jax.random.split(jax.random.key(seed), 18)
    frames = centred(splits[0], (TOKENS, D), 1.0, 6.0, ((0, 32),))
    out_grad = centred(splits[1], (TOKENS, D), 1.0, 6.0, ((0, 32),))
    bucket_len = draw_bucket_len(jax.random.fold_in(splits[17], 71), 0)
    batch_count = draw_batch_count(jax.random.fold_in(splits[17], 71), 0)
    utt_lengths = draw_utt_lengths(jax.random.fold_in(splits[17], 71), 0)
    owner_slots = draw_owner_slots(jax.random.fold_in(splits[17], 71), 0)
    masters = draw_masters(jax.random.fold_in(splits[17], 71), 0)
    first_moment = centred(splits[7], (NHG, SLOTS, D, BLOCKW), (0.0167 * TOKENS ** 0.5), 6.0, ((0, 4), (1, 8)), jnp.float32)
    second_moment = jnp.clip(jnp.exp(math.log(77.66016) - 1.3905226 * jax.random.uniform(splits[8], (NHG, SLOTS, D, BLOCKW), jnp.float32) ** steps_of(splits[8], (NHG, SLOTS, D, BLOCKW), ((0, 4), (1, 8)), -0.2, 0.2)), 19.33312, 77.66016)
    left_basis = draw_left_basis(jax.random.fold_in(splits[17], 71), 0)
    right_basis = draw_right_basis(jax.random.fold_in(splits[17], 71), 0)
    norm_params = draw_norm_params(jax.random.fold_in(splits[17], 71), 0)
    norm_first = centred(splits[12], (10, D), (0.0556 * TOKENS ** 0.5), 40.0, (), jnp.float32)
    norm_second = jnp.clip(jnp.exp(jax.random.uniform(splits[13], (10, D), jnp.float32, math.log(216.2688), math.log(861.7984))), 216.2688, 861.7984)
    conv_params = draw_conv_params(jax.random.fold_in(splits[17], 71), 0)
    conv_first = centred(splits[15], (D, KERNEL + 2), (0.0444 * TOKENS ** 0.5), 32.0, ((0, 4),), jnp.float32)
    conv_second = jnp.clip(jnp.exp(math.log(552.1408) - 1.38926618 * jax.random.uniform(splits[16], (D, KERNEL + 2), jnp.float32) ** steps_of(splits[16], (D, KERNEL + 2), ((0, 4),), -0.2, 0.2)), 137.6256, 552.1408)
    return {"frames": frames, "out_grad": out_grad, "bucket_len": bucket_len, "batch_count": batch_count, "utt_lengths": utt_lengths, "owner_slots": owner_slots, "masters": masters, "first_moment": first_moment, "second_moment": second_moment, "left_basis": left_basis, "right_basis": right_basis, "norm_params": norm_params, "norm_first": norm_first, "norm_second": norm_second, "conv_params": conv_params, "conv_first": conv_first, "conv_second": conv_second}


highest = lax.Precision.HIGHEST
beta_one = 0.9
beta_two = 0.95
step_rate = 0.05
weight_decay = 0.01
adam_eps = 1e-08
norm_eps = 1e-05
masked_score = -1e+30

@jax.custom_vjp
def low(v):
    return lax.optimization_barrier(v.astype(jnp.bfloat16)).astype(jnp.float32)

@jax.custom_vjp
def low_back(v):
    return v

def low_keep(v):
    return (low(v), None)

def low_pass(kept, grad):
    return (grad,)

def back_keep(v):
    return (v, None)

def back_low(kept, grad):
    return (low(grad),)
low.defvjp(low_keep, low_pass)
low_back.defvjp(back_keep, back_low)

def matmul(former, latter):
    return jnp.dot(former, latter, precision=highest)

def layer_norm(tensor, norm_gain, norm_shift):
    center = lax.optimization_barrier(jnp.mean(tensor, axis=-1, keepdims=True))
    offset = tensor - center
    spread_sq = lax.optimization_barrier(jnp.mean(offset * offset, axis=-1, keepdims=True))
    return offset * lax.rsqrt(spread_sq + norm_eps) * norm_gain + norm_shift

def apply_swish(tensor):
    return tensor * jax.nn.sigmoid(tensor)

def rotate(tensor, within, head_dim):
    half_dim = head_dim // 2
    frequency = jnp.exp(jnp.arange(half_dim, dtype=jnp.float32) * (-math.log(10000.0) / half_dim))
    angles = within.astype(jnp.float32)[:, None] * frequency[None, :]
    cosine = jnp.cos(angles)[:, None, :]
    sine_part = jnp.sin(angles)[:, None, :]
    shaped = tensor.reshape(tensor.shape[0], -1, head_dim)
    former = shaped[:, :, :half_dim]
    latter = shaped[:, :, half_dim:]
    turned = jnp.concatenate([former * cosine - latter * sine_part, latter * cosine + former * sine_part], axis=2)
    return turned.reshape(tensor.shape)

def depthwise(signal, kernel, utterance):
    tap_count = kernel.shape[1]
    before = tap_count // 2
    after_pad = tap_count - 1 - before
    frame_count = signal.shape[0]
    padded = jnp.pad(signal, ((before, after_pad), (0, 0)))
    labels = jnp.pad(utterance, (before, after_pad), constant_values=-1)
    result = jnp.zeros_like(signal)
    for tap_index in range(tap_count):
        same_utt = labels[tap_index:tap_index + frame_count] == utterance
        shifted = jnp.where(same_utt[:, None], padded[tap_index:tap_index + frame_count], 0.0)
        result = result + shifted * kernel[:, tap_index][None, :]
    return result

def frame_tables(bucket_len, batch_count, utt_lengths, group_rows):
    position = jnp.arange(group_rows, dtype=jnp.int32)[None, :]
    length_col = bucket_len[:, None]
    utterance = position // length_col
    within = position - utterance * length_col
    slot_ids = jnp.arange(utt_lengths.shape[1], dtype=jnp.int32)
    picked = utterance[:, :, None] == slot_ids[None, None, :]
    own_length = lax.optimization_barrier(jnp.sum(jnp.where(picked, utt_lengths[:, None, :], 0), axis=2))
    live_mask = (utterance < batch_count[:, None]) & (within < own_length)
    return (utterance, within, live_mask)

def attend(packed):
    queries, key_rows, value_rows, utterance, live_mask = packed
    scores = jnp.einsum('qhd,khd->hqk', queries, key_rows, precision=highest) * HD ** (-0.5)
    scores = low_back(scores)
    allowed = (utterance[:, None] == utterance[None, :]) & live_mask[None, :]
    scores = jnp.where(allowed[None, :, :], scores, masked_score)
    top_score = lax.optimization_barrier(jnp.max(scores, axis=2, keepdims=True))
    exp_scores = jnp.exp(scores - top_score)
    attn_weights = exp_scores / lax.optimization_barrier(jnp.sum(exp_scores, axis=2, keepdims=True))
    mixed_out = jnp.einsum('hqk,khd->qhd', low(attn_weights), value_rows, precision=highest)
    return jnp.where(live_mask[:, None, None], mixed_out, 0.0)

def forward(float_frames, col_slab, row_slab, norm_params, conv_params, global_utt, within, live_mask):

    def columns(begin, finish):
        return jnp.transpose(col_slab[:, :, begin:finish], (1, 0, 2)).reshape(D, -1)

    def rows_of(begin, finish):
        return row_slab[:, begin:finish, :].reshape(-1, D)
    in_one = columns(0, FFH)
    in_two = columns(FFH, 2 * FFH)
    query_w = columns(2 * FFH, 2 * FFH + CH)
    key_w = columns(2 * FFH + CH, 2 * FFH + 2 * CH)
    value_w = columns(2 * FFH + 2 * CH, 2 * FFH + 3 * CH)
    glu_value_w = columns(2 * FFH + 3 * CH, 2 * FFH + 4 * CH)
    glu_gate_w = columns(2 * FFH + 4 * CH, 2 * FFH + 5 * CH)
    out_one = rows_of(0, FFH)
    out_two = rows_of(FFH, 2 * FFH)
    attn_w = rows_of(2 * FFH, 2 * FFH + CH)
    point_w = rows_of(2 * FFH + CH, 2 * FFH + 2 * CH)
    live_float = live_mask.astype(jnp.float32)[:, None]

    def feed(residual, index, weight_in, weight_out):
        normed = low(layer_norm(residual, norm_params[index], norm_params[index + 5]))
        hidden = low_back(matmul(normed, weight_in))
        active = low(apply_swish(hidden))
        return low_back(matmul(active, weight_out))
    resid_one = float_frames + 0.5 * feed(float_frames, 0, in_one, out_one)
    normed = low(layer_norm(resid_one, norm_params[1], norm_params[6]))
    query_p = low_back(matmul(normed, query_w))
    key_p = low_back(matmul(normed, key_w))
    value_p = low_back(matmul(normed, value_w))
    queries = low(rotate(query_p, within, HD)).reshape(NG, TOK_DEV, HEADS, HD)
    key_rows = low(rotate(key_p, within, HD)).reshape(NG, TOK_DEV, HEADS, HD)
    value_rows = low(value_p).reshape(NG, TOK_DEV, HEADS, HD)
    mixed_out = lax.map(jax.checkpoint(attend), (queries, key_rows, value_rows, global_utt.reshape(NG, TOK_DEV), live_mask.reshape(NG, TOK_DEV)))
    mixed_out = low(low_back(mixed_out.reshape(TOKENS, D)))
    resid_two = resid_one + low_back(matmul(mixed_out, attn_w))
    normed = low(layer_norm(resid_two, norm_params[2], norm_params[7]))
    glu_value = low_back(matmul(normed, glu_value_w))
    glu_gate = low_back(matmul(normed, glu_gate_w))
    gated = glu_value * jax.nn.sigmoid(glu_gate) * live_float
    hidden = depthwise(gated, conv_params[:, :KERNEL], global_utt)
    weighted = hidden * live_float
    frame_total = jnp.sum(live_float)
    center = lax.optimization_barrier(jnp.sum(weighted, axis=0)) / frame_total
    spread_sq = lax.optimization_barrier(jnp.sum(weighted * hidden, axis=0)) / frame_total - center * center
    whitened = (hidden - center) * lax.rsqrt(spread_sq + norm_eps)
    bn_out = whitened * conv_params[:, KERNEL] + conv_params[:, KERNEL + 1]
    active = low(apply_swish(bn_out))
    resid_three = resid_two + low_back(matmul(active, point_w))
    resid_four = resid_three + 0.5 * feed(resid_three, 3, in_two, out_two)
    return layer_norm(resid_four, norm_params[4], norm_params[9])

def bias_factor():
    return step_rate * math.sqrt(1.0 - beta_two ** STEP) / (1.0 - beta_one ** STEP)

def turn_into(left_side, tensor, right_side):
    inner_prod = jnp.einsum('...ab,...ac->...bc', left_side, tensor, precision=highest)
    return jnp.einsum('...bc,...cd->...bd', inner_prod, right_side, precision=highest)

def turn_back(left_side, tensor, right_side):
    inner_prod = jnp.einsum('...ab,...bc->...ac', left_side, tensor, precision=highest)
    return jnp.einsum('...ac,...dc->...ad', inner_prod, right_side, precision=highest)

def soap_step(weight, gradient, moment_one, moment_two, left_side, right_side, factor):
    rotated = turn_into(left_side, gradient, right_side)
    one_new = beta_one * moment_one + (1.0 - beta_one) * gradient
    two_new = beta_two * moment_two + (1.0 - beta_two) * rotated * rotated
    scaled = turn_into(left_side, one_new, right_side) / (jnp.sqrt(two_new) + adam_eps)
    update = turn_back(left_side, scaled, right_side)
    return (weight - factor * update - step_rate * weight_decay * weight, one_new, two_new)

def adam_step(weight, gradient, moment_one, moment_two, factor):
    one_new = beta_one * moment_one + (1.0 - beta_one) * gradient
    two_new = beta_two * moment_two + (1.0 - beta_two) * gradient * gradient
    return (weight - factor * one_new / (jnp.sqrt(two_new) + adam_eps), one_new, two_new)

def reference(frames, out_grad, bucket_len, batch_count, utt_lengths, owner_slots, masters, first_moment, second_moment, left_basis, right_basis, norm_params, norm_first, norm_second, conv_params, conv_first, conv_second):
    utterance, within, live_mask = frame_tables(bucket_len, batch_count, utt_lengths, TOK_DEV)
    global_utt = (utterance + (jnp.arange(NG, dtype=jnp.int32) * MAXU)[:, None]).reshape(-1)
    within = within.reshape(-1)
    live_mask = live_mask.reshape(-1)
    inverse = jnp.zeros((SLOTS,), jnp.int32).at[owner_slots].set(jnp.arange(SLOTS, dtype=jnp.int32))
    working = low(masters)
    blocks = working[:, inverse[:NBLK]]
    col_slab = jnp.transpose(blocks[:, :NC], (0, 2, 1, 3)).reshape(NHG, D, NC * BLOCKW)
    row_slab = jnp.transpose(blocks[:, NC:], (0, 1, 3, 2)).reshape(NHG, NR * BLOCKW, D)

    def wrapped(float_frames, col_weights, row_weights, norm_weights, conv_weights):
        return forward(float_frames, col_weights, row_weights, norm_weights, conv_weights, global_utt, within, live_mask)
    layer_out, backward = jax.vjp(wrapped, frames.astype(jnp.float32), col_slab, row_slab, norm_params, conv_params)
    frames_grad, col_grad, row_grad, norm_grads, conv_grads = backward(out_grad.astype(jnp.float32))
    col_blocks = jnp.transpose(col_grad.reshape(NHG, D, NC, BLOCKW), (0, 2, 1, 3))
    row_blocks = jnp.transpose(row_grad.reshape(NHG, NR, BLOCKW, D), (0, 1, 3, 2))
    grads_all = jnp.concatenate([col_blocks, row_blocks], axis=1)
    grads_all = jnp.pad(grads_all, ((0, 0), (0, SLOTS - NBLK), (0, 0), (0, 0)))
    slotted = grads_all[:, owner_slots]
    factor = bias_factor()
    new_masters, new_first, new_second = soap_step(masters, slotted, first_moment, second_moment, left_basis, right_basis, factor)
    new_norms, norm_first_new, norm_second_new = adam_step(norm_params, norm_grads, norm_first, norm_second, 10.0 * factor)
    new_conv, conv_first_new, conv_second_new = adam_step(conv_params, conv_grads, conv_first, conv_second, 4.0 * factor)
    return (layer_out.astype(jnp.bfloat16), frames_grad, new_masters, new_first, new_second, norm_grads, new_norms, norm_first_new, norm_second_new, new_conv, conv_first_new, conv_second_new)
```

```python
import functools
import math

import jax
import jax.numpy as jnp
import numpy as np
from jax import lax
from jax.experimental import pallas as pl
from jax.experimental.pallas import tpu as pltpu
from jax.sharding import PartitionSpec as P

D = 512
FF = 2048
HD = 64
KERNEL = 32
BLOCKW = 64
STEP = 10
LONGEST = 1024
HALO = 16

beta_one = 0.9
beta_two = 0.95
step_rate = 0.05
weight_decay = 0.01
adam_eps = 1e-08
norm_eps = 1e-05
masked_score = -1e30
FACTOR = step_rate * math.sqrt(1.0 - beta_two**STEP) / (1.0 - beta_one**STEP)

F32 = jnp.float32
BF16 = jnp.bfloat16
MESH = pl.DeviceIdType.MESH
ANY = pl.BlockSpec(memory_space=pl.ANY)
VM = pl.BlockSpec(memory_space=pltpu.VMEM)
SM = pl.BlockSpec(memory_space=pltpu.SMEM)
MIB = 1 << 20


def params(mib, collective_id=None):
    if collective_id is None:
        return pltpu.CompilerParams(vmem_limit_bytes=mib * MIB)
    return pltpu.CompilerParams(
        vmem_limit_bytes=mib * MIB, collective_id=collective_id, has_side_effects=True
    )


class Copies:
    def __init__(self, sends):
        self.sends = sends
        self.used = 0
        self.open = []

    def send(self, src, dst, recv_sem, device):
        copy = pltpu.make_async_remote_copy(
            src_ref=src,
            dst_ref=dst,
            send_sem=self.sends.at[self.used],
            recv_sem=recv_sem,
            device_id=device,
            device_id_type=MESH,
        )
        copy.start()
        self.used += 1
        self.open.append(copy)

    def finish(self):
        for copy in self.open:
            copy.wait_send()


def arrived(ref, sem):
    pltpu.make_async_copy(ref, ref, sem).wait()


def greet(devices):
    barrier = pltpu.get_barrier_semaphore()
    for device in devices:
        pl.semaphore_signal(barrier, inc=1, device_id=device, device_id_type=MESH)
    pl.semaphore_wait(barrier, len(devices))


class Place:
    def __init__(self, ndp, nh):
        self.ndp, self.nh, self.nchip = ndp, nh, ndp // 2
        self.dp = lax.axis_index("dp")
        self.z = lax.axis_index("head")
        self.core = self.dp % 2
        self.chip = self.dp // 2
        self.group_core = self.z % 2
        self.part = 2 * (self.z // 2) + self.core

    def of_part(self, part):
        return (self.chip * 2 + part % 2, 2 * (part // 2) + self.group_core)

    def core_peer(self):
        return (self.chip * 2 + 1 - self.core, self.z)

    def swap_peer(self):
        return (self.chip * 2 + 1 - self.core, self.part)

    def x_chip(self):
        return self.chip + 1 - 2 * (self.chip % 2)

    def y_chip(self):
        return (self.chip + 2) % 4


def gather_kernel(ndp, nh, spd, own, frames, ograd, ints, conv, full, frames_o, ograd_o, ints_o, conv_o, sends, recvs, extra, local):
    me = Place(ndp, nh)
    dp, z, core, chip, nchip = me.dp, me.z, me.core, me.chip, me.nchip

    def shard(h, ch, c):
        return full.at[h, pl.ds((ch * 2 + c) * spd, spd)]

    def sem(h, ch, c, half=0):
        return recvs.at[h * ndp + ch * 2 + c, half]

    peer = me.core_peer()
    swap = me.core != me.z % 2
    columns = [(dp, (z + i) % nh) for i in range(1, nh)]
    square = nchip == 4
    if square:
        planes = [(me.x_chip() * 2 + core, z), (me.y_chip() * 2 + core, z)]
    else:
        planes = [(((chip + i) % nchip) * 2 + core, z) for i in range(1, nchip)]
    barrier = pltpu.get_barrier_semaphore()
    near = [peer] + columns + planes
    for device in near:
        pl.semaphore_signal(barrier, inc=1, device_id=device, device_id_type=MESH)

    @pl.when(swap)
    def _():
        pl.semaphore_signal(barrier, inc=1, device_id=me.swap_peer(), device_id_type=MESH)

    pl.semaphore_wait(barrier, len(near) + (core + z) % 2)

    copies = Copies(sends)
    mine = shard(z, chip, core)
    for device in columns:
        copies.send(own, mine, sem(z, chip, core), device)
    for device in planes:
        copies.send(own, mine, sem(z, chip, core), device)
    copies.send(own, mine, sem(z, chip, core), peer)
    keep = [
        pltpu.make_async_copy(own, mine, local.at[0]),
        pltpu.make_async_copy(ints, ints_o.at[core], local.at[1]),
        pltpu.make_async_copy(conv, conv_o.at[z], local.at[2]),
    ]
    for copy in keep:
        copy.start()
    copies.send(ints, ints_o.at[core], extra.at[0], peer)
    for device in columns:
        copies.send(conv, conv_o.at[z], extra.at[3 + z], device)

    @pl.when(swap)
    def _():
        for i, (src, dst) in enumerate(((frames, frames_o), (ograd, ograd_o))):
            pltpu.make_async_remote_copy(
                src_ref=src, dst_ref=dst, send_sem=local.at[3 + i], recv_sem=extra.at[1 + i],
                device_id=me.swap_peer(), device_id_type=MESH,
            ).start()

    @pl.when(jnp.logical_not(swap))
    def _():
        for i, (src, dst) in enumerate(((frames, frames_o), (ograd, ograd_o))):
            pltpu.make_async_copy(src, dst, local.at[3 + i]).start()

    def column(i):
        h = (z + nh - i) % nh
        if i > 0:
            arrived(shard(h, chip, core), sem(h, chip, core))
            for device in planes:
                copies.send(shard(h, chip, core), shard(h, chip, core), sem(h, chip, core), device)
            copies.send(shard(h, chip, core), shard(h, chip, core), sem(h, chip, core), peer)

    def beside(i):
        h = (z + nh - i) % nh
        if not square:
            for k in range(1, nchip):
                ch = (chip + k) % nchip
                arrived(shard(h, ch, core), sem(h, ch, core))
                copies.send(shard(h, ch, core), shard(h, ch, core), sem(h, ch, core), peer)
            return
        half = spd // 2
        for side, (ch, device) in enumerate(((me.x_chip(), planes[1]), (me.y_chip(), planes[0]))):
            arrived(shard(h, ch, core), sem(h, ch, core))
            piece = full.at[h, pl.ds((ch * 2 + core) * spd + side * half, half)]
            copies.send(piece, piece, sem(h, ch, core, side), device)
            copies.send(shard(h, ch, core), shard(h, ch, core), sem(h, ch, core), peer)

    def across(i):
        if not square:
            return
        h = (z + nh - i) % nh
        half = spd // 2
        ch = 3 - chip
        for side in range(2):
            piece = full.at[h, pl.ds((ch * 2 + core) * spd + side * half, half)]
            arrived(piece, sem(h, ch, core, side))
        copies.send(shard(h, ch, core), shard(h, ch, core), sem(h, ch, core), peer)

    for i in range(nh + 2):
        if i < nh:
            column(i)
        if 0 <= i - 1 < nh:
            beside(i - 1)
        if i >= 2:
            across(i - 2)
    for i in range(nh):
        h = (z + nh - i) % nh
        for k in range(nchip):
            ch = (chip + k) % nchip
            arrived(shard(h, ch, 1 - core), sem(h, ch, 1 - core))
    arrived(ints_o.at[1 - core], extra.at[0])
    for i in range(1, nh):
        h = (z + nh - i) % nh
        arrived(conv_o.at[h], extra.at[3 + h])

    @pl.when(swap)
    def _():
        arrived(frames_o, extra.at[1])
        arrived(ograd_o, extra.at[2])

    for i, ref in enumerate((frames, ograd)):
        arrived(ref, local.at[3 + i])
    for copy in keep:
        copy.wait()
    copies.finish()


def gather(ndp, nh, own, frames, ograd, ints, conv):
    spd = own.shape[0]
    nchip = ndp // 2
    plane = 2 if nchip == 4 else nchip - 1
    halves = 2 * nh if nchip == 4 else 0
    count = (nh - 1) + nh * (plane + 1) + (nh * (nchip - 1)) + halves + 1 + (nh - 1)
    shapes = [
        jax.ShapeDtypeStruct((nh, ndp * spd, BLOCKW, D), BF16),
        jax.ShapeDtypeStruct(frames.shape, BF16),
        jax.ShapeDtypeStruct(ograd.shape, BF16),
        jax.ShapeDtypeStruct((2,) + ints.shape, jnp.int32),
        jax.ShapeDtypeStruct((nh,) + conv.shape, F32),
    ]
    dma = pltpu.SemaphoreType.DMA
    return pl.pallas_call(
        functools.partial(gather_kernel, ndp, nh, spd),
        out_shape=shapes,
        in_specs=[ANY] * 5,
        out_specs=[ANY] * 5,
        scratch_shapes=[dma((count,)), dma((nh * ndp, 2)), dma((3 + nh,)), dma((5,))],
        compiler_params=params(8, 1),
        name="gather",
    )(own, frames, ograd, ints, conv)


def totals_step(me, small, first, second, copies, sem1, sem2, local):
    ndp, nh = me.ndp, me.nh

    def one():
        for i in range(1, ndp):
            copies.send(small, first.at[me.dp], sem1.at[me.dp], ((me.dp + i) % ndp, me.z))
        first[me.dp] = small[...]

    def two():
        for i in range(1, ndp):
            src = (me.dp + i) % ndp
            arrived(first.at[src], sem1.at[src])
        total = first[0]
        for i in range(1, ndp):
            total = total + first[i]
        second[me.z] = total
        for i in range(1, nh):
            copies.send(second.at[me.z], second.at[me.z], sem2.at[me.z], (me.dp, (me.z + i) % nh))

    def three():
        for i in range(1, nh):
            src = (me.z + i) % nh
            arrived(second.at[src], sem2.at[src])
        total = second[0]
        for i in range(1, nh):
            total = total + second[i]
        return total

    return one, two, three


def totals_peers(me):
    return [((me.dp + i) % me.ndp, me.z) for i in range(1, me.ndp)] + [
        (me.dp, (me.z + i) % me.nh) for i in range(1, me.nh)
    ]


def totals_kernel(ndp, nh, halos, *refs):
    me = Place(ndp, nh)
    small = refs[0]
    edges = refs[1 : 1 + halos]
    out = refs[1 + halos]
    edges_o = refs[2 + halos : 2 + 2 * halos]
    first, second, sends, sem1, sem2, hsem = refs[2 + 2 * halos :]
    greet(totals_peers(me))
    copies = Copies(sends)
    one, two, three = totals_step(me, small, first, second, copies, sem1, sem2, None)
    one()
    for i in range(halos):
        send_edges(me, edges[i], edges_o[i], copies, hsem.at[2 * i], hsem.at[2 * i + 1])
    two()
    out[...] = three()
    for i in range(halos):
        arrived(edges_o[i].at[pl.ds(0, HALO)], hsem.at[2 * i])
        arrived(edges_o[i].at[pl.ds(HALO, HALO)], hsem.at[2 * i + 1])
    copies.finish()


def window(me, rows):
    span = LONGEST // rows
    at = me.part % span
    return span, at, me.part - at


def send_edges(me, src, dst, copies, sem_before, sem_after):
    rows = src.shape[0]
    span, at, base = window(me, rows)
    after = me.of_part(base + (at + 1) % span)
    before = me.of_part(base + (at + span - 1) % span)
    copies.send(src.at[pl.ds(rows - HALO, HALO)], dst.at[pl.ds(0, HALO)], sem_before, after)
    copies.send(src.at[pl.ds(0, HALO)], dst.at[pl.ds(HALO, HALO)], sem_after, before)


def totals(ndp, nh, collective_id, small, edges=()):
    dma = pltpu.SemaphoreType.DMA
    n = len(edges)
    halo = [jax.ShapeDtypeStruct((2 * HALO, D), e.dtype) for e in edges]
    return pl.pallas_call(
        functools.partial(totals_kernel, ndp, nh, n),
        out_shape=[jax.ShapeDtypeStruct(small.shape, F32)] + halo,
        in_specs=[VM] + [ANY] * n,
        out_specs=[VM] + [ANY] * n,
        scratch_shapes=[
            pltpu.VMEM((ndp,) + small.shape, F32),
            pltpu.VMEM((nh,) + small.shape, F32),
            dma((ndp + nh - 2 + 2 * n,)),
            dma((ndp,)),
            dma((nh,)),
            dma((2 * n + 1,)),
        ],
        compiler_params=params(16, collective_id),
        name=f"totals_{collective_id}",
    )(small, *edges)


def keys_kernel(ndp, nh, kv, q, x1, kv_o, q_o, x1_o, sends, recvs, local):
    me = Place(ndp, nh)
    rows = kv.shape[0]
    span, at, base = window(me, rows)
    peers = [me.of_part(base + (at + i) % span) for i in range(1, span)]
    greet(peers)
    copies = Copies(sends)
    place = kv_o.at[pl.ds(at * rows, rows)]
    for device in peers:
        copies.send(kv, place, recvs.at[at], device)
    own = pltpu.make_async_copy(kv, place, local.at[0])
    own.start()
    for i, (src, dst) in enumerate(((q, q_o), (x1, x1_o))):
        send_edges(me, src, dst, copies, recvs.at[span + 2 * i], recvs.at[span + 2 * i + 1])
    for i in range(1, span):
        other = (at + i) % span
        arrived(kv_o.at[pl.ds(other * rows, rows)], recvs.at[other])
    for i, dst in enumerate((q_o, x1_o)):
        arrived(dst.at[pl.ds(0, HALO)], recvs.at[span + 2 * i])
        arrived(dst.at[pl.ds(HALO, HALO)], recvs.at[span + 2 * i + 1])
    own.wait()
    copies.finish()


def keys(ndp, nh, kv, q, x1):
    span = LONGEST // kv.shape[0]
    dma = pltpu.SemaphoreType.DMA
    return pl.pallas_call(
        functools.partial(keys_kernel, ndp, nh),
        out_shape=[
            jax.ShapeDtypeStruct((LONGEST, 2 * D), BF16),
            jax.ShapeDtypeStruct((2 * HALO, D), BF16),
            jax.ShapeDtypeStruct((2 * HALO, D), F32),
        ],
        in_specs=[ANY] * 3,
        out_specs=[ANY] * 3,
        scratch_shapes=[dma((span + 3,)), dma((span + 4,)), dma((1,))],
        compiler_params=params(8, 2),
        name="keys",
    )(kv, q, x1)


def key_grads_kernel(ndp, nh, part, out, sends, recvs):
    me = Place(ndp, nh)
    rows = out.shape[1]
    span, at, base = window(me, rows)
    greet([me.of_part(base + (at + i) % span) for i in range(1, span)])
    copies = Copies(sends)
    for i in range(1, span):
        other = (at + i) % span
        copies.send(part.at[pl.ds(other * rows, rows)], out.at[i - 1], recvs.at[i - 1], me.of_part(base + other))
    for i in range(1, span):
        arrived(out.at[i - 1], recvs.at[i - 1])
    copies.finish()


def key_grads(ndp, nh, part, rows):
    span = LONGEST // rows
    dma = pltpu.SemaphoreType.DMA
    return pl.pallas_call(
        functools.partial(key_grads_kernel, ndp, nh),
        out_shape=jax.ShapeDtypeStruct((span - 1, rows, 2 * D), BF16),
        in_specs=[ANY],
        out_specs=ANY,
        scratch_shapes=[dma((span - 1,)), dma((span - 1,))],
        compiler_params=params(8, 5),
        name="key_grads",
    )(part)


def scatter_kernel(ndp, nh, spd, grads, small, out_v, fgrad_v, owned, small_o, out_o, fgrad_o, part, cores, side_x, side_y, half_x, half_y, zrecv, first, second, sends, csem, psem, xsem, zsem, sem1, sem2, esem, local):
    me = Place(ndp, nh)
    dp, z, core, chip, nchip = me.dp, me.z, me.core, me.chip, me.nchip
    square = nchip == 4
    peer = me.core_peer()
    swap = me.core != me.z % 2
    half = spd // 2
    barrier = pltpu.get_barrier_semaphore()
    near = totals_peers(me)
    for device in near:
        pl.semaphore_signal(barrier, inc=1, device_id=device, device_id_type=MESH)

    @pl.when(swap)
    def _():
        pl.semaphore_signal(barrier, inc=1, device_id=me.swap_peer(), device_id_type=MESH)

    pl.semaphore_wait(barrier, len(near) + (core + z) % 2)
    copies = Copies(sends)
    order = [(z + i + 1) % nh for i in range(nh)]
    if square:
        chips = [3 - chip, me.x_chip(), me.y_chip(), chip]
    else:
        chips = [(chip + i + 1) % nchip for i in range(nchip)]
    loads = {}
    for i, h in enumerate(order):
        for k, ch in enumerate(chips):
            copies.send(grads.at[h, pl.ds((ch * 2 + 1 - core) * spd, spd)], cores.at[i, k], csem.at[i, k], peer)
            load = pltpu.make_async_copy(grads.at[h, pl.ds((ch * 2 + core) * spd, spd)], part.at[i, k], psem.at[i, k])
            load.start()
            loads[i, k] = load
    one, two, three = totals_step(me, small, first, second, copies, sem1, sem2, None)
    one()

    @pl.when(swap)
    def _():
        for i, (src, dst) in enumerate(((out_v, out_o), (fgrad_v, fgrad_o))):
            pltpu.make_async_remote_copy(
                src_ref=src, dst_ref=dst, send_sem=local.at[i], recv_sem=esem.at[i],
                device_id=me.swap_peer(), device_id_type=MESH,
            ).start()

    @pl.when(jnp.logical_not(swap))
    def _():
        for i, (src, dst) in enumerate(((out_v, out_o), (fgrad_v, fgrad_o))):
            pltpu.make_async_copy(src, dst, local.at[i]).start()

    def add(i, k, others, lo=0, n=spd):
        @pl.loop(0, n)
        def _(s):
            total = part[i, k, lo + s].astype(F32)
            for other in others:
                total = total + other(s).astype(F32)
            part[i, k, lo + s] = total.astype(BF16)

    def meet(i, k):
        loads[i, k].wait()
        arrived(cores.at[i, k], csem.at[i, k])

    planes = [(me.x_chip() * 2 + core, z), (me.y_chip() * 2 + core, z)]

    def stage_a(i):
        if square:
            meet(i, 0)
            add(i, 0, [lambda s: cores[i, 0, s]])
            copies.send(part.at[i, 0, pl.ds(0, half)], half_x.at[i], xsem.at[i, 0], planes[0])
            copies.send(part.at[i, 0, pl.ds(half, half)], half_y.at[i], xsem.at[i, 1], planes[1])
        else:
            for k in range(nchip - 1):
                meet(i, k)
                add(i, k, [lambda s: cores[i, k, s]])
                copies.send(part.at[i, k], side_x.at[i, k], xsem.at[i, k], (chips[k] * 2 + core, z))

    def stage_b(i):
        if not square:
            return
        meet(i, 1)
        add(i, 1, [lambda s: cores[i, 1, s]], 0, half)
        arrived(half_y.at[i], xsem.at[i, 1])
        add(i, 1, [lambda s: cores[i, 1, half + s], lambda s: half_y[i, s]], half, half)
        copies.send(part.at[i, 1], side_x.at[i, 0], xsem.at[i, 2], planes[0])
        meet(i, 2)
        add(i, 2, [lambda s: cores[i, 2, half + s]], half, half)
        arrived(half_x.at[i], xsem.at[i, 0])
        add(i, 2, [lambda s: cores[i, 2, s], lambda s: half_x[i, s]], 0, half)
        copies.send(part.at[i, 2], side_y.at[i], xsem.at[i, 3], planes[1])

    last = nchip - 1

    def stage_c(i):
        meet(i, last)
        if square:
            arrived(side_x.at[i, 0], xsem.at[i, 2])
            arrived(side_y.at[i], xsem.at[i, 3])
            others = [lambda s: cores[i, last, s], lambda s: side_x[i, 0, s], lambda s: side_y[i, s]]
        else:
            others = [lambda s: cores[i, last, s]]
            for k in range(nchip - 1):
                arrived(side_x.at[i, k], xsem.at[i, k])
                others.append(lambda s, k=k: side_x[i, k, s])
        add(i, last, others)
        if i < nh - 1:
            copies.send(part.at[i, last], zrecv.at[i], zsem.at[i], (dp, order[i]))

    for i in range(nh + 2):
        if i < nh:
            stage_a(i)
        if 0 <= i - 1 < nh:
            stage_b(i - 1)
        if i == 1:
            two()
        if i >= 2:
            stage_c(i - 2)
    small_o[...] = three()
    for i in range(nh - 1):
        arrived(zrecv.at[i], zsem.at[i])

    @pl.loop(0, spd)
    def _(s):
        total = part[nh - 1, last, s].astype(F32)
        for i in range(nh - 1):
            total = total + zrecv[i, s].astype(F32)
        owned[s] = total

    @pl.when(swap)
    def _():
        arrived(out_o, esem.at[0])
        arrived(fgrad_o, esem.at[1])

    arrived(out_v, local.at[0])
    arrived(fgrad_v, local.at[1])
    copies.finish()


def scatter(ndp, nh, grads, small, out_v, fgrad_v):
    spd = grads.shape[1] // ndp
    nchip = ndp // 2
    square = nchip == 4
    dma = pltpu.SemaphoreType.DMA
    block = (spd, BLOCKW, D)
    halfb = (max(spd // 2, 1), BLOCKW, D)
    sides = 1 if square else nchip - 1
    sent = nh * nchip + (ndp - 1) + (nh - 1) + (nh * 4 if square else nh * (nchip - 1)) + (nh - 1)
    return pl.pallas_call(
        functools.partial(scatter_kernel, ndp, nh, spd),
        out_shape=[
            jax.ShapeDtypeStruct(block, F32),
            jax.ShapeDtypeStruct(small.shape, F32),
            jax.ShapeDtypeStruct(out_v.shape, out_v.dtype),
            jax.ShapeDtypeStruct(fgrad_v.shape, fgrad_v.dtype),
        ],
        in_specs=[ANY, VM, ANY, ANY],
        out_specs=[VM, VM, ANY, ANY],
        scratch_shapes=[
            pltpu.VMEM((nh, nchip) + block, BF16),
            pltpu.VMEM((nh, nchip) + block, BF16),
            pltpu.VMEM((nh, sides) + block, BF16),
            pltpu.VMEM((nh,) + block, BF16),
            pltpu.VMEM((nh,) + halfb, BF16),
            pltpu.VMEM((nh,) + halfb, BF16),
            pltpu.VMEM((nh - 1,) + block, BF16),
            pltpu.VMEM((ndp,) + small.shape, F32),
            pltpu.VMEM((nh,) + small.shape, F32),
            dma((sent,)),
            dma((nh, nchip)),
            dma((nh, nchip)),
            dma((nh, max(4, nchip))),
            dma((nh,)),
            dma((ndp,)),
            dma((nh,)),
            dma((2,)),
            dma((2,)),
        ],
        compiler_params=params(56, 6),
        name="scatter",
    )(grads, small, out_v, fgrad_v)


def nn(a, b):
    return jnp.dot(a, b, preferred_element_type=F32)


def nt(a, b):
    return lax.dot_general(a, b, (((1,), (1,)), ((), ())), preferred_element_type=F32)


def tn(a, b):
    return lax.dot_general(a, b, (((0,), (0,)), ((), ())), preferred_element_type=F32)


def sigmoid(v):
    return 0.5 * jnp.tanh(0.5 * v) + 0.5


def slope_of(v, sig):
    return sig * (1.0 + v * (1.0 - sig))


class Blocks:
    def __init__(self, nh):
        self.nh = nh
        ff, ch = FF // nh // BLOCKW, D // nh // BLOCKW
        self.ff, self.ch = ff, ch
        self.in_one, self.in_two = 0, ff
        self.query = 2 * ff
        self.key = self.query + ch
        self.value = self.key + ch
        self.conv_value = self.value + ch
        self.conv_gate = self.conv_value + ch
        rows = self.conv_gate + ch
        self.out_one, self.out_two = rows, rows + ff
        self.attn = rows + 2 * ff
        self.point = self.attn + ch
        self.total = self.point + ch


def fetch(full, inv, dst, sem, base, count, part, row):
    for j in range(count):
        pltpu.make_async_copy(
            full.at[part, inv[base + j]], dst.at[pl.ds(row + j * BLOCKW, BLOCKW)], sem
        ).start()


def fetch_all(full, inv, dst, sem, base, count, nh, row=0):
    for part in range(nh):
        fetch(full, inv, dst, sem, base, count, part, row + part * count * BLOCKW)


def landed(dst, sem):
    pltpu.make_async_copy(dst, dst, sem).wait()


def put(grads, inv, src, sem, base, count, part, row):
    for j in range(count):
        pltpu.make_async_copy(
            src.at[pl.ds(row + j * BLOCKW, BLOCKW)], grads.at[part, inv[base + j]], sem
        ).start()


def put_all(grads, inv, src, sem, base, count, nh, row=0):
    for part in range(nh):
        put(grads, inv, src, sem, base, count, part, row + part * count * BLOCKW)


def tables(meta, frame):
    length, batch = meta[0], meta[1]
    utterance = jnp.zeros_like(frame)
    for i in range(1, 8):
        utterance = utterance + (frame >= i * length).astype(jnp.int32)
    within = frame - utterance * length
    own = jnp.zeros_like(frame)
    for i in range(8):
        own = jnp.where(utterance == i, meta[2 + i], own)
    live = (utterance < batch) & (within < own)
    return utterance, within, live


def live_rows(meta, start, count):
    frame = start + lax.broadcasted_iota(jnp.int32, (count, 1), 0)
    return tables(meta, frame)[2].astype(F32)


def hat(x):
    center = jnp.mean(x, axis=1, keepdims=True)
    offset = x - center
    spread = lax.rsqrt(jnp.mean(offset * offset, axis=1, keepdims=True) + norm_eps)
    return offset * spread, spread


def norm(x, norms, i):
    return hat(x)[0] * norms[i : i + 1, :] + norms[i + 5 : i + 6, :]


def norm_back(x, grad, gain):
    xhat, spread = hat(x)
    scaled = grad * gain
    inner = scaled - jnp.mean(scaled, axis=1, keepdims=True) - xhat * jnp.mean(scaled * xhat, axis=1, keepdims=True)
    return spread * inner, jnp.sum(grad * xhat, axis=0, keepdims=True), jnp.sum(grad, axis=0, keepdims=True)


BAND = 64


def bands(rows, body, init=()):
    return lax.fori_loop(0, rows // BAND, lambda i, c: body(pl.ds(pl.multiple_of(i * BAND, BAND), BAND), i, c), init)


def partner(x):
    lane = lax.broadcasted_iota(jnp.int32, x.shape, 1) % HD
    return jnp.where(lane < HD // 2, pltpu.roll(x, 128 - HD // 2, 1), pltpu.roll(x, HD // 2, 1))


def turn(x, cos, sin, sign):
    parts = []
    for i in range(D // 128):
        piece = x[:, i * 128 : (i + 1) * 128]
        parts.append(piece * cos + partner(piece) * (sign * sin))
    return jnp.concatenate(parts, axis=1)


def rope_tables():
    freq = np.exp(np.arange(HD // 2, dtype=np.float32) * np.float32(-math.log(10000.0) / (HD // 2)))
    angle = np.arange(LONGEST, dtype=np.float32)[:, None] * freq[None, :].astype(np.float32)
    cos = np.tile(np.cos(angle), (1, 4)).astype(np.float32)
    sin = np.sin(angle).astype(np.float32)
    return cos, np.concatenate([-sin, sin, -sin, sin], axis=1)


def place_of(meta, i):
    return pl.multiple_of(lax.rem(meta[10] + i * BAND, meta[0]), BAND)


def feed(n_ref, w_in, w_out, acc_ref, sem, sem2, nh):
    unit = FF // nh
    for part in range(nh):
        rows = pl.ds(part * unit, unit)
        landed(w_in.at[rows], sem.at[part])
        pre = nt(n_ref[...], w_in[rows, :])
        act = (pre * sigmoid(pre)).astype(BF16)
        landed(w_out.at[rows], sem2.at[part])
        if part == 0:
            acc_ref[...] = nn(act, w_out[rows, :])
        else:
            acc_ref[...] += nn(act, w_out[rows, :])


def feed_back(n_ref, gb_ref, w_in, w_out, acc_ref, g_in, g_out, grads, inv, base_in, base_out, sem_in, sem_out, count, nh):
    unit = FF // nh

    def body(part, carry):
        rows = pl.ds(pl.multiple_of(part * unit, unit), unit)
        n, gb, win, wout = n_ref[...], gb_ref[...], w_in[rows, :], w_out[rows, :]
        pre = nt(win, n)
        sig = sigmoid(pre)
        act = (pre * sig).astype(BF16)
        dpre = (nt(wout, gb) * slope_of(pre, sig)).astype(BF16)
        g_out[rows, :] = nn(act, gb).astype(BF16)
        g_in[rows, :] = nn(dpre, n).astype(BF16)
        acc_ref[...] += tn(dpre, win)
        put(grads, inv, g_out, sem_out, base_out, count, part, part * unit)
        put(grads, inv, g_in, sem_in, base_in, count, part, part * unit)
        return carry

    acc_ref[...] = jnp.zeros_like(acc_ref)
    lax.fori_loop(0, nh, body, 0)


def front_kernel(nh, meta, inv, frames, norms, cos, sin, full, x1, q, kv, w_in, w_out, w_qkv, n_ref, acc, sem, sem2, sem3):
    b = Blocks(nh)
    rows = frames.shape[0]
    unit = FF // nh
    for part in range(nh):
        fetch(full, inv, w_in, sem.at[part], b.in_one, b.ff, part, part * unit)
        fetch(full, inv, w_out, sem2.at[part], b.out_one, b.ff, part, part * unit)
    for i, base in enumerate((b.query, b.key, b.value)):
        fetch_all(full, inv, w_qkv, sem3.at[0], base, b.ch, nh, i * D)

    def first(at, i, c):
        n_ref[at, :] = norm(frames[at, :].astype(F32), norms, 0).astype(BF16)
        return c

    bands(rows, first)
    feed(n_ref, w_in, w_out, acc, sem, sem2, nh)

    def second(at, i, c):
        x = frames[at, :].astype(F32) + 0.5 * acc[at, :]
        x1[at, :] = x
        n_ref[at, :] = norm(x, norms, 1).astype(BF16)
        return c

    bands(rows, second)
    landed(w_qkv, sem3.at[0])
    for j, (dst, lo) in enumerate(((q, 0), (kv, 0), (kv, D))):
        acc[...] = nt(n_ref[...], w_qkv[j * D : (j + 1) * D, :])

        def third(at, i, c):
            x = acc[at, :]
            if j < 2:
                p = pl.ds(place_of(meta, i), BAND)
                x = turn(x, cos[p, :], sin[p, :], 1.0)
            dst[at, lo : lo + D] = x.astype(BF16)
            return c

        bands(rows, third)


def front(nh, meta, inv, frames, norms, cos, sin, full):
    rows = frames.shape[0]
    dma = pltpu.SemaphoreType.DMA
    return pl.pallas_call(
        functools.partial(front_kernel, nh),
        out_shape=[
            jax.ShapeDtypeStruct((rows, D), F32),
            jax.ShapeDtypeStruct((rows, D), BF16),
            jax.ShapeDtypeStruct((rows, 2 * D), BF16),
        ],
        in_specs=[SM, SM, VM, VM, VM, VM, ANY],
        out_specs=[VM, VM, VM],
        scratch_shapes=[
            pltpu.VMEM((FF, D), BF16),
            pltpu.VMEM((FF, D), BF16),
            pltpu.VMEM((3 * D, D), BF16),
            pltpu.VMEM((rows, D), BF16),
            pltpu.VMEM((rows, D), F32),
            dma((nh,)),
            dma((nh,)),
            dma((1,)),
        ],
        compiler_params=params(44),
        name="front",
    )(meta, inv, frames, norms, cos, sin, full)


def fill_chunk(meta, src, chunk, k, start):
    lead = lax.rem(start + k * 256, meta[0]) != 0
    trail = lax.rem(start + (k + 1) * 256, meta[0]) != 0
    chunk[0:HALO, :] = jnp.where(lead, src[k * 256 : k * 256 + HALO, :], 0.0)
    chunk[HALO : HALO + 256, :] = src[k * 256 + HALO : k * 256 + HALO + 256, :]
    chunk[HALO + 256 :, :] = jnp.where(trail, src[k * 256 + HALO + 256 : k * 256 + 2 * HALO + 256, :], 0.0)


def attend_kernel(nh, meta, inv, q, kvw, x1, qh, x1h, norms, taps, full, o_o, lse_o, x2_o, gated_o, h_o, sums_o, w_attn, w_glu, q_ext, o_ext, x_ext, bias, n_ref, val, gate, chunk, lse_s, sem):
    b = Blocks(nh)
    rows = q.shape[0]
    ext = rows + 2 * HALO
    start = meta[10]
    fetch_all(full, inv, w_attn, sem.at[0], b.attn, b.ch, nh)
    for i, base in enumerate((b.conv_value, b.conv_gate)):
        fetch_all(full, inv, w_glu, sem.at[1], base, b.ch, nh, i * D)
    q_ext[0:HALO, :] = qh[0:HALO, :]
    q_ext[HALO : HALO + rows, :] = q[...]
    q_ext[HALO + rows :, :] = qh[HALO:, :]
    x_ext[0:HALO, :] = x1h[0:HALO, :]
    x_ext[HALO : HALO + rows, :] = x1[...]
    x_ext[HALO + rows :, :] = x1h[HALO:, :]
    base = start - lax.rem(start, LONGEST)
    key_frame = base + lax.broadcasted_iota(jnp.int32, (1, LONGEST), 1)
    ukey, _, lkey = tables(meta, key_frame)
    ukey = jnp.where(lkey, ukey, -1)
    query_frame = start - HALO + lax.broadcasted_iota(jnp.int32, (ext, 1), 0)
    uquery, _, lquery = tables(meta, query_frame)
    live = lquery.astype(F32)
    bias[...] = jnp.where(ukey == uquery, 0.0, masked_score)
    half = ext // 2
    head_lane = lax.broadcasted_iota(jnp.int32, (half, 128), 1)

    for pair in range(D // 128):
        lanes = slice(pair * 128, (pair + 1) * 128)
        kp = kvw[:, lanes]
        vp = kvw[:, D + pair * 128 : D + (pair + 1) * 128]
        for blk in range(2):
            at = slice(blk * half, (blk + 1) * half)
            qp = q_ext[at, lanes] * 0.125
            outs = []
            for hh in range(2):
                mine = head_lane < HD if hh == 0 else head_lane >= HD
                qm = jnp.where(mine, qp, jnp.zeros_like(qp))
                s = nt(qm, kp) + bias[at, :]
                top = jnp.max(s, axis=1, keepdims=True)
                e = jnp.exp(s - top)
                total = jnp.sum(e, axis=1, keepdims=True)
                outs.append(nn(e.astype(BF16), vp) * (1.0 / total))
                lse_s[at, pair * 2 + hh : pair * 2 + hh + 1] = top + jnp.log(total)
            o = jnp.where(head_lane < HD, outs[0], outs[1]) * live[at, :]
            o_ext[at, lanes] = o.astype(BF16)
    o_o[...] = o_ext[HALO : HALO + rows, :]
    lse_o[...] = jnp.transpose(lse_s[HALO : HALO + rows, :])[0:8, :]
    landed(w_attn, sem.at[0])
    x_ext[...] += nn(o_ext[...], w_attn[...])
    x2_o[...] = x_ext[HALO : HALO + rows, :]

    def third(i, c):
        at = pl.ds(pl.multiple_of(i * 32, 32), 32)
        n_ref[at, :] = norm(x_ext[at, :], norms, 2).astype(BF16)
        return c

    lax.fori_loop(0, ext // 32, third, 0)
    landed(w_glu, sem.at[1])
    val[...] = nt(n_ref[...], w_glu[0:D, :])
    gate[...] = nt(n_ref[...], w_glu[D:, :])
    gated_o[...] = val[...] * sigmoid(gate[...]) * live
    sums_o[...] = jnp.zeros_like(sums_o)
    sums_o[2:3, :] = jnp.zeros((1, D), F32) + jnp.sum(live[HALO : HALO + rows, :])
    for k in range(rows // 256):
        fill_chunk(meta, gated_o, chunk, k, start)
        alive = live[HALO + k * 256 : HALO + (k + 1) * 256, :]
        for lc in range(D // 128):
            lanes = slice(lc * 128, (lc + 1) * 128)
            acc = chunk[0:256, lanes] * taps[0:1, lanes]
            for j in range(1, KERNEL):
                acc = acc + chunk[j : j + 256, lanes] * taps[j : j + 1, lanes]
            h_o[k * 256 : (k + 1) * 256, lanes] = acc
            weighted = acc * alive
            sums_o[0:1, lanes] += jnp.sum(weighted, axis=0, keepdims=True)
            sums_o[1:2, lanes] += jnp.sum(weighted * acc, axis=0, keepdims=True)


def attend(nh, meta, inv, q, kvw, x1, qh, x1h, norms, taps, full):
    rows = q.shape[0]
    ext = rows + 2 * HALO
    dma = pltpu.SemaphoreType.DMA
    f = jax.ShapeDtypeStruct
    return pl.pallas_call(
        functools.partial(attend_kernel, nh),
        out_shape=[
            f((rows, D), BF16),
            f((8, rows), F32),
            f((rows, D), F32),
            f((ext, D), F32),
            f((rows, D), F32),
            f((8, D), F32),
        ],
        in_specs=[SM, SM] + [VM] * 7 + [ANY],
        out_specs=[VM] * 6,
        scratch_shapes=[
            pltpu.VMEM((D, D), BF16),
            pltpu.VMEM((2 * D, D), BF16),
            pltpu.VMEM((ext, D), BF16),
            pltpu.VMEM((ext, D), BF16),
            pltpu.VMEM((ext, D), F32),
            pltpu.VMEM((ext, LONGEST), F32),
            pltpu.VMEM((ext, D), BF16),
            pltpu.VMEM((ext, D), F32),
            pltpu.VMEM((ext, D), F32),
            pltpu.VMEM((256 + 2 * HALO, D), F32),
            pltpu.VMEM((ext, 128), F32),
            dma((2,)),
        ],
        compiler_params=params(52),
        name="attend",
    )(meta, inv, q, kvw, x1, qh, x1h, norms, taps, full)


def bn_terms(stats):
    count = stats[2:3, :]
    center = stats[0:1, :] / count
    inv_std = lax.rsqrt(stats[1:2, :] / count - center * center + norm_eps)
    return count, center, inv_std


def middle_kernel(nh, meta, inv, x2, h, stats, ograd, norms, taps, full, out_o, g3_o, gz_o, sums_o, ng_o, grads, w_in, w_out, w_pt, n_ref, gb, y3, x3, x4, acc, g_in, g_out, g_pt, sem, sem2, sem3, gsem):
    b = Blocks(nh)
    rows = x2.shape[0]
    unit = FF // nh
    fetch_all(full, inv, w_pt, sem3.at[0], b.point, b.ch, nh)
    for part in range(nh):
        fetch(full, inv, w_in, sem.at[part], b.in_two, b.ff, part, part * unit)
        fetch(full, inv, w_out, sem2.at[part], b.out_two, b.ff, part, part * unit)
    count, center, inv_std = bn_terms(stats)
    gain, shift = taps[KERNEL : KERNEL + 1, :], taps[KERNEL + 1 : KERNEL + 2, :]

    def z_of(at):
        return (h[at, :] - center) * inv_std * gain + shift

    def first(at, i, c):
        z = z_of(at)
        y3[at, :] = (z * sigmoid(z)).astype(BF16)
        return c

    bands(rows, first)
    landed(w_pt, sem3.at[0])
    x3[...] = x2[...] + nn(y3[...], w_pt[...])

    def second(at, i, c):
        n_ref[at, :] = norm(x3[at, :], norms, 3).astype(BF16)
        return c

    bands(rows, second)
    feed(n_ref, w_in, w_out, acc, sem, sem2, nh)
    zero = jnp.zeros((1, D), F32)

    def last(at, i, c):
        x = x3[at, :] + 0.5 * acc[at, :]
        out_o[at, :] = norm(x, norms, 4).astype(BF16)
        dx, dg, db = norm_back(x, ograd[at, :].astype(F32), norms[4:5, :])
        x4[at, :] = dx
        gb[at, :] = (0.5 * dx).astype(BF16)
        return c[0] + dg, c[1] + db

    gain4, shift4 = bands(rows, last, (zero, zero))
    feed_back(n_ref, gb, w_in, w_out, acc, g_in, g_out, grads, inv, b.in_two, b.out_two, gsem.at[0], gsem.at[1], b.ff, nh)

    def back(at, i, c):
        dx, dg, db = norm_back(x3[at, :], acc[at, :], norms[3:4, :])
        g3 = x4[at, :] + dx
        g3_o[at, :] = g3
        gb[at, :] = g3.astype(BF16)
        return c[0] + dg, c[1] + db

    gain3, shift3 = bands(rows, back, (zero, zero))
    ng_o[...] = jnp.zeros_like(ng_o)
    ng_o[3:4, :] = gain3
    ng_o[4:5, :] = gain4
    ng_o[8:9, :] = shift3
    ng_o[9:10, :] = shift4
    acc[...] = nt(gb[...], w_pt[...])
    g_pt[...] = tn(y3[...], gb[...]).astype(BF16)
    put_all(grads, inv, g_pt, gsem.at[2], b.point, b.ch, nh)

    def gz_part(at, i, c):
        white = (h[at, :] - center) * inv_std
        z = white * gain + shift
        gz = acc[at, :] * slope_of(z, sigmoid(z))
        gz_o[at, :] = gz
        return c[0] + jnp.sum(gz, axis=0, keepdims=True), c[1] + jnp.sum(gz * white, axis=0, keepdims=True)

    sg, sx = bands(rows, gz_part, (zero, zero))
    sums_o[...] = jnp.zeros_like(sums_o)
    sums_o[0:1, :] = sg
    sums_o[1:2, :] = sx
    y3[0:BLOCKW, :] = jnp.zeros((BLOCKW, D), BF16)
    empty = [(i, part) for i in range(b.total, grads.shape[1]) for part in range(nh)]
    for k, (i, part) in enumerate(empty):
        put(grads, inv, y3, gsem.at[3 + k], i, 1, part, 0)
    landed(g_in, gsem.at[0])
    landed(g_out, gsem.at[1])
    landed(g_pt, gsem.at[2])
    for k in range(len(empty)):
        landed(y3.at[pl.ds(0, BLOCKW)], gsem.at[3 + k])


def middle(nh, meta, inv, x2, h, stats, ograd, norms, taps, full):
    rows = x2.shape[0]
    slots = full.shape[1]
    zeros = (slots - Blocks(nh).total) * nh
    dma = pltpu.SemaphoreType.DMA
    f = jax.ShapeDtypeStruct
    v = pltpu.VMEM
    return pl.pallas_call(
        functools.partial(middle_kernel, nh),
        out_shape=[
            f((rows, D), BF16),
            f((rows, D), F32),
            f((rows, D), F32),
            f((8, D), F32),
            f((16, D), F32),
            f((nh, slots, BLOCKW, D), BF16),
        ],
        in_specs=[SM, SM] + [VM] * 6 + [ANY],
        out_specs=[VM] * 5 + [ANY],
        scratch_shapes=[
            v((FF, D), BF16),
            v((FF, D), BF16),
            v((D, D), BF16),
            v((rows, D), BF16),
            v((rows, D), BF16),
            v((rows, D), BF16),
            v((rows, D), F32),
            v((rows, D), F32),
            v((rows, D), F32),
            v((FF, D), BF16),
            v((FF, D), BF16),
            v((D, D), BF16),
            dma((nh,)),
            dma((nh,)),
            dma((1,)),
            dma((3 + zeros,)),
        ],
        compiler_params=params(52),
        name="middle",
    )(meta, inv, x2, h, stats, ograd, norms, taps, full)


def conv_back_kernel(nh, meta, inv, gz, gzh, h, hh, stats, bsums, gated, x2, g3, o, norms, taps, full, ng_in, grads_in, g2_o, do_o, taps_o, ng_o, grads, w_attn, w_glu, n_ref, gb, dh, dgated, val, gate, dglu, g_attn, g_glu, chunk, chunk2, sem, gsem):
    del grads_in
    b = Blocks(nh)
    rows = gz.shape[0]
    ext = rows + 2 * HALO
    start = meta[10]
    fetch_all(full, inv, w_attn, sem.at[0], b.attn, b.ch, nh)
    for i, base in enumerate((b.conv_value, b.conv_gate)):
        fetch_all(full, inv, w_glu, sem.at[1], base, b.ch, nh, i * D)
    count, center, inv_std = bn_terms(stats)
    gain = taps[KERNEL : KERNEL + 1, :]
    sg, sx = bsums[0:1, :], bsums[1:2, :]

    def dh_of(gz_rows, h_rows, first):
        alive = live_rows(meta, first, gz_rows.shape[0])
        white = (h_rows - center) * inv_std
        return gain * inv_std * (gz_rows - alive / count * (sg + white * sx))

    def one(at, i, c):
        dh[pl.ds(pl.multiple_of(i * BAND + HALO, HALO), BAND), :] = dh_of(gz[at, :], h[at, :], start + i * BAND)
        n_ref[at, :] = norm(x2[at, :], norms, 2).astype(BF16)
        return c

    bands(rows, one)
    dh[0:HALO, :] = dh_of(gzh[0:HALO, :], hh[0:HALO, :], start - HALO)
    dh[HALO + rows :, :] = dh_of(gzh[HALO:, :], hh[HALO:, :], start + rows)
    taps_o[...] = jnp.zeros_like(taps_o)
    for k in range(rows // 256):
        fill_chunk(meta, gated, chunk, k, start)
        fill_chunk(meta, dh, chunk2, k, start)
        for lc in range(D // 128):
            lanes = slice(lc * 128, (lc + 1) * 128)
            own = chunk2[HALO : HALO + 256, lanes]
            acc = chunk2[KERNEL : KERNEL + 256, lanes] * taps[0:1, lanes]
            for j in range(1, KERNEL):
                acc = acc + chunk2[KERNEL - j : KERNEL - j + 256, lanes] * taps[j : j + 1, lanes]
            dgated[k * 256 : (k + 1) * 256, lanes] = acc
            for j in range(KERNEL):
                taps_o[j : j + 1, lanes] += jnp.sum(chunk[j : j + 256, lanes] * own, axis=0, keepdims=True)
    landed(w_glu, sem.at[1])
    val[...] = nt(n_ref[...], w_glu[0:D, :])
    gate[...] = nt(n_ref[...], w_glu[D:, :])

    def two(at, i, c):
        sig = sigmoid(gate[at, :])
        d = dgated[at, :] * live_rows(meta, start + i * BAND, BAND)
        dglu[at, 0:D] = (d * sig).astype(BF16)
        dglu[at, D:] = (d * val[at, :] * sig * (1.0 - sig)).astype(BF16)
        return c

    bands(rows, two)
    g_glu[...] = tn(dglu[...], n_ref[...]).astype(BF16)
    for i, base in enumerate((b.conv_value, b.conv_gate)):
        put_all(grads, inv, g_glu, gsem.at[0], base, b.ch, nh, i * D)
    val[...] = nn(dglu[...], w_glu[...])
    zero = jnp.zeros((1, D), F32)

    def three(at, i, c):
        dx, dg, db = norm_back(x2[at, :], val[at, :], norms[2:3, :])
        g2 = g3[at, :] + dx
        g2_o[at, :] = g2
        gb[at, :] = g2.astype(BF16)
        return c[0] + dg, c[1] + db

    dgain, dshift = bands(rows, three, (zero, zero))
    ng_o[...] = ng_in[...]
    ng_o[2:3, :] = dgain
    ng_o[7:8, :] = dshift
    landed(w_attn, sem.at[0])
    gate[...] = nt(gb[...], w_attn[...])
    g_attn[...] = tn(o[...], gb[...]).astype(BF16)
    put_all(grads, inv, g_attn, gsem.at[1], b.attn, b.ch, nh)

    def four(at, i, c):
        do_o[at, :] = (gate[at, :] * live_rows(meta, start + i * BAND, BAND)).astype(BF16)
        return c

    bands(rows, four)
    landed(g_glu, gsem.at[0])
    landed(g_attn, gsem.at[1])


def conv_back(nh, meta, inv, gz, gzh, h, hh, stats, bsums, gated, x2, g3, o, norms, taps, full, ng, grads):
    rows = gz.shape[0]
    ext = rows + 2 * HALO
    dma = pltpu.SemaphoreType.DMA
    f = jax.ShapeDtypeStruct
    v = pltpu.VMEM
    return pl.pallas_call(
        functools.partial(conv_back_kernel, nh),
        out_shape=[
            f((rows, D), F32),
            f((rows, D), BF16),
            f((KERNEL, D), F32),
            f((16, D), F32),
            f(grads.shape, BF16),
        ],
        in_specs=[SM, SM] + [VM] * 12 + [ANY, VM, ANY],
        out_specs=[VM] * 4 + [ANY],
        input_output_aliases={16: 4},
        scratch_shapes=[
            v((D, D), BF16),
            v((2 * D, D), BF16),
            v((rows, D), BF16),
            v((rows, D), BF16),
            v((ext, D), F32),
            v((rows, D), F32),
            v((rows, D), F32),
            v((rows, D), F32),
            v((rows, 2 * D), BF16),
            v((D, D), BF16),
            v((2 * D, D), BF16),
            v((256 + 2 * HALO, D), F32),
            v((256 + 2 * HALO, D), F32),
            dma((2,)),
            dma((2,)),
        ],
        compiler_params=params(52),
        name="conv_back",
    )(meta, inv, gz, gzh, h, hh, stats, bsums, gated, x2, g3, o, norms, taps, full, ng, grads)


def attend_back_kernel(meta, q, kvw, do, lse, dq_o, dkv_o, send_o, bias, dkp, dvp):
    rows = q.shape[0]
    start = meta[10]
    base = start - lax.rem(start, LONGEST)
    offset = pl.multiple_of(lax.rem(start, LONGEST), rows)
    ukey, _, lkey = tables(meta, base + lax.broadcasted_iota(jnp.int32, (LONGEST, 1), 0))
    ukey = jnp.where(lkey, ukey, -1)
    uquery, _, _ = tables(meta, start + lax.broadcasted_iota(jnp.int32, (1, rows), 1))
    bias[...] = jnp.where(ukey == uquery, 0.0, masked_score)
    lane_q = lax.broadcasted_iota(jnp.int32, (256, 128), 1)
    lane_k = lax.broadcasted_iota(jnp.int32, (LONGEST, 128), 1)
    for pair in range(D // 128):
        lanes = slice(pair * 128, (pair + 1) * 128)
        kp = kvw[:, lanes]
        vp = kvw[:, D + pair * 128 : D + (pair + 1) * 128]
        kms = [jnp.where(lane_k < HD, kp, jnp.zeros_like(kp)), jnp.where(lane_k >= HD, kp, jnp.zeros_like(kp))]
        dkp[...] = jnp.zeros_like(dkp)
        dvp[...] = jnp.zeros_like(dvp)
        for blk in range(rows // 256):
            at = slice(blk * 256, (blk + 1) * 256)
            qp = q[at, lanes] * 0.125
            dop = do[at, lanes]
            dq = jnp.zeros((256, 128), F32)
            for hh in range(2):
                mine = lane_q < HD if hh == 0 else lane_q >= HD
                qm = jnp.where(mine, qp, jnp.zeros_like(qp))
                dom = jnp.where(mine, dop, jnp.zeros_like(dop))
                s = nt(kp, qm) + bias[:, at]
                p = jnp.exp(s - lse[pair * 2 + hh : pair * 2 + hh + 1, at])
                dp = nt(vp, dom)
                inner = jnp.sum(p * dp, axis=0, keepdims=True)
                ds = (p * (dp - inner)).astype(BF16)
                dvp[...] += nn(p.astype(BF16), dom)
                dkp[...] += nn(ds, qm)
                dq = dq + tn(ds, kms[hh])
            dq_o[at, lanes] = dq * 0.125
        dkv_o[:, lanes] = dkp[pl.ds(offset, rows), :]
        dkv_o[:, D + pair * 128 : D + (pair + 1) * 128] = dvp[pl.ds(offset, rows), :]
        send_o[:, lanes] = dkp[...].astype(BF16)
        send_o[:, D + pair * 128 : D + (pair + 1) * 128] = dvp[...].astype(BF16)


def attend_back(meta, q, kvw, do, lse):
    rows = q.shape[0]
    f = jax.ShapeDtypeStruct
    v = pltpu.VMEM
    return pl.pallas_call(
        attend_back_kernel,
        out_shape=[f((rows, D), F32), f((rows, 2 * D), F32), f((LONGEST, 2 * D), BF16)],
        in_specs=[SM] + [VM] * 4,
        out_specs=[VM] * 3,
        scratch_shapes=[v((LONGEST, rows), F32), v((LONGEST, 128), F32), v((LONGEST, 128), F32)],
        compiler_params=params(52),
        name="attend_back",
    )(meta, q, kvw, do, lse)


def rear_kernel(nh, meta, inv, dq, dkv, recv, x1, frames, g2, norms, cos, sin, full, ng_in, grads_in, fg_o, ng_o, grads, w_in, w_out, w_qkv, n_ref, gb, dproj, x_ref, acc, g_in, g_out, g_qkv, sem, gsem):
    del grads_in
    b = Blocks(nh)
    rows = dq.shape[0]
    for i, base in enumerate((b.query, b.key, b.value)):
        fetch_all(full, inv, w_qkv, sem.at[0], base, b.ch, nh, i * D)
    fetch_all(full, inv, w_in, sem.at[1], b.in_one, b.ff, nh)
    fetch_all(full, inv, w_out, sem.at[2], b.out_one, b.ff, nh)
    spans = recv.shape[0]

    def one(at, i, c):
        p = pl.ds(place_of(meta, i), BAND)
        dproj[at, 0:D] = turn(dq[at, :], cos[p, :], sin[p, :], -1.0).astype(BF16)
        dk, dv = dkv[at, 0:D], dkv[at, D:]
        for s in range(spans):
            dk = dk + recv[s, at, 0:D].astype(F32)
            dv = dv + recv[s, at, D:].astype(F32)
        dproj[at, D : 2 * D] = turn(dk, cos[p, :], sin[p, :], -1.0).astype(BF16)
        dproj[at, 2 * D :] = dv.astype(BF16)
        n_ref[at, :] = norm(x1[at, :], norms, 1).astype(BF16)
        return c

    bands(rows, one)
    landed(w_qkv, sem.at[0])
    acc[...] = nn(dproj[...], w_qkv[...])
    for i in range(3):
        g_qkv[i * D : (i + 1) * D, :] = tn(dproj[:, i * D : (i + 1) * D], n_ref[...]).astype(BF16)
    for i, base in enumerate((b.query, b.key, b.value)):
        put_all(grads, inv, g_qkv, gsem.at[0], base, b.ch, nh, i * D)
    zero = jnp.zeros((1, D), F32)

    def two(at, i, c):
        dx, dg, db = norm_back(x1[at, :], acc[at, :], norms[1:2, :])
        g1 = g2[at, :] + dx
        x_ref[at, :] = g1
        gb[at, :] = (0.5 * g1).astype(BF16)
        n_ref[at, :] = norm(frames[at, :].astype(F32), norms, 0).astype(BF16)
        return c[0] + dg, c[1] + db

    gain1, shift1 = bands(rows, two, (zero, zero))
    landed(w_in, sem.at[1])
    landed(w_out, sem.at[2])
    feed_back(n_ref, gb, w_in, w_out, acc, g_in, g_out, grads, inv, b.in_one, b.out_one, gsem.at[1], gsem.at[2], b.ff, nh)

    def three(at, i, c):
        dx, dg, db = norm_back(frames[at, :].astype(F32), acc[at, :], norms[0:1, :])
        fg_o[at, :] = x_ref[at, :] + dx
        return c[0] + dg, c[1] + db

    gain0, shift0 = bands(rows, three, (zero, zero))
    ng_o[...] = ng_in[...]
    ng_o[0:1, :] = gain0
    ng_o[1:2, :] = gain1
    ng_o[5:6, :] = shift0
    ng_o[6:7, :] = shift1
    landed(g_qkv, gsem.at[0])
    landed(g_in, gsem.at[1])
    landed(g_out, gsem.at[2])


def rear(nh, meta, inv, dq, dkv, recv, x1, frames, g2, norms, cos, sin, full, ng, grads):
    rows = dq.shape[0]
    dma = pltpu.SemaphoreType.DMA
    f = jax.ShapeDtypeStruct
    v = pltpu.VMEM
    return pl.pallas_call(
        functools.partial(rear_kernel, nh),
        out_shape=[f((rows, D), F32), f((16, D), F32), f(grads.shape, BF16)],
        in_specs=[SM, SM] + [VM] * 9 + [ANY, VM, ANY],
        out_specs=[VM, VM, ANY],
        input_output_aliases={13: 2},
        scratch_shapes=[
            v((FF, D), BF16),
            v((FF, D), BF16),
            v((3 * D, D), BF16),
            v((rows, D), BF16),
            v((rows, D), BF16),
            v((rows, 3 * D), BF16),
            v((rows, D), F32),
            v((rows, D), F32),
            v((FF, D), BF16),
            v((FF, D), BF16),
            v((3 * D, D), BF16),
            dma((3,)),
            dma((3,)),
        ],
        compiler_params=params(56),
        name="rear",
    )(meta, inv, dq, dkv, recv, x1, frames, g2, norms, cos, sin, full, ng, grads)


def split(x):
    high = x.astype(BF16)
    return high, (x - high.astype(F32)).astype(BF16)


def three_products(dot, a, b):
    (ah, al), (bh, bl) = a, b
    return dot(ah, bh) + (dot(ah, bl) + dot(al, bh))


def soap_kernel(grad, masters, first, second, left, right, masters_o, first_o, second_o):
    g = grad[0]
    m1 = beta_one * first[0] + (1.0 - beta_one) * g
    first_o[0] = m1
    lefts, rights = split(left[0]), split(right[0])
    both = three_products(nn, split(jnp.concatenate([g, m1], axis=0)), lefts)
    rot = three_products(tn, rights, split(both[0:BLOCKW]))
    rot1 = three_products(tn, rights, split(both[BLOCKW:]))
    m2 = beta_two * second[0] + (1.0 - beta_two) * rot * rot
    second_o[0] = m2
    scaled = rot1 / (jnp.sqrt(m2) + adam_eps)
    back = three_products(nt, split(three_products(nn, rights, split(scaled))), lefts)
    w = masters[0]
    masters_o[0] = w - FACTOR * back - step_rate * weight_decay * w


def soap(grad, masters, first, second, left, right):
    spd = grad.shape[0]
    block = pl.BlockSpec((1, BLOCKW, D), lambda i: (i, 0, 0))
    return pl.pallas_call(
        soap_kernel,
        grid=(spd,),
        out_shape=[jax.ShapeDtypeStruct(grad.shape, F32)] * 3,
        in_specs=[block] * 4
        + [pl.BlockSpec((1, D, D), lambda i: (i, 0, 0)), pl.BlockSpec((1, BLOCKW, BLOCKW), lambda i: (i, 0, 0))],
        out_specs=[block] * 3,
        compiler_params=params(24),
        name="soap",
    )(grad, masters, first, second, left, right)


def adam_step(weight, gradient, moment_one, moment_two, factor):
    one_new = beta_one * moment_one + (1.0 - beta_one) * gradient
    two_new = beta_two * moment_two + (1.0 - beta_two) * gradient * gradient
    return (weight - factor * one_new / (jnp.sqrt(two_new) + adam_eps), one_new, two_new)


def per_device(
    ndp,
    nh,
    frames,
    out_grad,
    bucket_len,
    batch_count,
    utt_lengths,
    owner_slots,
    masters,
    first_moment,
    second_moment,
    left_basis,
    right_basis,
    norm_params,
    norm_first,
    norm_second,
    conv_params,
    conv_first,
    conv_second,
):
    rows = frames.shape[0]
    slots = owner_slots.shape[0]
    channels = D // nh

    def flip(a):
        return jnp.transpose(a[0], (0, 2, 1))

    masters_t = flip(masters)
    inv = jnp.sum(
        jnp.where(owner_slots[None, :] == jnp.arange(slots)[:, None], jnp.arange(slots)[None, :], 0), axis=1
    ).astype(jnp.int32)
    ints = jnp.concatenate([bucket_len, batch_count, utt_lengths[0]])
    ints = jnp.broadcast_to(jnp.pad(ints, (0, 128 - ints.shape[0]))[None], (8, 128)).astype(jnp.int32)
    conv_pad = jnp.pad(conv_params.T, ((0, 40 - KERNEL - 2), (0, 128 - channels)))
    full, frames_v, ograd_v, ints_all, conv_all = gather(
        ndp, nh, masters_t.astype(BF16), frames, out_grad, ints, conv_pad
    )
    z = lax.axis_index("head")
    core = lax.axis_index("dp") % 2
    part = 2 * (z // 2) + core
    meta = jnp.where(z % 2 == 0, ints_all[0, 0, 0:16], ints_all[1, 0, 0:16])
    meta = jnp.where(jnp.arange(16) == 10, part * rows, meta).astype(jnp.int32)
    taps = jnp.transpose(conv_all[:, :, :channels], (1, 0, 2)).reshape(40, D)
    cos, sin = (jnp.asarray(t) for t in rope_tables())
    x1, q, kv = front(nh, meta, inv, frames_v, norm_params, cos, sin, full)
    kvw, qh, x1h = keys(ndp, nh, kv, q, x1)
    o, lse, x2, gated, h, sums = attend(nh, meta, inv, q, kvw, x1, qh, x1h, norm_params, taps, full)
    (stats,) = totals(ndp, nh, 3, sums)
    out_v, g3, gz, bpart, ng, grads = middle(nh, meta, inv, x2, h, stats, ograd_v, norm_params, taps, full)
    bsums, gzh, hh = totals(ndp, nh, 4, bpart, (gz, h))
    g2, do, dtaps, ng, grads = conv_back(
        nh, meta, inv, gz, gzh, h, hh, stats, bsums, gated, x2, g3, o, norm_params, taps, full, ng, grads
    )
    dq, dkv, dkv_send = attend_back(meta, q, kvw, do, lse)
    recv = key_grads(ndp, nh, dkv_send, rows)
    fg_v, ng, grads = rear(
        nh, meta, inv, dq, dkv, recv, x1, frames_v, g2, norm_params, cos, sin, full, ng, grads
    )
    small = jnp.concatenate([ng, dtaps], axis=0)
    owned, small, layer_out, frames_grad = scatter(ndp, nh, grads, small, out_v, fg_v)
    norm_grads = small[0:10]
    new_m, new_f, new_s = soap(
        owned, masters_t, flip(first_moment), flip(second_moment), left_basis[0], right_basis[0]
    )
    new_norms, norm_first_new, norm_second_new = adam_step(
        norm_params, norm_grads, norm_first, norm_second, 10.0 * FACTOR
    )
    conv_grads = jnp.concatenate([small[16 : 16 + KERNEL], bsums[1:2], bsums[0:1]], axis=0)
    conv_grads = lax.dynamic_slice_in_dim(conv_grads, z * channels, channels, 1)
    new_conv, conv_first_new, conv_second_new = adam_step(
        conv_params.T, conv_grads, conv_first.T, conv_second.T, 4.0 * FACTOR
    )

    def unflip(a):
        return jnp.transpose(a, (0, 2, 1))[None]

    return (
        layer_out,
        frames_grad,
        unflip(new_m),
        unflip(new_f),
        unflip(new_s),
        norm_grads,
        new_norms,
        norm_first_new,
        norm_second_new,
        new_conv.T,
        conv_first_new.T,
        conv_second_new.T,
    )


def solution(mesh):
    both, blocks, chan = P(("dp", "head"), None), P("head", "dp", None, None), P("head", None)
    placed = (both, both, P("dp"), P("dp"), P("dp", None), P()) + (blocks,) * 5 + (P(),) * 3 + (chan,) * 3
    return jax.shard_map(
        functools.partial(per_device, mesh.shape["dp"], mesh.shape["head"]),
        mesh=mesh,
        in_specs=placed,
        out_specs=(both, both) + (blocks,) * 3 + (P(),) * 4 + (chan,) * 3,
        check_vma=False,
    )
```

```python
import functools
import math

import jax
import jax.numpy as jnp
import numpy as np
from jax import lax
from jax.experimental import pallas as pl
from jax.experimental.pallas import tpu as pltpu
from jax.sharding import PartitionSpec as P

D = 512
FF = 2048
HD = 64
KERNEL = 32
BLOCKW = 64
STEP = 10
LONGEST = 1024
HALO = 16

beta_one = 0.9
beta_two = 0.95
step_rate = 0.05
weight_decay = 0.01
adam_eps = 1e-08
norm_eps = 1e-05
masked_score = -1e30
FACTOR = step_rate * math.sqrt(1.0 - beta_two**STEP) / (1.0 - beta_one**STEP)

F32 = jnp.float32
BF16 = jnp.bfloat16
MESH = pl.DeviceIdType.MESH
ANY = pl.BlockSpec(memory_space=pl.ANY)
HBM = pl.BlockSpec(memory_space=pltpu.HBM)
VM = pl.BlockSpec(memory_space=pltpu.VMEM)
SM = pl.BlockSpec(memory_space=pltpu.SMEM)
MIB = 1 << 20


def params(mib, collective_id=None):
    if collective_id is None:
        return pltpu.CompilerParams(vmem_limit_bytes=mib * MIB)
    return pltpu.CompilerParams(
        vmem_limit_bytes=mib * MIB, collective_id=collective_id, has_side_effects=True
    )


def big(nh, slots):
    return max(nh, -(-64 * MIB // (slots * BLOCKW * D * 2)))


class Copies:
    def __init__(self, sends):
        self.sends = sends
        self.used = 0
        self.open = []

    def send(self, src, dst, recv_sem, device):
        copy = pltpu.make_async_remote_copy(
            src_ref=src,
            dst_ref=dst,
            send_sem=self.sends.at[self.used],
            recv_sem=recv_sem,
            device_id=device,
            device_id_type=MESH,
        )
        copy.start()
        self.used += 1
        self.open.append(copy)

    def finish(self):
        for copy in self.open:
            copy.wait_send()


def arrived(ref, sem):
    pltpu.make_async_copy(ref, ref, sem).wait()


def greet(devices):
    barrier = pltpu.get_barrier_semaphore()
    for device in devices:
        pl.semaphore_signal(barrier, inc=1, device_id=device, device_id_type=MESH)
    pl.semaphore_wait(barrier, len(devices))


class Place:
    def __init__(self, ndp, nh):
        self.ndp, self.nh, self.nchip = ndp, nh, ndp // 2
        self.dp = lax.axis_index("dp")
        self.z = lax.axis_index("head")
        self.core = self.dp % 2
        self.chip = self.dp // 2
        self.group_core = self.z % 2
        self.part = 2 * (self.z // 2) + self.core

    def of_part(self, part):
        return (self.chip * 2 + part % 2, 2 * (part // 2) + self.group_core)

    def core_peer(self):
        return (self.chip * 2 + 1 - self.core, self.z)

    def swap_peer(self):
        return (self.chip * 2 + 1 - self.core, self.part)

    def x_chip(self):
        return self.chip + 1 - 2 * (self.chip % 2)

    def y_chip(self):
        return (self.chip + 2) % 4


def gather_kernel(ndp, nh, spd, own, frames, ograd, ints, conv, full, frames_o, ograd_o, ints_o, conv_o, sends, recvs, extra, local):
    me = Place(ndp, nh)
    dp, z, core, chip, nchip = me.dp, me.z, me.core, me.chip, me.nchip

    def shard(h, ch, c):
        return full.at[h, pl.ds((ch * 2 + c) * spd, spd)]

    def sem(h, ch, c, half=0):
        return recvs.at[h * ndp + ch * 2 + c, half]

    peer = me.core_peer()
    swap = me.core != me.z % 2
    columns = [(dp, (z + i) % nh) for i in range(1, nh)]
    square = nchip == 4
    if square:
        planes = [(me.x_chip() * 2 + core, z), (me.y_chip() * 2 + core, z)]
    else:
        planes = [(((chip + i) % nchip) * 2 + core, z) for i in range(1, nchip)]
    barrier = pltpu.get_barrier_semaphore()
    near = [peer] + columns + planes
    for device in near:
        pl.semaphore_signal(barrier, inc=1, device_id=device, device_id_type=MESH)

    @pl.when(swap)
    def _():
        pl.semaphore_signal(barrier, inc=1, device_id=me.swap_peer(), device_id_type=MESH)

    pl.semaphore_wait(barrier, len(near) + (core + z) % 2)

    copies = Copies(sends)
    mine = shard(z, chip, core)
    for device in columns:
        copies.send(own, mine, sem(z, chip, core), device)
    for device in planes:
        copies.send(own, mine, sem(z, chip, core), device)
    copies.send(own, mine, sem(z, chip, core), peer)
    keep = [
        pltpu.make_async_copy(own, mine, local.at[0]),
        pltpu.make_async_copy(ints, ints_o.at[core], local.at[1]),
        pltpu.make_async_copy(conv, conv_o.at[z], local.at[2]),
    ]
    for copy in keep:
        copy.start()
    copies.send(ints, ints_o.at[core], extra.at[0], peer)
    for device in columns:
        copies.send(conv, conv_o.at[z], extra.at[3 + z], device)

    @pl.when(swap)
    def _():
        for i, (src, dst) in enumerate(((frames, frames_o), (ograd, ograd_o))):
            pltpu.make_async_remote_copy(
                src_ref=src, dst_ref=dst, send_sem=local.at[3 + i], recv_sem=extra.at[1 + i],
                device_id=me.swap_peer(), device_id_type=MESH,
            ).start()

    @pl.when(jnp.logical_not(swap))
    def _():
        for i, (src, dst) in enumerate(((frames, frames_o), (ograd, ograd_o))):
            pltpu.make_async_copy(src, dst, local.at[3 + i]).start()

    def column(i):
        h = (z + nh - i) % nh
        if i > 0:
            arrived(shard(h, chip, core), sem(h, chip, core))
            for device in planes:
                copies.send(shard(h, chip, core), shard(h, chip, core), sem(h, chip, core), device)
            copies.send(shard(h, chip, core), shard(h, chip, core), sem(h, chip, core), peer)

    def beside(i):
        h = (z + nh - i) % nh
        if not square:
            for k in range(1, nchip):
                ch = (chip + k) % nchip
                arrived(shard(h, ch, core), sem(h, ch, core))
                copies.send(shard(h, ch, core), shard(h, ch, core), sem(h, ch, core), peer)
            return
        half = spd // 2
        for side, (ch, device) in enumerate(((me.x_chip(), planes[1]), (me.y_chip(), planes[0]))):
            arrived(shard(h, ch, core), sem(h, ch, core))
            piece = full.at[h, pl.ds((ch * 2 + core) * spd + side * half, half)]
            copies.send(piece, piece, sem(h, ch, core, side), device)
            copies.send(shard(h, ch, core), shard(h, ch, core), sem(h, ch, core), peer)

    def across(i):
        if not square:
            return
        h = (z + nh - i) % nh
        half = spd // 2
        ch = 3 - chip
        for side in range(2):
            piece = full.at[h, pl.ds((ch * 2 + core) * spd + side * half, half)]
            arrived(piece, sem(h, ch, core, side))
        copies.send(shard(h, ch, core), shard(h, ch, core), sem(h, ch, core), peer)

    for i in range(nh + 2):
        if i < nh:
            column(i)
        if 0 <= i - 1 < nh:
            beside(i - 1)
        if i >= 2:
            across(i - 2)
    for i in range(nh):
        h = (z + nh - i) % nh
        for k in range(nchip):
            ch = (chip + k) % nchip
            arrived(shard(h, ch, 1 - core), sem(h, ch, 1 - core))
    arrived(ints_o.at[1 - core], extra.at[0])
    for i in range(1, nh):
        h = (z + nh - i) % nh
        arrived(conv_o.at[h], extra.at[3 + h])

    @pl.when(swap)
    def _():
        arrived(frames_o, extra.at[1])
        arrived(ograd_o, extra.at[2])

    for i, ref in enumerate((frames, ograd)):
        arrived(ref, local.at[3 + i])
    for copy in keep:
        copy.wait()
    copies.finish()


def gather(ndp, nh, own, frames, ograd, ints, conv):
    spd = own.shape[0]
    nchip = ndp // 2
    plane = 2 if nchip == 4 else nchip - 1
    halves = 2 * nh if nchip == 4 else 0
    count = (nh - 1) + nh * (plane + 1) + (nh * (nchip - 1)) + halves + 1 + (nh - 1)
    shapes = [
        jax.ShapeDtypeStruct((big(nh, ndp * spd), ndp * spd, BLOCKW, D), BF16),
        jax.ShapeDtypeStruct(frames.shape, BF16),
        jax.ShapeDtypeStruct(ograd.shape, BF16),
        jax.ShapeDtypeStruct((2,) + ints.shape, jnp.int32),
        jax.ShapeDtypeStruct((nh,) + conv.shape, F32),
    ]
    dma = pltpu.SemaphoreType.DMA
    return pl.pallas_call(
        functools.partial(gather_kernel, ndp, nh, spd),
        out_shape=shapes,
        in_specs=[ANY, HBM, HBM, ANY, ANY],
        out_specs=[HBM] * 3 + [ANY] * 2,
        scratch_shapes=[dma((count,)), dma((nh * ndp, 2)), dma((3 + nh,)), dma((5,))],
        compiler_params=params(8, 1),
        name="gather",
    )(own, frames, ograd, ints, conv)


def totals_step(me, small, first, second, copies, sem1, sem2, local):
    ndp, nh = me.ndp, me.nh

    def one():
        for i in range(1, ndp):
            copies.send(small, first.at[me.dp], sem1.at[me.dp], ((me.dp + i) % ndp, me.z))
        first[me.dp] = small[...]

    def two():
        for i in range(1, ndp):
            src = (me.dp + i) % ndp
            arrived(first.at[src], sem1.at[src])
        total = first[0]
        for i in range(1, ndp):
            total = total + first[i]
        second[me.z] = total
        for i in range(1, nh):
            copies.send(second.at[me.z], second.at[me.z], sem2.at[me.z], (me.dp, (me.z + i) % nh))

    def three():
        for i in range(1, nh):
            src = (me.z + i) % nh
            arrived(second.at[src], sem2.at[src])
        total = second[0]
        for i in range(1, nh):
            total = total + second[i]
        return total

    return one, two, three


def totals_peers(me):
    return [((me.dp + i) % me.ndp, me.z) for i in range(1, me.ndp)] + [
        (me.dp, (me.z + i) % me.nh) for i in range(1, me.nh)
    ]


def totals_kernel(ndp, nh, halos, *refs):
    me = Place(ndp, nh)
    small = refs[0]
    edges = refs[1 : 1 + halos]
    out = refs[1 + halos]
    edges_o = refs[2 + halos : 2 + 2 * halos]
    first, second, sends, sem1, sem2, hsem = refs[2 + 2 * halos :]
    greet(totals_peers(me))
    copies = Copies(sends)
    one, two, three = totals_step(me, small, first, second, copies, sem1, sem2, None)
    one()
    for i in range(halos):
        send_edges(me, edges[i], edges_o[i], copies, hsem.at[2 * i], hsem.at[2 * i + 1])
    two()
    out[...] = three()
    for i in range(halos):
        arrived(edges_o[i].at[pl.ds(0, HALO)], hsem.at[2 * i])
        arrived(edges_o[i].at[pl.ds(HALO, HALO)], hsem.at[2 * i + 1])
    copies.finish()


def window(me, rows):
    span = LONGEST // rows
    at = me.part % span
    return span, at, me.part - at


def send_edges(me, src, dst, copies, sem_before, sem_after):
    rows = src.shape[0]
    span, at, base = window(me, rows)
    after = me.of_part(base + (at + 1) % span)
    before = me.of_part(base + (at + span - 1) % span)
    copies.send(src.at[pl.ds(rows - HALO, HALO)], dst.at[pl.ds(0, HALO)], sem_before, after)
    copies.send(src.at[pl.ds(0, HALO)], dst.at[pl.ds(HALO, HALO)], sem_after, before)


def totals(ndp, nh, collective_id, small, edges=()):
    dma = pltpu.SemaphoreType.DMA
    n = len(edges)
    halo = [jax.ShapeDtypeStruct((2 * HALO, D), e.dtype) for e in edges]
    return pl.pallas_call(
        functools.partial(totals_kernel, ndp, nh, n),
        out_shape=[jax.ShapeDtypeStruct(small.shape, F32)] + halo,
        in_specs=[VM] + [ANY] * n,
        out_specs=[VM] + [ANY] * n,
        scratch_shapes=[
            pltpu.VMEM((ndp,) + small.shape, F32),
            pltpu.VMEM((nh,) + small.shape, F32),
            dma((ndp + nh - 2 + 2 * n,)),
            dma((ndp,)),
            dma((nh,)),
            dma((2 * n + 1,)),
        ],
        compiler_params=params(16, collective_id),
        name=f"totals_{collective_id}",
    )(small, *edges)


def keys_kernel(ndp, nh, kv, q, x1, kv_o, q_o, x1_o, sends, recvs, local):
    me = Place(ndp, nh)
    rows = kv.shape[0]
    span, at, base = window(me, rows)
    peers = [me.of_part(base + (at + i) % span) for i in range(1, span)]
    greet(peers)
    copies = Copies(sends)
    place = kv_o.at[pl.ds(at * rows, rows)]
    for device in peers:
        copies.send(kv, place, recvs.at[at], device)
    own = pltpu.make_async_copy(kv, place, local.at[0])
    own.start()
    for i, (src, dst) in enumerate(((q, q_o), (x1, x1_o))):
        send_edges(me, src, dst, copies, recvs.at[span + 2 * i], recvs.at[span + 2 * i + 1])
    for i in range(1, span):
        other = (at + i) % span
        arrived(kv_o.at[pl.ds(other * rows, rows)], recvs.at[other])
    for i, dst in enumerate((q_o, x1_o)):
        arrived(dst.at[pl.ds(0, HALO)], recvs.at[span + 2 * i])
        arrived(dst.at[pl.ds(HALO, HALO)], recvs.at[span + 2 * i + 1])
    own.wait()
    copies.finish()


def keys(ndp, nh, kv, q, x1):
    span = LONGEST // kv.shape[0]
    dma = pltpu.SemaphoreType.DMA
    return pl.pallas_call(
        functools.partial(keys_kernel, ndp, nh),
        out_shape=[
            jax.ShapeDtypeStruct((LONGEST, 2 * D), BF16),
            jax.ShapeDtypeStruct((2 * HALO, D), BF16),
            jax.ShapeDtypeStruct((2 * HALO, D), F32),
        ],
        in_specs=[ANY] * 3,
        out_specs=[ANY] * 3,
        scratch_shapes=[dma((span + 3,)), dma((span + 4,)), dma((1,))],
        compiler_params=params(8, 2),
        name="keys",
    )(kv, q, x1)


def key_grads_kernel(ndp, nh, part, out, sends, recvs):
    me = Place(ndp, nh)
    rows = out.shape[1]
    span, at, base = window(me, rows)
    greet([me.of_part(base + (at + i) % span) for i in range(1, span)])
    copies = Copies(sends)
    for i in range(1, span):
        other = (at + i) % span
        copies.send(part.at[pl.ds(other * rows, rows)], out.at[i - 1], recvs.at[i - 1], me.of_part(base + other))
    for i in range(1, span):
        arrived(out.at[i - 1], recvs.at[i - 1])
    copies.finish()


def key_grads(ndp, nh, part, rows):
    span = LONGEST // rows
    dma = pltpu.SemaphoreType.DMA
    return pl.pallas_call(
        functools.partial(key_grads_kernel, ndp, nh),
        out_shape=jax.ShapeDtypeStruct((span - 1, rows, 2 * D), BF16),
        in_specs=[ANY],
        out_specs=ANY,
        scratch_shapes=[dma((span - 1,)), dma((span - 1,))],
        compiler_params=params(8, 5),
        name="key_grads",
    )(part)


def scatter_kernel(ndp, nh, spd, grads, small, out_v, fgrad_v, owned, small_o, out_o, fgrad_o, part, cores, side_x, side_y, half_x, half_y, zrecv, first, second, sends, csem, psem, xsem, zsem, sem1, sem2, esem, local):
    me = Place(ndp, nh)
    dp, z, core, chip, nchip = me.dp, me.z, me.core, me.chip, me.nchip
    square = nchip == 4
    peer = me.core_peer()
    swap = me.core != me.z % 2
    half = spd // 2
    barrier = pltpu.get_barrier_semaphore()
    near = totals_peers(me)
    for device in near:
        pl.semaphore_signal(barrier, inc=1, device_id=device, device_id_type=MESH)

    @pl.when(swap)
    def _():
        pl.semaphore_signal(barrier, inc=1, device_id=me.swap_peer(), device_id_type=MESH)

    pl.semaphore_wait(barrier, len(near) + (core + z) % 2)
    copies = Copies(sends)
    order = [(z + i + 1) % nh for i in range(nh)]
    if square:
        chips = [3 - chip, me.x_chip(), me.y_chip(), chip]
    else:
        chips = [(chip + i + 1) % nchip for i in range(nchip)]
    loads = {}
    for i, h in enumerate(order):
        for k, ch in enumerate(chips):
            copies.send(grads.at[h, pl.ds((ch * 2 + 1 - core) * spd, spd)], cores.at[i, k], csem.at[i, k], peer)
            load = pltpu.make_async_copy(grads.at[h, pl.ds((ch * 2 + core) * spd, spd)], part.at[i, k], psem.at[i, k])
            load.start()
            loads[i, k] = load
    one, two, three = totals_step(me, small, first, second, copies, sem1, sem2, None)
    one()

    @pl.when(swap)
    def _():
        for i, (src, dst) in enumerate(((out_v, out_o), (fgrad_v, fgrad_o))):
            pltpu.make_async_remote_copy(
                src_ref=src, dst_ref=dst, send_sem=local.at[i], recv_sem=esem.at[i],
                device_id=me.swap_peer(), device_id_type=MESH,
            ).start()

    @pl.when(jnp.logical_not(swap))
    def _():
        for i, (src, dst) in enumerate(((out_v, out_o), (fgrad_v, fgrad_o))):
            pltpu.make_async_copy(src, dst, local.at[i]).start()

    def add(i, k, others, lo=0, n=spd):
        @pl.loop(0, n)
        def _(s):
            total = part[i, k, lo + s].astype(F32)
            for other in others:
                total = total + other(s).astype(F32)
            part[i, k, lo + s] = total.astype(BF16)

    def meet(i, k):
        loads[i, k].wait()
        arrived(cores.at[i, k], csem.at[i, k])

    planes = [(me.x_chip() * 2 + core, z), (me.y_chip() * 2 + core, z)]

    def stage_a(i):
        if square:
            meet(i, 0)
            add(i, 0, [lambda s: cores[i, 0, s]])
            copies.send(part.at[i, 0, pl.ds(0, half)], half_x.at[i], xsem.at[i, 0], planes[0])
            copies.send(part.at[i, 0, pl.ds(half, half)], half_y.at[i], xsem.at[i, 1], planes[1])
        else:
            for k in range(nchip - 1):
                meet(i, k)
                add(i, k, [lambda s: cores[i, k, s]])
                copies.send(part.at[i, k], side_x.at[i, k], xsem.at[i, k], (chips[k] * 2 + core, z))

    def stage_b(i):
        if not square:
            return
        meet(i, 1)
        add(i, 1, [lambda s: cores[i, 1, s]], 0, half)
        arrived(half_y.at[i], xsem.at[i, 1])
        add(i, 1, [lambda s: cores[i, 1, half + s], lambda s: half_y[i, s]], half, half)
        copies.send(part.at[i, 1], side_x.at[i, 0], xsem.at[i, 2], planes[0])
        meet(i, 2)
        add(i, 2, [lambda s: cores[i, 2, half + s]], half, half)
        arrived(half_x.at[i], xsem.at[i, 0])
        add(i, 2, [lambda s: cores[i, 2, s], lambda s: half_x[i, s]], 0, half)
        copies.send(part.at[i, 2], side_y.at[i], xsem.at[i, 3], planes[1])

    last = nchip - 1

    def stage_c(i):
        meet(i, last)
        if square:
            arrived(side_x.at[i, 0], xsem.at[i, 2])
            arrived(side_y.at[i], xsem.at[i, 3])
            others = [lambda s: cores[i, last, s], lambda s: side_x[i, 0, s], lambda s: side_y[i, s]]
        else:
            others = [lambda s: cores[i, last, s]]
            for k in range(nchip - 1):
                arrived(side_x.at[i, k], xsem.at[i, k])
                others.append(lambda s, k=k: side_x[i, k, s])
        add(i, last, others)
        if i < nh - 1:
            copies.send(part.at[i, last], zrecv.at[i], zsem.at[i], (dp, order[i]))

    for i in range(nh + 2):
        if i < nh:
            stage_a(i)
        if 0 <= i - 1 < nh:
            stage_b(i - 1)
        if i == 1:
            two()
        if i >= 2:
            stage_c(i - 2)
    small_o[...] = three()
    for i in range(nh - 1):
        arrived(zrecv.at[i], zsem.at[i])

    @pl.loop(0, spd)
    def _(s):
        total = part[nh - 1, last, s].astype(F32)
        for i in range(nh - 1):
            total = total + zrecv[i, s].astype(F32)
        owned[s] = total

    @pl.when(swap)
    def _():
        arrived(out_o, esem.at[0])
        arrived(fgrad_o, esem.at[1])

    arrived(out_v, local.at[0])
    arrived(fgrad_v, local.at[1])
    copies.finish()


def scatter(ndp, nh, grads, small, out_v, fgrad_v):
    spd = grads.shape[1] // ndp
    nchip = ndp // 2
    square = nchip == 4
    dma = pltpu.SemaphoreType.DMA
    block = (spd, BLOCKW, D)
    halfb = (max(spd // 2, 1), BLOCKW, D)
    sides = 1 if square else nchip - 1
    sent = nh * nchip + (ndp - 1) + (nh - 1) + (nh * 4 if square else nh * (nchip - 1)) + (nh - 1)
    return pl.pallas_call(
        functools.partial(scatter_kernel, ndp, nh, spd),
        out_shape=[
            jax.ShapeDtypeStruct(block, F32),
            jax.ShapeDtypeStruct(small.shape, F32),
            jax.ShapeDtypeStruct(out_v.shape, out_v.dtype),
            jax.ShapeDtypeStruct(fgrad_v.shape, fgrad_v.dtype),
        ],
        in_specs=[HBM, VM, HBM, HBM],
        out_specs=[VM, VM, HBM, HBM],
        scratch_shapes=[
            pltpu.VMEM((nh, nchip) + block, BF16),
            pltpu.VMEM((nh, nchip) + block, BF16),
            pltpu.VMEM((nh, sides) + block, BF16),
            pltpu.VMEM((nh,) + block, BF16),
            pltpu.VMEM((nh,) + halfb, BF16),
            pltpu.VMEM((nh,) + halfb, BF16),
            pltpu.VMEM((nh - 1,) + block, BF16),
            pltpu.VMEM((ndp,) + small.shape, F32),
            pltpu.VMEM((nh,) + small.shape, F32),
            dma((sent,)),
            dma((nh, nchip)),
            dma((nh, nchip)),
            dma((nh, max(4, nchip))),
            dma((nh,)),
            dma((ndp,)),
            dma((nh,)),
            dma((2,)),
            dma((2,)),
        ],
        compiler_params=params(28, 6),
        name="scatter",
    )(grads, small, out_v, fgrad_v)


def nn(a, b):
    return jnp.dot(a, b, preferred_element_type=F32)


def nt(a, b):
    return lax.dot_general(a, b, (((1,), (1,)), ((), ())), preferred_element_type=F32)


def tn(a, b):
    return lax.dot_general(a, b, (((0,), (0,)), ((), ())), preferred_element_type=F32)


def sigmoid(v):
    return 0.5 * jnp.tanh(0.5 * v) + 0.5


def slope_of(v, sig):
    return sig * (1.0 + v * (1.0 - sig))


class Blocks:
    def __init__(self, nh):
        self.nh = nh
        ff, ch = FF // nh // BLOCKW, D // nh // BLOCKW
        self.ff, self.ch = ff, ch
        self.in_one, self.in_two = 0, ff
        self.query = 2 * ff
        self.key = self.query + ch
        self.value = self.key + ch
        self.conv_value = self.value + ch
        self.conv_gate = self.conv_value + ch
        rows = self.conv_gate + ch
        self.out_one, self.out_two = rows, rows + ff
        self.attn = rows + 2 * ff
        self.point = self.attn + ch
        self.total = self.point + ch


def fetch(full, inv, dst, sem, base, count, part, row):
    for j in range(count):
        pltpu.make_async_copy(
            full.at[part, inv[base + j]], dst.at[pl.ds(row + j * BLOCKW, BLOCKW)], sem
        ).start()


def fetch_all(full, inv, dst, sem, base, count, nh, row=0):
    for part in range(nh):
        fetch(full, inv, dst, sem, base, count, part, row + part * count * BLOCKW)


def landed(dst, sem):
    pltpu.make_async_copy(dst, dst, sem).wait()


def put(grads, inv, src, sem, base, count, part, row):
    for j in range(count):
        pltpu.make_async_copy(
            src.at[pl.ds(row + j * BLOCKW, BLOCKW)], grads.at[part, inv[base + j]], sem
        ).start()


def put_all(grads, inv, src, sem, base, count, nh, row=0):
    for part in range(nh):
        put(grads, inv, src, sem, base, count, part, row + part * count * BLOCKW)


def tables(meta, frame):
    length, batch = meta[0], meta[1]
    utterance = jnp.zeros_like(frame)
    for i in range(1, 8):
        utterance = utterance + (frame >= i * length).astype(jnp.int32)
    within = frame - utterance * length
    own = jnp.zeros_like(frame)
    for i in range(8):
        own = jnp.where(utterance == i, meta[2 + i], own)
    live = (utterance < batch) & (within < own)
    return utterance, within, live


def live_rows(meta, start, count):
    frame = start + lax.broadcasted_iota(jnp.int32, (count, 1), 0)
    return tables(meta, frame)[2].astype(F32)


def hat(x):
    center = jnp.mean(x, axis=1, keepdims=True)
    offset = x - center
    spread = lax.rsqrt(jnp.mean(offset * offset, axis=1, keepdims=True) + norm_eps)
    return offset * spread, spread


def norm(x, norms, i):
    return hat(x)[0] * norms[i : i + 1, :] + norms[i + 5 : i + 6, :]


def norm_back(x, grad, gain):
    return hat_back(*hat(x), grad, gain)


def hat_back(xhat, spread, grad, gain):
    scaled = grad * gain
    inner = scaled - jnp.mean(scaled, axis=1, keepdims=True) - xhat * jnp.mean(scaled * xhat, axis=1, keepdims=True)
    return spread * inner, jnp.sum(grad * xhat, axis=0, keepdims=True), jnp.sum(grad, axis=0, keepdims=True)


BAND = 64


def bands(rows, body, init=()):
    return lax.fori_loop(0, rows // BAND, lambda i, c: body(pl.ds(pl.multiple_of(i * BAND, BAND), BAND), i, c), init, unroll=True)


def partner(x):
    lane = lax.broadcasted_iota(jnp.int32, x.shape, 1) % HD
    return jnp.where(lane < HD // 2, pltpu.roll(x, 128 - HD // 2, 1), pltpu.roll(x, HD // 2, 1))


def turn(x, cos, sin, sign):
    parts = []
    for i in range(D // 128):
        piece = x[:, i * 128 : (i + 1) * 128]
        parts.append(piece * cos + partner(piece) * (sign * sin))
    return jnp.concatenate(parts, axis=1)


def rope_tables():
    freq = np.exp(np.arange(HD // 2, dtype=np.float32) * np.float32(-math.log(10000.0) / (HD // 2)))
    angle = np.arange(LONGEST, dtype=np.float32)[:, None] * freq[None, :].astype(np.float32)
    cos = np.tile(np.cos(angle), (1, 4)).astype(np.float32)
    sin = np.sin(angle).astype(np.float32)
    return cos, np.concatenate([-sin, sin, -sin, sin], axis=1)


def place_of(meta, i):
    return pl.multiple_of(lax.rem(meta[10] + i * BAND, meta[0]), BAND)


def feed(n_ref, w_in, w_out, acc_ref, sem, sem2, nh):
    unit = FF // nh
    for part in range(nh):
        rows = pl.ds(part * unit, unit)
        landed(w_in.at[rows], sem.at[part])
        pre = nt(n_ref[...], w_in[rows, :])
        act = (pre * sigmoid(pre)).astype(BF16)
        landed(w_out.at[rows], sem2.at[part])
        if part == 0:
            acc_ref[...] = nn(act, w_out[rows, :])
        else:
            acc_ref[...] += nn(act, w_out[rows, :])


def feed_back(n_ref, gb_ref, w_in, w_out, acc_ref, g_in, g_out, grads, inv, base_in, base_out, sem_in, sem_out, count, nh):
    unit = FF // nh

    def body(part, carry):
        rows = pl.ds(pl.multiple_of(part * unit, unit), unit)
        n, gb, win, wout = n_ref[...], gb_ref[...], w_in[rows, :], w_out[rows, :]
        pre = nt(win, n)
        sig = sigmoid(pre)
        act = (pre * sig).astype(BF16)
        dpre = (nt(wout, gb) * slope_of(pre, sig)).astype(BF16)
        g_out[rows, :] = nn(act, gb).astype(BF16)
        g_in[rows, :] = nn(dpre, n).astype(BF16)
        acc_ref[...] += tn(dpre, win)
        put(grads, inv, g_out, sem_out, base_out, count, part, part * unit)
        put(grads, inv, g_in, sem_in, base_in, count, part, part * unit)
        return carry

    acc_ref[...] = jnp.zeros_like(acc_ref)
    lax.fori_loop(0, nh, body, 0)


def front_kernel(nh, meta, inv, frames, norms, cos, sin, full, x1, q, kv, w_in, w_out, w_qkv, n_ref, acc, sem, sem2, sem3):
    b = Blocks(nh)
    rows = frames.shape[0]
    unit = FF // nh
    for part in range(nh):
        fetch(full, inv, w_in, sem.at[part], b.in_one, b.ff, part, part * unit)
        fetch(full, inv, w_out, sem2.at[part], b.out_one, b.ff, part, part * unit)
    for i, base in enumerate((b.query, b.key, b.value)):
        fetch_all(full, inv, w_qkv, sem3.at[0], base, b.ch, nh, i * D)

    def first(at, i, c):
        n_ref[at, :] = norm(frames[at, :].astype(F32), norms, 0).astype(BF16)
        return c

    bands(rows, first)
    feed(n_ref, w_in, w_out, acc, sem, sem2, nh)

    def second(at, i, c):
        x = frames[at, :].astype(F32) + 0.5 * acc[at, :]
        x1[at, :] = x
        n_ref[at, :] = norm(x, norms, 1).astype(BF16)
        return c

    bands(rows, second)
    landed(w_qkv, sem3.at[0])
    for j, (dst, lo) in enumerate(((q, 0), (kv, 0), (kv, D))):
        acc[...] = nt(n_ref[...], w_qkv[j * D : (j + 1) * D, :])

        def third(at, i, c):
            x = acc[at, :]
            if j < 2:
                p = pl.ds(place_of(meta, i), BAND)
                x = turn(x, cos[p, :], sin[p, :], 1.0)
            dst[at, lo : lo + D] = x.astype(BF16)
            return c

        bands(rows, third)


def front(nh, meta, inv, frames, norms, cos, sin, full):
    rows = frames.shape[0]
    dma = pltpu.SemaphoreType.DMA
    return pl.pallas_call(
        functools.partial(front_kernel, nh),
        out_shape=[
            jax.ShapeDtypeStruct((rows, D), F32),
            jax.ShapeDtypeStruct((rows, D), BF16),
            jax.ShapeDtypeStruct((rows, 2 * D), BF16),
        ],
        in_specs=[SM, SM, VM, VM, VM, VM, HBM],
        out_specs=[VM, VM, VM],
        scratch_shapes=[
            pltpu.VMEM((FF, D), BF16),
            pltpu.VMEM((FF, D), BF16),
            pltpu.VMEM((3 * D, D), BF16),
            pltpu.VMEM((rows, D), BF16),
            pltpu.VMEM((rows, D), F32),
            dma((nh,)),
            dma((nh,)),
            dma((1,)),
        ],
        compiler_params=params(18),
        name="front",
    )(meta, inv, frames, norms, cos, sin, full)


def fill_chunk(meta, src, chunk, k, start):
    lead = lax.rem(start + k * 256, meta[0]) != 0
    trail = lax.rem(start + (k + 1) * 256, meta[0]) != 0
    chunk[0:HALO, :] = jnp.where(lead, src[k * 256 : k * 256 + HALO, :], 0.0)
    chunk[HALO : HALO + 256, :] = src[k * 256 + HALO : k * 256 + HALO + 256, :]
    chunk[HALO + 256 :, :] = jnp.where(trail, src[k * 256 + HALO + 256 : k * 256 + 2 * HALO + 256, :], 0.0)


def shift_rows(chunk, moved):
    rows = chunk.shape[0]
    moved[0] = chunk[...]
    for b in range(1, 8):
        moved[b, 0 : rows - 8, :] = chunk[b : b + rows - 8, :]


def attend_kernel(nh, meta, inv, q, kvw, x1, qh, x1h, norms, taps, full, o_o, lse_o, x2_o, gated_o, h_o, sums_o, w_attn, w_glu, q_ext, o_ext, x_ext, bias, n_ref, val, gate, chunk, moved, lse_s, sem):
    b = Blocks(nh)
    rows = q.shape[0]
    ext = rows + 2 * HALO
    start = meta[10]
    fetch_all(full, inv, w_attn, sem.at[0], b.attn, b.ch, nh)
    for i, base in enumerate((b.conv_value, b.conv_gate)):
        fetch_all(full, inv, w_glu, sem.at[1], base, b.ch, nh, i * D)
    q_ext[0:HALO, :] = qh[0:HALO, :]
    q_ext[HALO : HALO + rows, :] = q[...]
    q_ext[HALO + rows :, :] = qh[HALO:, :]
    x_ext[0:HALO, :] = x1h[0:HALO, :]
    x_ext[HALO : HALO + rows, :] = x1[...]
    x_ext[HALO + rows :, :] = x1h[HALO:, :]
    base = start - lax.rem(start, LONGEST)
    key_frame = base + lax.broadcasted_iota(jnp.int32, (1, LONGEST), 1)
    ukey, _, lkey = tables(meta, key_frame)
    ukey = jnp.where(lkey, ukey, -1)
    query_frame = start - HALO + lax.broadcasted_iota(jnp.int32, (ext, 1), 0)
    uquery, _, lquery = tables(meta, query_frame)
    live = lquery.astype(F32)
    bias[...] = jnp.where(ukey == uquery, 0.0, masked_score)
    half = ext // 2
    head_lane = lax.broadcasted_iota(jnp.int32, (half, 128), 1)

    for pair in range(D // 128):
        lanes = slice(pair * 128, (pair + 1) * 128)
        kp = kvw[:, lanes]
        vp = kvw[:, D + pair * 128 : D + (pair + 1) * 128]
        for blk in range(2):
            at = slice(blk * half, (blk + 1) * half)
            qp = q_ext[at, lanes] * 0.125
            outs = []
            for hh in range(2):
                mine = head_lane < HD if hh == 0 else head_lane >= HD
                qm = jnp.where(mine, qp, jnp.zeros_like(qp))
                s = nt(qm, kp) + bias[at, :]
                top = jnp.max(s, axis=1, keepdims=True)
                e = jnp.exp(s - top)
                total = jnp.sum(e, axis=1, keepdims=True)
                outs.append(nn(e.astype(BF16), vp) * (1.0 / total))
                lse_s[at, pair * 2 + hh : pair * 2 + hh + 1] = top + jnp.log(total)
            o = jnp.where(head_lane < HD, outs[0], outs[1]) * live[at, :]
            o_ext[at, lanes] = o.astype(BF16)
    o_o[...] = o_ext[HALO : HALO + rows, :]
    lse_o[...] = jnp.transpose(lse_s[HALO : HALO + rows, :])[0:8, :]
    landed(w_attn, sem.at[0])
    x_ext[...] += nn(o_ext[...], w_attn[...])
    x2_o[...] = x_ext[HALO : HALO + rows, :]

    def third(i, c):
        at = pl.ds(pl.multiple_of(i * 32, 32), 32)
        n_ref[at, :] = norm(x_ext[at, :], norms, 2).astype(BF16)
        return c

    lax.fori_loop(0, ext // 32, third, 0, unroll=True)
    landed(w_glu, sem.at[1])
    val[...] = nt(n_ref[...], w_glu[0:D, :])
    gate[...] = nt(n_ref[...], w_glu[D:, :])
    gated_o[...] = val[...] * sigmoid(gate[...]) * live
    sums_o[...] = jnp.zeros_like(sums_o)
    sums_o[2:3, :] = jnp.zeros((1, D), F32) + jnp.sum(live[HALO : HALO + rows, :])
    for k in range(rows // 256):
        fill_chunk(meta, gated_o, chunk, k, start)
        alive = live[HALO + k * 256 : HALO + (k + 1) * 256, :]
        shift_rows(chunk, moved)
        for lc in range(D // 128):
            lanes = slice(lc * 128, (lc + 1) * 128)
            acc = moved[0, 0:256, lanes] * taps[0:1, lanes]
            for j in range(1, KERNEL):
                lo = j - j % 8
                acc = acc + moved[j % 8, lo : lo + 256, lanes] * taps[j : j + 1, lanes]
            h_o[k * 256 : (k + 1) * 256, lanes] = acc
            weighted = acc * alive
            sums_o[0:1, lanes] += jnp.sum(weighted, axis=0, keepdims=True)
            sums_o[1:2, lanes] += jnp.sum(weighted * acc, axis=0, keepdims=True)


def attend(nh, meta, inv, q, kvw, x1, qh, x1h, norms, taps, full):
    rows = q.shape[0]
    ext = rows + 2 * HALO
    dma = pltpu.SemaphoreType.DMA
    f = jax.ShapeDtypeStruct
    return pl.pallas_call(
        functools.partial(attend_kernel, nh),
        out_shape=[
            f((rows, D), BF16),
            f((8, rows), F32),
            f((rows, D), F32),
            f((ext, D), F32),
            f((rows, D), F32),
            f((8, D), F32),
        ],
        in_specs=[SM, SM] + [VM] * 7 + [HBM],
        out_specs=[VM] * 6,
        scratch_shapes=[
            pltpu.VMEM((D, D), BF16),
            pltpu.VMEM((2 * D, D), BF16),
            pltpu.VMEM((ext, D), BF16),
            pltpu.VMEM((ext, D), BF16),
            pltpu.VMEM((ext, D), F32),
            pltpu.VMEM((ext, LONGEST), F32),
            pltpu.VMEM((ext, D), BF16),
            pltpu.VMEM((ext, D), F32),
            pltpu.VMEM((ext, D), F32),
            pltpu.VMEM((256 + 2 * HALO, D), F32),
            pltpu.VMEM((8, 256 + 2 * HALO, D), F32),
            pltpu.VMEM((ext, 128), F32),
            dma((2,)),
        ],
        compiler_params=params(30),
        name="attend",
    )(meta, inv, q, kvw, x1, qh, x1h, norms, taps, full)


def bn_terms(stats):
    count = stats[2:3, :]
    center = stats[0:1, :] / count
    inv_std = lax.rsqrt(stats[1:2, :] / count - center * center + norm_eps)
    return count, center, inv_std


def middle_kernel(nh, meta, inv, x2, h, stats, ograd, norms, taps, full, out_o, g3_o, gz_o, sums_o, ng_o, grads, w_in, w_out, w_pt, n_ref, gb, y3, x3, x4, acc, g_in, g_out, g_pt, sem, sem2, sem3, gsem):
    b = Blocks(nh)
    rows = x2.shape[0]
    unit = FF // nh
    fetch_all(full, inv, w_pt, sem3.at[0], b.point, b.ch, nh)
    for part in range(nh):
        fetch(full, inv, w_in, sem.at[part], b.in_two, b.ff, part, part * unit)
        fetch(full, inv, w_out, sem2.at[part], b.out_two, b.ff, part, part * unit)
    count, center, inv_std = bn_terms(stats)
    gain, shift = taps[KERNEL : KERNEL + 1, :], taps[KERNEL + 1 : KERNEL + 2, :]

    def z_of(at):
        return (h[at, :] - center) * inv_std * gain + shift

    def first(at, i, c):
        z = z_of(at)
        y3[at, :] = (z * sigmoid(z)).astype(BF16)
        return c

    bands(rows, first)
    landed(w_pt, sem3.at[0])
    x3[...] = x2[...] + nn(y3[...], w_pt[...])

    def second(at, i, c):
        n_ref[at, :] = norm(x3[at, :], norms, 3).astype(BF16)
        return c

    bands(rows, second)
    feed(n_ref, w_in, w_out, acc, sem, sem2, nh)
    zero = jnp.zeros((1, D), F32)

    def last(at, i, c):
        x = x3[at, :] + 0.5 * acc[at, :]
        xhat, spread = hat(x)
        out_o[at, :] = (xhat * norms[4:5, :] + norms[9:10, :]).astype(BF16)
        dx, dg, db = hat_back(xhat, spread, ograd[at, :].astype(F32), norms[4:5, :])
        x4[at, :] = dx
        gb[at, :] = (0.5 * dx).astype(BF16)
        return c[0] + dg, c[1] + db

    gain4, shift4 = bands(rows, last, (zero, zero))
    feed_back(n_ref, gb, w_in, w_out, acc, g_in, g_out, grads, inv, b.in_two, b.out_two, gsem.at[0], gsem.at[1], b.ff, nh)

    def back(at, i, c):
        dx, dg, db = norm_back(x3[at, :], acc[at, :], norms[3:4, :])
        g3 = x4[at, :] + dx
        g3_o[at, :] = g3
        gb[at, :] = g3.astype(BF16)
        return c[0] + dg, c[1] + db

    gain3, shift3 = bands(rows, back, (zero, zero))
    ng_o[...] = jnp.zeros_like(ng_o)
    ng_o[3:4, :] = gain3
    ng_o[4:5, :] = gain4
    ng_o[8:9, :] = shift3
    ng_o[9:10, :] = shift4
    acc[...] = nt(gb[...], w_pt[...])
    g_pt[...] = tn(y3[...], gb[...]).astype(BF16)
    put_all(grads, inv, g_pt, gsem.at[2], b.point, b.ch, nh)

    def gz_part(at, i, c):
        white = (h[at, :] - center) * inv_std
        z = white * gain + shift
        gz = acc[at, :] * slope_of(z, sigmoid(z))
        gz_o[at, :] = gz
        return c[0] + jnp.sum(gz, axis=0, keepdims=True), c[1] + jnp.sum(gz * white, axis=0, keepdims=True)

    sg, sx = bands(rows, gz_part, (zero, zero))
    sums_o[...] = jnp.zeros_like(sums_o)
    sums_o[0:1, :] = sg
    sums_o[1:2, :] = sx
    y3[0:BLOCKW, :] = jnp.zeros((BLOCKW, D), BF16)
    empty = [(i, part) for i in range(b.total, grads.shape[1]) for part in range(nh)]
    for k, (i, part) in enumerate(empty):
        put(grads, inv, y3, gsem.at[3 + k], i, 1, part, 0)
    landed(g_in, gsem.at[0])
    landed(g_out, gsem.at[1])
    landed(g_pt, gsem.at[2])
    for k in range(len(empty)):
        landed(y3.at[pl.ds(0, BLOCKW)], gsem.at[3 + k])


def middle(nh, meta, inv, x2, h, stats, ograd, norms, taps, full):
    rows = x2.shape[0]
    slots = full.shape[1]
    zeros = (slots - Blocks(nh).total) * nh
    dma = pltpu.SemaphoreType.DMA
    f = jax.ShapeDtypeStruct
    v = pltpu.VMEM
    return pl.pallas_call(
        functools.partial(middle_kernel, nh),
        out_shape=[
            f((rows, D), BF16),
            f((rows, D), F32),
            f((rows, D), F32),
            f((8, D), F32),
            f((16, D), F32),
            f((big(nh, slots), slots, BLOCKW, D), BF16),
        ],
        in_specs=[SM, SM] + [VM] * 6 + [HBM],
        out_specs=[VM] * 5 + [HBM],
        scratch_shapes=[
            v((FF, D), BF16),
            v((FF, D), BF16),
            v((D, D), BF16),
            v((rows, D), BF16),
            v((rows, D), BF16),
            v((rows, D), BF16),
            v((rows, D), F32),
            v((rows, D), F32),
            v((rows, D), F32),
            v((FF, D), BF16),
            v((FF, D), BF16),
            v((D, D), BF16),
            dma((nh,)),
            dma((nh,)),
            dma((1,)),
            dma((3 + zeros,)),
        ],
        compiler_params=params(26),
        name="middle",
    )(meta, inv, x2, h, stats, ograd, norms, taps, full)


def conv_back_kernel(nh, meta, inv, gz, gzh, h, hh, stats, bsums, gated, x2, g3, o, norms, taps, full, ng_in, grads_in, g2_o, do_o, taps_o, ng_o, grads, w_attn, w_glu, n_ref, gb, dh, dgated, val, gate, dglu, g_attn, g_glu, chunk, moved, tsum, sem, gsem):
    del grads_in
    b = Blocks(nh)
    rows = gz.shape[0]
    ext = rows + 2 * HALO
    start = meta[10]
    fetch_all(full, inv, w_attn, sem.at[0], b.attn, b.ch, nh)
    for i, base in enumerate((b.conv_value, b.conv_gate)):
        fetch_all(full, inv, w_glu, sem.at[1], base, b.ch, nh, i * D)
    count, center, inv_std = bn_terms(stats)
    gain = taps[KERNEL : KERNEL + 1, :]
    sg, sx = bsums[0:1, :], bsums[1:2, :]

    def dh_of(gz_rows, h_rows, first):
        alive = live_rows(meta, first, gz_rows.shape[0])
        white = (h_rows - center) * inv_std
        return gain * inv_std * (gz_rows - alive / count * (sg + white * sx))

    def one(at, i, c):
        dh[pl.ds(pl.multiple_of(i * BAND + HALO, HALO), BAND), :] = dh_of(gz[at, :], h[at, :], start + i * BAND)
        n_ref[at, :] = norm(x2[at, :], norms, 2).astype(BF16)
        return c

    bands(rows, one)
    dh[0:HALO, :] = dh_of(gzh[0:HALO, :], hh[0:HALO, :], start - HALO)
    dh[HALO + rows :, :] = dh_of(gzh[HALO:, :], hh[HALO:, :], start + rows)
    tsum[...] = jnp.zeros_like(tsum)
    for k in range(rows // 256):
        fill_chunk(meta, dh, chunk, k, start)
        shift_rows(chunk, moved)

        def piece(i, c):
            lanes = pl.ds(pl.multiple_of(i // 2 * 128, 128), 128)
            row = pl.multiple_of(i % 2 * 128, 128)
            own = gated[pl.ds(pl.multiple_of(row + HALO + k * 256, HALO), 128), lanes]
            acc = jnp.zeros((128, 128), F32)
            for j in range(KERNEL):
                off = KERNEL - j
                there = moved[off % 8, pl.ds(pl.multiple_of(row + off - off % 8, 8), 128), lanes]
                acc = acc + there * taps[j : j + 1, lanes]
                tsum[j, :, lanes] += jnp.sum((there * own).reshape(16, 8, 128), axis=0)
            dgated[pl.ds(pl.multiple_of(row + k * 256, 128), 128), lanes] = acc
            return c

        lax.fori_loop(0, 2 * D // 128, piece, 0)
    taps_o[...] = jnp.sum(tsum[...], axis=1)
    landed(w_glu, sem.at[1])
    val[...] = nt(n_ref[...], w_glu[0:D, :])
    gate[...] = nt(n_ref[...], w_glu[D:, :])

    def two(at, i, c):
        sig = sigmoid(gate[at, :])
        d = dgated[at, :] * live_rows(meta, start + i * BAND, BAND)
        dglu[at, 0:D] = (d * sig).astype(BF16)
        dglu[at, D:] = (d * val[at, :] * sig * (1.0 - sig)).astype(BF16)
        return c

    bands(rows, two)
    g_glu[...] = tn(dglu[...], n_ref[...]).astype(BF16)
    for i, base in enumerate((b.conv_value, b.conv_gate)):
        put_all(grads, inv, g_glu, gsem.at[0], base, b.ch, nh, i * D)
    val[...] = nn(dglu[...], w_glu[...])
    zero = jnp.zeros((1, D), F32)

    def three(at, i, c):
        dx, dg, db = norm_back(x2[at, :], val[at, :], norms[2:3, :])
        g2 = g3[at, :] + dx
        g2_o[at, :] = g2
        gb[at, :] = g2.astype(BF16)
        return c[0] + dg, c[1] + db

    dgain, dshift = bands(rows, three, (zero, zero))
    ng_o[...] = ng_in[...]
    ng_o[2:3, :] = dgain
    ng_o[7:8, :] = dshift
    landed(w_attn, sem.at[0])
    gate[...] = nt(gb[...], w_attn[...])
    g_attn[...] = tn(o[...], gb[...]).astype(BF16)
    put_all(grads, inv, g_attn, gsem.at[1], b.attn, b.ch, nh)

    def four(at, i, c):
        do_o[at, :] = (gate[at, :] * live_rows(meta, start + i * BAND, BAND)).astype(BF16)
        return c

    bands(rows, four)
    landed(g_glu, gsem.at[0])
    landed(g_attn, gsem.at[1])


def conv_back(nh, meta, inv, gz, gzh, h, hh, stats, bsums, gated, x2, g3, o, norms, taps, full, ng, grads):
    rows = gz.shape[0]
    ext = rows + 2 * HALO
    dma = pltpu.SemaphoreType.DMA
    f = jax.ShapeDtypeStruct
    v = pltpu.VMEM
    return pl.pallas_call(
        functools.partial(conv_back_kernel, nh),
        out_shape=[
            f((rows, D), F32),
            f((rows, D), BF16),
            f((KERNEL, D), F32),
            f((16, D), F32),
            f(grads.shape, BF16),
        ],
        in_specs=[SM, SM] + [VM] * 12 + [HBM, VM, HBM],
        out_specs=[VM] * 4 + [HBM],
        input_output_aliases={16: 4},
        scratch_shapes=[
            v((D, D), BF16),
            v((2 * D, D), BF16),
            v((rows, D), BF16),
            v((rows, D), BF16),
            v((ext, D), F32),
            v((rows, D), F32),
            v((rows, D), F32),
            v((rows, D), F32),
            v((rows, 2 * D), BF16),
            v((D, D), BF16),
            v((2 * D, D), BF16),
            v((256 + 2 * HALO, D), F32),
            v((8, 256 + 2 * HALO, D), F32),
            v((KERNEL, 8, D), F32),
            dma((2,)),
            dma((2,)),
        ],
        compiler_params=params(28),
        name="conv_back",
    )(meta, inv, gz, gzh, h, hh, stats, bsums, gated, x2, g3, o, norms, taps, full, ng, grads)


def attend_back_kernel(meta, q, kvw, do, lse, dq_o, dkv_o, send_o, bias, dkp, dvp):
    rows = q.shape[0]
    start = meta[10]
    base = start - lax.rem(start, LONGEST)
    offset = pl.multiple_of(lax.rem(start, LONGEST), rows)
    ukey, _, lkey = tables(meta, base + lax.broadcasted_iota(jnp.int32, (LONGEST, 1), 0))
    ukey = jnp.where(lkey, ukey, -1)
    uquery, _, _ = tables(meta, start + lax.broadcasted_iota(jnp.int32, (1, rows), 1))
    bias[...] = jnp.where(ukey == uquery, 0.0, masked_score)
    lane_q = lax.broadcasted_iota(jnp.int32, (rows, 128), 1)
    lane_k = lax.broadcasted_iota(jnp.int32, (LONGEST, 128), 1)
    for pair in range(D // 128):
        lanes = slice(pair * 128, (pair + 1) * 128)
        kp = kvw[:, lanes]
        vp = kvw[:, D + pair * 128 : D + (pair + 1) * 128]
        kms = [jnp.where(lane_k < HD, kp, jnp.zeros_like(kp)), jnp.where(lane_k >= HD, kp, jnp.zeros_like(kp))]
        qp = q[:, lanes] * 0.125
        dop = do[:, lanes]
        for hh in range(2):
            mine = lane_q < HD if hh == 0 else lane_q >= HD
            qm = jnp.where(mine, qp, jnp.zeros_like(qp))
            dom = jnp.where(mine, dop, jnp.zeros_like(dop))
            s = nt(kp, qm) + bias[...]
            p = jnp.exp(s - lse[pair * 2 + hh : pair * 2 + hh + 1, :])
            dp = nt(vp, dom)
            inner = jnp.sum(p * dp, axis=0, keepdims=True)
            ds = (p * (dp - inner)).astype(BF16)
            dv, dk, dq = nn(p.astype(BF16), dom), nn(ds, qm), tn(ds, kms[hh]) * 0.125
            if hh == 0:
                dvp[...], dkp[...], dq_o[:, lanes] = dv, dk, dq
            else:
                dvp[...] += dv
                dkp[...] += dk
                dq_o[:, lanes] += dq
        dkv_o[:, lanes] = dkp[pl.ds(offset, rows), :]
        dkv_o[:, D + pair * 128 : D + (pair + 1) * 128] = dvp[pl.ds(offset, rows), :]
        send_o[:, lanes] = dkp[...].astype(BF16)
        send_o[:, D + pair * 128 : D + (pair + 1) * 128] = dvp[...].astype(BF16)


def attend_back(meta, q, kvw, do, lse):
    rows = q.shape[0]
    f = jax.ShapeDtypeStruct
    v = pltpu.VMEM
    return pl.pallas_call(
        attend_back_kernel,
        out_shape=[f((rows, D), F32), f((rows, 2 * D), F32), f((LONGEST, 2 * D), BF16)],
        in_specs=[SM] + [VM] * 4,
        out_specs=[VM] * 3,
        scratch_shapes=[v((LONGEST, rows), F32), v((LONGEST, 128), F32), v((LONGEST, 128), F32)],
        compiler_params=params(26),
        name="attend_back",
    )(meta, q, kvw, do, lse)


def rear_kernel(nh, meta, inv, dq, dkv, recv, x1, frames, g2, norms, cos, sin, full, ng_in, grads_in, fg_o, ng_o, grads, w_in, w_out, w_qkv, n_ref, gb, dproj, x_ref, acc, g_in, g_out, g_qkv, sem, gsem):
    del grads_in
    b = Blocks(nh)
    rows = dq.shape[0]
    for i, base in enumerate((b.query, b.key, b.value)):
        fetch_all(full, inv, w_qkv, sem.at[0], base, b.ch, nh, i * D)
    fetch_all(full, inv, w_in, sem.at[1], b.in_one, b.ff, nh)
    fetch_all(full, inv, w_out, sem.at[2], b.out_one, b.ff, nh)
    spans = recv.shape[0]

    def one(at, i, c):
        p = pl.ds(place_of(meta, i), BAND)
        dproj[at, 0:D] = turn(dq[at, :], cos[p, :], sin[p, :], -1.0).astype(BF16)
        dk, dv = dkv[at, 0:D], dkv[at, D:]
        for s in range(spans):
            dk = dk + recv[s, at, 0:D].astype(F32)
            dv = dv + recv[s, at, D:].astype(F32)
        dproj[at, D : 2 * D] = turn(dk, cos[p, :], sin[p, :], -1.0).astype(BF16)
        dproj[at, 2 * D :] = dv.astype(BF16)
        n_ref[at, :] = norm(x1[at, :], norms, 1).astype(BF16)
        return c

    bands(rows, one)
    landed(w_qkv, sem.at[0])
    acc[...] = nn(dproj[...], w_qkv[...])
    for i in range(3):
        g_qkv[i * D : (i + 1) * D, :] = tn(dproj[:, i * D : (i + 1) * D], n_ref[...]).astype(BF16)
    for i, base in enumerate((b.query, b.key, b.value)):
        put_all(grads, inv, g_qkv, gsem.at[0], base, b.ch, nh, i * D)
    zero = jnp.zeros((1, D), F32)

    def two(at, i, c):
        dx, dg, db = norm_back(x1[at, :], acc[at, :], norms[1:2, :])
        g1 = g2[at, :] + dx
        x_ref[at, :] = g1
        gb[at, :] = (0.5 * g1).astype(BF16)
        n_ref[at, :] = norm(frames[at, :].astype(F32), norms, 0).astype(BF16)
        return c[0] + dg, c[1] + db

    gain1, shift1 = bands(rows, two, (zero, zero))
    landed(w_in, sem.at[1])
    landed(w_out, sem.at[2])
    feed_back(n_ref, gb, w_in, w_out, acc, g_in, g_out, grads, inv, b.in_one, b.out_one, gsem.at[1], gsem.at[2], b.ff, nh)

    def three(at, i, c):
        dx, dg, db = norm_back(frames[at, :].astype(F32), acc[at, :], norms[0:1, :])
        fg_o[at, :] = x_ref[at, :] + dx
        return c[0] + dg, c[1] + db

    gain0, shift0 = bands(rows, three, (zero, zero))
    ng_o[...] = ng_in[...]
    ng_o[0:1, :] = gain0
    ng_o[1:2, :] = gain1
    ng_o[5:6, :] = shift0
    ng_o[6:7, :] = shift1
    landed(g_qkv, gsem.at[0])
    landed(g_in, gsem.at[1])
    landed(g_out, gsem.at[2])


def rear(nh, meta, inv, dq, dkv, recv, x1, frames, g2, norms, cos, sin, full, ng, grads):
    rows = dq.shape[0]
    dma = pltpu.SemaphoreType.DMA
    f = jax.ShapeDtypeStruct
    v = pltpu.VMEM
    return pl.pallas_call(
        functools.partial(rear_kernel, nh),
        out_shape=[f((rows, D), F32), f((16, D), F32), f(grads.shape, BF16)],
        in_specs=[SM, SM] + [VM] * 9 + [HBM, VM, HBM],
        out_specs=[VM, VM, HBM],
        input_output_aliases={13: 2},
        scratch_shapes=[
            v((FF, D), BF16),
            v((FF, D), BF16),
            v((3 * D, D), BF16),
            v((rows, D), BF16),
            v((rows, D), BF16),
            v((rows, 3 * D), BF16),
            v((rows, D), F32),
            v((rows, D), F32),
            v((FF, D), BF16),
            v((FF, D), BF16),
            v((3 * D, D), BF16),
            dma((3,)),
            dma((3,)),
        ],
        compiler_params=params(28),
        name="rear",
    )(meta, inv, dq, dkv, recv, x1, frames, g2, norms, cos, sin, full, ng, grads)


def split(x):
    high = x.astype(BF16)
    return high, (x - high.astype(F32)).astype(BF16)


def three_products(dot, a, b):
    (ah, al), (bh, bl) = a, b
    return dot(ah, bh) + (dot(ah, bl) + dot(al, bh))


def adam_step(weight, gradient, moment_one, moment_two, factor):
    one_new = beta_one * moment_one + (1.0 - beta_one) * gradient
    two_new = beta_two * moment_two + (1.0 - beta_two) * gradient * gradient
    return (weight - factor * one_new / (jnp.sqrt(two_new) + adam_eps), one_new, two_new)


def update_kernel(nh, head, grad, masters, first, second, left, right, small, bsums, norms, norm1, norm2, conv, conv1, conv2, out_v, fgrad_v, masters_o, first_o, second_o, ng_o, norms_o, norm1_o, norm2_o, conv_o, conv1_o, conv2_o, out_o, fgrad_o, sem):
    moves = [
        pltpu.make_async_copy(out_v, out_o, sem.at[0]),
        pltpu.make_async_copy(fgrad_v, fgrad_o, sem.at[1]),
    ]
    step = pl.program_id(0)

    @pl.when(step == 0)
    def _():
        for move in moves:
            move.start()
        grads = small[0:10, :]
        ng_o[...] = grads
        norms_o[...], norm1_o[...], norm2_o[...] = adam_step(norms[...], grads, norm1[...], norm2[...], 10.0 * FACTOR)
        width = conv.shape[1]
        rows = jnp.concatenate([small[16 : 16 + KERNEL, :], bsums[1:2, :], bsums[0:1, :]], axis=0)
        mine = rows[:, 0:width]
        for h in range(1, nh):
            mine = jnp.where(head[0] == h, rows[:, h * width : (h + 1) * width], mine)
        conv_o[...], conv1_o[...], conv2_o[...] = adam_step(conv[...], mine, conv1[...], conv2[...], 4.0 * FACTOR)

    g = grad[0]
    m1 = beta_one * first[0] + (1.0 - beta_one) * g
    first_o[0] = m1
    lefts, rights = split(left[0]), split(right[0])
    both = three_products(nn, split(jnp.concatenate([g, m1], axis=0)), lefts)
    rot = three_products(tn, rights, split(both[0:BLOCKW]))
    rot1 = three_products(tn, rights, split(both[BLOCKW:]))
    m2 = beta_two * second[0] + (1.0 - beta_two) * rot * rot
    second_o[0] = m2
    scaled = rot1 / (jnp.sqrt(m2) + adam_eps)
    back = three_products(nt, split(three_products(nn, rights, split(scaled))), lefts)
    w = masters[0]
    masters_o[0] = w - FACTOR * back - step_rate * weight_decay * w

    @pl.when(step == pl.num_programs(0) - 1)
    def _():
        for move in moves:
            move.wait()


def update(nh, head, grad, masters, first, second, left, right, small, bsums, norms, norm1, norm2, conv, conv1, conv2, out_v, fgrad_v):
    spd = grad.shape[0]
    block = pl.BlockSpec((1, BLOCKW, D), lambda i: (i, 0, 0))

    def whole(a):
        return pl.BlockSpec(a.shape, lambda i: (0, 0))

    f = jax.ShapeDtypeStruct
    return pl.pallas_call(
        functools.partial(update_kernel, nh),
        grid=(spd,),
        out_shape=[f(grad.shape, F32)] * 3
        + [f(norms.shape, F32)] * 4
        + [f(conv.shape, F32)] * 3
        + [f(out_v.shape, out_v.dtype), f(fgrad_v.shape, F32)],
        in_specs=[SM]
        + [block] * 4
        + [pl.BlockSpec((1, D, D), lambda i: (i, 0, 0)), pl.BlockSpec((1, BLOCKW, BLOCKW), lambda i: (i, 0, 0))]
        + [whole(a) for a in (small, bsums, norms, norm1, norm2, conv, conv1, conv2)]
        + [HBM, HBM],
        out_specs=[block] * 3 + [whole(norms)] * 4 + [whole(conv)] * 3 + [HBM, HBM],
        scratch_shapes=[pltpu.SemaphoreType.DMA((2,))],
        compiler_params=params(20),
        name="update",
    )(head, grad, masters, first, second, left, right, small, bsums, norms, norm1, norm2, conv, conv1, conv2, out_v, fgrad_v)


def per_device(
    ndp,
    nh,
    frames,
    out_grad,
    bucket_len,
    batch_count,
    utt_lengths,
    owner_slots,
    masters,
    first_moment,
    second_moment,
    left_basis,
    right_basis,
    norm_params,
    norm_first,
    norm_second,
    conv_params,
    conv_first,
    conv_second,
):
    rows = frames.shape[0]
    slots = owner_slots.shape[0]
    channels = D // nh

    def flip(a):
        return jnp.transpose(a[0], (0, 2, 1))

    masters_t = flip(masters)
    inv = jnp.sum(
        jnp.where(owner_slots[None, :] == jnp.arange(slots)[:, None], jnp.arange(slots)[None, :], 0), axis=1
    ).astype(jnp.int32)
    ints = jnp.concatenate([bucket_len, batch_count, utt_lengths[0]])
    ints = jnp.broadcast_to(jnp.pad(ints, (0, 128 - ints.shape[0]))[None], (8, 128)).astype(jnp.int32)
    conv_pad = jnp.pad(conv_params.T, ((0, 40 - KERNEL - 2), (0, 128 - channels)))
    full, frames_v, ograd_v, ints_all, conv_all = gather(
        ndp, nh, masters_t.astype(BF16), frames, out_grad, ints, conv_pad
    )
    z = lax.axis_index("head")
    core = lax.axis_index("dp") % 2
    part = 2 * (z // 2) + core
    meta = jnp.where(z % 2 == 0, ints_all[0, 0, 0:16], ints_all[1, 0, 0:16])
    meta = jnp.where(jnp.arange(16) == 10, part * rows, meta).astype(jnp.int32)
    taps = jnp.transpose(conv_all[:, :, :channels], (1, 0, 2)).reshape(40, D)
    cos, sin = (jnp.asarray(t) for t in rope_tables())
    x1, q, kv = front(nh, meta, inv, frames_v, norm_params, cos, sin, full)
    kvw, qh, x1h = keys(ndp, nh, kv, q, x1)
    o, lse, x2, gated, h, sums = attend(nh, meta, inv, q, kvw, x1, qh, x1h, norm_params, taps, full)
    (stats,) = totals(ndp, nh, 3, sums)
    out_v, g3, gz, bpart, ng, grads = middle(nh, meta, inv, x2, h, stats, ograd_v, norm_params, taps, full)
    bsums, gzh, hh = totals(ndp, nh, 4, bpart, (gz, h))
    g2, do, dtaps, ng, grads = conv_back(
        nh, meta, inv, gz, gzh, h, hh, stats, bsums, gated, x2, g3, o, norm_params, taps, full, ng, grads
    )
    dq, dkv, dkv_send = attend_back(meta, q, kvw, do, lse)
    recv = key_grads(ndp, nh, dkv_send, rows)
    fg_v, ng, grads = rear(
        nh, meta, inv, dq, dkv, recv, x1, frames_v, g2, norm_params, cos, sin, full, ng, grads
    )
    small = jnp.concatenate([ng, dtaps], axis=0)
    owned, small, out_w, fg_w = scatter(ndp, nh, grads, small, out_v, fg_v)
    (
        new_m,
        new_f,
        new_s,
        norm_grads,
        new_norms,
        norm_first_new,
        norm_second_new,
        new_conv,
        conv_first_new,
        conv_second_new,
        layer_out,
        frames_grad,
    ) = update(
        nh,
        jnp.reshape(z, (1,)),
        owned,
        masters_t,
        flip(first_moment),
        flip(second_moment),
        left_basis[0],
        right_basis[0],
        small,
        bsums,
        norm_params,
        norm_first,
        norm_second,
        conv_params.T,
        conv_first.T,
        conv_second.T,
        out_w,
        fg_w,
    )

    def unflip(a):
        return jnp.transpose(a, (0, 2, 1))[None]

    return (
        layer_out,
        frames_grad,
        unflip(new_m),
        unflip(new_f),
        unflip(new_s),
        norm_grads,
        new_norms,
        norm_first_new,
        norm_second_new,
        new_conv.T,
        conv_first_new.T,
        conv_second_new.T,
    )


def solution(mesh):
    both, blocks, chan = P(("dp", "head"), None), P("head", "dp", None, None), P("head", None)
    placed = (both, both, P("dp"), P("dp"), P("dp", None), P()) + (blocks,) * 5 + (P(),) * 3 + (chan,) * 3
    return jax.shard_map(
        functools.partial(per_device, mesh.shape["dp"], mesh.shape["head"]),
        mesh=mesh,
        in_specs=placed,
        out_specs=(both, both) + (blocks,) * 3 + (P(),) * 4 + (chan,) * 3,
        check_vma=False,
    )
```

```python
import functools
import math

import jax
import jax.numpy as jnp
import numpy as np
from jax import lax
from jax.experimental import pallas as pl
from jax.experimental.pallas import tpu as pltpu
from jax.sharding import PartitionSpec as P

D = 512
FF = 2048
HD = 64
KERNEL = 32
BLOCKW = 64
STEP = 10
LONGEST = 1024
HALO = 16

beta_one = 0.9
beta_two = 0.95
step_rate = 0.05
weight_decay = 0.01
adam_eps = 1e-08
norm_eps = 1e-05
masked_score = -1e30
FACTOR = step_rate * math.sqrt(1.0 - beta_two**STEP) / (1.0 - beta_one**STEP)

F32 = jnp.float32
BF16 = jnp.bfloat16
MESH = pl.DeviceIdType.MESH
ANY = pl.BlockSpec(memory_space=pl.ANY)
HBM = pl.BlockSpec(memory_space=pltpu.HBM)
VM = pl.BlockSpec(memory_space=pltpu.VMEM)
SM = pl.BlockSpec(memory_space=pltpu.SMEM)
MIB = 1 << 20


def cost(us):
    return pl.CostEstimate(flops=0, bytes_accessed=int(us * 3.6e6), transcendentals=0)


def params(mib, collective_id=None):
    if collective_id is None:
        return pltpu.CompilerParams(vmem_limit_bytes=mib * MIB)
    return pltpu.CompilerParams(
        vmem_limit_bytes=mib * MIB, collective_id=collective_id, has_side_effects=True
    )


def big(nh, slots):
    return max(nh, -(-64 * MIB // (slots * BLOCKW * D * 2)))


class Copies:
    def __init__(self, sends):
        self.sends = sends
        self.used = 0
        self.open = []

    def send(self, src, dst, recv_sem, device, when=None):
        copy = pltpu.make_async_remote_copy(
            src_ref=src,
            dst_ref=dst,
            send_sem=self.sends.at[self.used],
            recv_sem=recv_sem,
            device_id=device,
            device_id_type=MESH,
        )
        (pl.when(when) if when is not None else call)(copy.start)
        self.used += 1
        self.open.append((copy, when))

    def finish(self):
        for copy, when in self.open:
            (pl.when(when) if when is not None else call)(copy.wait_send)


def call(f):
    return f()


def arrived(ref, sem):
    pltpu.make_async_copy(ref, ref, sem).wait()


def greet(devices):
    barrier = pltpu.get_barrier_semaphore()
    for device in devices:
        pl.semaphore_signal(barrier, inc=1, device_id=device, device_id_type=MESH)
    pl.semaphore_wait(barrier, len(devices))


class Place:
    def __init__(self, ndp, nh):
        self.ndp, self.nh, self.nchip = ndp, nh, ndp // 2
        self.dp = lax.axis_index("dp")
        self.z = lax.axis_index("head")
        self.core = self.dp % 2
        self.chip = self.dp // 2
        self.group_core = self.z % 2
        self.part = 2 * (self.z // 2) + self.core

    def of_part(self, part):
        return (self.chip * 2 + part % 2, 2 * (part // 2) + self.group_core)

    def core_peer(self):
        return (self.chip * 2 + 1 - self.core, self.z)

    def swap_peer(self):
        return (self.chip * 2 + 1 - self.core, self.part)

    def x_chip(self):
        return self.chip + 1 - 2 * (self.chip % 2)

    def y_chip(self):
        return (self.chip + 2) % 4


def gather_kernel(ndp, nh, spd, own, frames, ograd, bucket, batch, utts, conv, full, frames_o, ograd_o, ints_o, conv_o, ints, sends, recvs, extra, isem, local):
    me = Place(ndp, nh)
    dp, z, core, chip, nchip = me.dp, me.z, me.core, me.chip, me.nchip

    def shard(h, ch, c):
        return full.at[h, pl.ds((ch * 2 + c) * spd, spd)]

    def sem(h, ch, c, half=0):
        return recvs.at[h * ndp + ch * 2 + c, half]

    peer = me.core_peer()
    swap = me.core != me.z % 2
    columns = [(dp, (z + i) % nh) for i in range(1, nh)]
    square = nchip == 4
    if square:
        planes = [(me.x_chip() * 2 + core, z), (me.y_chip() * 2 + core, z)]
    else:
        planes = [(((chip + i) % nchip) * 2 + core, z) for i in range(1, nchip)]
    ints[...] = jnp.zeros_like(ints)
    ints[0:1, 0:1] = bucket[...]
    ints[0:1, 1:2] = batch[...]
    ints[0:1, 2:10] = utts[...]
    barrier = pltpu.get_barrier_semaphore()
    near = totals_peers(me)
    for device in near:
        pl.semaphore_signal(barrier, inc=1, device_id=device, device_id_type=MESH)

    @pl.when(swap)
    def _():
        pl.semaphore_signal(barrier, inc=1, device_id=me.swap_peer(), device_id_type=MESH)

    pl.semaphore_wait(barrier, len(near) + (core + z) % 2)

    copies = Copies(sends)
    mine = shard(z, chip, core)
    below, above = (dp, (z + nh - 1) % nh), (dp, (z + 1) % nh)
    copies.send(own, mine, sem(z, chip, core), above, z < nh - 1)
    copies.send(own, mine, sem(z, chip, core), below, z > 0)
    for device in planes:
        copies.send(own, mine, sem(z, chip, core), device)
    copies.send(own, mine, sem(z, chip, core), peer)
    keep = [
        pltpu.make_async_copy(own, mine, local.at[0]),
        pltpu.make_async_copy(ints, ints_o.at[dp], local.at[1]),
        pltpu.make_async_copy(conv, conv_o.at[z], local.at[2]),
    ]
    for copy in keep:
        copy.start()

    @pl.when(jnp.logical_not(swap))
    def _():
        for k, (src, dst) in enumerate(((frames, frames_o), (ograd, ograd_o))):
            pltpu.make_async_copy(src, dst, local.at[3 + k]).start()

    def column(step, up):
        h = z - step if up else z + step
        there = z >= step if up else z + step < nh
        onward = z < nh - 1 if up else z > 0
        h = jnp.where(there, h, z)
        s, r = shard(h, chip, core), sem(h, chip, core)

        @pl.when(there)
        def _():
            arrived(s, r)

        if step < nh - 1:
            copies.send(s, s, r, above if up else below, jnp.logical_and(there, onward))
        for device in planes:
            copies.send(s, s, r, device, there)
        copies.send(s, s, r, peer, there)

    def beside(step, up):
        h = z - step if up else z + step
        there = z >= step if up else z + step < nh
        h = jnp.where(there, h, z)
        if not square:
            for k in range(1, nchip):
                ch = (chip + k) % nchip

                @pl.when(there)
                def _():
                    arrived(shard(h, ch, core), sem(h, ch, core))

                copies.send(shard(h, ch, core), shard(h, ch, core), sem(h, ch, core), peer, there)
            return
        half = spd // 2
        for side, (ch, device) in enumerate(((me.x_chip(), planes[1]), (me.y_chip(), planes[0]))):

            @pl.when(there)
            def _():
                arrived(shard(h, ch, core), sem(h, ch, core))

            piece = full.at[h, pl.ds((ch * 2 + core) * spd + side * half, half)]
            copies.send(piece, piece, sem(h, ch, core, side), device, there)
            copies.send(shard(h, ch, core), shard(h, ch, core), sem(h, ch, core), peer, there)

    def across(step, up):
        if not square:
            return
        h = z - step if up else z + step
        there = z >= step if up else z + step < nh
        h = jnp.where(there, h, z)
        half = spd // 2
        ch = 3 - chip

        @pl.when(there)
        def _():
            for side in range(2):
                piece = full.at[h, pl.ds((ch * 2 + core) * spd + side * half, half)]
                arrived(piece, sem(h, ch, core, side))

        copies.send(shard(h, ch, core), shard(h, ch, core), sem(h, ch, core), peer, there)

    visits = [(0, True)] + [(step, up) for step in range(1, nh) for up in (True, False)]
    lag = 2
    for i in range(len(visits) + 2 * lag):
        if 0 < i < len(visits):
            column(*visits[i])
        if i == len(visits) - 1:
            for device in columns:
                copies.send(conv, conv_o.at[z], extra.at[3 + z], device)
            for k in range(1, ndp):
                copies.send(ints, ints_o.at[dp], isem.at[dp], ((dp + k) % ndp, z))

            @pl.when(swap)
            def _():
                for k, (src, dst) in enumerate(((frames, frames_o), (ograd, ograd_o))):
                    pltpu.make_async_remote_copy(
                        src_ref=src, dst_ref=dst, send_sem=local.at[3 + k], recv_sem=extra.at[1 + k],
                        device_id=me.swap_peer(), device_id_type=MESH,
                    ).start()

        if 0 <= i - lag < len(visits):
            beside(*visits[i - lag])
        if i >= 2 * lag:
            across(*visits[i - 2 * lag])
    for i in range(nh):
        h = (z + nh - i) % nh
        for k in range(nchip):
            ch = (chip + k) % nchip
            arrived(shard(h, ch, 1 - core), sem(h, ch, 1 - core))
    for k in range(1, ndp):
        arrived(ints_o.at[(dp + k) % ndp], isem.at[(dp + k) % ndp])
    for i in range(1, nh):
        h = (z + nh - i) % nh
        arrived(conv_o.at[h], extra.at[3 + h])

    @pl.when(swap)
    def _():
        arrived(frames_o, extra.at[1])
        arrived(ograd_o, extra.at[2])

    for i, ref in enumerate((frames, ograd)):
        arrived(ref, local.at[3 + i])
    for copy in keep:
        copy.wait()
    copies.finish()


def gather(ndp, nh, own, frames, ograd, bucket, batch, utts, conv):
    spd = own.shape[0]
    nchip = ndp // 2
    plane = 2 if nchip == 4 else nchip - 1
    visits = 2 * nh - 1
    halves = 2 * visits if nchip == 4 else 0
    count = 2 * visits + visits * (plane + 1) + visits * (nchip - 1) + halves + (ndp - 1) + (nh - 1)
    shapes = [
        jax.ShapeDtypeStruct((big(nh, ndp * spd), ndp * spd, BLOCKW, D), BF16),
        jax.ShapeDtypeStruct(frames.shape, BF16),
        jax.ShapeDtypeStruct(ograd.shape, BF16),
        jax.ShapeDtypeStruct((ndp, 8, 128), jnp.int32),
        jax.ShapeDtypeStruct((nh,) + conv.shape, F32),
    ]
    dma = pltpu.SemaphoreType.DMA
    return pl.pallas_call(
        functools.partial(gather_kernel, ndp, nh, spd),
        out_shape=shapes,
        in_specs=[ANY, HBM, HBM, VM, VM, VM, ANY],
        out_specs=[HBM] * 3 + [ANY] * 2,
        scratch_shapes=[
            pltpu.VMEM((8, 128), jnp.int32),
            dma((count,)),
            dma((nh * ndp, 2)),
            dma((3 + nh,)),
            dma((ndp,)),
            dma((5,)),
        ],
        compiler_params=params(52, 1),
        cost_estimate=cost(60),
        name="gather",
    )(own, frames, ograd, bucket, batch, utts, conv)


def totals_step(me, small, first, second, copies, sem1, sem2, local):
    ndp, nh = me.ndp, me.nh

    def one():
        for i in range(1, ndp):
            copies.send(small, first.at[me.dp], sem1.at[me.dp], ((me.dp + i) % ndp, me.z))
        first[me.dp] = small[...]

    def two():
        for i in range(1, ndp):
            src = (me.dp + i) % ndp
            arrived(first.at[src], sem1.at[src])
        total = first[0]
        for i in range(1, ndp):
            total = total + first[i]
        second[me.z] = total
        for i in range(1, nh):
            copies.send(second.at[me.z], second.at[me.z], sem2.at[me.z], (me.dp, (me.z + i) % nh))

    def three():
        for i in range(1, nh):
            src = (me.z + i) % nh
            arrived(second.at[src], sem2.at[src])
        total = second[0]
        for i in range(1, nh):
            total = total + second[i]
        return total

    return one, two, three


def totals_peers(me):
    return [((me.dp + i) % me.ndp, me.z) for i in range(1, me.ndp)] + [
        (me.dp, (me.z + i) % me.nh) for i in range(1, me.nh)
    ]


def totals_kernel(ndp, nh, halos, *refs):
    me = Place(ndp, nh)
    small = refs[0]
    edges = refs[1 : 1 + halos]
    out = refs[1 + halos]
    edges_o = refs[2 + halos : 2 + 2 * halos]
    first, second, sends, sem1, sem2, hsem = refs[2 + 2 * halos :]
    greet(totals_peers(me))
    copies = Copies(sends)
    one, two, three = totals_step(me, small, first, second, copies, sem1, sem2, None)
    one()
    for i in range(halos):
        send_edges(me, edges[i], edges_o[i], copies, hsem.at[2 * i], hsem.at[2 * i + 1])
    two()
    out[...] = three()
    for i in range(halos):
        arrived(edges_o[i].at[pl.ds(0, HALO)], hsem.at[2 * i])
        arrived(edges_o[i].at[pl.ds(HALO, HALO)], hsem.at[2 * i + 1])
    copies.finish()


def window(me, rows):
    span = LONGEST // rows
    at = me.part % span
    return span, at, me.part - at


def send_edges(me, src, dst, copies, sem_before, sem_after):
    rows = src.shape[0]
    span, at, base = window(me, rows)
    after = me.of_part(base + (at + 1) % span)
    before = me.of_part(base + (at + span - 1) % span)
    copies.send(src.at[pl.ds(rows - HALO, HALO)], dst.at[pl.ds(0, HALO)], sem_before, after)
    copies.send(src.at[pl.ds(0, HALO)], dst.at[pl.ds(HALO, HALO)], sem_after, before)


def totals(ndp, nh, collective_id, small, edges=()):
    dma = pltpu.SemaphoreType.DMA
    n = len(edges)
    halo = [jax.ShapeDtypeStruct((2 * HALO, D), e.dtype) for e in edges]
    return pl.pallas_call(
        functools.partial(totals_kernel, ndp, nh, n),
        out_shape=[jax.ShapeDtypeStruct(small.shape, F32)] + halo,
        in_specs=[VM] + [ANY] * n,
        out_specs=[VM] + [ANY] * n,
        scratch_shapes=[
            pltpu.VMEM((ndp,) + small.shape, F32),
            pltpu.VMEM((nh,) + small.shape, F32),
            dma((ndp + nh - 2 + 2 * n,)),
            dma((ndp,)),
            dma((nh,)),
            dma((2 * n + 1,)),
        ],
        compiler_params=params(16, collective_id),
        cost_estimate=cost(8),
        name=f"totals_{collective_id}",
    )(small, *edges)


def keys_kernel(ndp, nh, kv, q, x1, kv_o, q_o, x1_o, sends, recvs, local):
    me = Place(ndp, nh)
    rows = kv.shape[0]
    span, at, base = window(me, rows)
    peers = [me.of_part(base + (at + i) % span) for i in range(1, span)]
    greet(peers)
    copies = Copies(sends)
    place = kv_o.at[pl.ds(at * rows, rows)]
    for device in peers:
        copies.send(kv, place, recvs.at[at], device)
    own = pltpu.make_async_copy(kv, place, local.at[0])
    own.start()
    for i, (src, dst) in enumerate(((q, q_o), (x1, x1_o))):
        send_edges(me, src, dst, copies, recvs.at[span + 2 * i], recvs.at[span + 2 * i + 1])
    for i in range(1, span):
        other = (at + i) % span
        arrived(kv_o.at[pl.ds(other * rows, rows)], recvs.at[other])
    for i, dst in enumerate((q_o, x1_o)):
        arrived(dst.at[pl.ds(0, HALO)], recvs.at[span + 2 * i])
        arrived(dst.at[pl.ds(HALO, HALO)], recvs.at[span + 2 * i + 1])
    own.wait()
    copies.finish()


def keys(ndp, nh, kv, q, x1):
    span = LONGEST // kv.shape[0]
    dma = pltpu.SemaphoreType.DMA
    return pl.pallas_call(
        functools.partial(keys_kernel, ndp, nh),
        out_shape=[
            jax.ShapeDtypeStruct((LONGEST, 2 * D), BF16),
            jax.ShapeDtypeStruct((2 * HALO, D), BF16),
            jax.ShapeDtypeStruct((2 * HALO, D), F32),
        ],
        in_specs=[ANY] * 3,
        out_specs=[ANY] * 3,
        scratch_shapes=[dma((span + 3,)), dma((span + 4,)), dma((1,))],
        compiler_params=params(8, 2),
        cost_estimate=cost(3),
        name="keys",
    )(kv, q, x1)


def key_grads_kernel(ndp, nh, part, out, sends, recvs):
    me = Place(ndp, nh)
    rows = out.shape[1]
    span, at, base = window(me, rows)
    greet([me.of_part(base + (at + i) % span) for i in range(1, span)])
    copies = Copies(sends)
    for i in range(1, span):
        other = (at + i) % span
        copies.send(part.at[pl.ds(other * rows, rows)], out.at[i - 1], recvs.at[i - 1], me.of_part(base + other))
    for i in range(1, span):
        arrived(out.at[i - 1], recvs.at[i - 1])
    copies.finish()


def key_grads(ndp, nh, part, rows):
    span = LONGEST // rows
    dma = pltpu.SemaphoreType.DMA
    return pl.pallas_call(
        functools.partial(key_grads_kernel, ndp, nh),
        out_shape=jax.ShapeDtypeStruct((span - 1, rows, 2 * D), BF16),
        in_specs=[ANY],
        out_specs=ANY,
        scratch_shapes=[dma((span - 1,)), dma((span - 1,))],
        compiler_params=params(8, 5),
        cost_estimate=cost(3),
        name="key_grads",
    )(part)


def far_first(z, nh):
    orders = [sorted(range(nh), key=lambda h: (-abs(h - at), h)) for at in range(nh)]
    return [sum((orders[at][i] * (z == at).astype(jnp.int32) for at in range(nh)), 0) for i in range(nh)]


def scatter_kernel(ndp, nh, spd, grads, small, out_v, fgrad_v, owned, small_o, out_o, fgrad_o, part, cores, side_x, side_y, half_x, half_y, zrecv, first, second, sends, csem, psem, xsem, zsem, sem1, sem2, esem, local):
    me = Place(ndp, nh)
    dp, z, core, chip, nchip = me.dp, me.z, me.core, me.chip, me.nchip
    square = nchip == 4
    peer = me.core_peer()
    swap = me.core != me.z % 2
    half = spd // 2
    barrier = pltpu.get_barrier_semaphore()
    near = totals_peers(me)
    for device in near:
        pl.semaphore_signal(barrier, inc=1, device_id=device, device_id_type=MESH)

    @pl.when(swap)
    def _():
        pl.semaphore_signal(barrier, inc=1, device_id=me.swap_peer(), device_id_type=MESH)

    pl.semaphore_wait(barrier, len(near) + (core + z) % 2)
    copies = Copies(sends)
    order = far_first(z, nh)
    if square:
        chips = [3 - chip, me.x_chip(), me.y_chip(), chip]
    else:
        chips = [(chip + i + 1) % nchip for i in range(nchip)]
    loads = {}

    def begin(i):
        for k, ch in enumerate(chips):
            copies.send(grads.at[order[i], pl.ds((ch * 2 + 1 - core) * spd, spd)], cores.at[i, k], csem.at[i, k], peer)
            load = pltpu.make_async_copy(
                grads.at[order[i], pl.ds((ch * 2 + core) * spd, spd)], part.at[i, k], psem.at[i, k]
            )
            load.start()
            loads[i, k] = load

    begin(0)
    one, two, three = totals_step(me, small, first, second, copies, sem1, sem2, None)
    one()

    @pl.when(swap)
    def _():
        for i, (src, dst) in enumerate(((out_v, out_o), (fgrad_v, fgrad_o))):
            pltpu.make_async_remote_copy(
                src_ref=src, dst_ref=dst, send_sem=local.at[i], recv_sem=esem.at[i],
                device_id=me.swap_peer(), device_id_type=MESH,
            ).start()

    @pl.when(jnp.logical_not(swap))
    def _():
        for i, (src, dst) in enumerate(((out_v, out_o), (fgrad_v, fgrad_o))):
            pltpu.make_async_copy(src, dst, local.at[i]).start()

    def add(i, k, others, lo=0, n=spd):
        @pl.loop(0, n, unroll=True)
        def _(s):
            total = part[i, k, lo + s].astype(F32)
            for other in others:
                total = total + other(s).astype(F32)
            part[i, k, lo + s] = total.astype(BF16)

    def meet(i, k):
        loads[i, k].wait()
        arrived(cores.at[i, k], csem.at[i, k])

    planes = [(me.x_chip() * 2 + core, z), (me.y_chip() * 2 + core, z)]

    def stage_a(i):
        if square:
            meet(i, 0)
            add(i, 0, [lambda s: cores[i, 0, s]])
            copies.send(part.at[i, 0, pl.ds(0, half)], half_x.at[i], xsem.at[i, 0], planes[0])
            copies.send(part.at[i, 0, pl.ds(half, half)], half_y.at[i], xsem.at[i, 1], planes[1])
        else:
            for k in range(nchip - 1):
                meet(i, k)
                add(i, k, [lambda s: cores[i, k, s]])
                copies.send(part.at[i, k], side_x.at[i, k], xsem.at[i, k], (chips[k] * 2 + core, z))

    def stage_b(i):
        if not square:
            return
        meet(i, 1)
        add(i, 1, [lambda s: cores[i, 1, s]], 0, half)
        arrived(half_y.at[i], xsem.at[i, 1])
        add(i, 1, [lambda s: cores[i, 1, half + s], lambda s: half_y[i, s]], half, half)
        copies.send(part.at[i, 1], side_x.at[i, 0], xsem.at[i, 2], planes[0])
        meet(i, 2)
        add(i, 2, [lambda s: cores[i, 2, half + s]], half, half)
        arrived(half_x.at[i], xsem.at[i, 0])
        add(i, 2, [lambda s: cores[i, 2, s], lambda s: half_x[i, s]], 0, half)
        copies.send(part.at[i, 2], side_y.at[i], xsem.at[i, 3], planes[1])

    last = nchip - 1

    def stage_c(i):
        meet(i, last)
        if square:
            arrived(side_x.at[i, 0], xsem.at[i, 2])
            arrived(side_y.at[i], xsem.at[i, 3])
            others = [lambda s: cores[i, last, s], lambda s: side_x[i, 0, s], lambda s: side_y[i, s]]
        else:
            others = [lambda s: cores[i, last, s]]
            for k in range(nchip - 1):
                arrived(side_x.at[i, k], xsem.at[i, k])
                others.append(lambda s, k=k: side_x[i, k, s])
        add(i, last, others)
        if i < nh - 1:
            copies.send(part.at[i, last], zrecv.at[z], zsem.at[z], (dp, order[i]))

    for i in range(nh + 2):
        if i + 1 < nh:
            begin(i + 1)
        if i < nh:
            stage_a(i)
        if 0 <= i - 1 < nh:
            stage_b(i - 1)
        if i == 1:
            two()
        if i >= 2:
            stage_c(i - 2)
    small_o[...] = three()
    sources = [(z + i) % nh for i in range(1, nh)]
    for src in sources:
        arrived(zrecv.at[src], zsem.at[src])

    @pl.loop(0, spd)
    def _(s):
        total = part[nh - 1, last, s].astype(F32)
        for src in sources:
            total = total + zrecv[src, s].astype(F32)
        owned[s] = total

    @pl.when(swap)
    def _():
        arrived(out_o, esem.at[0])
        arrived(fgrad_o, esem.at[1])

    arrived(out_v, local.at[0])
    arrived(fgrad_v, local.at[1])
    copies.finish()


def scatter(ndp, nh, grads, small, out_v, fgrad_v):
    spd = grads.shape[1] // ndp
    nchip = ndp // 2
    square = nchip == 4
    dma = pltpu.SemaphoreType.DMA
    block = (spd, BLOCKW, D)
    halfb = (max(spd // 2, 1), BLOCKW, D)
    sides = 1 if square else nchip - 1
    sent = nh * nchip + (ndp - 1) + (nh - 1) + (nh * 4 if square else nh * (nchip - 1)) + (nh - 1)
    return pl.pallas_call(
        functools.partial(scatter_kernel, ndp, nh, spd),
        out_shape=[
            jax.ShapeDtypeStruct(block, F32),
            jax.ShapeDtypeStruct(small.shape, F32),
            jax.ShapeDtypeStruct(out_v.shape, out_v.dtype),
            jax.ShapeDtypeStruct(fgrad_v.shape, fgrad_v.dtype),
        ],
        in_specs=[HBM, VM, HBM, HBM],
        out_specs=[VM, VM, HBM, HBM],
        scratch_shapes=[
            pltpu.VMEM((nh, nchip) + block, BF16),
            pltpu.VMEM((nh, nchip) + block, BF16),
            pltpu.VMEM((nh, sides) + block, BF16),
            pltpu.VMEM((nh,) + block, BF16),
            pltpu.VMEM((nh,) + halfb, BF16),
            pltpu.VMEM((nh,) + halfb, BF16),
            pltpu.VMEM((nh,) + block, BF16),
            pltpu.VMEM((ndp,) + small.shape, F32),
            pltpu.VMEM((nh,) + small.shape, F32),
            dma((sent,)),
            dma((nh, nchip)),
            dma((nh, nchip)),
            dma((nh, max(4, nchip))),
            dma((nh,)),
            dma((ndp,)),
            dma((nh,)),
            dma((2,)),
            dma((2,)),
        ],
        compiler_params=params(28, 6),
        cost_estimate=cost(65),
        name="scatter",
    )(grads, small, out_v, fgrad_v)


def nn(a, b):
    return jnp.dot(a, b, preferred_element_type=F32)


def nt(a, b):
    return lax.dot_general(a, b, (((1,), (1,)), ((), ())), preferred_element_type=F32)


def tn(a, b):
    return lax.dot_general(a, b, (((0,), (0,)), ((), ())), preferred_element_type=F32)


def sigmoid(v):
    return 0.5 * jnp.tanh(0.5 * v) + 0.5


def slope_of(v, sig):
    return sig * (1.0 + v * (1.0 - sig))


class Blocks:
    def __init__(self, nh):
        self.nh = nh
        ff, ch = FF // nh // BLOCKW, D // nh // BLOCKW
        self.ff, self.ch = ff, ch
        self.in_one, self.in_two = 0, ff
        self.query = 2 * ff
        self.key = self.query + ch
        self.value = self.key + ch
        self.conv_value = self.value + ch
        self.conv_gate = self.conv_value + ch
        rows = self.conv_gate + ch
        self.out_one, self.out_two = rows, rows + ff
        self.attn = rows + 2 * ff
        self.point = self.attn + ch
        self.total = self.point + ch


def fetch(full, inv, dst, sem, base, count, part, row):
    for j in range(count):
        pltpu.make_async_copy(
            full.at[part, inv[base + j]], dst.at[pl.ds(row + j * BLOCKW, BLOCKW)], sem
        ).start()


def fetch_all(full, inv, dst, sem, base, count, nh, row=0):
    for part in range(nh):
        fetch(full, inv, dst, sem, base, count, part, row + part * count * BLOCKW)


def landed(dst, sem):
    pltpu.make_async_copy(dst, dst, sem).wait()


def put(grads, inv, src, sem, base, count, part, row):
    for j in range(count):
        pltpu.make_async_copy(
            src.at[pl.ds(row + j * BLOCKW, BLOCKW)], grads.at[part, inv[base + j]], sem
        ).start()


def put_all(grads, inv, src, sem, base, count, nh, row=0):
    for part in range(nh):
        put(grads, inv, src, sem, base, count, part, row + part * count * BLOCKW)


def tables(meta, frame):
    length, batch = meta[0], meta[1]
    utterance = jnp.zeros_like(frame)
    for i in range(1, 8):
        utterance = utterance + (frame >= i * length).astype(jnp.int32)
    within = frame - utterance * length
    own = jnp.zeros_like(frame)
    for i in range(8):
        own = jnp.where(utterance == i, meta[2 + i], own)
    live = (utterance < batch) & (within < own)
    return utterance, within, live


def live_rows(meta, start, count):
    frame = start + lax.broadcasted_iota(jnp.int32, (count, 1), 0)
    return tables(meta, frame)[2].astype(F32)


def hat(x):
    center = jnp.mean(x, axis=1, keepdims=True)
    offset = x - center
    spread = lax.rsqrt(jnp.mean(offset * offset, axis=1, keepdims=True) + norm_eps)
    return offset * spread, spread


def norm(x, norms, i):
    return hat(x)[0] * norms[i : i + 1, :] + norms[i + 5 : i + 6, :]


def norm_back(x, grad, gain):
    return hat_back(*hat(x), grad, gain)


def hat_back(xhat, spread, grad, gain):
    scaled = grad * gain
    inner = scaled - jnp.mean(scaled, axis=1, keepdims=True) - xhat * jnp.mean(scaled * xhat, axis=1, keepdims=True)
    return spread * inner, jnp.sum(grad * xhat, axis=0, keepdims=True), jnp.sum(grad, axis=0, keepdims=True)


BAND = 64


def bands(rows, body, init=()):
    return lax.fori_loop(0, rows // BAND, lambda i, c: body(pl.ds(pl.multiple_of(i * BAND, BAND), BAND), i, c), init, unroll=True)


def partner(x):
    lane = lax.broadcasted_iota(jnp.int32, x.shape, 1) % HD
    return jnp.where(lane < HD // 2, pltpu.roll(x, 128 - HD // 2, 1), pltpu.roll(x, HD // 2, 1))


def turn(x, table, sign):
    first = lax.broadcasted_iota(jnp.int32, table.shape, 1) % HD < HD // 2
    cos = jnp.where(first, table, pltpu.roll(table, HD // 2, 1))
    sin = jnp.where(first, -pltpu.roll(table, 128 - HD // 2, 1), table)
    parts = []
    for i in range(D // 128):
        piece = x[:, i * 128 : (i + 1) * 128]
        parts.append(piece * cos + partner(piece) * (sign * sin))
    return jnp.concatenate(parts, axis=1)


def rope_table():
    freq = np.exp(np.arange(HD // 2, dtype=np.float32) * np.float32(-math.log(10000.0) / (HD // 2)))
    angle = np.arange(LONGEST, dtype=np.float32)[:, None] * freq[None, :].astype(np.float32)
    return np.tile(np.concatenate([np.cos(angle), np.sin(angle)], axis=1), (1, 2)).astype(np.float32)


def place_of(meta, i):
    return pl.multiple_of(lax.rem(meta[10] + i * BAND, meta[0]), BAND)


def feed(n_ref, w_in, w_out, acc_ref, sem, sem2, nh):
    unit = FF // nh
    for part in range(nh):
        rows = pl.ds(part * unit, unit)
        landed(w_in.at[rows], sem.at[part])
        pre = nt(n_ref[...], w_in[rows, :])
        act = (pre * sigmoid(pre)).astype(BF16)
        landed(w_out.at[rows], sem2.at[part])
        if part == 0:
            acc_ref[...] = nn(act, w_out[rows, :])
        else:
            acc_ref[...] += nn(act, w_out[rows, :])


def feed_back(n_ref, gb_ref, w_in, w_out, acc_ref, g_in, g_out, grads, inv, base_in, base_out, sem_in, sem_out, count, nh):
    unit = FF // nh

    def body(part, carry):
        rows = pl.ds(pl.multiple_of(part * unit, unit), unit)
        n, gb, win, wout = n_ref[...], gb_ref[...], w_in[rows, :], w_out[rows, :]
        pre = nt(win, n)
        sig = sigmoid(pre)
        act = (pre * sig).astype(BF16)
        dpre = (nt(wout, gb) * slope_of(pre, sig)).astype(BF16)
        g_out[rows, :] = nn(act, gb).astype(BF16)
        g_in[rows, :] = nn(dpre, n).astype(BF16)
        acc_ref[...] += tn(dpre, win)
        put(grads, inv, g_out, sem_out, base_out, count, part, part * unit)
        put(grads, inv, g_in, sem_in, base_in, count, part, part * unit)
        return carry

    acc_ref[...] = jnp.zeros_like(acc_ref)
    lax.fori_loop(0, nh, body, 0)


def front_kernel(ndp, nh, owner, place, ints, conv, frames, norms, table, full, x1, q, kv, meta, inv, taps, w_in, w_out, w_qkv, n_ref, acc, groups, sem, sem2, sem3):
    b = Blocks(nh)
    known = pltpu.make_async_copy(ints, groups, sem3.at[1])
    known.start()

    def slot(i, c):
        inv[owner[i]] = i
        return c

    lax.fori_loop(0, owner.shape[0], slot, 0)
    rows = frames.shape[0]
    unit = FF // nh
    for part in range(nh):
        fetch(full, inv, w_in, sem.at[part], b.in_one, b.ff, part, part * unit)
        fetch(full, inv, w_out, sem2.at[part], b.out_one, b.ff, part, part * unit)
    for i, base in enumerate((b.query, b.key, b.value)):
        fetch_all(full, inv, w_qkv, sem3.at[0], base, b.ch, nh, i * D)

    def first(at, i, c):
        n_ref[at, :] = norm(frames[at, :].astype(F32), norms, 0).astype(BF16)
        return c

    bands(rows, first)
    known.wait()
    for i in range(16):
        meta[i] = groups[place[0], 0, i]
    meta[10] = place[1] * rows

    def count(d, total):
        for u in range(8):
            total += jnp.where(u < groups[d, 0, 1], jnp.minimum(groups[d, 0, 2 + u], groups[d, 0, 0]), 0)
        return total

    meta[11] = lax.fori_loop(0, ndp, count, 0)
    taps[...] = jnp.zeros_like(taps)
    width = conv.shape[2]
    for h in range(nh):
        taps[0 : KERNEL + 2, h * width : (h + 1) * width] = conv[h]
    feed(n_ref, w_in, w_out, acc, sem, sem2, nh)

    def second(at, i, c):
        x = frames[at, :].astype(F32) + 0.5 * acc[at, :]
        x1[at, :] = x
        n_ref[at, :] = norm(x, norms, 1).astype(BF16)
        return c

    bands(rows, second)
    landed(w_qkv, sem3.at[0])
    for j, (dst, lo) in enumerate(((q, 0), (kv, 0), (kv, D))):
        acc[...] = nt(n_ref[...], w_qkv[j * D : (j + 1) * D, :])

        def third(at, i, c):
            x = acc[at, :]
            if j < 2:
                p = pl.ds(place_of(meta, i), BAND)
                x = turn(x, table[p, :], 1.0)
            dst[at, lo : lo + D] = x.astype(BF16)
            return c

        bands(rows, third)


def front(ndp, nh, owner, place, ints, conv, frames, norms, table, full):
    rows = frames.shape[0]
    dma = pltpu.SemaphoreType.DMA
    return pl.pallas_call(
        functools.partial(front_kernel, ndp, nh),
        out_shape=[
            jax.ShapeDtypeStruct((rows, D), F32),
            jax.ShapeDtypeStruct((rows, D), BF16),
            jax.ShapeDtypeStruct((rows, 2 * D), BF16),
            jax.ShapeDtypeStruct((16,), jnp.int32),
            jax.ShapeDtypeStruct(owner.shape, jnp.int32),
            jax.ShapeDtypeStruct((40, D), F32),
        ],
        in_specs=[SM, SM, ANY, VM, VM, VM, VM, HBM],
        out_specs=[VM, VM, VM, SM, SM, VM],
        scratch_shapes=[
            pltpu.VMEM((FF, D), BF16),
            pltpu.VMEM((FF, D), BF16),
            pltpu.VMEM((3 * D, D), BF16),
            pltpu.VMEM((rows, D), BF16),
            pltpu.VMEM((rows, D), F32),
            pltpu.SMEM((ndp, 8, 128), jnp.int32),
            dma((nh,)),
            dma((nh,)),
            dma((2,)),
        ],
        compiler_params=params(18),
        cost_estimate=cost(7),
        name="front",
    )(owner, place, ints, conv, frames, norms, table, full)


def fill_chunk(meta, src, chunk, k, start):
    lead = lax.rem(start + k * 256, meta[0]) != 0
    trail = lax.rem(start + (k + 1) * 256, meta[0]) != 0
    chunk[0:HALO, :] = jnp.where(lead, src[k * 256 : k * 256 + HALO, :], 0.0)
    chunk[HALO : HALO + 256, :] = src[k * 256 + HALO : k * 256 + HALO + 256, :]
    chunk[HALO + 256 :, :] = jnp.where(trail, src[k * 256 + HALO + 256 : k * 256 + 2 * HALO + 256, :], 0.0)


def shift_rows(chunk, moved):
    rows = chunk.shape[0]
    moved[0] = chunk[...]
    for b in range(1, 8):
        moved[b, 0 : rows - 8, :] = chunk[b : b + rows - 8, :]


def attend_kernel(nh, meta, inv, q, kvw, x1, qh, x1h, norms, taps, full, o_o, lse_o, x2_o, gated_o, h_o, sums_o, w_attn, w_glu, q_ext, o_ext, x_ext, bias, n_ref, val, gate, chunk, moved, lse_s, sem):
    b = Blocks(nh)
    rows = q.shape[0]
    ext = rows + 2 * HALO
    start = meta[10]
    fetch_all(full, inv, w_attn, sem.at[0], b.attn, b.ch, nh)
    for i, base in enumerate((b.conv_value, b.conv_gate)):
        fetch_all(full, inv, w_glu, sem.at[1], base, b.ch, nh, i * D)
    q_ext[0:HALO, :] = qh[0:HALO, :]
    q_ext[HALO : HALO + rows, :] = q[...]
    q_ext[HALO + rows :, :] = qh[HALO:, :]
    x_ext[0:HALO, :] = x1h[0:HALO, :]
    x_ext[HALO : HALO + rows, :] = x1[...]
    x_ext[HALO + rows :, :] = x1h[HALO:, :]
    base = start - lax.rem(start, LONGEST)
    key_frame = base + lax.broadcasted_iota(jnp.int32, (1, LONGEST), 1)
    ukey, _, lkey = tables(meta, key_frame)
    ukey = jnp.where(lkey, ukey, -1)
    query_frame = start - HALO + lax.broadcasted_iota(jnp.int32, (ext, 1), 0)
    uquery, _, lquery = tables(meta, query_frame)
    live = lquery.astype(F32)
    bias[...] = jnp.where(ukey == uquery, 0.0, masked_score)
    half = ext // 2
    head_lane = lax.broadcasted_iota(jnp.int32, (half, 128), 1)

    for pair in range(D // 128):
        lanes = slice(pair * 128, (pair + 1) * 128)
        kp = kvw[:, lanes]
        vp = kvw[:, D + pair * 128 : D + (pair + 1) * 128]
        for blk in range(2):
            at = slice(blk * half, (blk + 1) * half)
            qp = q_ext[at, lanes] * 0.125
            outs = []
            for hh in range(2):
                mine = head_lane < HD if hh == 0 else head_lane >= HD
                qm = jnp.where(mine, qp, jnp.zeros_like(qp))
                s = nt(qm, kp) + bias[at, :]
                top = jnp.max(s, axis=1, keepdims=True)
                e = jnp.exp(s - top)
                total = jnp.sum(e, axis=1, keepdims=True)
                outs.append(nn(e.astype(BF16), vp) * (1.0 / total))
                lse_s[at, pair * 2 + hh : pair * 2 + hh + 1] = top + jnp.log(total)
            o = jnp.where(head_lane < HD, outs[0], outs[1]) * live[at, :]
            o_ext[at, lanes] = o.astype(BF16)
    o_o[...] = o_ext[HALO : HALO + rows, :]
    lse_o[...] = jnp.transpose(lse_s[HALO : HALO + rows, :])[0:8, :]
    landed(w_attn, sem.at[0])
    x_ext[...] += nn(o_ext[...], w_attn[...])
    x2_o[...] = x_ext[HALO : HALO + rows, :]

    def third(i, c):
        at = pl.ds(pl.multiple_of(i * 32, 32), 32)
        n_ref[at, :] = norm(x_ext[at, :], norms, 2).astype(BF16)
        return c

    lax.fori_loop(0, ext // 32, third, 0, unroll=True)
    landed(w_glu, sem.at[1])
    val[...] = nt(n_ref[...], w_glu[0:D, :])
    gate[...] = nt(n_ref[...], w_glu[D:, :])
    gated_o[...] = val[...] * sigmoid(gate[...]) * live
    sums = [[0.0] * (D // 128) for _ in range(2)]
    for k in range(rows // 256):
        fill_chunk(meta, gated_o, chunk, k, start)
        alive = live[HALO + k * 256 : HALO + (k + 1) * 256, :]
        shift_rows(chunk, moved)
        for lc in range(D // 128):
            lanes = slice(lc * 128, (lc + 1) * 128)
            acc = moved[0, 0:256, lanes] * taps[0:1, lanes]
            for j in range(1, KERNEL):
                lo = j - j % 8
                acc = acc + moved[j % 8, lo : lo + 256, lanes] * taps[j : j + 1, lanes]
            h_o[k * 256 : (k + 1) * 256, lanes] = acc
            weighted = acc * alive
            sums[0][lc] += jnp.sum(weighted, axis=0, keepdims=True)
            sums[1][lc] += jnp.sum(weighted * acc, axis=0, keepdims=True)
    sums_o[...] = jnp.concatenate(sums[0] + sums[1], axis=0)


def attend(nh, meta, inv, q, kvw, x1, qh, x1h, norms, taps, full):
    rows = q.shape[0]
    ext = rows + 2 * HALO
    dma = pltpu.SemaphoreType.DMA
    f = jax.ShapeDtypeStruct
    return pl.pallas_call(
        functools.partial(attend_kernel, nh),
        out_shape=[
            f((rows, D), BF16),
            f((8, rows), F32),
            f((rows, D), F32),
            f((ext, D), F32),
            f((rows, D), F32),
            f((2 * D // 128, 128), F32),
        ],
        in_specs=[SM, SM] + [VM] * 7 + [HBM],
        out_specs=[VM] * 6,
        scratch_shapes=[
            pltpu.VMEM((D, D), BF16),
            pltpu.VMEM((2 * D, D), BF16),
            pltpu.VMEM((ext, D), BF16),
            pltpu.VMEM((ext, D), BF16),
            pltpu.VMEM((ext, D), F32),
            pltpu.VMEM((ext, LONGEST), F32),
            pltpu.VMEM((ext, D), BF16),
            pltpu.VMEM((ext, D), F32),
            pltpu.VMEM((ext, D), F32),
            pltpu.VMEM((256 + 2 * HALO, D), F32),
            pltpu.VMEM((8, 256 + 2 * HALO, D), F32),
            pltpu.VMEM((ext, 128), F32),
            dma((2,)),
        ],
        compiler_params=params(30),
        cost_estimate=cost(13),
        name="attend",
    )(meta, inv, q, kvw, x1, qh, x1h, norms, taps, full)


def compact(rows_of):
    pieces = [r[:, i * 128 : (i + 1) * 128] for r in rows_of for i in range(D // 128)]
    return jnp.concatenate(pieces, axis=0)


def spread(packed, row):
    n = D // 128
    return jnp.concatenate([packed[row * n + i : row * n + i + 1, :] for i in range(n)], axis=1)


def bn_terms(meta, packed):
    count = jnp.full((1, 1), meta[11], jnp.int32).astype(F32)
    stats = [spread(packed, 0), spread(packed, 1)]
    center = stats[0] / count
    inv_std = lax.rsqrt(stats[1] / count - center * center + norm_eps)
    return count, center, inv_std


def middle_kernel(nh, meta, inv, x2, h, stats, ograd, norms, taps, full, out_o, g3_o, gz_o, sums_o, ng_o, grads, w_in, w_out, w_pt, n_ref, gb, y3, x3, x4, acc, g_in, g_out, g_pt, sem, sem2, sem3, gsem):
    b = Blocks(nh)
    rows = x2.shape[0]
    unit = FF // nh
    fetch_all(full, inv, w_pt, sem3.at[0], b.point, b.ch, nh)
    for part in range(nh):
        fetch(full, inv, w_in, sem.at[part], b.in_two, b.ff, part, part * unit)
        fetch(full, inv, w_out, sem2.at[part], b.out_two, b.ff, part, part * unit)
    count, center, inv_std = bn_terms(meta, stats)
    gain, shift = taps[KERNEL : KERNEL + 1, :], taps[KERNEL + 1 : KERNEL + 2, :]

    def z_of(at):
        return (h[at, :] - center) * inv_std * gain + shift

    def first(at, i, c):
        z = z_of(at)
        y3[at, :] = (z * sigmoid(z)).astype(BF16)
        return c

    bands(rows, first)
    landed(w_pt, sem3.at[0])
    x3[...] = x2[...] + nn(y3[...], w_pt[...])

    def second(at, i, c):
        n_ref[at, :] = norm(x3[at, :], norms, 3).astype(BF16)
        return c

    bands(rows, second)
    feed(n_ref, w_in, w_out, acc, sem, sem2, nh)
    zero = jnp.zeros((1, D), F32)

    def last(at, i, c):
        x = x3[at, :] + 0.5 * acc[at, :]
        xhat, spread = hat(x)
        out_o[at, :] = (xhat * norms[4:5, :] + norms[9:10, :]).astype(BF16)
        dx, dg, db = hat_back(xhat, spread, ograd[at, :].astype(F32), norms[4:5, :])
        x4[at, :] = dx
        gb[at, :] = (0.5 * dx).astype(BF16)
        return c[0] + dg, c[1] + db

    gain4, shift4 = bands(rows, last, (zero, zero))
    feed_back(n_ref, gb, w_in, w_out, acc, g_in, g_out, grads, inv, b.in_two, b.out_two, gsem.at[0], gsem.at[1], b.ff, nh)

    def back(at, i, c):
        dx, dg, db = norm_back(x3[at, :], acc[at, :], norms[3:4, :])
        g3 = x4[at, :] + dx
        g3_o[at, :] = g3
        gb[at, :] = g3.astype(BF16)
        return c[0] + dg, c[1] + db

    gain3, shift3 = bands(rows, back, (zero, zero))
    ng_o[...] = jnp.zeros_like(ng_o)
    ng_o[3:4, :] = gain3
    ng_o[4:5, :] = gain4
    ng_o[8:9, :] = shift3
    ng_o[9:10, :] = shift4
    acc[...] = nt(gb[...], w_pt[...])
    g_pt[...] = tn(y3[...], gb[...]).astype(BF16)
    put_all(grads, inv, g_pt, gsem.at[2], b.point, b.ch, nh)

    def gz_part(at, i, c):
        white = (h[at, :] - center) * inv_std
        z = white * gain + shift
        gz = acc[at, :] * slope_of(z, sigmoid(z))
        gz_o[at, :] = gz
        return c[0] + jnp.sum(gz, axis=0, keepdims=True), c[1] + jnp.sum(gz * white, axis=0, keepdims=True)

    sg, sx = bands(rows, gz_part, (zero, zero))
    sums_o[...] = compact([sg, sx])
    y3[0:BLOCKW, :] = jnp.zeros((BLOCKW, D), BF16)
    empty = [(i, part) for i in range(b.total, grads.shape[1]) for part in range(nh)]
    for k, (i, part) in enumerate(empty):
        put(grads, inv, y3, gsem.at[3 + k], i, 1, part, 0)
    landed(g_in, gsem.at[0])
    landed(g_out, gsem.at[1])
    landed(g_pt, gsem.at[2])
    for k in range(len(empty)):
        landed(y3.at[pl.ds(0, BLOCKW)], gsem.at[3 + k])


def middle(nh, meta, inv, x2, h, stats, ograd, norms, taps, full):
    rows = x2.shape[0]
    slots = full.shape[1]
    zeros = (slots - Blocks(nh).total) * nh
    dma = pltpu.SemaphoreType.DMA
    f = jax.ShapeDtypeStruct
    v = pltpu.VMEM
    return pl.pallas_call(
        functools.partial(middle_kernel, nh),
        out_shape=[
            f((rows, D), BF16),
            f((rows, D), F32),
            f((rows, D), F32),
            f((2 * D // 128, 128), F32),
            f((16, D), F32),
            f((big(nh, slots), slots, BLOCKW, D), BF16),
        ],
        in_specs=[SM, SM] + [VM] * 6 + [HBM],
        out_specs=[VM] * 5 + [HBM],
        scratch_shapes=[
            v((FF, D), BF16),
            v((FF, D), BF16),
            v((D, D), BF16),
            v((rows, D), BF16),
            v((rows, D), BF16),
            v((rows, D), BF16),
            v((rows, D), F32),
            v((rows, D), F32),
            v((rows, D), F32),
            v((FF, D), BF16),
            v((FF, D), BF16),
            v((D, D), BF16),
            dma((nh,)),
            dma((nh,)),
            dma((1,)),
            dma((3 + zeros,)),
        ],
        compiler_params=params(26),
        cost_estimate=cost(17),
        name="middle",
    )(meta, inv, x2, h, stats, ograd, norms, taps, full)


def conv_back_kernel(nh, meta, inv, gz, gzh, h, hh, stats, bsums, gated, x2, g3, o, norms, taps, full, ng_in, grads_in, g2_o, do_o, taps_o, ng_o, grads, w_attn, w_glu, n_ref, gb, dh, dgated, val, gate, dglu, g_attn, g_glu, chunk, moved, tsum, sem, gsem):
    del grads_in
    b = Blocks(nh)
    rows = gz.shape[0]
    ext = rows + 2 * HALO
    start = meta[10]
    fetch_all(full, inv, w_attn, sem.at[0], b.attn, b.ch, nh)
    for i, base in enumerate((b.conv_value, b.conv_gate)):
        fetch_all(full, inv, w_glu, sem.at[1], base, b.ch, nh, i * D)
    count, center, inv_std = bn_terms(meta, stats)
    gain = taps[KERNEL : KERNEL + 1, :]
    sg, sx = spread(bsums, 0), spread(bsums, 1)

    def dh_of(gz_rows, h_rows, first):
        alive = live_rows(meta, first, gz_rows.shape[0])
        white = (h_rows - center) * inv_std
        return gain * inv_std * (gz_rows - alive / count * (sg + white * sx))

    def one(at, i, c):
        dh[pl.ds(pl.multiple_of(i * BAND + HALO, HALO), BAND), :] = dh_of(gz[at, :], h[at, :], start + i * BAND)
        n_ref[at, :] = norm(x2[at, :], norms, 2).astype(BF16)
        return c

    bands(rows, one)
    dh[0:HALO, :] = dh_of(gzh[0:HALO, :], hh[0:HALO, :], start - HALO)
    dh[HALO + rows :, :] = dh_of(gzh[HALO:, :], hh[HALO:, :], start + rows)
    tsum[...] = jnp.zeros_like(tsum)
    for k in range(rows // 256):
        fill_chunk(meta, dh, chunk, k, start)
        shift_rows(chunk, moved)

        for i in range(4 * D // 128):
            lanes = slice(i // 4 * 128, i // 4 * 128 + 128)
            row = i % 4 * 64
            own = gated[row + HALO + k * 256 : row + HALO + k * 256 + 64, lanes]
            acc = jnp.zeros((64, 128), F32)
            for j in range(KERNEL):
                off = KERNEL - j
                there = moved[off % 8, row + off - off % 8 : row + off - off % 8 + 64, lanes]
                acc = acc + there * taps[j : j + 1, lanes]
                tsum[j, :, lanes] += jnp.sum((there * own).reshape(8, 8, 128), axis=0)
            dgated[row + k * 256 : row + k * 256 + 64, lanes] = acc
    taps_o[...] = jnp.sum(tsum[...], axis=1)
    landed(w_glu, sem.at[1])
    val[...] = nt(n_ref[...], w_glu[0:D, :])
    gate[...] = nt(n_ref[...], w_glu[D:, :])

    def two(at, i, c):
        sig = sigmoid(gate[at, :])
        d = dgated[at, :] * live_rows(meta, start + i * BAND, BAND)
        dglu[at, 0:D] = (d * sig).astype(BF16)
        dglu[at, D:] = (d * val[at, :] * sig * (1.0 - sig)).astype(BF16)
        return c

    bands(rows, two)
    g_glu[...] = tn(dglu[...], n_ref[...]).astype(BF16)
    for i, base in enumerate((b.conv_value, b.conv_gate)):
        put_all(grads, inv, g_glu, gsem.at[0], base, b.ch, nh, i * D)
    val[...] = nn(dglu[...], w_glu[...])
    zero = jnp.zeros((1, D), F32)

    def three(at, i, c):
        dx, dg, db = norm_back(x2[at, :], val[at, :], norms[2:3, :])
        g2 = g3[at, :] + dx
        g2_o[at, :] = g2
        gb[at, :] = g2.astype(BF16)
        return c[0] + dg, c[1] + db

    dgain, dshift = bands(rows, three, (zero, zero))
    ng_o[...] = ng_in[...]
    ng_o[2:3, :] = dgain
    ng_o[7:8, :] = dshift
    landed(w_attn, sem.at[0])
    gate[...] = nt(gb[...], w_attn[...])
    g_attn[...] = tn(o[...], gb[...]).astype(BF16)
    put_all(grads, inv, g_attn, gsem.at[1], b.attn, b.ch, nh)

    def four(at, i, c):
        do_o[at, :] = (gate[at, :] * live_rows(meta, start + i * BAND, BAND)).astype(BF16)
        return c

    bands(rows, four)
    landed(g_glu, gsem.at[0])
    landed(g_attn, gsem.at[1])


def conv_back(nh, meta, inv, gz, gzh, h, hh, stats, bsums, gated, x2, g3, o, norms, taps, full, ng, grads):
    rows = gz.shape[0]
    ext = rows + 2 * HALO
    dma = pltpu.SemaphoreType.DMA
    f = jax.ShapeDtypeStruct
    v = pltpu.VMEM
    return pl.pallas_call(
        functools.partial(conv_back_kernel, nh),
        out_shape=[
            f((rows, D), F32),
            f((rows, D), BF16),
            f((KERNEL, D), F32),
            f((16, D), F32),
            f(grads.shape, BF16),
        ],
        in_specs=[SM, SM] + [VM] * 12 + [HBM, VM, HBM],
        out_specs=[VM] * 4 + [HBM],
        input_output_aliases={16: 4},
        scratch_shapes=[
            v((D, D), BF16),
            v((2 * D, D), BF16),
            v((rows, D), BF16),
            v((rows, D), BF16),
            v((ext, D), F32),
            v((rows, D), F32),
            v((rows, D), F32),
            v((rows, D), F32),
            v((rows, 2 * D), BF16),
            v((D, D), BF16),
            v((2 * D, D), BF16),
            v((256 + 2 * HALO, D), F32),
            v((8, 256 + 2 * HALO, D), F32),
            v((KERNEL, 8, D), F32),
            dma((2,)),
            dma((2,)),
        ],
        compiler_params=params(28),
        cost_estimate=cost(13),
        name="conv_back",
    )(meta, inv, gz, gzh, h, hh, stats, bsums, gated, x2, g3, o, norms, taps, full, ng, grads)


def attend_back_kernel(meta, q, kvw, do, lse, dq_o, dkv_o, send_o, bias, dkp, dvp):
    rows = q.shape[0]
    start = meta[10]
    base = start - lax.rem(start, LONGEST)
    offset = pl.multiple_of(lax.rem(start, LONGEST), rows)
    ukey, _, lkey = tables(meta, base + lax.broadcasted_iota(jnp.int32, (LONGEST, 1), 0))
    ukey = jnp.where(lkey, ukey, -1)
    uquery, _, _ = tables(meta, start + lax.broadcasted_iota(jnp.int32, (1, rows), 1))
    bias[...] = jnp.where(ukey == uquery, 0.0, masked_score)
    lane_q = lax.broadcasted_iota(jnp.int32, (rows, 128), 1)
    lane_k = lax.broadcasted_iota(jnp.int32, (LONGEST, 128), 1)
    for pair in range(D // 128):
        lanes = slice(pair * 128, (pair + 1) * 128)
        kp = kvw[:, lanes]
        vp = kvw[:, D + pair * 128 : D + (pair + 1) * 128]
        kms = [jnp.where(lane_k < HD, kp, jnp.zeros_like(kp)), jnp.where(lane_k >= HD, kp, jnp.zeros_like(kp))]
        qp = q[:, lanes] * 0.125
        dop = do[:, lanes]
        for hh in range(2):
            mine = lane_q < HD if hh == 0 else lane_q >= HD
            qm = jnp.where(mine, qp, jnp.zeros_like(qp))
            dom = jnp.where(mine, dop, jnp.zeros_like(dop))
            s = nt(kp, qm) + bias[...]
            p = jnp.exp(s - lse[pair * 2 + hh : pair * 2 + hh + 1, :])
            dp = nt(vp, dom)
            inner = jnp.sum(p * dp, axis=0, keepdims=True)
            ds = (p * (dp - inner)).astype(BF16)
            dv, dk, dq = nn(p.astype(BF16), dom), nn(ds, qm), tn(ds, kms[hh]) * 0.125
            if hh == 0:
                dvp[...], dkp[...], dq_o[:, lanes] = dv, dk, dq
            else:
                dvp[...] += dv
                dkp[...] += dk
                dq_o[:, lanes] += dq
        dkv_o[:, lanes] = dkp[pl.ds(offset, rows), :]
        dkv_o[:, D + pair * 128 : D + (pair + 1) * 128] = dvp[pl.ds(offset, rows), :]
        send_o[:, lanes] = dkp[...].astype(BF16)
        send_o[:, D + pair * 128 : D + (pair + 1) * 128] = dvp[...].astype(BF16)


def attend_back(meta, q, kvw, do, lse):
    rows = q.shape[0]
    f = jax.ShapeDtypeStruct
    v = pltpu.VMEM
    return pl.pallas_call(
        attend_back_kernel,
        out_shape=[f((rows, D), F32), f((rows, 2 * D), F32), f((LONGEST, 2 * D), BF16)],
        in_specs=[SM] + [VM] * 4,
        out_specs=[VM] * 3,
        scratch_shapes=[v((LONGEST, rows), F32), v((LONGEST, 128), F32), v((LONGEST, 128), F32)],
        compiler_params=params(26),
        cost_estimate=cost(14),
        name="attend_back",
    )(meta, q, kvw, do, lse)


def rear_kernel(nh, meta, inv, dq, dkv, recv, x1, frames, g2, norms, table, full, ng_in, grads_in, fg_o, ng_o, grads, w_in, w_out, w_qkv, n_ref, gb, dproj, x_ref, acc, g_in, g_out, g_qkv, sem, gsem):
    del grads_in
    b = Blocks(nh)
    rows = dq.shape[0]
    for i, base in enumerate((b.query, b.key, b.value)):
        fetch_all(full, inv, w_qkv, sem.at[0], base, b.ch, nh, i * D)
    fetch_all(full, inv, w_in, sem.at[1], b.in_one, b.ff, nh)
    fetch_all(full, inv, w_out, sem.at[2], b.out_one, b.ff, nh)
    spans = recv.shape[0]

    def one(at, i, c):
        p = pl.ds(place_of(meta, i), BAND)
        dproj[at, 0:D] = turn(dq[at, :], table[p, :], -1.0).astype(BF16)
        dk, dv = dkv[at, 0:D], dkv[at, D:]
        for s in range(spans):
            dk = dk + recv[s, at, 0:D].astype(F32)
            dv = dv + recv[s, at, D:].astype(F32)
        dproj[at, D : 2 * D] = turn(dk, table[p, :], -1.0).astype(BF16)
        dproj[at, 2 * D :] = dv.astype(BF16)
        n_ref[at, :] = norm(x1[at, :], norms, 1).astype(BF16)
        return c

    bands(rows, one)
    landed(w_qkv, sem.at[0])
    acc[...] = nn(dproj[...], w_qkv[...])
    for i in range(3):
        g_qkv[i * D : (i + 1) * D, :] = tn(dproj[:, i * D : (i + 1) * D], n_ref[...]).astype(BF16)
    for i, base in enumerate((b.query, b.key, b.value)):
        put_all(grads, inv, g_qkv, gsem.at[0], base, b.ch, nh, i * D)
    zero = jnp.zeros((1, D), F32)

    def two(at, i, c):
        dx, dg, db = norm_back(x1[at, :], acc[at, :], norms[1:2, :])
        g1 = g2[at, :] + dx
        x_ref[at, :] = g1
        gb[at, :] = (0.5 * g1).astype(BF16)
        n_ref[at, :] = norm(frames[at, :].astype(F32), norms, 0).astype(BF16)
        return c[0] + dg, c[1] + db

    gain1, shift1 = bands(rows, two, (zero, zero))
    landed(w_in, sem.at[1])
    landed(w_out, sem.at[2])
    feed_back(n_ref, gb, w_in, w_out, acc, g_in, g_out, grads, inv, b.in_one, b.out_one, gsem.at[1], gsem.at[2], b.ff, nh)

    def three(at, i, c):
        dx, dg, db = norm_back(frames[at, :].astype(F32), acc[at, :], norms[0:1, :])
        fg_o[at, :] = x_ref[at, :] + dx
        return c[0] + dg, c[1] + db

    gain0, shift0 = bands(rows, three, (zero, zero))
    ng_o[...] = ng_in[...]
    ng_o[0:1, :] = gain0
    ng_o[1:2, :] = gain1
    ng_o[5:6, :] = shift0
    ng_o[6:7, :] = shift1
    landed(g_qkv, gsem.at[0])
    landed(g_in, gsem.at[1])
    landed(g_out, gsem.at[2])


def rear(nh, meta, inv, dq, dkv, recv, x1, frames, g2, norms, table, full, ng, grads):
    rows = dq.shape[0]
    dma = pltpu.SemaphoreType.DMA
    f = jax.ShapeDtypeStruct
    v = pltpu.VMEM
    return pl.pallas_call(
        functools.partial(rear_kernel, nh),
        out_shape=[f((rows, D), F32), f((16, D), F32), f(grads.shape, BF16)],
        in_specs=[SM, SM] + [VM] * 8 + [HBM, VM, HBM],
        out_specs=[VM, VM, HBM],
        input_output_aliases={12: 2},
        scratch_shapes=[
            v((FF, D), BF16),
            v((FF, D), BF16),
            v((3 * D, D), BF16),
            v((rows, D), BF16),
            v((rows, D), BF16),
            v((rows, 3 * D), BF16),
            v((rows, D), F32),
            v((rows, D), F32),
            v((FF, D), BF16),
            v((FF, D), BF16),
            v((3 * D, D), BF16),
            dma((3,)),
            dma((3,)),
        ],
        compiler_params=params(28),
        cost_estimate=cost(13),
        name="rear",
    )(meta, inv, dq, dkv, recv, x1, frames, g2, norms, table, full, ng, grads)


def split(x):
    high = x.astype(BF16)
    return high, (x - high.astype(F32)).astype(BF16)


def three_products(dot, a, b):
    (ah, al), (bh, bl) = a, b
    return dot(ah, bh) + (dot(ah, bl) + dot(al, bh))


def adam_step(weight, gradient, moment_one, moment_two, factor):
    one_new = beta_one * moment_one + (1.0 - beta_one) * gradient
    two_new = beta_two * moment_two + (1.0 - beta_two) * gradient * gradient
    return (weight - factor * one_new / (jnp.sqrt(two_new) + adam_eps), one_new, two_new)


def update_kernel(nh, head, grad, masters, first, second, left, right, small, bsums, norms, norm1, norm2, conv, conv1, conv2, out_v, fgrad_v, masters_o, first_o, second_o, ng_o, norms_o, norm1_o, norm2_o, conv_o, conv1_o, conv2_o, out_o, fgrad_o, sem):
    moves = [
        pltpu.make_async_copy(out_v, out_o, sem.at[0]),
        pltpu.make_async_copy(fgrad_v, fgrad_o, sem.at[1]),
    ]
    step = pl.program_id(0)

    @pl.when(step == 0)
    def _():
        for move in moves:
            move.start()
        grads = small[0:10, :]
        ng_o[...] = grads
        norms_o[...], norm1_o[...], norm2_o[...] = adam_step(norms[...], grads, norm1[...], norm2[...], 10.0 * FACTOR)
        width = conv.shape[1]
        rows = jnp.concatenate([small[16 : 16 + KERNEL, :], spread(bsums, 1), spread(bsums, 0)], axis=0)
        mine = rows[:, 0:width]
        for h in range(1, nh):
            mine = jnp.where(head[0] == h, rows[:, h * width : (h + 1) * width], mine)
        conv_o[...], conv1_o[...], conv2_o[...] = adam_step(conv[...], mine, conv1[...], conv2[...], 4.0 * FACTOR)

    g = grad[0]
    m1 = beta_one * first[0] + (1.0 - beta_one) * g
    first_o[0] = m1
    lefts, rights = split(left[0]), split(right[0])
    both = three_products(nn, split(jnp.concatenate([g, m1], axis=0)), lefts)
    rot = three_products(tn, rights, split(both[0:BLOCKW]))
    rot1 = three_products(tn, rights, split(both[BLOCKW:]))
    m2 = beta_two * second[0] + (1.0 - beta_two) * rot * rot
    second_o[0] = m2
    scaled = rot1 / (jnp.sqrt(m2) + adam_eps)
    back = three_products(nt, split(three_products(nn, rights, split(scaled))), lefts)
    w = masters[0]
    masters_o[0] = w - FACTOR * back - step_rate * weight_decay * w

    @pl.when(step == pl.num_programs(0) - 1)
    def _():
        for move in moves:
            move.wait()


def update(nh, head, grad, masters, first, second, left, right, small, bsums, norms, norm1, norm2, conv, conv1, conv2, out_v, fgrad_v):
    spd = grad.shape[0]
    block = pl.BlockSpec((1, BLOCKW, D), lambda i: (i, 0, 0))

    def whole(a):
        return pl.BlockSpec(a.shape, lambda i: (0, 0))

    f = jax.ShapeDtypeStruct
    return pl.pallas_call(
        functools.partial(update_kernel, nh),
        grid=(spd,),
        out_shape=[f(grad.shape, F32)] * 3
        + [f(norms.shape, F32)] * 4
        + [f(conv.shape, F32)] * 3
        + [f(out_v.shape, out_v.dtype), f(fgrad_v.shape, F32)],
        in_specs=[SM]
        + [block] * 4
        + [pl.BlockSpec((1, D, D), lambda i: (i, 0, 0)), pl.BlockSpec((1, BLOCKW, BLOCKW), lambda i: (i, 0, 0))]
        + [whole(a) for a in (small, bsums, norms, norm1, norm2, conv, conv1, conv2)]
        + [HBM, HBM],
        out_specs=[block] * 3 + [whole(norms)] * 4 + [whole(conv)] * 3 + [HBM, HBM],
        scratch_shapes=[pltpu.SemaphoreType.DMA((2,))],
        compiler_params=params(20),
        cost_estimate=cost(9),
        name="update",
    )(head, grad, masters, first, second, left, right, small, bsums, norms, norm1, norm2, conv, conv1, conv2, out_v, fgrad_v)


def per_device(
    ndp,
    nh,
    frames,
    out_grad,
    bucket_len,
    batch_count,
    utt_lengths,
    owner_slots,
    masters,
    first_moment,
    second_moment,
    left_basis,
    right_basis,
    norm_params,
    norm_first,
    norm_second,
    conv_params,
    conv_first,
    conv_second,
):
    rows = frames.shape[0]

    def flip(a):
        return jnp.transpose(a[0], (0, 2, 1))

    masters_t = flip(masters)
    z = lax.axis_index("head")
    dp = lax.axis_index("dp")
    place = jnp.stack([dp - dp % 2 + z % 2, 2 * (z // 2) + dp % 2])
    full, frames_v, ograd_v, ints, conv_all = gather(
        ndp,
        nh,
        masters_t.astype(BF16),
        frames,
        out_grad,
        bucket_len[None],
        batch_count[None],
        utt_lengths,
        conv_params.T,
    )
    table = jnp.asarray(rope_table())
    x1, q, kv, meta, inv, taps = front(
        ndp, nh, owner_slots, place, ints, conv_all, frames_v, norm_params, table, full
    )
    kvw, qh, x1h = keys(ndp, nh, kv, q, x1)
    o, lse, x2, gated, h, sums = attend(nh, meta, inv, q, kvw, x1, qh, x1h, norm_params, taps, full)
    (stats,) = totals(ndp, nh, 3, sums)
    out_v, g3, gz, bpart, ng, grads = middle(nh, meta, inv, x2, h, stats, ograd_v, norm_params, taps, full)
    bsums, gzh, hh = totals(ndp, nh, 4, bpart, (gz, h))
    g2, do, dtaps, ng, grads = conv_back(
        nh, meta, inv, gz, gzh, h, hh, stats, bsums, gated, x2, g3, o, norm_params, taps, full, ng, grads
    )
    dq, dkv, dkv_send = attend_back(meta, q, kvw, do, lse)
    recv = key_grads(ndp, nh, dkv_send, rows)
    fg_v, ng, grads = rear(
        nh, meta, inv, dq, dkv, recv, x1, frames_v, g2, norm_params, table, full, ng, grads
    )
    small = jnp.concatenate([ng, dtaps], axis=0)
    owned, small, out_w, fg_w = scatter(ndp, nh, grads, small, out_v, fg_v)
    (
        new_m,
        new_f,
        new_s,
        norm_grads,
        new_norms,
        norm_first_new,
        norm_second_new,
        new_conv,
        conv_first_new,
        conv_second_new,
        layer_out,
        frames_grad,
    ) = update(
        nh,
        jnp.reshape(z, (1,)),
        owned,
        masters_t,
        flip(first_moment),
        flip(second_moment),
        left_basis[0],
        right_basis[0],
        small,
        bsums,
        norm_params,
        norm_first,
        norm_second,
        conv_params.T,
        conv_first.T,
        conv_second.T,
        out_w,
        fg_w,
    )

    def unflip(a):
        return jnp.transpose(a, (0, 2, 1))[None]

    return (
        layer_out,
        frames_grad,
        unflip(new_m),
        unflip(new_f),
        unflip(new_s),
        norm_grads,
        new_norms,
        norm_first_new,
        norm_second_new,
        new_conv.T,
        conv_first_new.T,
        conv_second_new.T,
    )


def solution(mesh):
    both, blocks, chan = P(("dp", "head"), None), P("head", "dp", None, None), P("head", None)
    placed = (both, both, P("dp"), P("dp"), P("dp", None), P()) + (blocks,) * 5 + (P(),) * 3 + (chan,) * 3
    return jax.shard_map(
        functools.partial(per_device, mesh.shape["dp"], mesh.shape["head"]),
        mesh=mesh,
        in_specs=placed,
        out_specs=(both, both) + (blocks,) * 3 + (P(),) * 4 + (chan,) * 3,
        check_vma=False,
    )
```

```python
import functools
import math

import jax
import jax.numpy as jnp
import numpy as np
from jax import lax
from jax.experimental import pallas as pl
from jax.experimental.pallas import tpu as pltpu
from jax.sharding import PartitionSpec as P

D = 512
FF = 2048
HD = 64
KERNEL = 32
BLOCKW = 64
STEP = 10
LONGEST = 1024
HALO = 16

beta_one = 0.9
beta_two = 0.95
step_rate = 0.05
weight_decay = 0.01
adam_eps = 1e-08
norm_eps = 1e-05
masked_score = -1e30
FACTOR = step_rate * math.sqrt(1.0 - beta_two**STEP) / (1.0 - beta_one**STEP)

F32 = jnp.float32
BF16 = jnp.bfloat16
MESH = pl.DeviceIdType.MESH
ANY = pl.BlockSpec(memory_space=pl.ANY)
HBM = pl.BlockSpec(memory_space=pltpu.HBM)
VM = pl.BlockSpec(memory_space=pltpu.VMEM)
SM = pl.BlockSpec(memory_space=pltpu.SMEM)
MIB = 1 << 20


def cost(us):
    return pl.CostEstimate(flops=0, bytes_accessed=int(us * 3.6e6), transcendentals=0)


def params(mib, collective_id=None):
    if collective_id is None:
        return pltpu.CompilerParams(vmem_limit_bytes=mib * MIB)
    return pltpu.CompilerParams(
        vmem_limit_bytes=mib * MIB, collective_id=collective_id, has_side_effects=True
    )


def big(nh, slots):
    return max(nh, -(-64 * MIB // (slots * BLOCKW * D * 2)))


class Copies:
    def __init__(self, sends):
        self.sends = sends
        self.used = 0
        self.open = []

    def send(self, src, dst, recv_sem, device, when=None):
        copy = pltpu.make_async_remote_copy(
            src_ref=src,
            dst_ref=dst,
            send_sem=self.sends.at[self.used],
            recv_sem=recv_sem,
            device_id=device,
            device_id_type=MESH,
        )
        (pl.when(when) if when is not None else call)(copy.start)
        self.used += 1
        self.open.append((copy, when))

    def finish(self):
        for copy, when in self.open:
            (pl.when(when) if when is not None else call)(copy.wait_send)


def call(f):
    return f()


def arrived(ref, sem):
    pltpu.make_async_copy(ref, ref, sem).wait()


def greet(devices):
    barrier = pltpu.get_barrier_semaphore()
    for device in devices:
        pl.semaphore_signal(barrier, inc=1, device_id=device, device_id_type=MESH)
    pl.semaphore_wait(barrier, len(devices))


class Place:
    def __init__(self, ndp, nh):
        self.ndp, self.nh, self.nchip = ndp, nh, ndp // 2
        self.dp = lax.axis_index("dp")
        self.z = lax.axis_index("head")
        self.core = self.dp % 2
        self.chip = self.dp // 2
        self.group_core = self.z % 2
        self.part = 2 * (self.z // 2) + self.core

    def of_part(self, part):
        return (self.chip * 2 + part % 2, 2 * (part // 2) + self.group_core)

    def core_peer(self):
        return (self.chip * 2 + 1 - self.core, self.z)

    def swap_peer(self):
        return (self.chip * 2 + 1 - self.core, self.part)

    def x_chip(self):
        return self.chip + 1 - 2 * (self.chip % 2)

    def y_chip(self):
        return (self.chip + 2) % 4


def gather_kernel(ndp, nh, spd, own, frames, ograd, bucket, batch, utts, conv, full, frames_o, ograd_o, ints_o, conv_o, ints, sends, recvs, extra, isem, local):
    me = Place(ndp, nh)
    dp, z, core, chip, nchip = me.dp, me.z, me.core, me.chip, me.nchip

    def shard(h, ch, c):
        return full.at[h, pl.ds((ch * 2 + c) * spd, spd)]

    def sem(h, ch, c, half=0):
        return recvs.at[h * ndp + ch * 2 + c, half]

    peer = me.core_peer()
    swap = me.core != me.z % 2
    columns = [(dp, (z + i) % nh) for i in range(1, nh)]
    square = nchip == 4
    if square:
        planes = [(me.x_chip() * 2 + core, z), (me.y_chip() * 2 + core, z)]
    else:
        planes = [(((chip + i) % nchip) * 2 + core, z) for i in range(1, nchip)]
    ints[...] = jnp.zeros_like(ints)
    ints[0:1, 0:1] = bucket[...]
    ints[0:1, 1:2] = batch[...]
    ints[0:1, 2:10] = utts[...]
    barrier = pltpu.get_barrier_semaphore()
    near = totals_peers(me)
    for device in near:
        pl.semaphore_signal(barrier, inc=1, device_id=device, device_id_type=MESH)

    @pl.when(swap)
    def _():
        pl.semaphore_signal(barrier, inc=1, device_id=me.swap_peer(), device_id_type=MESH)

    pl.semaphore_wait(barrier, len(near) + (core + z) % 2)

    copies = Copies(sends)
    mine = shard(z, chip, core)
    below, above = (dp, (z + nh - 1) % nh), (dp, (z + 1) % nh)
    copies.send(own, mine, sem(z, chip, core), above, z < nh - 1)
    copies.send(own, mine, sem(z, chip, core), below, z > 0)
    for device in planes:
        copies.send(own, mine, sem(z, chip, core), device)
    copies.send(own, mine, sem(z, chip, core), peer)
    keep = [
        pltpu.make_async_copy(own, mine, local.at[0]),
        pltpu.make_async_copy(ints, ints_o.at[dp], local.at[1]),
        pltpu.make_async_copy(conv, conv_o.at[z], local.at[2]),
    ]
    for copy in keep:
        copy.start()

    @pl.when(jnp.logical_not(swap))
    def _():
        for k, (src, dst) in enumerate(((frames, frames_o), (ograd, ograd_o))):
            pltpu.make_async_copy(src, dst, local.at[3 + k]).start()

    def column(step, up):
        h = z - step if up else z + step
        there = z >= step if up else z + step < nh
        onward = z < nh - 1 if up else z > 0
        h = jnp.where(there, h, z)
        s, r = shard(h, chip, core), sem(h, chip, core)

        @pl.when(there)
        def _():
            arrived(s, r)

        if step < nh - 1:
            copies.send(s, s, r, above if up else below, jnp.logical_and(there, onward))
        for device in planes:
            copies.send(s, s, r, device, there)
        copies.send(s, s, r, peer, there)

    def beside(step, up):
        h = z - step if up else z + step
        there = z >= step if up else z + step < nh
        h = jnp.where(there, h, z)
        if not square:
            for k in range(1, nchip):
                ch = (chip + k) % nchip

                @pl.when(there)
                def _():
                    arrived(shard(h, ch, core), sem(h, ch, core))

                copies.send(shard(h, ch, core), shard(h, ch, core), sem(h, ch, core), peer, there)
            return
        half = spd // 2
        for side, (ch, device) in enumerate(((me.x_chip(), planes[1]), (me.y_chip(), planes[0]))):

            @pl.when(there)
            def _():
                arrived(shard(h, ch, core), sem(h, ch, core))

            piece = full.at[h, pl.ds((ch * 2 + core) * spd + side * half, half)]
            copies.send(piece, piece, sem(h, ch, core, side), device, there)
            copies.send(shard(h, ch, core), shard(h, ch, core), sem(h, ch, core), peer, there)

    def across(step, up):
        if not square:
            return
        h = z - step if up else z + step
        there = z >= step if up else z + step < nh
        h = jnp.where(there, h, z)
        half = spd // 2
        ch = 3 - chip

        @pl.when(there)
        def _():
            for side in range(2):
                piece = full.at[h, pl.ds((ch * 2 + core) * spd + side * half, half)]
                arrived(piece, sem(h, ch, core, side))

        copies.send(shard(h, ch, core), shard(h, ch, core), sem(h, ch, core), peer, there)

    visits = [(0, True)] + [(step, up) for step in range(1, nh) for up in (True, False)]
    lag = 2
    for i in range(len(visits) + 2 * lag):
        if 0 < i < len(visits):
            column(*visits[i])
        if i == len(visits) - 1:
            for device in columns:
                copies.send(conv, conv_o.at[z], extra.at[3 + z], device)
            for k in range(1, ndp):
                copies.send(ints, ints_o.at[dp], isem.at[dp], ((dp + k) % ndp, z))

            @pl.when(swap)
            def _():
                for k, (src, dst) in enumerate(((frames, frames_o), (ograd, ograd_o))):
                    pltpu.make_async_remote_copy(
                        src_ref=src, dst_ref=dst, send_sem=local.at[3 + k], recv_sem=extra.at[1 + k],
                        device_id=me.swap_peer(), device_id_type=MESH,
                    ).start()

        if 0 <= i - lag < len(visits):
            beside(*visits[i - lag])
        if i >= 2 * lag:
            across(*visits[i - 2 * lag])
    for i in range(nh):
        h = (z + nh - i) % nh
        for k in range(nchip):
            ch = (chip + k) % nchip
            arrived(shard(h, ch, 1 - core), sem(h, ch, 1 - core))
    for k in range(1, ndp):
        arrived(ints_o.at[(dp + k) % ndp], isem.at[(dp + k) % ndp])
    for i in range(1, nh):
        h = (z + nh - i) % nh
        arrived(conv_o.at[h], extra.at[3 + h])

    @pl.when(swap)
    def _():
        arrived(frames_o, extra.at[1])
        arrived(ograd_o, extra.at[2])

    for i, ref in enumerate((frames, ograd)):
        arrived(ref, local.at[3 + i])
    for copy in keep:
        copy.wait()
    copies.finish()


def gather(ndp, nh, own, frames, ograd, bucket, batch, utts, conv):
    spd = own.shape[0]
    nchip = ndp // 2
    plane = 2 if nchip == 4 else nchip - 1
    visits = 2 * nh - 1
    halves = 2 * visits if nchip == 4 else 0
    count = 2 * visits + visits * (plane + 1) + visits * (nchip - 1) + halves + (ndp - 1) + (nh - 1)
    shapes = [
        jax.ShapeDtypeStruct((big(nh, ndp * spd), ndp * spd, BLOCKW, D), BF16),
        jax.ShapeDtypeStruct(frames.shape, BF16),
        jax.ShapeDtypeStruct(ograd.shape, BF16),
        jax.ShapeDtypeStruct((ndp, 8, 128), jnp.int32),
        jax.ShapeDtypeStruct((nh,) + conv.shape, F32),
    ]
    dma = pltpu.SemaphoreType.DMA
    return pl.pallas_call(
        functools.partial(gather_kernel, ndp, nh, spd),
        out_shape=shapes,
        in_specs=[ANY, HBM, HBM, VM, VM, VM, ANY],
        out_specs=[HBM] * 3 + [ANY] * 2,
        scratch_shapes=[
            pltpu.VMEM((8, 128), jnp.int32),
            dma((count,)),
            dma((nh * ndp, 2)),
            dma((3 + nh,)),
            dma((ndp,)),
            dma((5,)),
        ],
        compiler_params=params(52, 1),
        cost_estimate=cost(60),
        name="gather",
    )(own, frames, ograd, bucket, batch, utts, conv)


def totals_step(me, small, first, second, copies, sem1, sem2, local):
    ndp, nh = me.ndp, me.nh

    def one():
        for i in range(1, ndp):
            copies.send(small, first.at[me.dp], sem1.at[me.dp], ((me.dp + i) % ndp, me.z))
        first[me.dp] = small[...]

    def two():
        for i in range(1, ndp):
            src = (me.dp + i) % ndp
            arrived(first.at[src], sem1.at[src])
        total = first[0]
        for i in range(1, ndp):
            total = total + first[i]
        second[me.z] = total
        for i in range(1, nh):
            copies.send(second.at[me.z], second.at[me.z], sem2.at[me.z], (me.dp, (me.z + i) % nh))

    def three():
        for i in range(1, nh):
            src = (me.z + i) % nh
            arrived(second.at[src], sem2.at[src])
        total = second[0]
        for i in range(1, nh):
            total = total + second[i]
        return total

    return one, two, three


def totals_peers(me):
    return [((me.dp + i) % me.ndp, me.z) for i in range(1, me.ndp)] + [
        (me.dp, (me.z + i) % me.nh) for i in range(1, me.nh)
    ]


def totals_kernel(ndp, nh, halos, *refs):
    me = Place(ndp, nh)
    small = refs[0]
    edges = refs[1 : 1 + halos]
    out = refs[1 + halos]
    edges_o = refs[2 + halos : 2 + 2 * halos]
    first, second, sends, sem1, sem2, hsem = refs[2 + 2 * halos :]
    greet(totals_peers(me))
    copies = Copies(sends)
    one, two, three = totals_step(me, small, first, second, copies, sem1, sem2, None)
    one()
    for i in range(halos):
        send_edges(me, edges[i], edges_o[i], copies, hsem.at[2 * i], hsem.at[2 * i + 1])
    two()
    out[...] = three()
    for i in range(halos):
        arrived(edges_o[i].at[pl.ds(0, HALO)], hsem.at[2 * i])
        arrived(edges_o[i].at[pl.ds(HALO, HALO)], hsem.at[2 * i + 1])
    copies.finish()


def window(me, rows):
    span = LONGEST // rows
    at = me.part % span
    return span, at, me.part - at


def send_edges(me, src, dst, copies, sem_before, sem_after):
    rows = src.shape[0]
    span, at, base = window(me, rows)
    after = me.of_part(base + (at + 1) % span)
    before = me.of_part(base + (at + span - 1) % span)
    copies.send(src.at[pl.ds(rows - HALO, HALO)], dst.at[pl.ds(0, HALO)], sem_before, after)
    copies.send(src.at[pl.ds(0, HALO)], dst.at[pl.ds(HALO, HALO)], sem_after, before)


def totals(ndp, nh, collective_id, small, edges=()):
    dma = pltpu.SemaphoreType.DMA
    n = len(edges)
    halo = [jax.ShapeDtypeStruct((2 * HALO, D), e.dtype) for e in edges]
    return pl.pallas_call(
        functools.partial(totals_kernel, ndp, nh, n),
        out_shape=[jax.ShapeDtypeStruct(small.shape, F32)] + halo,
        in_specs=[VM] + [ANY] * n,
        out_specs=[VM] + [ANY] * n,
        scratch_shapes=[
            pltpu.VMEM((ndp,) + small.shape, F32),
            pltpu.VMEM((nh,) + small.shape, F32),
            dma((ndp + nh - 2 + 2 * n,)),
            dma((ndp,)),
            dma((nh,)),
            dma((2 * n + 1,)),
        ],
        compiler_params=params(16, collective_id),
        cost_estimate=cost(8),
        name=f"totals_{collective_id}",
    )(small, *edges)


def keys_kernel(ndp, nh, kv, q, x1, kv_o, q_o, x1_o, sends, recvs, local):
    me = Place(ndp, nh)
    rows = kv.shape[0]
    span, at, base = window(me, rows)
    peers = [me.of_part(base + (at + i) % span) for i in range(1, span)]
    greet(peers)
    copies = Copies(sends)
    place = kv_o.at[pl.ds(at * rows, rows)]
    for device in peers:
        copies.send(kv, place, recvs.at[at], device)
    own = pltpu.make_async_copy(kv, place, local.at[0])
    own.start()
    for i, (src, dst) in enumerate(((q, q_o), (x1, x1_o))):
        send_edges(me, src, dst, copies, recvs.at[span + 2 * i], recvs.at[span + 2 * i + 1])
    for i in range(1, span):
        other = (at + i) % span
        arrived(kv_o.at[pl.ds(other * rows, rows)], recvs.at[other])
    for i, dst in enumerate((q_o, x1_o)):
        arrived(dst.at[pl.ds(0, HALO)], recvs.at[span + 2 * i])
        arrived(dst.at[pl.ds(HALO, HALO)], recvs.at[span + 2 * i + 1])
    own.wait()
    copies.finish()


def keys(ndp, nh, kv, q, x1):
    span = LONGEST // kv.shape[0]
    dma = pltpu.SemaphoreType.DMA
    return pl.pallas_call(
        functools.partial(keys_kernel, ndp, nh),
        out_shape=[
            jax.ShapeDtypeStruct((LONGEST, 2 * D), BF16),
            jax.ShapeDtypeStruct((2 * HALO, D), BF16),
            jax.ShapeDtypeStruct((2 * HALO, D), F32),
        ],
        in_specs=[ANY] * 3,
        out_specs=[ANY] * 3,
        scratch_shapes=[dma((span + 3,)), dma((span + 4,)), dma((1,))],
        compiler_params=params(8, 2),
        cost_estimate=cost(3),
        name="keys",
    )(kv, q, x1)


def key_grads_kernel(ndp, nh, part, out, sends, recvs):
    me = Place(ndp, nh)
    rows = out.shape[1]
    span, at, base = window(me, rows)
    greet([me.of_part(base + (at + i) % span) for i in range(1, span)])
    copies = Copies(sends)
    for i in range(1, span):
        other = (at + i) % span
        copies.send(part.at[pl.ds(other * rows, rows)], out.at[i - 1], recvs.at[i - 1], me.of_part(base + other))
    for i in range(1, span):
        arrived(out.at[i - 1], recvs.at[i - 1])
    copies.finish()


def key_grads(ndp, nh, part, rows):
    span = LONGEST // rows
    dma = pltpu.SemaphoreType.DMA
    return pl.pallas_call(
        functools.partial(key_grads_kernel, ndp, nh),
        out_shape=jax.ShapeDtypeStruct((span - 1, rows, 2 * D), BF16),
        in_specs=[ANY],
        out_specs=ANY,
        scratch_shapes=[dma((span - 1,)), dma((span - 1,))],
        compiler_params=params(8, 5),
        cost_estimate=cost(3),
        name="key_grads",
    )(part)


def far_first(z, nh):
    orders = [sorted(range(nh), key=lambda h: (-abs(h - at), h)) for at in range(nh)]
    return [sum((orders[at][i] * (z == at).astype(jnp.int32) for at in range(nh)), 0) for i in range(nh)]


def scatter_kernel(ndp, nh, spd, grads, small, out_v, fgrad_v, owned, small_o, out_o, fgrad_o, part, cores, side_x, side_y, half_x, half_y, zrecv, first, second, sends, csem, psem, xsem, zsem, sem1, sem2, esem, local):
    me = Place(ndp, nh)
    dp, z, core, chip, nchip = me.dp, me.z, me.core, me.chip, me.nchip
    square = nchip == 4
    peer = me.core_peer()
    swap = me.core != me.z % 2
    half = spd // 2
    barrier = pltpu.get_barrier_semaphore()
    near = totals_peers(me)
    for device in near:
        pl.semaphore_signal(barrier, inc=1, device_id=device, device_id_type=MESH)

    @pl.when(swap)
    def _():
        pl.semaphore_signal(barrier, inc=1, device_id=me.swap_peer(), device_id_type=MESH)

    pl.semaphore_wait(barrier, len(near) + (core + z) % 2)
    copies = Copies(sends)
    order = far_first(z, nh)
    if square:
        chips = [3 - chip, me.x_chip(), me.y_chip(), chip]
    else:
        chips = [(chip + i + 1) % nchip for i in range(nchip)]
    loads = {}

    def begin(i):
        for k, ch in enumerate(chips):
            copies.send(grads.at[order[i], pl.ds((ch * 2 + 1 - core) * spd, spd)], cores.at[i, k], csem.at[i, k], peer)
            load = pltpu.make_async_copy(
                grads.at[order[i], pl.ds((ch * 2 + core) * spd, spd)], part.at[i, k], psem.at[i, k]
            )
            load.start()
            loads[i, k] = load

    begin(0)
    one, two, three = totals_step(me, small, first, second, copies, sem1, sem2, None)
    one()

    @pl.when(swap)
    def _():
        for i, (src, dst) in enumerate(((out_v, out_o), (fgrad_v, fgrad_o))):
            pltpu.make_async_remote_copy(
                src_ref=src, dst_ref=dst, send_sem=local.at[i], recv_sem=esem.at[i],
                device_id=me.swap_peer(), device_id_type=MESH,
            ).start()

    @pl.when(jnp.logical_not(swap))
    def _():
        for i, (src, dst) in enumerate(((out_v, out_o), (fgrad_v, fgrad_o))):
            pltpu.make_async_copy(src, dst, local.at[i]).start()

    def add(i, k, others, lo=0, n=spd):
        @pl.loop(0, n, unroll=True)
        def _(s):
            total = part[i, k, lo + s].astype(F32)
            for other in others:
                total = total + other(s).astype(F32)
            part[i, k, lo + s] = total.astype(BF16)

    def meet(i, k):
        loads[i, k].wait()
        arrived(cores.at[i, k], csem.at[i, k])

    planes = [(me.x_chip() * 2 + core, z), (me.y_chip() * 2 + core, z)]

    def stage_a(i):
        if square:
            meet(i, 0)
            add(i, 0, [lambda s: cores[i, 0, s]])
            copies.send(part.at[i, 0, pl.ds(0, half)], half_x.at[i], xsem.at[i, 0], planes[0])
            copies.send(part.at[i, 0, pl.ds(half, half)], half_y.at[i], xsem.at[i, 1], planes[1])
        else:
            for k in range(nchip - 1):
                meet(i, k)
                add(i, k, [lambda s: cores[i, k, s]])
                copies.send(part.at[i, k], side_x.at[i, k], xsem.at[i, k], (chips[k] * 2 + core, z))

    def stage_b(i):
        if not square:
            return
        meet(i, 1)
        add(i, 1, [lambda s: cores[i, 1, s]], 0, half)
        arrived(half_y.at[i], xsem.at[i, 1])
        add(i, 1, [lambda s: cores[i, 1, half + s], lambda s: half_y[i, s]], half, half)
        copies.send(part.at[i, 1], side_x.at[i, 0], xsem.at[i, 2], planes[0])
        meet(i, 2)
        add(i, 2, [lambda s: cores[i, 2, half + s]], half, half)
        arrived(half_x.at[i], xsem.at[i, 0])
        add(i, 2, [lambda s: cores[i, 2, s], lambda s: half_x[i, s]], 0, half)
        copies.send(part.at[i, 2], side_y.at[i], xsem.at[i, 3], planes[1])

    last = nchip - 1

    def stage_c(i):
        meet(i, last)
        if square:
            arrived(side_x.at[i, 0], xsem.at[i, 2])
            arrived(side_y.at[i], xsem.at[i, 3])
            others = [lambda s: cores[i, last, s], lambda s: side_x[i, 0, s], lambda s: side_y[i, s]]
        else:
            others = [lambda s: cores[i, last, s]]
            for k in range(nchip - 1):
                arrived(side_x.at[i, k], xsem.at[i, k])
                others.append(lambda s, k=k: side_x[i, k, s])
        add(i, last, others)
        if i < nh - 1:
            copies.send(part.at[i, last], zrecv.at[z], zsem.at[z], (dp, order[i]))

    for i in range(nh + 2):
        if i + 1 < nh:
            begin(i + 1)
        if i < nh:
            stage_a(i)
        if 0 <= i - 1 < nh:
            stage_b(i - 1)
        if i == 1:
            two()
        if i >= 2:
            stage_c(i - 2)
    small_o[...] = three()
    sources = [(z + i) % nh for i in range(1, nh)]
    for src in sources:
        arrived(zrecv.at[src], zsem.at[src])

    @pl.loop(0, spd)
    def _(s):
        total = part[nh - 1, last, s].astype(F32)
        for src in sources:
            total = total + zrecv[src, s].astype(F32)
        owned[s] = total

    @pl.when(swap)
    def _():
        arrived(out_o, esem.at[0])
        arrived(fgrad_o, esem.at[1])

    arrived(out_v, local.at[0])
    arrived(fgrad_v, local.at[1])
    copies.finish()


def scatter(ndp, nh, grads, small, out_v, fgrad_v):
    spd = grads.shape[1] // ndp
    nchip = ndp // 2
    square = nchip == 4
    dma = pltpu.SemaphoreType.DMA
    block = (spd, BLOCKW, D)
    halfb = (max(spd // 2, 1), BLOCKW, D)
    sides = 1 if square else nchip - 1
    sent = nh * nchip + (ndp - 1) + (nh - 1) + (nh * 4 if square else nh * (nchip - 1)) + (nh - 1)
    return pl.pallas_call(
        functools.partial(scatter_kernel, ndp, nh, spd),
        out_shape=[
            jax.ShapeDtypeStruct(block, F32),
            jax.ShapeDtypeStruct(small.shape, F32),
            jax.ShapeDtypeStruct(out_v.shape, out_v.dtype),
            jax.ShapeDtypeStruct(fgrad_v.shape, fgrad_v.dtype),
        ],
        in_specs=[HBM, VM, HBM, HBM],
        out_specs=[VM, VM, HBM, HBM],
        scratch_shapes=[
            pltpu.VMEM((nh, nchip) + block, BF16),
            pltpu.VMEM((nh, nchip) + block, BF16),
            pltpu.VMEM((nh, sides) + block, BF16),
            pltpu.VMEM((nh,) + block, BF16),
            pltpu.VMEM((nh,) + halfb, BF16),
            pltpu.VMEM((nh,) + halfb, BF16),
            pltpu.VMEM((nh,) + block, BF16),
            pltpu.VMEM((ndp,) + small.shape, F32),
            pltpu.VMEM((nh,) + small.shape, F32),
            dma((sent,)),
            dma((nh, nchip)),
            dma((nh, nchip)),
            dma((nh, max(4, nchip))),
            dma((nh,)),
            dma((ndp,)),
            dma((nh,)),
            dma((2,)),
            dma((2,)),
        ],
        compiler_params=params(28, 6),
        cost_estimate=cost(65),
        name="scatter",
    )(grads, small, out_v, fgrad_v)


def nn(a, b):
    return jnp.dot(a, b, preferred_element_type=F32)


def nt(a, b):
    return lax.dot_general(a, b, (((1,), (1,)), ((), ())), preferred_element_type=F32)


def tn(a, b):
    return lax.dot_general(a, b, (((0,), (0,)), ((), ())), preferred_element_type=F32)


def sigmoid(v):
    return 0.5 * jnp.tanh(0.5 * v) + 0.5


def slope_of(v, sig):
    return sig * (1.0 + v * (1.0 - sig))


class Blocks:
    def __init__(self, nh):
        self.nh = nh
        ff, ch = FF // nh // BLOCKW, D // nh // BLOCKW
        self.ff, self.ch = ff, ch
        self.in_one, self.in_two = 0, ff
        self.query = 2 * ff
        self.key = self.query + ch
        self.value = self.key + ch
        self.conv_value = self.value + ch
        self.conv_gate = self.conv_value + ch
        rows = self.conv_gate + ch
        self.out_one, self.out_two = rows, rows + ff
        self.attn = rows + 2 * ff
        self.point = self.attn + ch
        self.total = self.point + ch


def fetch(full, inv, dst, sem, base, count, part, row):
    for j in range(count):
        pltpu.make_async_copy(
            full.at[part, inv[base + j]], dst.at[pl.ds(row + j * BLOCKW, BLOCKW)], sem
        ).start()


def fetch_all(full, inv, dst, sem, base, count, nh, row=0):
    for part in range(nh):
        fetch(full, inv, dst, sem, base, count, part, row + part * count * BLOCKW)


def landed(dst, sem):
    pltpu.make_async_copy(dst, dst, sem).wait()


def put(grads, inv, src, sem, base, count, part, row):
    for j in range(count):
        pltpu.make_async_copy(
            src.at[pl.ds(row + j * BLOCKW, BLOCKW)], grads.at[part, inv[base + j]], sem
        ).start()


def put_all(grads, inv, src, sem, base, count, nh, row=0):
    for part in range(nh):
        put(grads, inv, src, sem, base, count, part, row + part * count * BLOCKW)


def tables(meta, frame):
    length, batch = meta[0], meta[1]
    utterance = jnp.zeros_like(frame)
    for i in range(1, 8):
        utterance = utterance + (frame >= i * length).astype(jnp.int32)
    within = frame - utterance * length
    own = jnp.zeros_like(frame)
    for i in range(8):
        own = jnp.where(utterance == i, meta[2 + i], own)
    live = (utterance < batch) & (within < own)
    return utterance, within, live


def live_rows(meta, start, count):
    frame = start + lax.broadcasted_iota(jnp.int32, (count, 1), 0)
    return tables(meta, frame)[2].astype(F32)


def hat(x):
    center = jnp.mean(x, axis=1, keepdims=True)
    offset = x - center
    spread = lax.rsqrt(jnp.mean(offset * offset, axis=1, keepdims=True) + norm_eps)
    return offset * spread, spread


def norm(x, norms, i):
    return hat(x)[0] * norms[i : i + 1, :] + norms[i + 5 : i + 6, :]


def norm_back(x, grad, gain):
    return hat_back(*hat(x), grad, gain)


def hat_back(xhat, spread, grad, gain):
    scaled = grad * gain
    inner = scaled - jnp.mean(scaled, axis=1, keepdims=True) - xhat * jnp.mean(scaled * xhat, axis=1, keepdims=True)
    return spread * inner, jnp.sum(grad * xhat, axis=0, keepdims=True), jnp.sum(grad, axis=0, keepdims=True)


BAND = 64


def bands(rows, body, init=()):
    return lax.fori_loop(0, rows // BAND, lambda i, c: body(pl.ds(pl.multiple_of(i * BAND, BAND), BAND), i, c), init, unroll=True)


def partner(x):
    lane = lax.broadcasted_iota(jnp.int32, x.shape, 1) % HD
    return jnp.where(lane < HD // 2, pltpu.roll(x, 128 - HD // 2, 1), pltpu.roll(x, HD // 2, 1))


def turn(x, table, sign):
    first = lax.broadcasted_iota(jnp.int32, table.shape, 1) % HD < HD // 2
    cos = jnp.where(first, table, pltpu.roll(table, HD // 2, 1))
    sin = jnp.where(first, -pltpu.roll(table, 128 - HD // 2, 1), table)
    parts = []
    for i in range(D // 128):
        piece = x[:, i * 128 : (i + 1) * 128]
        parts.append(piece * cos + partner(piece) * (sign * sin))
    return jnp.concatenate(parts, axis=1)


def rope_table():
    freq = np.exp(np.arange(HD // 2, dtype=np.float32) * np.float32(-math.log(10000.0) / (HD // 2)))
    angle = np.arange(LONGEST, dtype=np.float32)[:, None] * freq[None, :].astype(np.float32)
    return np.tile(np.concatenate([np.cos(angle), np.sin(angle)], axis=1), (1, 2)).astype(np.float32)


def place_of(meta, i):
    return pl.multiple_of(lax.rem(meta[10] + i * BAND, meta[0]), BAND)


def feed(n_ref, w_in, w_out, acc_ref, sem, sem2, nh):
    unit = FF // nh
    for part in range(nh):
        rows = pl.ds(part * unit, unit)
        landed(w_in.at[rows], sem.at[part])
        pre = nt(n_ref[...], w_in[rows, :])
        act = (pre * sigmoid(pre)).astype(BF16)
        landed(w_out.at[rows], sem2.at[part])
        if part == 0:
            acc_ref[...] = nn(act, w_out[rows, :])
        else:
            acc_ref[...] += nn(act, w_out[rows, :])


def feed_back(n_ref, gb_ref, w_in, w_out, acc_ref, g_in, g_out, grads, inv, base_in, base_out, sem_in, sem_out, count, nh):
    unit = FF // nh

    def body(part, carry):
        rows = pl.ds(pl.multiple_of(part * unit, unit), unit)
        n, gb, win, wout = n_ref[...], gb_ref[...], w_in[rows, :], w_out[rows, :]
        pre = nt(win, n)
        sig = sigmoid(pre)
        act = (pre * sig).astype(BF16)
        dpre = (nt(wout, gb) * slope_of(pre, sig)).astype(BF16)
        g_out[rows, :] = nn(act, gb).astype(BF16)
        g_in[rows, :] = nn(dpre, n).astype(BF16)
        acc_ref[...] += tn(dpre, win)
        put(grads, inv, g_out, sem_out, base_out, count, part, part * unit)
        put(grads, inv, g_in, sem_in, base_in, count, part, part * unit)
        return carry

    acc_ref[...] = jnp.zeros_like(acc_ref)
    lax.fori_loop(0, nh, body, 0)


def front_kernel(ndp, nh, owner, place, ints, conv, frames, norms, table, full, x1, q, kv, meta, inv, taps, w_in, w_out, w_qkv, n_ref, acc, groups, sem, sem2, sem3):
    b = Blocks(nh)
    known = pltpu.make_async_copy(ints, groups, sem3.at[1])
    known.start()

    def slot(i, c):
        inv[owner[i]] = i
        return c

    lax.fori_loop(0, owner.shape[0], slot, 0)
    rows = frames.shape[0]
    unit = FF // nh
    for part in range(nh):
        fetch(full, inv, w_in, sem.at[part], b.in_one, b.ff, part, part * unit)
        fetch(full, inv, w_out, sem2.at[part], b.out_one, b.ff, part, part * unit)
    for i, base in enumerate((b.query, b.key, b.value)):
        fetch_all(full, inv, w_qkv, sem3.at[0], base, b.ch, nh, i * D)

    def first(at, i, c):
        n_ref[at, :] = norm(frames[at, :].astype(F32), norms, 0).astype(BF16)
        return c

    bands(rows, first)
    known.wait()
    for i in range(16):
        meta[i] = groups[place[0], 0, i]
    meta[10] = place[1] * rows

    def count(d, total):
        for u in range(8):
            total += jnp.where(u < groups[d, 0, 1], jnp.minimum(groups[d, 0, 2 + u], groups[d, 0, 0]), 0)
        return total

    meta[11] = lax.fori_loop(0, ndp, count, 0)
    taps[...] = jnp.zeros_like(taps)
    width = conv.shape[2]
    for h in range(nh):
        taps[0 : KERNEL + 2, h * width : (h + 1) * width] = conv[h]
    feed(n_ref, w_in, w_out, acc, sem, sem2, nh)

    def second(at, i, c):
        x = frames[at, :].astype(F32) + 0.5 * acc[at, :]
        x1[at, :] = x
        n_ref[at, :] = norm(x, norms, 1).astype(BF16)
        return c

    bands(rows, second)
    landed(w_qkv, sem3.at[0])
    for j, (dst, lo) in enumerate(((q, 0), (kv, 0), (kv, D))):
        acc[...] = nt(n_ref[...], w_qkv[j * D : (j + 1) * D, :])

        def third(at, i, c):
            x = acc[at, :]
            if j < 2:
                p = pl.ds(place_of(meta, i), BAND)
                x = turn(x, table[p, :], 1.0)
            dst[at, lo : lo + D] = x.astype(BF16)
            return c

        bands(rows, third)


def front(ndp, nh, owner, place, ints, conv, frames, norms, table, full):
    rows = frames.shape[0]
    dma = pltpu.SemaphoreType.DMA
    return pl.pallas_call(
        functools.partial(front_kernel, ndp, nh),
        out_shape=[
            jax.ShapeDtypeStruct((rows, D), F32),
            jax.ShapeDtypeStruct((rows, D), BF16),
            jax.ShapeDtypeStruct((rows, 2 * D), BF16),
            jax.ShapeDtypeStruct((16,), jnp.int32),
            jax.ShapeDtypeStruct(owner.shape, jnp.int32),
            jax.ShapeDtypeStruct((40, D), F32),
        ],
        in_specs=[SM, SM, ANY, VM, VM, VM, VM, HBM],
        out_specs=[VM, VM, VM, SM, SM, VM],
        scratch_shapes=[
            pltpu.VMEM((FF, D), BF16),
            pltpu.VMEM((FF, D), BF16),
            pltpu.VMEM((3 * D, D), BF16),
            pltpu.VMEM((rows, D), BF16),
            pltpu.VMEM((rows, D), F32),
            pltpu.SMEM((ndp, 8, 128), jnp.int32),
            dma((nh,)),
            dma((nh,)),
            dma((2,)),
        ],
        compiler_params=params(18),
        cost_estimate=cost(7),
        name="front",
    )(owner, place, ints, conv, frames, norms, table, full)


def fill_chunk(meta, src, chunk, k, start):
    lead = lax.rem(start + k * 256, meta[0]) != 0
    trail = lax.rem(start + (k + 1) * 256, meta[0]) != 0
    chunk[0:HALO, :] = jnp.where(lead, src[k * 256 : k * 256 + HALO, :], 0.0)
    chunk[HALO : HALO + 256, :] = src[k * 256 + HALO : k * 256 + HALO + 256, :]
    chunk[HALO + 256 :, :] = jnp.where(trail, src[k * 256 + HALO + 256 : k * 256 + 2 * HALO + 256, :], 0.0)


def shift_rows(chunk, moved):
    rows = chunk.shape[0]
    moved[0] = chunk[...]
    for b in range(1, 8):
        moved[b, 0 : rows - 8, :] = chunk[b : b + rows - 8, :]


def attend_kernel(nh, meta, inv, q, kvw, x1, qh, x1h, norms, taps, full, o_o, lse_o, x2_o, gated_o, h_o, sums_o, w_attn, w_glu, q_ext, o_ext, x_ext, bias, n_ref, val, gate, chunk, moved, lse_s, sem):
    b = Blocks(nh)
    rows = q.shape[0]
    ext = rows + 2 * HALO
    start = meta[10]
    fetch_all(full, inv, w_attn, sem.at[0], b.attn, b.ch, nh)
    for i, base in enumerate((b.conv_value, b.conv_gate)):
        fetch_all(full, inv, w_glu, sem.at[1], base, b.ch, nh, i * D)
    q_ext[0:HALO, :] = qh[0:HALO, :]
    q_ext[HALO : HALO + rows, :] = q[...]
    q_ext[HALO + rows :, :] = qh[HALO:, :]
    x_ext[0:HALO, :] = x1h[0:HALO, :]
    x_ext[HALO : HALO + rows, :] = x1[...]
    x_ext[HALO + rows :, :] = x1h[HALO:, :]
    base = start - lax.rem(start, LONGEST)
    key_frame = base + lax.broadcasted_iota(jnp.int32, (1, LONGEST), 1)
    ukey, _, lkey = tables(meta, key_frame)
    ukey = jnp.where(lkey, ukey, -1)
    query_frame = start - HALO + lax.broadcasted_iota(jnp.int32, (ext, 1), 0)
    uquery, _, lquery = tables(meta, query_frame)
    live = lquery.astype(F32)
    bias[...] = jnp.where(ukey == uquery, 0.0, masked_score)
    half = ext // 2
    head_lane = lax.broadcasted_iota(jnp.int32, (half, 128), 1)

    for pair in range(D // 128):
        lanes = slice(pair * 128, (pair + 1) * 128)
        kp = kvw[:, lanes]
        vp = kvw[:, D + pair * 128 : D + (pair + 1) * 128]
        for blk in range(2):
            at = slice(blk * half, (blk + 1) * half)
            qp = q_ext[at, lanes] * 0.125
            outs = []
            for hh in range(2):
                mine = head_lane < HD if hh == 0 else head_lane >= HD
                qm = jnp.where(mine, qp, jnp.zeros_like(qp))
                s = nt(qm, kp) + bias[at, :]
                top = jnp.max(s, axis=1, keepdims=True)
                e = jnp.exp(s - top)
                total = jnp.sum(e, axis=1, keepdims=True)
                outs.append(nn(e.astype(BF16), vp) * (1.0 / total))
                lse_s[at, pair * 2 + hh : pair * 2 + hh + 1] = top + jnp.log(total)
            o = jnp.where(head_lane < HD, outs[0], outs[1]) * live[at, :]
            o_ext[at, lanes] = o.astype(BF16)
    o_o[...] = o_ext[HALO : HALO + rows, :]
    lse_o[...] = jnp.transpose(lse_s[HALO : HALO + rows, :])[0:8, :]
    landed(w_attn, sem.at[0])
    x_ext[...] += nn(o_ext[...], w_attn[...])
    x2_o[...] = x_ext[HALO : HALO + rows, :]

    def third(i, c):
        at = pl.ds(pl.multiple_of(i * 32, 32), 32)
        n_ref[at, :] = norm(x_ext[at, :], norms, 2).astype(BF16)
        return c

    lax.fori_loop(0, ext // 32, third, 0, unroll=True)
    landed(w_glu, sem.at[1])
    val[...] = nt(n_ref[...], w_glu[0:D, :])
    gate[...] = nt(n_ref[...], w_glu[D:, :])
    gated_o[...] = val[...] * sigmoid(gate[...]) * live
    sums = [[0.0] * (D // 128) for _ in range(2)]
    for k in range(rows // 256):
        fill_chunk(meta, gated_o, chunk, k, start)
        alive = live[HALO + k * 256 : HALO + (k + 1) * 256, :]
        shift_rows(chunk, moved)
        for lc in range(D // 128):
            lanes = slice(lc * 128, (lc + 1) * 128)
            acc = moved[0, 0:256, lanes] * taps[0:1, lanes]
            for j in range(1, KERNEL):
                lo = j - j % 8
                acc = acc + moved[j % 8, lo : lo + 256, lanes] * taps[j : j + 1, lanes]
            h_o[k * 256 : (k + 1) * 256, lanes] = acc
            weighted = acc * alive
            sums[0][lc] += jnp.sum(weighted, axis=0, keepdims=True)
            sums[1][lc] += jnp.sum(weighted * acc, axis=0, keepdims=True)
    sums_o[...] = jnp.concatenate(sums[0] + sums[1], axis=0)


def attend(nh, meta, inv, q, kvw, x1, qh, x1h, norms, taps, full):
    rows = q.shape[0]
    ext = rows + 2 * HALO
    dma = pltpu.SemaphoreType.DMA
    f = jax.ShapeDtypeStruct
    return pl.pallas_call(
        functools.partial(attend_kernel, nh),
        out_shape=[
            f((rows, D), BF16),
            f((8, rows), F32),
            f((rows, D), F32),
            f((ext, D), F32),
            f((rows, D), F32),
            f((2 * D // 128, 128), F32),
        ],
        in_specs=[SM, SM] + [VM] * 7 + [HBM],
        out_specs=[VM] * 6,
        scratch_shapes=[
            pltpu.VMEM((D, D), BF16),
            pltpu.VMEM((2 * D, D), BF16),
            pltpu.VMEM((ext, D), BF16),
            pltpu.VMEM((ext, D), BF16),
            pltpu.VMEM((ext, D), F32),
            pltpu.VMEM((ext, LONGEST), F32),
            pltpu.VMEM((ext, D), BF16),
            pltpu.VMEM((ext, D), F32),
            pltpu.VMEM((ext, D), F32),
            pltpu.VMEM((256 + 2 * HALO, D), F32),
            pltpu.VMEM((8, 256 + 2 * HALO, D), F32),
            pltpu.VMEM((ext, 128), F32),
            dma((2,)),
        ],
        compiler_params=params(30),
        cost_estimate=cost(13),
        name="attend",
    )(meta, inv, q, kvw, x1, qh, x1h, norms, taps, full)


def compact(rows_of):
    pieces = [r[:, i * 128 : (i + 1) * 128] for r in rows_of for i in range(D // 128)]
    return jnp.concatenate(pieces, axis=0)


def spread(packed, row):
    n = D // 128
    return jnp.concatenate([packed[row * n + i : row * n + i + 1, :] for i in range(n)], axis=1)


def bn_terms(meta, packed):
    count = jnp.full((1, 1), meta[11], jnp.int32).astype(F32)
    stats = [spread(packed, 0), spread(packed, 1)]
    center = stats[0] / count
    inv_std = lax.rsqrt(stats[1] / count - center * center + norm_eps)
    return count, center, inv_std


def middle_kernel(nh, meta, inv, x2, h, stats, ograd, norms, taps, full, out_o, g3_o, gz_o, sums_o, ng_o, grads, w_in, w_out, w_pt, n_ref, gb, y3, x3, x4, acc, g_in, g_out, g_pt, sem, sem2, sem3, gsem):
    b = Blocks(nh)
    rows = x2.shape[0]
    unit = FF // nh
    fetch_all(full, inv, w_pt, sem3.at[0], b.point, b.ch, nh)
    for part in range(nh):
        fetch(full, inv, w_in, sem.at[part], b.in_two, b.ff, part, part * unit)
        fetch(full, inv, w_out, sem2.at[part], b.out_two, b.ff, part, part * unit)
    count, center, inv_std = bn_terms(meta, stats)
    gain, shift = taps[KERNEL : KERNEL + 1, :], taps[KERNEL + 1 : KERNEL + 2, :]

    def z_of(at):
        return (h[at, :] - center) * inv_std * gain + shift

    def first(at, i, c):
        z = z_of(at)
        y3[at, :] = (z * sigmoid(z)).astype(BF16)
        return c

    bands(rows, first)
    landed(w_pt, sem3.at[0])
    x3[...] = x2[...] + nn(y3[...], w_pt[...])

    def second(at, i, c):
        n_ref[at, :] = norm(x3[at, :], norms, 3).astype(BF16)
        return c

    bands(rows, second)
    feed(n_ref, w_in, w_out, acc, sem, sem2, nh)
    zero = jnp.zeros((1, D), F32)

    def last(at, i, c):
        x = x3[at, :] + 0.5 * acc[at, :]
        xhat, spread = hat(x)
        out_o[at, :] = (xhat * norms[4:5, :] + norms[9:10, :]).astype(BF16)
        dx, dg, db = hat_back(xhat, spread, ograd[at, :].astype(F32), norms[4:5, :])
        x4[at, :] = dx
        gb[at, :] = (0.5 * dx).astype(BF16)
        return c[0] + dg, c[1] + db

    gain4, shift4 = bands(rows, last, (zero, zero))
    feed_back(n_ref, gb, w_in, w_out, acc, g_in, g_out, grads, inv, b.in_two, b.out_two, gsem.at[0], gsem.at[1], b.ff, nh)

    def back(at, i, c):
        dx, dg, db = norm_back(x3[at, :], acc[at, :], norms[3:4, :])
        g3 = x4[at, :] + dx
        g3_o[at, :] = g3
        gb[at, :] = g3.astype(BF16)
        return c[0] + dg, c[1] + db

    gain3, shift3 = bands(rows, back, (zero, zero))
    ng_o[...] = jnp.zeros_like(ng_o)
    ng_o[3:4, :] = gain3
    ng_o[4:5, :] = gain4
    ng_o[8:9, :] = shift3
    ng_o[9:10, :] = shift4
    acc[...] = nt(gb[...], w_pt[...])
    g_pt[...] = tn(y3[...], gb[...]).astype(BF16)
    put_all(grads, inv, g_pt, gsem.at[2], b.point, b.ch, nh)

    def gz_part(at, i, c):
        white = (h[at, :] - center) * inv_std
        z = white * gain + shift
        gz = acc[at, :] * slope_of(z, sigmoid(z))
        gz_o[at, :] = gz
        return c[0] + jnp.sum(gz, axis=0, keepdims=True), c[1] + jnp.sum(gz * white, axis=0, keepdims=True)

    sg, sx = bands(rows, gz_part, (zero, zero))
    sums_o[...] = compact([sg, sx])
    y3[0:BLOCKW, :] = jnp.zeros((BLOCKW, D), BF16)
    empty = [(i, part) for i in range(b.total, grads.shape[1]) for part in range(nh)]
    for k, (i, part) in enumerate(empty):
        put(grads, inv, y3, gsem.at[3 + k], i, 1, part, 0)
    landed(g_in, gsem.at[0])
    landed(g_out, gsem.at[1])
    landed(g_pt, gsem.at[2])
    for k in range(len(empty)):
        landed(y3.at[pl.ds(0, BLOCKW)], gsem.at[3 + k])


def middle(nh, meta, inv, x2, h, stats, ograd, norms, taps, full):
    rows = x2.shape[0]
    slots = full.shape[1]
    zeros = (slots - Blocks(nh).total) * nh
    dma = pltpu.SemaphoreType.DMA
    f = jax.ShapeDtypeStruct
    v = pltpu.VMEM
    return pl.pallas_call(
        functools.partial(middle_kernel, nh),
        out_shape=[
            f((rows, D), BF16),
            f((rows, D), F32),
            f((rows, D), F32),
            f((2 * D // 128, 128), F32),
            f((16, D), F32),
            f((big(nh, slots), slots, BLOCKW, D), BF16),
        ],
        in_specs=[SM, SM] + [VM] * 6 + [HBM],
        out_specs=[VM] * 5 + [HBM],
        scratch_shapes=[
            v((FF, D), BF16),
            v((FF, D), BF16),
            v((D, D), BF16),
            v((rows, D), BF16),
            v((rows, D), BF16),
            v((rows, D), BF16),
            v((rows, D), F32),
            v((rows, D), F32),
            v((rows, D), F32),
            v((FF, D), BF16),
            v((FF, D), BF16),
            v((D, D), BF16),
            dma((nh,)),
            dma((nh,)),
            dma((1,)),
            dma((3 + zeros,)),
        ],
        compiler_params=params(26),
        cost_estimate=cost(17),
        name="middle",
    )(meta, inv, x2, h, stats, ograd, norms, taps, full)


def conv_back_kernel(nh, meta, inv, gz, gzh, h, hh, stats, bsums, gated, x2, g3, o, norms, taps, full, ng_in, grads_in, g2_o, do_o, taps_o, ng_o, grads, w_attn, w_glu, n_ref, gb, dh, dgated, val, gate, dglu, g_attn, g_glu, chunk, moved, tsum, sem, gsem):
    del grads_in
    b = Blocks(nh)
    rows = gz.shape[0]
    ext = rows + 2 * HALO
    start = meta[10]
    fetch_all(full, inv, w_attn, sem.at[0], b.attn, b.ch, nh)
    for i, base in enumerate((b.conv_value, b.conv_gate)):
        fetch_all(full, inv, w_glu, sem.at[1], base, b.ch, nh, i * D)
    count, center, inv_std = bn_terms(meta, stats)
    gain = taps[KERNEL : KERNEL + 1, :]
    sg, sx = spread(bsums, 0), spread(bsums, 1)

    def dh_of(gz_rows, h_rows, first):
        alive = live_rows(meta, first, gz_rows.shape[0])
        white = (h_rows - center) * inv_std
        return gain * inv_std * (gz_rows - alive / count * (sg + white * sx))

    def one(at, i, c):
        dh[pl.ds(pl.multiple_of(i * BAND + HALO, HALO), BAND), :] = dh_of(gz[at, :], h[at, :], start + i * BAND)
        n_ref[at, :] = norm(x2[at, :], norms, 2).astype(BF16)
        return c

    bands(rows, one)
    dh[0:HALO, :] = dh_of(gzh[0:HALO, :], hh[0:HALO, :], start - HALO)
    dh[HALO + rows :, :] = dh_of(gzh[HALO:, :], hh[HALO:, :], start + rows)
    tsum[...] = jnp.zeros_like(tsum)
    for k in range(rows // 256):
        fill_chunk(meta, dh, chunk, k, start)
        shift_rows(chunk, moved)

        for i in range(4 * D // 128):
            lanes = slice(i // 4 * 128, i // 4 * 128 + 128)
            row = i % 4 * 64
            own = gated[row + HALO + k * 256 : row + HALO + k * 256 + 64, lanes]
            acc = jnp.zeros((64, 128), F32)
            for j in range(KERNEL):
                off = KERNEL - j
                there = moved[off % 8, row + off - off % 8 : row + off - off % 8 + 64, lanes]
                acc = acc + there * taps[j : j + 1, lanes]
                tsum[j, :, lanes] += jnp.sum((there * own).reshape(8, 8, 128), axis=0)
            dgated[row + k * 256 : row + k * 256 + 64, lanes] = acc
    taps_o[...] = jnp.sum(tsum[...], axis=1)
    landed(w_glu, sem.at[1])
    val[...] = nt(n_ref[...], w_glu[0:D, :])
    gate[...] = nt(n_ref[...], w_glu[D:, :])

    def two(at, i, c):
        sig = sigmoid(gate[at, :])
        d = dgated[at, :] * live_rows(meta, start + i * BAND, BAND)
        dglu[at, 0:D] = (d * sig).astype(BF16)
        dglu[at, D:] = (d * val[at, :] * sig * (1.0 - sig)).astype(BF16)
        return c

    bands(rows, two)
    g_glu[...] = tn(dglu[...], n_ref[...]).astype(BF16)
    for i, base in enumerate((b.conv_value, b.conv_gate)):
        put_all(grads, inv, g_glu, gsem.at[0], base, b.ch, nh, i * D)
    val[...] = nn(dglu[...], w_glu[...])
    zero = jnp.zeros((1, D), F32)

    def three(at, i, c):
        dx, dg, db = norm_back(x2[at, :], val[at, :], norms[2:3, :])
        g2 = g3[at, :] + dx
        g2_o[at, :] = g2
        gb[at, :] = g2.astype(BF16)
        return c[0] + dg, c[1] + db

    dgain, dshift = bands(rows, three, (zero, zero))
    ng_o[...] = ng_in[...]
    ng_o[2:3, :] = dgain
    ng_o[7:8, :] = dshift
    landed(w_attn, sem.at[0])
    gate[...] = nt(gb[...], w_attn[...])
    g_attn[...] = tn(o[...], gb[...]).astype(BF16)
    put_all(grads, inv, g_attn, gsem.at[1], b.attn, b.ch, nh)

    def four(at, i, c):
        do_o[at, :] = (gate[at, :] * live_rows(meta, start + i * BAND, BAND)).astype(BF16)
        return c

    bands(rows, four)
    landed(g_glu, gsem.at[0])
    landed(g_attn, gsem.at[1])


def conv_back(nh, meta, inv, gz, gzh, h, hh, stats, bsums, gated, x2, g3, o, norms, taps, full, ng, grads):
    rows = gz.shape[0]
    ext = rows + 2 * HALO
    dma = pltpu.SemaphoreType.DMA
    f = jax.ShapeDtypeStruct
    v = pltpu.VMEM
    return pl.pallas_call(
        functools.partial(conv_back_kernel, nh),
        out_shape=[
            f((rows, D), F32),
            f((rows, D), BF16),
            f((KERNEL, D), F32),
            f((16, D), F32),
            f(grads.shape, BF16),
        ],
        in_specs=[SM, SM] + [VM] * 12 + [HBM, VM, HBM],
        out_specs=[VM] * 4 + [HBM],
        input_output_aliases={16: 4},
        scratch_shapes=[
            v((D, D), BF16),
            v((2 * D, D), BF16),
            v((rows, D), BF16),
            v((rows, D), BF16),
            v((ext, D), F32),
            v((rows, D), F32),
            v((rows, D), F32),
            v((rows, D), F32),
            v((rows, 2 * D), BF16),
            v((D, D), BF16),
            v((2 * D, D), BF16),
            v((256 + 2 * HALO, D), F32),
            v((8, 256 + 2 * HALO, D), F32),
            v((KERNEL, 8, D), F32),
            dma((2,)),
            dma((2,)),
        ],
        compiler_params=params(28),
        cost_estimate=cost(13),
        name="conv_back",
    )(meta, inv, gz, gzh, h, hh, stats, bsums, gated, x2, g3, o, norms, taps, full, ng, grads)


def attend_back_kernel(meta, q, kvw, do, lse, dq_o, dkv_o, send_o, bias, dkp, dvp):
    rows = q.shape[0]
    start = meta[10]
    base = start - lax.rem(start, LONGEST)
    offset = pl.multiple_of(lax.rem(start, LONGEST), rows)
    ukey, _, lkey = tables(meta, base + lax.broadcasted_iota(jnp.int32, (LONGEST, 1), 0))
    ukey = jnp.where(lkey, ukey, -1)
    uquery, _, _ = tables(meta, start + lax.broadcasted_iota(jnp.int32, (1, rows), 1))
    bias[...] = jnp.where(ukey == uquery, 0.0, masked_score)
    lane_q = lax.broadcasted_iota(jnp.int32, (rows, 128), 1)
    lane_k = lax.broadcasted_iota(jnp.int32, (LONGEST, 128), 1)
    for pair in range(D // 128):
        lanes = slice(pair * 128, (pair + 1) * 128)
        kp = kvw[:, lanes]
        vp = kvw[:, D + pair * 128 : D + (pair + 1) * 128]
        kms = [jnp.where(lane_k < HD, kp, jnp.zeros_like(kp)), jnp.where(lane_k >= HD, kp, jnp.zeros_like(kp))]
        qp = q[:, lanes] * 0.125
        dop = do[:, lanes]
        for hh in range(2):
            mine = lane_q < HD if hh == 0 else lane_q >= HD
            qm = jnp.where(mine, qp, jnp.zeros_like(qp))
            dom = jnp.where(mine, dop, jnp.zeros_like(dop))
            s = nt(kp, qm) + bias[...]
            p = jnp.exp(s - lse[pair * 2 + hh : pair * 2 + hh + 1, :])
            dp = nt(vp, dom)
            inner = jnp.sum(p * dp, axis=0, keepdims=True)
            ds = (p * (dp - inner)).astype(BF16)
            dv, dk, dq = nn(p.astype(BF16), dom), nn(ds, qm), tn(ds, kms[hh]) * 0.125
            if hh == 0:
                dvp[...], dkp[...], dq_o[:, lanes] = dv, dk, dq
            else:
                dvp[...] += dv
                dkp[...] += dk
                dq_o[:, lanes] += dq
        dkv_o[:, lanes] = dkp[pl.ds(offset, rows), :]
        dkv_o[:, D + pair * 128 : D + (pair + 1) * 128] = dvp[pl.ds(offset, rows), :]
        send_o[:, lanes] = dkp[...].astype(BF16)
        send_o[:, D + pair * 128 : D + (pair + 1) * 128] = dvp[...].astype(BF16)


def attend_back(meta, q, kvw, do, lse):
    rows = q.shape[0]
    f = jax.ShapeDtypeStruct
    v = pltpu.VMEM
    return pl.pallas_call(
        attend_back_kernel,
        out_shape=[f((rows, D), F32), f((rows, 2 * D), F32), f((LONGEST, 2 * D), BF16)],
        in_specs=[SM] + [VM] * 4,
        out_specs=[VM] * 3,
        scratch_shapes=[v((LONGEST, rows), F32), v((LONGEST, 128), F32), v((LONGEST, 128), F32)],
        compiler_params=params(26),
        cost_estimate=cost(14),
        name="attend_back",
    )(meta, q, kvw, do, lse)


def rear_kernel(nh, meta, inv, dq, dkv, recv, x1, frames, g2, norms, table, full, ng_in, grads_in, fg_o, ng_o, grads, w_in, w_out, w_qkv, n_ref, gb, dproj, x_ref, acc, g_in, g_out, g_qkv, sem, gsem):
    del grads_in
    b = Blocks(nh)
    rows = dq.shape[0]
    for i, base in enumerate((b.query, b.key, b.value)):
        fetch_all(full, inv, w_qkv, sem.at[0], base, b.ch, nh, i * D)
    fetch_all(full, inv, w_in, sem.at[1], b.in_one, b.ff, nh)
    fetch_all(full, inv, w_out, sem.at[2], b.out_one, b.ff, nh)
    spans = recv.shape[0]

    def one(at, i, c):
        p = pl.ds(place_of(meta, i), BAND)
        dproj[at, 0:D] = turn(dq[at, :], table[p, :], -1.0).astype(BF16)
        dk, dv = dkv[at, 0:D], dkv[at, D:]
        for s in range(spans):
            dk = dk + recv[s, at, 0:D].astype(F32)
            dv = dv + recv[s, at, D:].astype(F32)
        dproj[at, D : 2 * D] = turn(dk, table[p, :], -1.0).astype(BF16)
        dproj[at, 2 * D :] = dv.astype(BF16)
        n_ref[at, :] = norm(x1[at, :], norms, 1).astype(BF16)
        return c

    bands(rows, one)
    landed(w_qkv, sem.at[0])
    acc[...] = nn(dproj[...], w_qkv[...])
    for i in range(3):
        g_qkv[i * D : (i + 1) * D, :] = tn(dproj[:, i * D : (i + 1) * D], n_ref[...]).astype(BF16)
    for i, base in enumerate((b.query, b.key, b.value)):
        put_all(grads, inv, g_qkv, gsem.at[0], base, b.ch, nh, i * D)
    zero = jnp.zeros((1, D), F32)

    def two(at, i, c):
        dx, dg, db = norm_back(x1[at, :], acc[at, :], norms[1:2, :])
        g1 = g2[at, :] + dx
        x_ref[at, :] = g1
        gb[at, :] = (0.5 * g1).astype(BF16)
        n_ref[at, :] = norm(frames[at, :].astype(F32), norms, 0).astype(BF16)
        return c[0] + dg, c[1] + db

    gain1, shift1 = bands(rows, two, (zero, zero))
    landed(w_in, sem.at[1])
    landed(w_out, sem.at[2])
    feed_back(n_ref, gb, w_in, w_out, acc, g_in, g_out, grads, inv, b.in_one, b.out_one, gsem.at[1], gsem.at[2], b.ff, nh)

    def three(at, i, c):
        dx, dg, db = norm_back(frames[at, :].astype(F32), acc[at, :], norms[0:1, :])
        fg_o[at, :] = x_ref[at, :] + dx
        return c[0] + dg, c[1] + db

    gain0, shift0 = bands(rows, three, (zero, zero))
    ng_o[...] = ng_in[...]
    ng_o[0:1, :] = gain0
    ng_o[1:2, :] = gain1
    ng_o[5:6, :] = shift0
    ng_o[6:7, :] = shift1
    landed(g_qkv, gsem.at[0])
    landed(g_in, gsem.at[1])
    landed(g_out, gsem.at[2])


def rear(nh, meta, inv, dq, dkv, recv, x1, frames, g2, norms, table, full, ng, grads):
    rows = dq.shape[0]
    dma = pltpu.SemaphoreType.DMA
    f = jax.ShapeDtypeStruct
    v = pltpu.VMEM
    return pl.pallas_call(
        functools.partial(rear_kernel, nh),
        out_shape=[f((rows, D), F32), f((16, D), F32), f(grads.shape, BF16)],
        in_specs=[SM, SM] + [VM] * 8 + [HBM, VM, HBM],
        out_specs=[VM, VM, HBM],
        input_output_aliases={12: 2},
        scratch_shapes=[
            v((FF, D), BF16),
            v((FF, D), BF16),
            v((3 * D, D), BF16),
            v((rows, D), BF16),
            v((rows, D), BF16),
            v((rows, 3 * D), BF16),
            v((rows, D), F32),
            v((rows, D), F32),
            v((FF, D), BF16),
            v((FF, D), BF16),
            v((3 * D, D), BF16),
            dma((3,)),
            dma((3,)),
        ],
        compiler_params=params(28),
        cost_estimate=cost(13),
        name="rear",
    )(meta, inv, dq, dkv, recv, x1, frames, g2, norms, table, full, ng, grads)


def split(x):
    high = x.astype(BF16)
    return high, (x - high.astype(F32)).astype(BF16)


def three_products(dot, a, b):
    (ah, al), (bh, bl) = a, b
    return dot(ah, bh) + (dot(ah, bl) + dot(al, bh))


def wide_product(dot, a, b):
    rows = a.shape[0]
    ah, al = split(a)
    stacked = dot(jnp.concatenate([ah, al], axis=0), b[0])
    return stacked[0:rows] + (stacked[rows:] + dot(ah, b[1]))


def adam_step(weight, gradient, moment_one, moment_two, factor):
    one_new = beta_one * moment_one + (1.0 - beta_one) * gradient
    two_new = beta_two * moment_two + (1.0 - beta_two) * gradient * gradient
    return (weight - factor * one_new / (jnp.sqrt(two_new) + adam_eps), one_new, two_new)


def update_kernel(nh, head, grad, masters, first, second, left, right, small, bsums, norms, norm1, norm2, conv, conv1, conv2, out_v, fgrad_v, masters_o, first_o, second_o, ng_o, norms_o, norm1_o, norm2_o, conv_o, conv1_o, conv2_o, out_o, fgrad_o, sem):
    moves = [
        pltpu.make_async_copy(out_v, out_o, sem.at[0]),
        pltpu.make_async_copy(fgrad_v, fgrad_o, sem.at[1]),
    ]
    step = pl.program_id(0)

    @pl.when(step == 0)
    def _():
        for move in moves:
            move.start()
        grads = small[0:10, :]
        ng_o[...] = grads
        norms_o[...], norm1_o[...], norm2_o[...] = adam_step(norms[...], grads, norm1[...], norm2[...], 10.0 * FACTOR)
        width = conv.shape[1]
        rows = jnp.concatenate([small[16 : 16 + KERNEL, :], spread(bsums, 1), spread(bsums, 0)], axis=0)
        mine = rows[:, 0:width]
        for h in range(1, nh):
            mine = jnp.where(head[0] == h, rows[:, h * width : (h + 1) * width], mine)
        conv_o[...], conv1_o[...], conv2_o[...] = adam_step(conv[...], mine, conv1[...], conv2[...], 4.0 * FACTOR)

    for i in range(grad.shape[0]):
        g = grad[i]
        m1 = beta_one * first[i] + (1.0 - beta_one) * g
        first_o[i] = m1
        lefts, rights = split(left[i]), split(right[i])
        both = wide_product(nn, jnp.concatenate([g, m1], axis=0), lefts)
        rot = three_products(tn, rights, split(both[0:BLOCKW]))
        rot1 = three_products(tn, rights, split(both[BLOCKW:]))
        m2 = beta_two * second[i] + (1.0 - beta_two) * rot * rot
        second_o[i] = m2
        scaled = rot1 / (jnp.sqrt(m2) + adam_eps)
        back = wide_product(nt, three_products(nn, rights, split(scaled)), lefts)
        w = masters[i]
        masters_o[i] = w - FACTOR * back - step_rate * weight_decay * w

    @pl.when(step == pl.num_programs(0) - 1)
    def _():
        for move in moves:
            move.wait()


def update(nh, head, grad, masters, first, second, left, right, small, bsums, norms, norm1, norm2, conv, conv1, conv2, out_v, fgrad_v):
    spd = grad.shape[0]
    n = 2 if spd % 2 == 0 else 1
    block = pl.BlockSpec((n, BLOCKW, D), lambda i: (i, 0, 0))

    def whole(a):
        return pl.BlockSpec(a.shape, lambda i: (0, 0))

    f = jax.ShapeDtypeStruct
    return pl.pallas_call(
        functools.partial(update_kernel, nh),
        grid=(spd // n,),
        out_shape=[f(grad.shape, F32)] * 3
        + [f(norms.shape, F32)] * 4
        + [f(conv.shape, F32)] * 3
        + [f(out_v.shape, out_v.dtype), f(fgrad_v.shape, F32)],
        in_specs=[SM]
        + [block] * 4
        + [pl.BlockSpec((n, D, D), lambda i: (i, 0, 0)), pl.BlockSpec((n, BLOCKW, BLOCKW), lambda i: (i, 0, 0))]
        + [whole(a) for a in (small, bsums, norms, norm1, norm2, conv, conv1, conv2)]
        + [HBM, HBM],
        out_specs=[block] * 3 + [whole(norms)] * 4 + [whole(conv)] * 3 + [HBM, HBM],
        scratch_shapes=[pltpu.SemaphoreType.DMA((2,))],
        compiler_params=params(20),
        cost_estimate=cost(9),
        name="update",
    )(head, grad, masters, first, second, left, right, small, bsums, norms, norm1, norm2, conv, conv1, conv2, out_v, fgrad_v)


def per_device(
    ndp,
    nh,
    frames,
    out_grad,
    bucket_len,
    batch_count,
    utt_lengths,
    owner_slots,
    masters,
    first_moment,
    second_moment,
    left_basis,
    right_basis,
    norm_params,
    norm_first,
    norm_second,
    conv_params,
    conv_first,
    conv_second,
):
    rows = frames.shape[0]

    def flip(a):
        return jnp.transpose(a[0], (0, 2, 1))

    masters_t = flip(masters)
    z = lax.axis_index("head")
    dp = lax.axis_index("dp")
    place = jnp.stack([dp - dp % 2 + z % 2, 2 * (z // 2) + dp % 2])
    full, frames_v, ograd_v, ints, conv_all = gather(
        ndp,
        nh,
        masters_t.astype(BF16),
        frames,
        out_grad,
        bucket_len[None],
        batch_count[None],
        utt_lengths,
        conv_params.T,
    )
    table = jnp.asarray(rope_table())
    x1, q, kv, meta, inv, taps = front(
        ndp, nh, owner_slots, place, ints, conv_all, frames_v, norm_params, table, full
    )
    kvw, qh, x1h = keys(ndp, nh, kv, q, x1)
    o, lse, x2, gated, h, sums = attend(nh, meta, inv, q, kvw, x1, qh, x1h, norm_params, taps, full)
    (stats,) = totals(ndp, nh, 3, sums)
    out_v, g3, gz, bpart, ng, grads = middle(nh, meta, inv, x2, h, stats, ograd_v, norm_params, taps, full)
    bsums, gzh, hh = totals(ndp, nh, 4, bpart, (gz, h))
    g2, do, dtaps, ng, grads = conv_back(
        nh, meta, inv, gz, gzh, h, hh, stats, bsums, gated, x2, g3, o, norm_params, taps, full, ng, grads
    )
    dq, dkv, dkv_send = attend_back(meta, q, kvw, do, lse)
    recv = key_grads(ndp, nh, dkv_send, rows)
    fg_v, ng, grads = rear(
        nh, meta, inv, dq, dkv, recv, x1, frames_v, g2, norm_params, table, full, ng, grads
    )
    small = jnp.concatenate([ng, dtaps], axis=0)
    owned, small, out_w, fg_w = scatter(ndp, nh, grads, small, out_v, fg_v)
    (
        new_m,
        new_f,
        new_s,
        norm_grads,
        new_norms,
        norm_first_new,
        norm_second_new,
        new_conv,
        conv_first_new,
        conv_second_new,
        layer_out,
        frames_grad,
    ) = update(
        nh,
        jnp.reshape(z, (1,)),
        owned,
        masters_t,
        flip(first_moment),
        flip(second_moment),
        left_basis[0],
        right_basis[0],
        small,
        bsums,
        norm_params,
        norm_first,
        norm_second,
        conv_params.T,
        conv_first.T,
        conv_second.T,
        out_w,
        fg_w,
    )

    def unflip(a):
        return jnp.transpose(a, (0, 2, 1))[None]

    return (
        layer_out,
        frames_grad,
        unflip(new_m),
        unflip(new_f),
        unflip(new_s),
        norm_grads,
        new_norms,
        norm_first_new,
        norm_second_new,
        new_conv.T,
        conv_first_new.T,
        conv_second_new.T,
    )


def solution(mesh):
    both, blocks, chan = P(("dp", "head"), None), P("head", "dp", None, None), P("head", None)
    placed = (both, both, P("dp"), P("dp"), P("dp", None), P()) + (blocks,) * 5 + (P(),) * 3 + (chan,) * 3
    return jax.shard_map(
        functools.partial(per_device, mesh.shape["dp"], mesh.shape["head"]),
        mesh=mesh,
        in_specs=placed,
        out_specs=(both, both) + (blocks,) * 3 + (P(),) * 4 + (chan,) * 3,
        check_vma=False,
    )
```

```python
import functools
import math

import jax
import jax.numpy as jnp
import numpy as np
from jax import lax
from jax.experimental import pallas as pl
from jax.experimental.pallas import tpu as pltpu
from jax.sharding import PartitionSpec as P

D = 512
FF = 2048
HD = 64
KERNEL = 32
BLOCKW = 64
STEP = 10
LONGEST = 1024
HALO = 16

beta_one = 0.9
beta_two = 0.95
step_rate = 0.05
weight_decay = 0.01
adam_eps = 1e-08
norm_eps = 1e-05
masked_score = -1e30
FACTOR = step_rate * math.sqrt(1.0 - beta_two**STEP) / (1.0 - beta_one**STEP)

F32 = jnp.float32
BF16 = jnp.bfloat16
MESH = pl.DeviceIdType.MESH
ANY = pl.BlockSpec(memory_space=pl.ANY)
HBM = pl.BlockSpec(memory_space=pltpu.HBM)
VM = pl.BlockSpec(memory_space=pltpu.VMEM)
SM = pl.BlockSpec(memory_space=pltpu.SMEM)
MIB = 1 << 20


def cost(us):
    return pl.CostEstimate(flops=0, bytes_accessed=int(us * 3.6e6), transcendentals=0)


def params(mib, collective_id=None):
    if collective_id is None:
        return pltpu.CompilerParams(vmem_limit_bytes=mib * MIB)
    return pltpu.CompilerParams(
        vmem_limit_bytes=mib * MIB, collective_id=collective_id, has_side_effects=True
    )


def big(nh, slots):
    return max(nh, -(-64 * MIB // (slots * BLOCKW * D * 2)))


class Copies:
    def __init__(self, sends):
        self.sends = sends
        self.used = 0
        self.open = []

    def send(self, src, dst, recv_sem, device, when=None):
        copy = pltpu.make_async_remote_copy(
            src_ref=src,
            dst_ref=dst,
            send_sem=self.sends.at[self.used],
            recv_sem=recv_sem,
            device_id=device,
            device_id_type=MESH,
        )
        (pl.when(when) if when is not None else call)(copy.start)
        self.used += 1
        self.open.append((copy, when))

    def finish(self):
        for copy, when in self.open:
            (pl.when(when) if when is not None else call)(copy.wait_send)


def call(f):
    return f()


def arrived(ref, sem):
    pltpu.make_async_copy(ref, ref, sem).wait()


def greet(devices):
    barrier = pltpu.get_barrier_semaphore()
    for device in devices:
        pl.semaphore_signal(barrier, inc=1, device_id=device, device_id_type=MESH)
    pl.semaphore_wait(barrier, len(devices))


class Place:
    def __init__(self, ndp, nh):
        self.ndp, self.nh, self.nchip = ndp, nh, ndp // 2
        self.dp = lax.axis_index("dp")
        self.z = lax.axis_index("head")
        self.core = self.dp % 2
        self.chip = self.dp // 2
        self.group_core = self.z % 2
        self.part = 2 * (self.z // 2) + self.core

    def of_part(self, part):
        return (self.chip * 2 + part % 2, 2 * (part // 2) + self.group_core)

    def core_peer(self):
        return (self.chip * 2 + 1 - self.core, self.z)

    def swap_peer(self):
        return (self.chip * 2 + 1 - self.core, self.part)

    def x_chip(self):
        return self.chip + 1 - 2 * (self.chip % 2)

    def y_chip(self):
        return (self.chip + 2) % 4


def gather_kernel(ndp, nh, spd, own, frames, ograd, bucket, batch, utts, conv, full, frames_o, ograd_o, ints_o, conv_o, ints, sends, recvs, extra, isem, local):
    me = Place(ndp, nh)
    dp, z, core, chip, nchip = me.dp, me.z, me.core, me.chip, me.nchip

    def shard(h, ch, c):
        return full.at[h, pl.ds((ch * 2 + c) * spd, spd)]

    def sem(h, ch, c, half=0):
        return recvs.at[h * ndp + ch * 2 + c, half]

    peer = me.core_peer()
    swap = me.core != me.z % 2
    columns = [(dp, (z + i) % nh) for i in range(1, nh)]
    square = nchip == 4
    if square:
        planes = [(me.x_chip() * 2 + core, z), (me.y_chip() * 2 + core, z)]
    else:
        planes = [(((chip + i) % nchip) * 2 + core, z) for i in range(1, nchip)]
    ints[...] = jnp.zeros_like(ints)
    ints[0:1, 0:1] = bucket[...]
    ints[0:1, 1:2] = batch[...]
    ints[0:1, 2:10] = utts[...]
    barrier = pltpu.get_barrier_semaphore()
    near = totals_peers(me)
    for device in near:
        pl.semaphore_signal(barrier, inc=1, device_id=device, device_id_type=MESH)

    @pl.when(swap)
    def _():
        pl.semaphore_signal(barrier, inc=1, device_id=me.swap_peer(), device_id_type=MESH)

    pl.semaphore_wait(barrier, len(near) + (core + z) % 2)

    copies = Copies(sends)
    mine = shard(z, chip, core)
    below, above = (dp, (z + nh - 1) % nh), (dp, (z + 1) % nh)
    copies.send(own, mine, sem(z, chip, core), above, z < nh - 1)
    copies.send(own, mine, sem(z, chip, core), below, z > 0)
    for device in planes:
        copies.send(own, mine, sem(z, chip, core), device)
    copies.send(own, mine, sem(z, chip, core), peer)
    keep = [
        pltpu.make_async_copy(own, mine, local.at[0]),
        pltpu.make_async_copy(ints, ints_o.at[dp], local.at[1]),
        pltpu.make_async_copy(conv, conv_o.at[z], local.at[2]),
    ]
    for copy in keep:
        copy.start()

    @pl.when(jnp.logical_not(swap))
    def _():
        for k, (src, dst) in enumerate(((frames, frames_o), (ograd, ograd_o))):
            pltpu.make_async_copy(src, dst, local.at[3 + k]).start()

    def column(step, up):
        h = z - step if up else z + step
        there = z >= step if up else z + step < nh
        onward = z < nh - 1 if up else z > 0
        h = jnp.where(there, h, z)
        s, r = shard(h, chip, core), sem(h, chip, core)

        @pl.when(there)
        def _():
            arrived(s, r)

        if step < nh - 1:
            copies.send(s, s, r, above if up else below, jnp.logical_and(there, onward))
        for device in planes:
            copies.send(s, s, r, device, there)
        copies.send(s, s, r, peer, there)

    def beside(step, up):
        h = z - step if up else z + step
        there = z >= step if up else z + step < nh
        h = jnp.where(there, h, z)
        if not square:
            for k in range(1, nchip):
                ch = (chip + k) % nchip

                @pl.when(there)
                def _():
                    arrived(shard(h, ch, core), sem(h, ch, core))

                copies.send(shard(h, ch, core), shard(h, ch, core), sem(h, ch, core), peer, there)
            return
        half = spd // 2
        for side, (ch, device) in enumerate(((me.x_chip(), planes[1]), (me.y_chip(), planes[0]))):

            @pl.when(there)
            def _():
                arrived(shard(h, ch, core), sem(h, ch, core))

            piece = full.at[h, pl.ds((ch * 2 + core) * spd + side * half, half)]
            copies.send(piece, piece, sem(h, ch, core, side), device, there)
            copies.send(shard(h, ch, core), shard(h, ch, core), sem(h, ch, core), peer, there)

    def across(step, up):
        if not square:
            return
        h = z - step if up else z + step
        there = z >= step if up else z + step < nh
        h = jnp.where(there, h, z)
        half = spd // 2
        ch = 3 - chip

        @pl.when(there)
        def _():
            for side in range(2):
                piece = full.at[h, pl.ds((ch * 2 + core) * spd + side * half, half)]
                arrived(piece, sem(h, ch, core, side))

        copies.send(shard(h, ch, core), shard(h, ch, core), sem(h, ch, core), peer, there)

    visits = [(0, True)] + [(step, up) for step in range(1, nh) for up in (True, False)]
    lag = 2
    for i in range(len(visits) + 2 * lag):
        if 0 < i < len(visits):
            column(*visits[i])
        if i == len(visits) - 1:
            for device in columns:
                copies.send(conv, conv_o.at[z], extra.at[3 + z], device)
            for k in range(1, ndp):
                copies.send(ints, ints_o.at[dp], isem.at[dp], ((dp + k) % ndp, z))

            @pl.when(swap)
            def _():
                for k, (src, dst) in enumerate(((frames, frames_o), (ograd, ograd_o))):
                    pltpu.make_async_remote_copy(
                        src_ref=src, dst_ref=dst, send_sem=local.at[3 + k], recv_sem=extra.at[1 + k],
                        device_id=me.swap_peer(), device_id_type=MESH,
                    ).start()

        if 0 <= i - lag < len(visits):
            beside(*visits[i - lag])
        if i >= 2 * lag:
            across(*visits[i - 2 * lag])
    for i in range(nh):
        h = (z + nh - i) % nh
        for k in range(nchip):
            ch = (chip + k) % nchip
            arrived(shard(h, ch, 1 - core), sem(h, ch, 1 - core))
    for k in range(1, ndp):
        arrived(ints_o.at[(dp + k) % ndp], isem.at[(dp + k) % ndp])
    for i in range(1, nh):
        h = (z + nh - i) % nh
        arrived(conv_o.at[h], extra.at[3 + h])

    @pl.when(swap)
    def _():
        arrived(frames_o, extra.at[1])
        arrived(ograd_o, extra.at[2])

    for i, ref in enumerate((frames, ograd)):
        arrived(ref, local.at[3 + i])
    for copy in keep:
        copy.wait()
    copies.finish()


def gather(ndp, nh, own, frames, ograd, bucket, batch, utts, conv):
    spd = own.shape[0]
    nchip = ndp // 2
    plane = 2 if nchip == 4 else nchip - 1
    visits = 2 * nh - 1
    halves = 2 * visits if nchip == 4 else 0
    count = 2 * visits + visits * (plane + 1) + visits * (nchip - 1) + halves + (ndp - 1) + (nh - 1)
    shapes = [
        jax.ShapeDtypeStruct((big(nh, ndp * spd), ndp * spd, BLOCKW, D), BF16),
        jax.ShapeDtypeStruct(frames.shape, BF16),
        jax.ShapeDtypeStruct(ograd.shape, BF16),
        jax.ShapeDtypeStruct((ndp, 8, 128), jnp.int32),
        jax.ShapeDtypeStruct((nh,) + conv.shape, F32),
    ]
    dma = pltpu.SemaphoreType.DMA
    return pl.pallas_call(
        functools.partial(gather_kernel, ndp, nh, spd),
        out_shape=shapes,
        in_specs=[ANY, HBM, HBM, VM, VM, VM, ANY],
        out_specs=[HBM] * 3 + [ANY] * 2,
        scratch_shapes=[
            pltpu.VMEM((8, 128), jnp.int32),
            dma((count,)),
            dma((nh * ndp, 2)),
            dma((3 + nh,)),
            dma((ndp,)),
            dma((5,)),
        ],
        compiler_params=params(52, 1),
        cost_estimate=cost(60),
        name="gather",
    )(own, frames, ograd, bucket, batch, utts, conv)


def totals_step(me, small, first, second, copies, sem1, sem2, local):
    ndp, nh = me.ndp, me.nh

    def one():
        for i in range(1, ndp):
            copies.send(small, first.at[me.dp], sem1.at[me.dp], ((me.dp + i) % ndp, me.z))
        first[me.dp] = small[...]

    def two():
        for i in range(1, ndp):
            src = (me.dp + i) % ndp
            arrived(first.at[src], sem1.at[src])
        total = first[0]
        for i in range(1, ndp):
            total = total + first[i]
        second[me.z] = total
        for i in range(1, nh):
            copies.send(second.at[me.z], second.at[me.z], sem2.at[me.z], (me.dp, (me.z + i) % nh))

    def three():
        for i in range(1, nh):
            src = (me.z + i) % nh
            arrived(second.at[src], sem2.at[src])
        total = second[0]
        for i in range(1, nh):
            total = total + second[i]
        return total

    return one, two, three


def totals_peers(me):
    return [((me.dp + i) % me.ndp, me.z) for i in range(1, me.ndp)] + [
        (me.dp, (me.z + i) % me.nh) for i in range(1, me.nh)
    ]


def totals_kernel(ndp, nh, halos, *refs):
    me = Place(ndp, nh)
    small = refs[0]
    edges = refs[1 : 1 + halos]
    out = refs[1 + halos]
    edges_o = refs[2 + halos : 2 + 2 * halos]
    first, second, sends, sem1, sem2, hsem = refs[2 + 2 * halos :]
    greet(totals_peers(me))
    copies = Copies(sends)
    one, two, three = totals_step(me, small, first, second, copies, sem1, sem2, None)
    one()
    for i in range(halos):
        send_edges(me, edges[i], edges_o[i], copies, hsem.at[2 * i], hsem.at[2 * i + 1])
    two()
    out[...] = three()
    for i in range(halos):
        arrived(edges_o[i].at[pl.ds(0, HALO)], hsem.at[2 * i])
        arrived(edges_o[i].at[pl.ds(HALO, HALO)], hsem.at[2 * i + 1])
    copies.finish()


def window(me, rows):
    span = LONGEST // rows
    at = me.part % span
    return span, at, me.part - at


def send_edges(me, src, dst, copies, sem_before, sem_after):
    rows = src.shape[0]
    span, at, base = window(me, rows)
    after = me.of_part(base + (at + 1) % span)
    before = me.of_part(base + (at + span - 1) % span)
    copies.send(src.at[pl.ds(rows - HALO, HALO)], dst.at[pl.ds(0, HALO)], sem_before, after)
    copies.send(src.at[pl.ds(0, HALO)], dst.at[pl.ds(HALO, HALO)], sem_after, before)


def totals(ndp, nh, collective_id, small, edges=()):
    dma = pltpu.SemaphoreType.DMA
    n = len(edges)
    halo = [jax.ShapeDtypeStruct((2 * HALO, D), e.dtype) for e in edges]
    return pl.pallas_call(
        functools.partial(totals_kernel, ndp, nh, n),
        out_shape=[jax.ShapeDtypeStruct(small.shape, F32)] + halo,
        in_specs=[VM] + [ANY] * n,
        out_specs=[VM] + [ANY] * n,
        scratch_shapes=[
            pltpu.VMEM((ndp,) + small.shape, F32),
            pltpu.VMEM((nh,) + small.shape, F32),
            dma((ndp + nh - 2 + 2 * n,)),
            dma((ndp,)),
            dma((nh,)),
            dma((2 * n + 1,)),
        ],
        compiler_params=params(16, collective_id),
        cost_estimate=cost(8),
        name=f"totals_{collective_id}",
    )(small, *edges)


def keys_kernel(ndp, nh, kv, q, x1, kv_o, q_o, x1_o, sends, recvs, local):
    me = Place(ndp, nh)
    rows = kv.shape[0]
    span, at, base = window(me, rows)
    peers = [me.of_part(base + (at + i) % span) for i in range(1, span)]
    greet(peers)
    copies = Copies(sends)
    place = kv_o.at[pl.ds(at * rows, rows)]
    for device in peers:
        copies.send(kv, place, recvs.at[at], device)
    own = pltpu.make_async_copy(kv, place, local.at[0])
    own.start()
    for i, (src, dst) in enumerate(((q, q_o), (x1, x1_o))):
        send_edges(me, src, dst, copies, recvs.at[span + 2 * i], recvs.at[span + 2 * i + 1])
    for i in range(1, span):
        other = (at + i) % span
        arrived(kv_o.at[pl.ds(other * rows, rows)], recvs.at[other])
    for i, dst in enumerate((q_o, x1_o)):
        arrived(dst.at[pl.ds(0, HALO)], recvs.at[span + 2 * i])
        arrived(dst.at[pl.ds(HALO, HALO)], recvs.at[span + 2 * i + 1])
    own.wait()
    copies.finish()


def keys(ndp, nh, kv, q, x1):
    span = LONGEST // kv.shape[0]
    dma = pltpu.SemaphoreType.DMA
    return pl.pallas_call(
        functools.partial(keys_kernel, ndp, nh),
        out_shape=[
            jax.ShapeDtypeStruct((LONGEST, 2 * D), BF16),
            jax.ShapeDtypeStruct((2 * HALO, D), BF16),
            jax.ShapeDtypeStruct((2 * HALO, D), F32),
        ],
        in_specs=[ANY] * 3,
        out_specs=[ANY] * 3,
        scratch_shapes=[dma((span + 3,)), dma((span + 4,)), dma((1,))],
        compiler_params=params(8, 2),
        cost_estimate=cost(3),
        name="keys",
    )(kv, q, x1)


def key_grads_kernel(ndp, nh, part, out, sends, recvs):
    me = Place(ndp, nh)
    rows = out.shape[1]
    span, at, base = window(me, rows)
    greet([me.of_part(base + (at + i) % span) for i in range(1, span)])
    copies = Copies(sends)
    for i in range(1, span):
        other = (at + i) % span
        copies.send(part.at[pl.ds(other * rows, rows)], out.at[i - 1], recvs.at[i - 1], me.of_part(base + other))
    for i in range(1, span):
        arrived(out.at[i - 1], recvs.at[i - 1])
    copies.finish()


def key_grads(ndp, nh, part, rows):
    span = LONGEST // rows
    dma = pltpu.SemaphoreType.DMA
    return pl.pallas_call(
        functools.partial(key_grads_kernel, ndp, nh),
        out_shape=jax.ShapeDtypeStruct((span - 1, rows, 2 * D), BF16),
        in_specs=[ANY],
        out_specs=ANY,
        scratch_shapes=[dma((span - 1,)), dma((span - 1,))],
        compiler_params=params(8, 5),
        cost_estimate=cost(3),
        name="key_grads",
    )(part)


def far_first(z, nh):
    orders = [sorted(range(nh), key=lambda h: (-abs(h - at), h)) for at in range(nh)]
    return [sum((orders[at][i] * (z == at).astype(jnp.int32) for at in range(nh)), 0) for i in range(nh)]


def scatter_kernel(ndp, nh, spd, grads, small, out_v, fgrad_v, owned, small_o, out_o, fgrad_o, part, cores, side_x, side_y, half_x, half_y, zrecv, first, second, sends, csem, psem, xsem, zsem, sem1, sem2, esem, local):
    me = Place(ndp, nh)
    dp, z, core, chip, nchip = me.dp, me.z, me.core, me.chip, me.nchip
    square = nchip == 4
    peer = me.core_peer()
    swap = me.core != me.z % 2
    half = spd // 2
    barrier = pltpu.get_barrier_semaphore()
    near = totals_peers(me)
    for device in near:
        pl.semaphore_signal(barrier, inc=1, device_id=device, device_id_type=MESH)

    @pl.when(swap)
    def _():
        pl.semaphore_signal(barrier, inc=1, device_id=me.swap_peer(), device_id_type=MESH)

    pl.semaphore_wait(barrier, len(near) + (core + z) % 2)
    copies = Copies(sends)
    order = far_first(z, nh)
    if square:
        chips = [3 - chip, me.x_chip(), me.y_chip(), chip]
    else:
        chips = [(chip + i + 1) % nchip for i in range(nchip)]
    loads = {}

    def begin(i):
        for k, ch in enumerate(chips):
            copies.send(grads.at[order[i], pl.ds((ch * 2 + 1 - core) * spd, spd)], cores.at[i, k], csem.at[i, k], peer)
            load = pltpu.make_async_copy(
                grads.at[order[i], pl.ds((ch * 2 + core) * spd, spd)], part.at[i, k], psem.at[i, k]
            )
            load.start()
            loads[i, k] = load

    begin(0)
    one, two, three = totals_step(me, small, first, second, copies, sem1, sem2, None)
    one()

    @pl.when(swap)
    def _():
        for i, (src, dst) in enumerate(((out_v, out_o), (fgrad_v, fgrad_o))):
            pltpu.make_async_remote_copy(
                src_ref=src, dst_ref=dst, send_sem=local.at[i], recv_sem=esem.at[i],
                device_id=me.swap_peer(), device_id_type=MESH,
            ).start()

    @pl.when(jnp.logical_not(swap))
    def _():
        for i, (src, dst) in enumerate(((out_v, out_o), (fgrad_v, fgrad_o))):
            pltpu.make_async_copy(src, dst, local.at[i]).start()

    def add(i, k, others, lo=0, n=spd):
        @pl.loop(0, n, unroll=True)
        def _(s):
            total = part[i, k, lo + s].astype(F32)
            for other in others:
                total = total + other(s).astype(F32)
            part[i, k, lo + s] = total.astype(BF16)

    def meet(i, k):
        loads[i, k].wait()
        arrived(cores.at[i, k], csem.at[i, k])

    planes = [(me.x_chip() * 2 + core, z), (me.y_chip() * 2 + core, z)]

    def stage_a(i):
        if square:
            meet(i, 0)
            add(i, 0, [lambda s: cores[i, 0, s]])
            copies.send(part.at[i, 0, pl.ds(0, half)], half_x.at[i], xsem.at[i, 0], planes[0])
            copies.send(part.at[i, 0, pl.ds(half, half)], half_y.at[i], xsem.at[i, 1], planes[1])
        else:
            for k in range(nchip - 1):
                meet(i, k)
                add(i, k, [lambda s: cores[i, k, s]])
                copies.send(part.at[i, k], side_x.at[i, k], xsem.at[i, k], (chips[k] * 2 + core, z))

    def stage_b(i):
        if not square:
            return
        meet(i, 1)
        add(i, 1, [lambda s: cores[i, 1, s]], 0, half)
        arrived(half_y.at[i], xsem.at[i, 1])
        add(i, 1, [lambda s: cores[i, 1, half + s], lambda s: half_y[i, s]], half, half)
        copies.send(part.at[i, 1], side_x.at[i, 0], xsem.at[i, 2], planes[0])
        meet(i, 2)
        add(i, 2, [lambda s: cores[i, 2, half + s]], half, half)
        arrived(half_x.at[i], xsem.at[i, 0])
        add(i, 2, [lambda s: cores[i, 2, s], lambda s: half_x[i, s]], 0, half)
        copies.send(part.at[i, 2], side_y.at[i], xsem.at[i, 3], planes[1])

    last = nchip - 1

    def stage_c(i):
        meet(i, last)
        if square:
            arrived(side_x.at[i, 0], xsem.at[i, 2])
            arrived(side_y.at[i], xsem.at[i, 3])
            others = [lambda s: cores[i, last, s], lambda s: side_x[i, 0, s], lambda s: side_y[i, s]]
        else:
            others = [lambda s: cores[i, last, s]]
            for k in range(nchip - 1):
                arrived(side_x.at[i, k], xsem.at[i, k])
                others.append(lambda s, k=k: side_x[i, k, s])
        add(i, last, others)
        if i < nh - 1:
            copies.send(part.at[i, last], zrecv.at[z], zsem.at[z], (dp, order[i]))

    for i in range(nh + 2):
        if i + 1 < nh:
            begin(i + 1)
        if i < nh:
            stage_a(i)
        if 0 <= i - 1 < nh:
            stage_b(i - 1)
        if i == 1:
            two()
        if i >= 2:
            stage_c(i - 2)
    small_o[...] = three()
    sources = [(z + i) % nh for i in range(1, nh)]
    for src in sources:
        arrived(zrecv.at[src], zsem.at[src])

    @pl.loop(0, spd)
    def _(s):
        total = part[nh - 1, last, s].astype(F32)
        for src in sources:
            total = total + zrecv[src, s].astype(F32)
        owned[s] = total

    @pl.when(swap)
    def _():
        arrived(out_o, esem.at[0])
        arrived(fgrad_o, esem.at[1])

    arrived(out_v, local.at[0])
    arrived(fgrad_v, local.at[1])
    copies.finish()


def scatter(ndp, nh, grads, small, out_v, fgrad_v):
    spd = grads.shape[1] // ndp
    nchip = ndp // 2
    square = nchip == 4
    dma = pltpu.SemaphoreType.DMA
    block = (spd, BLOCKW, D)
    halfb = (max(spd // 2, 1), BLOCKW, D)
    sides = 1 if square else nchip - 1
    sent = nh * nchip + (ndp - 1) + (nh - 1) + (nh * 4 if square else nh * (nchip - 1)) + (nh - 1)
    return pl.pallas_call(
        functools.partial(scatter_kernel, ndp, nh, spd),
        out_shape=[
            jax.ShapeDtypeStruct(block, F32),
            jax.ShapeDtypeStruct(small.shape, F32),
            jax.ShapeDtypeStruct(out_v.shape, out_v.dtype),
            jax.ShapeDtypeStruct(fgrad_v.shape, fgrad_v.dtype),
        ],
        in_specs=[HBM, VM, HBM, HBM],
        out_specs=[VM, VM, HBM, HBM],
        scratch_shapes=[
            pltpu.VMEM((nh, nchip) + block, BF16),
            pltpu.VMEM((nh, nchip) + block, BF16),
            pltpu.VMEM((nh, sides) + block, BF16),
            pltpu.VMEM((nh,) + block, BF16),
            pltpu.VMEM((nh,) + halfb, BF16),
            pltpu.VMEM((nh,) + halfb, BF16),
            pltpu.VMEM((nh,) + block, BF16),
            pltpu.VMEM((ndp,) + small.shape, F32),
            pltpu.VMEM((nh,) + small.shape, F32),
            dma((sent,)),
            dma((nh, nchip)),
            dma((nh, nchip)),
            dma((nh, max(4, nchip))),
            dma((nh,)),
            dma((ndp,)),
            dma((nh,)),
            dma((2,)),
            dma((2,)),
        ],
        compiler_params=params(28, 6),
        cost_estimate=cost(65),
        name="scatter",
    )(grads, small, out_v, fgrad_v)


def nn(a, b):
    return jnp.dot(a, b, preferred_element_type=F32)


def nt(a, b):
    return lax.dot_general(a, b, (((1,), (1,)), ((), ())), preferred_element_type=F32)


def tn(a, b):
    return lax.dot_general(a, b, (((0,), (0,)), ((), ())), preferred_element_type=F32)


def sigmoid(v):
    return 0.5 * jnp.tanh(0.5 * v) + 0.5


def slope_of(v, sig):
    return sig * (1.0 + v * (1.0 - sig))


class Blocks:
    def __init__(self, nh):
        self.nh = nh
        ff, ch = FF // nh // BLOCKW, D // nh // BLOCKW
        self.ff, self.ch = ff, ch
        self.in_one, self.in_two = 0, ff
        self.query = 2 * ff
        self.key = self.query + ch
        self.value = self.key + ch
        self.conv_value = self.value + ch
        self.conv_gate = self.conv_value + ch
        rows = self.conv_gate + ch
        self.out_one, self.out_two = rows, rows + ff
        self.attn = rows + 2 * ff
        self.point = self.attn + ch
        self.total = self.point + ch


def fetch(full, inv, dst, sem, base, count, part, row):
    for j in range(count):
        pltpu.make_async_copy(
            full.at[part, inv[base + j]], dst.at[pl.ds(row + j * BLOCKW, BLOCKW)], sem
        ).start()


def fetch_all(full, inv, dst, sem, base, count, nh, row=0):
    for part in range(nh):
        fetch(full, inv, dst, sem, base, count, part, row + part * count * BLOCKW)


def landed(dst, sem):
    pltpu.make_async_copy(dst, dst, sem).wait()


def put(grads, inv, src, sem, base, count, part, row):
    for j in range(count):
        pltpu.make_async_copy(
            src.at[pl.ds(row + j * BLOCKW, BLOCKW)], grads.at[part, inv[base + j]], sem
        ).start()


def put_all(grads, inv, src, sem, base, count, nh, row=0):
    for part in range(nh):
        put(grads, inv, src, sem, base, count, part, row + part * count * BLOCKW)


def tables(meta, frame):
    length, batch = meta[0], meta[1]
    utterance = jnp.zeros_like(frame)
    for i in range(1, 8):
        utterance = utterance + (frame >= i * length).astype(jnp.int32)
    within = frame - utterance * length
    own = jnp.zeros_like(frame)
    for i in range(8):
        own = jnp.where(utterance == i, meta[2 + i], own)
    live = (utterance < batch) & (within < own)
    return utterance, within, live


def live_rows(meta, start, count):
    frame = start + lax.broadcasted_iota(jnp.int32, (count, 1), 0)
    return tables(meta, frame)[2].astype(F32)


def hat(x):
    center = jnp.mean(x, axis=1, keepdims=True)
    offset = x - center
    spread = lax.rsqrt(jnp.mean(offset * offset, axis=1, keepdims=True) + norm_eps)
    return offset * spread, spread


def norm(x, norms, i):
    return hat(x)[0] * norms[i : i + 1, :] + norms[i + 5 : i + 6, :]


def norm_back(x, grad, gain):
    return hat_back(*hat(x), grad, gain)


def hat_back(xhat, spread, grad, gain):
    scaled = grad * gain
    inner = scaled - jnp.mean(scaled, axis=1, keepdims=True) - xhat * jnp.mean(scaled * xhat, axis=1, keepdims=True)
    return spread * inner, jnp.sum(grad * xhat, axis=0, keepdims=True), jnp.sum(grad, axis=0, keepdims=True)


BAND = 64


def bands(rows, body, init=()):
    return lax.fori_loop(0, rows // BAND, lambda i, c: body(pl.ds(pl.multiple_of(i * BAND, BAND), BAND), i, c), init, unroll=True)


def partner(x):
    lane = lax.broadcasted_iota(jnp.int32, x.shape, 1) % HD
    return jnp.where(lane < HD // 2, pltpu.roll(x, 128 - HD // 2, 1), pltpu.roll(x, HD // 2, 1))


def turn(x, table, sign):
    first = lax.broadcasted_iota(jnp.int32, table.shape, 1) % HD < HD // 2
    cos = jnp.where(first, table, pltpu.roll(table, HD // 2, 1))
    sin = jnp.where(first, -pltpu.roll(table, 128 - HD // 2, 1), table)
    parts = []
    for i in range(D // 128):
        piece = x[:, i * 128 : (i + 1) * 128]
        parts.append(piece * cos + partner(piece) * (sign * sin))
    return jnp.concatenate(parts, axis=1)


def rope_table():
    freq = np.exp(np.arange(HD // 2, dtype=np.float32) * np.float32(-math.log(10000.0) / (HD // 2)))
    angle = np.arange(LONGEST, dtype=np.float32)[:, None] * freq[None, :].astype(np.float32)
    return np.tile(np.concatenate([np.cos(angle), np.sin(angle)], axis=1), (1, 2)).astype(np.float32)


def place_of(meta, i):
    return pl.multiple_of(lax.rem(meta[10] + i * BAND, meta[0]), BAND)


def feed(n_ref, w_in, w_out, acc_ref, sem, sem2, nh):
    unit = FF // nh
    for part in range(nh):
        rows = pl.ds(part * unit, unit)
        landed(w_in.at[rows], sem.at[part])
        pre = nt(n_ref[...], w_in[rows, :])
        act = (pre * sigmoid(pre)).astype(BF16)
        landed(w_out.at[rows], sem2.at[part])
        if part == 0:
            acc_ref[...] = nn(act, w_out[rows, :])
        else:
            acc_ref[...] += nn(act, w_out[rows, :])


def feed_back(n_ref, gb_ref, w_in, w_out, acc_ref, g_in, g_out, grads, inv, base_in, base_out, sem_in, sem_out, count, nh):
    unit = FF // nh

    def body(part, carry):
        rows = pl.ds(pl.multiple_of(part * unit, unit), unit)
        n, gb, win, wout = n_ref[...], gb_ref[...], w_in[rows, :], w_out[rows, :]
        pre = nt(win, n)
        sig = sigmoid(pre)
        act = (pre * sig).astype(BF16)
        dpre = (nt(wout, gb) * slope_of(pre, sig)).astype(BF16)
        g_out[rows, :] = nn(act, gb).astype(BF16)
        g_in[rows, :] = nn(dpre, n).astype(BF16)
        acc_ref[...] += tn(dpre, win)
        put(grads, inv, g_out, sem_out, base_out, count, part, part * unit)
        put(grads, inv, g_in, sem_in, base_in, count, part, part * unit)
        return carry

    acc_ref[...] = jnp.zeros_like(acc_ref)
    lax.fori_loop(0, nh, body, 0, unroll=True)


def front_kernel(ndp, nh, owner, place, ints, conv, frames, norms, table, full, x1, q, kv, meta, inv, taps, w_in, w_out, w_qkv, n_ref, acc, groups, sem, sem2, sem3):
    b = Blocks(nh)
    known = pltpu.make_async_copy(ints, groups, sem3.at[1])
    known.start()

    def slot(i, c):
        inv[owner[i]] = i
        return c

    lax.fori_loop(0, owner.shape[0], slot, 0)
    rows = frames.shape[0]
    unit = FF // nh
    for part in range(nh):
        fetch(full, inv, w_in, sem.at[part], b.in_one, b.ff, part, part * unit)
        fetch(full, inv, w_out, sem2.at[part], b.out_one, b.ff, part, part * unit)
    for i, base in enumerate((b.query, b.key, b.value)):
        fetch_all(full, inv, w_qkv, sem3.at[0], base, b.ch, nh, i * D)

    def first(at, i, c):
        n_ref[at, :] = norm(frames[at, :].astype(F32), norms, 0).astype(BF16)
        return c

    bands(rows, first)
    known.wait()
    for i in range(16):
        meta[i] = groups[place[0], 0, i]
    meta[10] = place[1] * rows

    def count(d, total):
        for u in range(8):
            total += jnp.where(u < groups[d, 0, 1], jnp.minimum(groups[d, 0, 2 + u], groups[d, 0, 0]), 0)
        return total

    meta[11] = lax.fori_loop(0, ndp, count, 0)
    taps[...] = jnp.zeros_like(taps)
    width = conv.shape[2]
    for h in range(nh):
        taps[0 : KERNEL + 2, h * width : (h + 1) * width] = conv[h]
    feed(n_ref, w_in, w_out, acc, sem, sem2, nh)

    def second(at, i, c):
        x = frames[at, :].astype(F32) + 0.5 * acc[at, :]
        x1[at, :] = x
        n_ref[at, :] = norm(x, norms, 1).astype(BF16)
        return c

    bands(rows, second)
    landed(w_qkv, sem3.at[0])
    for j, (dst, lo) in enumerate(((q, 0), (kv, 0), (kv, D))):
        acc[...] = nt(n_ref[...], w_qkv[j * D : (j + 1) * D, :])

        def third(at, i, c):
            x = acc[at, :]
            if j < 2:
                p = pl.ds(place_of(meta, i), BAND)
                x = turn(x, table[p, :], 1.0)
            dst[at, lo : lo + D] = x.astype(BF16)
            return c

        bands(rows, third)


def front(ndp, nh, owner, place, ints, conv, frames, norms, table, full):
    rows = frames.shape[0]
    dma = pltpu.SemaphoreType.DMA
    return pl.pallas_call(
        functools.partial(front_kernel, ndp, nh),
        out_shape=[
            jax.ShapeDtypeStruct((rows, D), F32),
            jax.ShapeDtypeStruct((rows, D), BF16),
            jax.ShapeDtypeStruct((rows, 2 * D), BF16),
            jax.ShapeDtypeStruct((16,), jnp.int32),
            jax.ShapeDtypeStruct(owner.shape, jnp.int32),
            jax.ShapeDtypeStruct((40, D), F32),
        ],
        in_specs=[SM, SM, ANY, VM, VM, VM, VM, HBM],
        out_specs=[VM, VM, VM, SM, SM, VM],
        scratch_shapes=[
            pltpu.VMEM((FF, D), BF16),
            pltpu.VMEM((FF, D), BF16),
            pltpu.VMEM((3 * D, D), BF16),
            pltpu.VMEM((rows, D), BF16),
            pltpu.VMEM((rows, D), F32),
            pltpu.SMEM((ndp, 8, 128), jnp.int32),
            dma((nh,)),
            dma((nh,)),
            dma((2,)),
        ],
        compiler_params=params(18),
        cost_estimate=cost(7),
        name="front",
    )(owner, place, ints, conv, frames, norms, table, full)


def fill_chunk(meta, src, chunk, k, start):
    lead = lax.rem(start + k * 256, meta[0]) != 0
    trail = lax.rem(start + (k + 1) * 256, meta[0]) != 0
    chunk[0:HALO, :] = jnp.where(lead, src[k * 256 : k * 256 + HALO, :], 0.0)
    chunk[HALO : HALO + 256, :] = src[k * 256 + HALO : k * 256 + HALO + 256, :]
    chunk[HALO + 256 :, :] = jnp.where(trail, src[k * 256 + HALO + 256 : k * 256 + 2 * HALO + 256, :], 0.0)


def shift_rows(chunk, moved):
    rows = chunk.shape[0]
    moved[0] = chunk[...]
    for b in range(1, 8):
        moved[b, 0 : rows - 8, :] = chunk[b : b + rows - 8, :]


def attend_kernel(nh, meta, inv, q, kvw, x1, qh, x1h, norms, taps, full, o_o, lse_o, x2_o, gated_o, h_o, sums_o, n_ref, val, sig, w_attn, w_glu, q_ext, o_ext, x_ext, bias, chunk, moved, lse_s, sem):
    b = Blocks(nh)
    rows = q.shape[0]
    ext = rows + 2 * HALO
    start = meta[10]
    fetch_all(full, inv, w_attn, sem.at[0], b.attn, b.ch, nh)
    for i, base in enumerate((b.conv_value, b.conv_gate)):
        fetch_all(full, inv, w_glu, sem.at[1], base, b.ch, nh, i * D)
    q_ext[0:HALO, :] = qh[0:HALO, :]
    q_ext[HALO : HALO + rows, :] = q[...]
    q_ext[HALO + rows :, :] = qh[HALO:, :]
    x_ext[0:HALO, :] = x1h[0:HALO, :]
    x_ext[HALO : HALO + rows, :] = x1[...]
    x_ext[HALO + rows :, :] = x1h[HALO:, :]
    base = start - lax.rem(start, LONGEST)
    key_frame = base + lax.broadcasted_iota(jnp.int32, (1, LONGEST), 1)
    ukey, _, lkey = tables(meta, key_frame)
    ukey = jnp.where(lkey, ukey, -1)
    query_frame = start - HALO + lax.broadcasted_iota(jnp.int32, (ext, 1), 0)
    uquery, _, lquery = tables(meta, query_frame)
    live = lquery.astype(F32)
    bias[...] = jnp.where(ukey == uquery, 0.0, masked_score)
    half = ext // 2
    head_lane = lax.broadcasted_iota(jnp.int32, (half, 128), 1)

    for pair in range(D // 128):
        lanes = slice(pair * 128, (pair + 1) * 128)
        kp = kvw[:, lanes]
        vp = kvw[:, D + pair * 128 : D + (pair + 1) * 128]
        for blk in range(2):
            at = slice(blk * half, (blk + 1) * half)
            qp = q_ext[at, lanes] * 0.125
            outs = []
            for hh in range(2):
                mine = head_lane < HD if hh == 0 else head_lane >= HD
                qm = jnp.where(mine, qp, jnp.zeros_like(qp))
                s = nt(qm, kp) + bias[at, :]
                top = jnp.max(s, axis=1, keepdims=True)
                e = jnp.exp(s - top)
                total = jnp.sum(e, axis=1, keepdims=True)
                outs.append(nn(e.astype(BF16), vp) * (1.0 / total))
                lse_s[at, pair * 2 + hh : pair * 2 + hh + 1] = top + jnp.log(total)
            o = jnp.where(head_lane < HD, outs[0], outs[1]) * live[at, :]
            o_ext[at, lanes] = o.astype(BF16)
    o_o[...] = o_ext[HALO : HALO + rows, :]
    lse_o[...] = jnp.transpose(lse_s[HALO : HALO + rows, :])[0:8, :]
    landed(w_attn, sem.at[0])
    x_ext[...] += nn(o_ext[...], w_attn[...])
    x2_o[...] = x_ext[HALO : HALO + rows, :]

    def third(i, c):
        at = pl.ds(pl.multiple_of(i * 32, 32), 32)
        n_ref[at, :] = norm(x_ext[at, :], norms, 2).astype(BF16)
        return c

    lax.fori_loop(0, ext // 32, third, 0, unroll=True)
    landed(w_glu, sem.at[1])
    val[...] = nt(n_ref[...], w_glu[0:D, :])
    sig[...] = sigmoid(nt(n_ref[...], w_glu[D:, :]))
    gated_o[...] = val[...] * sig[...] * live
    sums = [[0.0] * (D // 128) for _ in range(2)]
    for k in range(rows // 256):
        fill_chunk(meta, gated_o, chunk, k, start)
        alive = live[HALO + k * 256 : HALO + (k + 1) * 256, :]
        shift_rows(chunk, moved)
        for lc in range(D // 128):
            lanes = slice(lc * 128, (lc + 1) * 128)
            acc = moved[0, 0:256, lanes] * taps[0:1, lanes]
            for j in range(1, KERNEL):
                lo = j - j % 8
                acc = acc + moved[j % 8, lo : lo + 256, lanes] * taps[j : j + 1, lanes]
            h_o[k * 256 : (k + 1) * 256, lanes] = acc
            weighted = acc * alive
            sums[0][lc] += jnp.sum(weighted, axis=0, keepdims=True)
            sums[1][lc] += jnp.sum(weighted * acc, axis=0, keepdims=True)
    sums_o[...] = jnp.concatenate(sums[0] + sums[1], axis=0)


def attend(nh, meta, inv, q, kvw, x1, qh, x1h, norms, taps, full):
    rows = q.shape[0]
    ext = rows + 2 * HALO
    dma = pltpu.SemaphoreType.DMA
    f = jax.ShapeDtypeStruct
    return pl.pallas_call(
        functools.partial(attend_kernel, nh),
        out_shape=[
            f((rows, D), BF16),
            f((8, rows), F32),
            f((rows, D), F32),
            f((ext, D), F32),
            f((rows, D), F32),
            f((2 * D // 128, 128), F32),
            f((ext, D), BF16),
            f((ext, D), F32),
            f((ext, D), F32),
        ],
        in_specs=[SM, SM] + [VM] * 7 + [HBM],
        out_specs=[VM] * 9,
        scratch_shapes=[
            pltpu.VMEM((D, D), BF16),
            pltpu.VMEM((2 * D, D), BF16),
            pltpu.VMEM((ext, D), BF16),
            pltpu.VMEM((ext, D), BF16),
            pltpu.VMEM((ext, D), F32),
            pltpu.VMEM((ext, LONGEST), F32),
            pltpu.VMEM((256 + 2 * HALO, D), F32),
            pltpu.VMEM((8, 256 + 2 * HALO, D), F32),
            pltpu.VMEM((ext, 128), F32),
            dma((2,)),
        ],
        compiler_params=params(34),
        cost_estimate=cost(13),
        name="attend",
    )(meta, inv, q, kvw, x1, qh, x1h, norms, taps, full)


def compact(rows_of):
    pieces = [r[:, i * 128 : (i + 1) * 128] for r in rows_of for i in range(D // 128)]
    return jnp.concatenate(pieces, axis=0)


def spread(packed, row):
    n = D // 128
    return jnp.concatenate([packed[row * n + i : row * n + i + 1, :] for i in range(n)], axis=1)


def bn_terms(meta, packed):
    count = jnp.full((1, 1), meta[11], jnp.int32).astype(F32)
    stats = [spread(packed, 0), spread(packed, 1)]
    center = stats[0] / count
    inv_std = lax.rsqrt(stats[1] / count - center * center + norm_eps)
    return count, center, inv_std


def middle_kernel(nh, meta, inv, x2, h, stats, ograd, norms, taps, full, out_o, g3_o, gz_o, sums_o, ng_o, grads, w_in, w_out, w_pt, n_ref, gb, y3, x3, x4, acc, g_in, g_out, g_pt, sem, sem2, sem3, gsem):
    b = Blocks(nh)
    rows = x2.shape[0]
    unit = FF // nh
    fetch_all(full, inv, w_pt, sem3.at[0], b.point, b.ch, nh)
    for part in range(nh):
        fetch(full, inv, w_in, sem.at[part], b.in_two, b.ff, part, part * unit)
        fetch(full, inv, w_out, sem2.at[part], b.out_two, b.ff, part, part * unit)
    count, center, inv_std = bn_terms(meta, stats)
    gain, shift = taps[KERNEL : KERNEL + 1, :], taps[KERNEL + 1 : KERNEL + 2, :]

    def z_of(at):
        return (h[at, :] - center) * inv_std * gain + shift

    def first(at, i, c):
        z = z_of(at)
        y3[at, :] = (z * sigmoid(z)).astype(BF16)
        return c

    bands(rows, first)
    landed(w_pt, sem3.at[0])
    x3[...] = x2[...] + nn(y3[...], w_pt[...])

    def second(at, i, c):
        n_ref[at, :] = norm(x3[at, :], norms, 3).astype(BF16)
        return c

    bands(rows, second)
    feed(n_ref, w_in, w_out, acc, sem, sem2, nh)
    zero = jnp.zeros((1, D), F32)

    def last(at, i, c):
        x = x3[at, :] + 0.5 * acc[at, :]
        xhat, spread = hat(x)
        out_o[at, :] = (xhat * norms[4:5, :] + norms[9:10, :]).astype(BF16)
        dx, dg, db = hat_back(xhat, spread, ograd[at, :].astype(F32), norms[4:5, :])
        x4[at, :] = dx
        gb[at, :] = (0.5 * dx).astype(BF16)
        return c[0] + dg, c[1] + db

    gain4, shift4 = bands(rows, last, (zero, zero))
    feed_back(n_ref, gb, w_in, w_out, acc, g_in, g_out, grads, inv, b.in_two, b.out_two, gsem.at[0], gsem.at[1], b.ff, nh)

    def back(at, i, c):
        dx, dg, db = norm_back(x3[at, :], acc[at, :], norms[3:4, :])
        g3 = x4[at, :] + dx
        g3_o[at, :] = g3
        gb[at, :] = g3.astype(BF16)
        return c[0] + dg, c[1] + db

    gain3, shift3 = bands(rows, back, (zero, zero))
    ng_o[...] = jnp.zeros_like(ng_o)
    ng_o[3:4, :] = gain3
    ng_o[4:5, :] = gain4
    ng_o[8:9, :] = shift3
    ng_o[9:10, :] = shift4
    acc[...] = nt(gb[...], w_pt[...])
    g_pt[...] = tn(y3[...], gb[...]).astype(BF16)
    put_all(grads, inv, g_pt, gsem.at[2], b.point, b.ch, nh)

    def gz_part(at, i, c):
        white = (h[at, :] - center) * inv_std
        z = white * gain + shift
        gz = acc[at, :] * slope_of(z, sigmoid(z))
        gz_o[at, :] = gz
        return c[0] + jnp.sum(gz, axis=0, keepdims=True), c[1] + jnp.sum(gz * white, axis=0, keepdims=True)

    sg, sx = bands(rows, gz_part, (zero, zero))
    sums_o[...] = compact([sg, sx])
    y3[0:BLOCKW, :] = jnp.zeros((BLOCKW, D), BF16)
    empty = [(i, part) for i in range(b.total, grads.shape[1]) for part in range(nh)]
    for k, (i, part) in enumerate(empty):
        put(grads, inv, y3, gsem.at[3 + k], i, 1, part, 0)
    landed(g_in, gsem.at[0])
    landed(g_out, gsem.at[1])
    landed(g_pt, gsem.at[2])
    for k in range(len(empty)):
        landed(y3.at[pl.ds(0, BLOCKW)], gsem.at[3 + k])


def middle(nh, meta, inv, x2, h, stats, ograd, norms, taps, full):
    rows = x2.shape[0]
    slots = full.shape[1]
    zeros = (slots - Blocks(nh).total) * nh
    dma = pltpu.SemaphoreType.DMA
    f = jax.ShapeDtypeStruct
    v = pltpu.VMEM
    return pl.pallas_call(
        functools.partial(middle_kernel, nh),
        out_shape=[
            f((rows, D), BF16),
            f((rows, D), F32),
            f((rows, D), F32),
            f((2 * D // 128, 128), F32),
            f((16, D), F32),
            f((big(nh, slots), slots, BLOCKW, D), BF16),
        ],
        in_specs=[SM, SM] + [VM] * 6 + [HBM],
        out_specs=[VM] * 5 + [HBM],
        scratch_shapes=[
            v((FF, D), BF16),
            v((FF, D), BF16),
            v((D, D), BF16),
            v((rows, D), BF16),
            v((rows, D), BF16),
            v((rows, D), BF16),
            v((rows, D), F32),
            v((rows, D), F32),
            v((rows, D), F32),
            v((FF, D), BF16),
            v((FF, D), BF16),
            v((D, D), BF16),
            dma((nh,)),
            dma((nh,)),
            dma((1,)),
            dma((3 + zeros,)),
        ],
        compiler_params=params(26),
        cost_estimate=cost(17),
        name="middle",
    )(meta, inv, x2, h, stats, ograd, norms, taps, full)


def conv_back_kernel(nh, meta, inv, gz, gzh, h, hh, stats, bsums, gated, n3, val, sig, x2, g3, o, norms, taps, full, ng_in, grads_in, g2_o, do_o, taps_o, ng_o, grads, w_attn, w_glu, gb, dh, dgated, res, dglu, g_attn, g_glu, chunk, moved, tsum, sem, gsem):
    del grads_in
    b = Blocks(nh)
    rows = gz.shape[0]
    ext = rows + 2 * HALO
    start = meta[10]
    fetch_all(full, inv, w_attn, sem.at[0], b.attn, b.ch, nh)
    for i, base in enumerate((b.conv_value, b.conv_gate)):
        fetch_all(full, inv, w_glu, sem.at[1], base, b.ch, nh, i * D)
    count, center, inv_std = bn_terms(meta, stats)
    gain = taps[KERNEL : KERNEL + 1, :]
    sg, sx = spread(bsums, 0), spread(bsums, 1)

    def dh_of(gz_rows, h_rows, first):
        alive = live_rows(meta, first, gz_rows.shape[0])
        white = (h_rows - center) * inv_std
        return gain * inv_std * (gz_rows - alive / count * (sg + white * sx))

    def one(at, i, c):
        dh[pl.ds(pl.multiple_of(i * BAND + HALO, HALO), BAND), :] = dh_of(gz[at, :], h[at, :], start + i * BAND)
        return c

    bands(rows, one)
    dh[0:HALO, :] = dh_of(gzh[0:HALO, :], hh[0:HALO, :], start - HALO)
    dh[HALO + rows :, :] = dh_of(gzh[HALO:, :], hh[HALO:, :], start + rows)
    tsum[...] = jnp.zeros_like(tsum)
    for k in range(rows // 256):
        fill_chunk(meta, dh, chunk, k, start)
        shift_rows(chunk, moved)

        for i in range(4 * D // 128):
            lanes = slice(i // 4 * 128, i // 4 * 128 + 128)
            row = i % 4 * 64
            own = gated[row + HALO + k * 256 : row + HALO + k * 256 + 64, lanes]
            acc = jnp.zeros((64, 128), F32)
            for j in range(KERNEL):
                off = KERNEL - j
                there = moved[off % 8, row + off - off % 8 : row + off - off % 8 + 64, lanes]
                acc = acc + there * taps[j : j + 1, lanes]
                tsum[j, :, lanes] += jnp.sum((there * own).reshape(8, 8, 128), axis=0)
            dgated[row + k * 256 : row + k * 256 + 64, lanes] = acc
    taps_o[...] = jnp.sum(tsum[...], axis=1)

    def two(at, i, c):
        own = pl.ds(pl.multiple_of(i * BAND + HALO, HALO), BAND)
        s = sig[own, :]
        d = dgated[at, :] * live_rows(meta, start + i * BAND, BAND)
        dglu[at, 0:D] = (d * s).astype(BF16)
        dglu[at, D:] = (d * val[own, :] * s * (1.0 - s)).astype(BF16)
        return c

    bands(rows, two)
    g_glu[...] = tn(dglu[...], n3[HALO : HALO + rows, :]).astype(BF16)
    landed(w_glu, sem.at[1])
    for i, base in enumerate((b.conv_value, b.conv_gate)):
        put_all(grads, inv, g_glu, gsem.at[0], base, b.ch, nh, i * D)
    res[...] = nn(dglu[...], w_glu[...])
    zero = jnp.zeros((1, D), F32)

    def three(at, i, c):
        dx, dg, db = norm_back(x2[at, :], res[at, :], norms[2:3, :])
        g2 = g3[at, :] + dx
        g2_o[at, :] = g2
        gb[at, :] = g2.astype(BF16)
        return c[0] + dg, c[1] + db

    dgain, dshift = bands(rows, three, (zero, zero))
    ng_o[...] = ng_in[...]
    ng_o[2:3, :] = dgain
    ng_o[7:8, :] = dshift
    landed(w_attn, sem.at[0])
    res[...] = nt(gb[...], w_attn[...])
    g_attn[...] = tn(o[...], gb[...]).astype(BF16)
    put_all(grads, inv, g_attn, gsem.at[1], b.attn, b.ch, nh)

    def four(at, i, c):
        do_o[at, :] = (res[at, :] * live_rows(meta, start + i * BAND, BAND)).astype(BF16)
        return c

    bands(rows, four)
    landed(g_glu, gsem.at[0])
    landed(g_attn, gsem.at[1])


def conv_back(nh, meta, inv, gz, gzh, h, hh, stats, bsums, gated, n3, val, sig, x2, g3, o, norms, taps, full, ng, grads):
    rows = gz.shape[0]
    ext = rows + 2 * HALO
    dma = pltpu.SemaphoreType.DMA
    f = jax.ShapeDtypeStruct
    v = pltpu.VMEM
    return pl.pallas_call(
        functools.partial(conv_back_kernel, nh),
        out_shape=[
            f((rows, D), F32),
            f((rows, D), BF16),
            f((KERNEL, D), F32),
            f((16, D), F32),
            f(grads.shape, BF16),
        ],
        in_specs=[SM, SM] + [VM] * 15 + [HBM, VM, HBM],
        out_specs=[VM] * 4 + [HBM],
        input_output_aliases={19: 4},
        scratch_shapes=[
            v((D, D), BF16),
            v((2 * D, D), BF16),
            v((rows, D), BF16),
            v((ext, D), F32),
            v((rows, D), F32),
            v((rows, D), F32),
            v((rows, 2 * D), BF16),
            v((D, D), BF16),
            v((2 * D, D), BF16),
            v((256 + 2 * HALO, D), F32),
            v((8, 256 + 2 * HALO, D), F32),
            v((KERNEL, 8, D), F32),
            dma((2,)),
            dma((2,)),
        ],
        compiler_params=params(28),
        cost_estimate=cost(13),
        name="conv_back",
    )(meta, inv, gz, gzh, h, hh, stats, bsums, gated, n3, val, sig, x2, g3, o, norms, taps, full, ng, grads)


def attend_back_kernel(meta, q, kvw, do, lse, dq_o, dkv_o, send_o, bias, dkp, dvp):
    rows = q.shape[0]
    start = meta[10]
    base = start - lax.rem(start, LONGEST)
    offset = pl.multiple_of(lax.rem(start, LONGEST), rows)
    ukey, _, lkey = tables(meta, base + lax.broadcasted_iota(jnp.int32, (LONGEST, 1), 0))
    ukey = jnp.where(lkey, ukey, -1)
    uquery, _, _ = tables(meta, start + lax.broadcasted_iota(jnp.int32, (1, rows), 1))
    bias[...] = jnp.where(ukey == uquery, 0.0, masked_score)
    lane_q = lax.broadcasted_iota(jnp.int32, (rows, 128), 1)
    lane_k = lax.broadcasted_iota(jnp.int32, (LONGEST, 128), 1)
    for pair in range(D // 128):
        lanes = slice(pair * 128, (pair + 1) * 128)
        kp = kvw[:, lanes]
        vp = kvw[:, D + pair * 128 : D + (pair + 1) * 128]
        kms = [jnp.where(lane_k < HD, kp, jnp.zeros_like(kp)), jnp.where(lane_k >= HD, kp, jnp.zeros_like(kp))]
        qp = q[:, lanes] * 0.125
        dop = do[:, lanes]
        for hh in range(2):
            mine = lane_q < HD if hh == 0 else lane_q >= HD
            qm = jnp.where(mine, qp, jnp.zeros_like(qp))
            dom = jnp.where(mine, dop, jnp.zeros_like(dop))
            s = nt(kp, qm) + bias[...]
            p = jnp.exp(s - lse[pair * 2 + hh : pair * 2 + hh + 1, :])
            dp = nt(vp, dom)
            inner = jnp.sum(p * dp, axis=0, keepdims=True)
            ds = (p * (dp - inner)).astype(BF16)
            dv, dk, dq = nn(p.astype(BF16), dom), nn(ds, qm), tn(ds, kms[hh]) * 0.125
            if hh == 0:
                dvp[...], dkp[...], dq_o[:, lanes] = dv, dk, dq
            else:
                dvp[...] += dv
                dkp[...] += dk
                dq_o[:, lanes] += dq
        dkv_o[:, lanes] = dkp[pl.ds(offset, rows), :]
        dkv_o[:, D + pair * 128 : D + (pair + 1) * 128] = dvp[pl.ds(offset, rows), :]
        send_o[:, lanes] = dkp[...].astype(BF16)
        send_o[:, D + pair * 128 : D + (pair + 1) * 128] = dvp[...].astype(BF16)


def attend_back(meta, q, kvw, do, lse):
    rows = q.shape[0]
    f = jax.ShapeDtypeStruct
    v = pltpu.VMEM
    return pl.pallas_call(
        attend_back_kernel,
        out_shape=[f((rows, D), F32), f((rows, 2 * D), F32), f((LONGEST, 2 * D), BF16)],
        in_specs=[SM] + [VM] * 4,
        out_specs=[VM] * 3,
        scratch_shapes=[v((LONGEST, rows), F32), v((LONGEST, 128), F32), v((LONGEST, 128), F32)],
        compiler_params=params(26),
        cost_estimate=cost(14),
        name="attend_back",
    )(meta, q, kvw, do, lse)


def rear_kernel(nh, meta, inv, dq, dkv, recv, x1, frames, g2, norms, table, full, ng_in, grads_in, fg_o, ng_o, grads, w_in, w_out, w_qkv, n_ref, gb, dproj, x_ref, acc, g_in, g_out, g_qkv, sem, gsem):
    del grads_in
    b = Blocks(nh)
    rows = dq.shape[0]
    for i, base in enumerate((b.query, b.key, b.value)):
        fetch_all(full, inv, w_qkv, sem.at[0], base, b.ch, nh, i * D)
    fetch_all(full, inv, w_in, sem.at[1], b.in_one, b.ff, nh)
    fetch_all(full, inv, w_out, sem.at[2], b.out_one, b.ff, nh)
    spans = recv.shape[0]

    def one(at, i, c):
        p = pl.ds(place_of(meta, i), BAND)
        dproj[at, 0:D] = turn(dq[at, :], table[p, :], -1.0).astype(BF16)
        dk, dv = dkv[at, 0:D], dkv[at, D:]
        for s in range(spans):
            dk = dk + recv[s, at, 0:D].astype(F32)
            dv = dv + recv[s, at, D:].astype(F32)
        dproj[at, D : 2 * D] = turn(dk, table[p, :], -1.0).astype(BF16)
        dproj[at, 2 * D :] = dv.astype(BF16)
        n_ref[at, :] = norm(x1[at, :], norms, 1).astype(BF16)
        return c

    bands(rows, one)
    landed(w_qkv, sem.at[0])
    acc[...] = nn(dproj[...], w_qkv[...])
    for i in range(3):
        g_qkv[i * D : (i + 1) * D, :] = tn(dproj[:, i * D : (i + 1) * D], n_ref[...]).astype(BF16)
    for i, base in enumerate((b.query, b.key, b.value)):
        put_all(grads, inv, g_qkv, gsem.at[0], base, b.ch, nh, i * D)
    zero = jnp.zeros((1, D), F32)

    def two(at, i, c):
        dx, dg, db = norm_back(x1[at, :], acc[at, :], norms[1:2, :])
        g1 = g2[at, :] + dx
        x_ref[at, :] = g1
        gb[at, :] = (0.5 * g1).astype(BF16)
        n_ref[at, :] = norm(frames[at, :].astype(F32), norms, 0).astype(BF16)
        return c[0] + dg, c[1] + db

    gain1, shift1 = bands(rows, two, (zero, zero))
    landed(w_in, sem.at[1])
    landed(w_out, sem.at[2])
    feed_back(n_ref, gb, w_in, w_out, acc, g_in, g_out, grads, inv, b.in_one, b.out_one, gsem.at[1], gsem.at[2], b.ff, nh)

    def three(at, i, c):
        dx, dg, db = norm_back(frames[at, :].astype(F32), acc[at, :], norms[0:1, :])
        fg_o[at, :] = x_ref[at, :] + dx
        return c[0] + dg, c[1] + db

    gain0, shift0 = bands(rows, three, (zero, zero))
    ng_o[...] = ng_in[...]
    ng_o[0:1, :] = gain0
    ng_o[1:2, :] = gain1
    ng_o[5:6, :] = shift0
    ng_o[6:7, :] = shift1
    landed(g_qkv, gsem.at[0])
    landed(g_in, gsem.at[1])
    landed(g_out, gsem.at[2])


def rear(nh, meta, inv, dq, dkv, recv, x1, frames, g2, norms, table, full, ng, grads):
    rows = dq.shape[0]
    dma = pltpu.SemaphoreType.DMA
    f = jax.ShapeDtypeStruct
    v = pltpu.VMEM
    return pl.pallas_call(
        functools.partial(rear_kernel, nh),
        out_shape=[f((rows, D), F32), f((16, D), F32), f(grads.shape, BF16)],
        in_specs=[SM, SM] + [VM] * 8 + [HBM, VM, HBM],
        out_specs=[VM, VM, HBM],
        input_output_aliases={12: 2},
        scratch_shapes=[
            v((FF, D), BF16),
            v((FF, D), BF16),
            v((3 * D, D), BF16),
            v((rows, D), BF16),
            v((rows, D), BF16),
            v((rows, 3 * D), BF16),
            v((rows, D), F32),
            v((rows, D), F32),
            v((FF, D), BF16),
            v((FF, D), BF16),
            v((3 * D, D), BF16),
            dma((3,)),
            dma((3,)),
        ],
        compiler_params=params(28),
        cost_estimate=cost(13),
        name="rear",
    )(meta, inv, dq, dkv, recv, x1, frames, g2, norms, table, full, ng, grads)


def split(x):
    high = x.astype(BF16)
    return high, (x - high.astype(F32)).astype(BF16)


def three_products(dot, a, b):
    (ah, al), (bh, bl) = a, b
    return dot(ah, bh) + (dot(ah, bl) + dot(al, bh))


def wide_product(dot, a, b):
    rows = a.shape[0]
    ah, al = split(a)
    stacked = dot(jnp.concatenate([ah, al], axis=0), b[0])
    return stacked[0:rows] + (stacked[rows:] + dot(ah, b[1]))


def adam_step(weight, gradient, moment_one, moment_two, factor):
    one_new = beta_one * moment_one + (1.0 - beta_one) * gradient
    two_new = beta_two * moment_two + (1.0 - beta_two) * gradient * gradient
    return (weight - factor * one_new / (jnp.sqrt(two_new) + adam_eps), one_new, two_new)


def update_kernel(nh, head, grad, masters, first, second, left, right, small, bsums, norms, norm1, norm2, conv, conv1, conv2, out_v, fgrad_v, masters_o, first_o, second_o, ng_o, norms_o, norm1_o, norm2_o, conv_o, conv1_o, conv2_o, out_o, fgrad_o, sem):
    moves = [
        pltpu.make_async_copy(out_v, out_o, sem.at[0]),
        pltpu.make_async_copy(fgrad_v, fgrad_o, sem.at[1]),
    ]
    step = pl.program_id(0)

    @pl.when(step == 0)
    def _():
        for move in moves:
            move.start()
        grads = small[0:10, :]
        ng_o[...] = grads
        norms_o[...], norm1_o[...], norm2_o[...] = adam_step(norms[...], grads, norm1[...], norm2[...], 10.0 * FACTOR)
        width = conv.shape[1]
        rows = jnp.concatenate([small[16 : 16 + KERNEL, :], spread(bsums, 1), spread(bsums, 0)], axis=0)
        mine = rows[:, 0:width]
        for h in range(1, nh):
            mine = jnp.where(head[0] == h, rows[:, h * width : (h + 1) * width], mine)
        conv_o[...], conv1_o[...], conv2_o[...] = adam_step(conv[...], mine, conv1[...], conv2[...], 4.0 * FACTOR)

    for i in range(grad.shape[0]):
        g = grad[i]
        m1 = beta_one * first[i] + (1.0 - beta_one) * g
        first_o[i] = m1
        lefts, rights = split(left[i]), split(right[i])
        both = wide_product(nn, jnp.concatenate([g, m1], axis=0), lefts)
        rot = three_products(tn, rights, split(both[0:BLOCKW]))
        rot1 = three_products(tn, rights, split(both[BLOCKW:]))
        m2 = beta_two * second[i] + (1.0 - beta_two) * rot * rot
        second_o[i] = m2
        scaled = rot1 / (jnp.sqrt(m2) + adam_eps)
        back = wide_product(nt, three_products(nn, rights, split(scaled)), lefts)
        w = masters[i]
        masters_o[i] = w - FACTOR * back - step_rate * weight_decay * w

    @pl.when(step == pl.num_programs(0) - 1)
    def _():
        for move in moves:
            move.wait()


def update(nh, head, grad, masters, first, second, left, right, small, bsums, norms, norm1, norm2, conv, conv1, conv2, out_v, fgrad_v):
    spd = grad.shape[0]
    n = 2 if spd % 2 == 0 else 1
    block = pl.BlockSpec((n, BLOCKW, D), lambda i: (i, 0, 0))

    def whole(a):
        return pl.BlockSpec(a.shape, lambda i: (0, 0))

    f = jax.ShapeDtypeStruct
    return pl.pallas_call(
        functools.partial(update_kernel, nh),
        grid=(spd // n,),
        out_shape=[f(grad.shape, F32)] * 3
        + [f(norms.shape, F32)] * 4
        + [f(conv.shape, F32)] * 3
        + [f(out_v.shape, out_v.dtype), f(fgrad_v.shape, F32)],
        in_specs=[SM]
        + [block] * 4
        + [pl.BlockSpec((n, D, D), lambda i: (i, 0, 0)), pl.BlockSpec((n, BLOCKW, BLOCKW), lambda i: (i, 0, 0))]
        + [whole(a) for a in (small, bsums, norms, norm1, norm2, conv, conv1, conv2)]
        + [HBM, HBM],
        out_specs=[block] * 3 + [whole(norms)] * 4 + [whole(conv)] * 3 + [HBM, HBM],
        scratch_shapes=[pltpu.SemaphoreType.DMA((2,))],
        compiler_params=params(20),
        cost_estimate=cost(9),
        name="update",
    )(head, grad, masters, first, second, left, right, small, bsums, norms, norm1, norm2, conv, conv1, conv2, out_v, fgrad_v)


def per_device(
    ndp,
    nh,
    frames,
    out_grad,
    bucket_len,
    batch_count,
    utt_lengths,
    owner_slots,
    masters,
    first_moment,
    second_moment,
    left_basis,
    right_basis,
    norm_params,
    norm_first,
    norm_second,
    conv_params,
    conv_first,
    conv_second,
):
    rows = frames.shape[0]

    def flip(a):
        return jnp.transpose(a[0], (0, 2, 1))

    masters_t = flip(masters)
    z = lax.axis_index("head")
    dp = lax.axis_index("dp")
    place = jnp.stack([dp - dp % 2 + z % 2, 2 * (z // 2) + dp % 2])
    full, frames_v, ograd_v, ints, conv_all = gather(
        ndp,
        nh,
        masters_t.astype(BF16),
        frames,
        out_grad,
        bucket_len[None],
        batch_count[None],
        utt_lengths,
        conv_params.T,
    )
    table = jnp.asarray(rope_table())
    x1, q, kv, meta, inv, taps = front(
        ndp, nh, owner_slots, place, ints, conv_all, frames_v, norm_params, table, full
    )
    kvw, qh, x1h = keys(ndp, nh, kv, q, x1)
    o, lse, x2, gated, h, sums, n3, val, sig = attend(nh, meta, inv, q, kvw, x1, qh, x1h, norm_params, taps, full)
    (stats,) = totals(ndp, nh, 3, sums)
    out_v, g3, gz, bpart, ng, grads = middle(nh, meta, inv, x2, h, stats, ograd_v, norm_params, taps, full)
    bsums, gzh, hh = totals(ndp, nh, 4, bpart, (gz, h))
    g2, do, dtaps, ng, grads = conv_back(
        nh, meta, inv, gz, gzh, h, hh, stats, bsums, gated, n3, val, sig, x2, g3, o, norm_params, taps, full, ng, grads
    )
    dq, dkv, dkv_send = attend_back(meta, q, kvw, do, lse)
    recv = key_grads(ndp, nh, dkv_send, rows)
    fg_v, ng, grads = rear(
        nh, meta, inv, dq, dkv, recv, x1, frames_v, g2, norm_params, table, full, ng, grads
    )
    small = jnp.concatenate([ng, dtaps], axis=0)
    owned, small, out_w, fg_w = scatter(ndp, nh, grads, small, out_v, fg_v)
    (
        new_m,
        new_f,
        new_s,
        norm_grads,
        new_norms,
        norm_first_new,
        norm_second_new,
        new_conv,
        conv_first_new,
        conv_second_new,
        layer_out,
        frames_grad,
    ) = update(
        nh,
        jnp.reshape(z, (1,)),
        owned,
        masters_t,
        flip(first_moment),
        flip(second_moment),
        left_basis[0],
        right_basis[0],
        small,
        bsums,
        norm_params,
        norm_first,
        norm_second,
        conv_params.T,
        conv_first.T,
        conv_second.T,
        out_w,
        fg_w,
    )

    def unflip(a):
        return jnp.transpose(a, (0, 2, 1))[None]

    return (
        layer_out,
        frames_grad,
        unflip(new_m),
        unflip(new_f),
        unflip(new_s),
        norm_grads,
        new_norms,
        norm_first_new,
        norm_second_new,
        new_conv.T,
        conv_first_new.T,
        conv_second_new.T,
    )


def solution(mesh):
    both, blocks, chan = P(("dp", "head"), None), P("head", "dp", None, None), P("head", None)
    placed = (both, both, P("dp"), P("dp"), P("dp", None), P()) + (blocks,) * 5 + (P(),) * 3 + (chan,) * 3
    return jax.shard_map(
        functools.partial(per_device, mesh.shape["dp"], mesh.shape["head"]),
        mesh=mesh,
        in_specs=placed,
        out_specs=(both, both) + (blocks,) * 3 + (P(),) * 4 + (chan,) * 3,
        check_vma=False,
    )
```

```python
import functools
import math

import jax
import jax.numpy as jnp
import numpy as np
from jax import lax
from jax.experimental import pallas as pl
from jax.experimental.pallas import tpu as pltpu
from jax.sharding import PartitionSpec as P

D = 512
FF = 2048
HD = 64
KERNEL = 32
BLOCKW = 64
STEP = 10
LONGEST = 1024
HALO = 16

beta_one = 0.9
beta_two = 0.95
step_rate = 0.05
weight_decay = 0.01
adam_eps = 1e-08
norm_eps = 1e-05
masked_score = -1e30
FACTOR = step_rate * math.sqrt(1.0 - beta_two**STEP) / (1.0 - beta_one**STEP)

F32 = jnp.float32
BF16 = jnp.bfloat16
MESH = pl.DeviceIdType.MESH
ANY = pl.BlockSpec(memory_space=pl.ANY)
HBM = pl.BlockSpec(memory_space=pltpu.HBM)
VM = pl.BlockSpec(memory_space=pltpu.VMEM)
SM = pl.BlockSpec(memory_space=pltpu.SMEM)
MIB = 1 << 20


def cost(us):
    return pl.CostEstimate(flops=0, bytes_accessed=int(us * 3.6e6), transcendentals=0)


def params(mib, collective_id=None):
    if collective_id is None:
        return pltpu.CompilerParams(vmem_limit_bytes=mib * MIB)
    return pltpu.CompilerParams(
        vmem_limit_bytes=mib * MIB, collective_id=collective_id, has_side_effects=True
    )


def big(nh, slots):
    return max(nh, -(-64 * MIB // (slots * BLOCKW * D * 2)))


class Copies:
    def __init__(self, sends):
        self.sends = sends
        self.used = 0
        self.open = []

    def send(self, src, dst, recv_sem, device, when=None):
        copy = pltpu.make_async_remote_copy(
            src_ref=src,
            dst_ref=dst,
            send_sem=self.sends.at[self.used],
            recv_sem=recv_sem,
            device_id=device,
            device_id_type=MESH,
        )
        (pl.when(when) if when is not None else call)(copy.start)
        self.used += 1
        self.open.append((copy, when))

    def finish(self):
        for copy, when in self.open:
            (pl.when(when) if when is not None else call)(copy.wait_send)


def call(f):
    return f()


def arrived(ref, sem):
    pltpu.make_async_copy(ref, ref, sem).wait()


def greet(devices):
    barrier = pltpu.get_barrier_semaphore()
    for device in devices:
        pl.semaphore_signal(barrier, inc=1, device_id=device, device_id_type=MESH)
    pl.semaphore_wait(barrier, len(devices))


class Place:
    def __init__(self, ndp, nh):
        self.ndp, self.nh, self.nchip = ndp, nh, ndp // 2
        self.dp = lax.axis_index("dp")
        self.z = lax.axis_index("head")
        self.core = self.dp % 2
        self.chip = self.dp // 2
        self.group_core = self.z % 2
        self.part = 2 * (self.z // 2) + self.core

    def of_part(self, part):
        return (self.chip * 2 + part % 2, 2 * (part // 2) + self.group_core)

    def core_peer(self):
        return (self.chip * 2 + 1 - self.core, self.z)

    def swap_peer(self):
        return (self.chip * 2 + 1 - self.core, self.part)

    def x_chip(self):
        return self.chip + 1 - 2 * (self.chip % 2)

    def y_chip(self):
        return (self.chip + 2) % 4


def gather_kernel(ndp, nh, spd, own, frames, ograd, bucket, batch, utts, conv, full, frames_o, ograd_o, ints_o, conv_o, ints, sends, recvs, extra, isem, local):
    me = Place(ndp, nh)
    dp, z, core, chip, nchip = me.dp, me.z, me.core, me.chip, me.nchip

    def shard(h, ch, c):
        return full.at[h, pl.ds((ch * 2 + c) * spd, spd)]

    def sem(h, ch, c, half=0):
        return recvs.at[h * ndp + ch * 2 + c, half]

    peer = me.core_peer()
    swap = me.core != me.z % 2
    columns = [(dp, (z + i) % nh) for i in range(1, nh)]
    square = nchip == 4
    if square:
        planes = [(me.x_chip() * 2 + core, z), (me.y_chip() * 2 + core, z)]
    else:
        planes = [(((chip + i) % nchip) * 2 + core, z) for i in range(1, nchip)]
    ints[...] = jnp.zeros_like(ints)
    ints[0:1, 0:1] = bucket[...]
    ints[0:1, 1:2] = batch[...]
    ints[0:1, 2:10] = utts[...]
    barrier = pltpu.get_barrier_semaphore()
    near = totals_peers(me)
    for device in near:
        pl.semaphore_signal(barrier, inc=1, device_id=device, device_id_type=MESH)

    @pl.when(swap)
    def _():
        pl.semaphore_signal(barrier, inc=1, device_id=me.swap_peer(), device_id_type=MESH)

    pl.semaphore_wait(barrier, len(near) + (core + z) % 2)

    copies = Copies(sends)
    mine = shard(z, chip, core)
    below, above = (dp, (z + nh - 1) % nh), (dp, (z + 1) % nh)
    copies.send(own, mine, sem(z, chip, core), above, z < nh - 1)
    copies.send(own, mine, sem(z, chip, core), below, z > 0)
    for device in planes:
        copies.send(own, mine, sem(z, chip, core), device)
    copies.send(own, mine, sem(z, chip, core), peer)
    keep = [
        pltpu.make_async_copy(own, mine, local.at[0]),
        pltpu.make_async_copy(ints, ints_o.at[dp], local.at[1]),
        pltpu.make_async_copy(conv, conv_o.at[z], local.at[2]),
    ]
    for copy in keep:
        copy.start()

    @pl.when(jnp.logical_not(swap))
    def _():
        for k, (src, dst) in enumerate(((frames, frames_o), (ograd, ograd_o))):
            pltpu.make_async_copy(src, dst, local.at[3 + k]).start()

    def column(step, up):
        h = z - step if up else z + step
        there = z >= step if up else z + step < nh
        onward = z < nh - 1 if up else z > 0
        h = jnp.where(there, h, z)
        s, r = shard(h, chip, core), sem(h, chip, core)

        @pl.when(there)
        def _():
            arrived(s, r)

        if step < nh - 1:
            copies.send(s, s, r, above if up else below, jnp.logical_and(there, onward))
        for device in planes:
            copies.send(s, s, r, device, there)
        copies.send(s, s, r, peer, there)

    def beside(step, up):
        h = z - step if up else z + step
        there = z >= step if up else z + step < nh
        h = jnp.where(there, h, z)
        if not square:
            for k in range(1, nchip):
                ch = (chip + k) % nchip

                @pl.when(there)
                def _():
                    arrived(shard(h, ch, core), sem(h, ch, core))

                copies.send(shard(h, ch, core), shard(h, ch, core), sem(h, ch, core), peer, there)
            return
        half = spd // 2
        for side, (ch, device) in enumerate(((me.x_chip(), planes[1]), (me.y_chip(), planes[0]))):

            @pl.when(there)
            def _():
                arrived(shard(h, ch, core), sem(h, ch, core))

            piece = full.at[h, pl.ds((ch * 2 + core) * spd + side * half, half)]
            copies.send(piece, piece, sem(h, ch, core, side), device, there)
            copies.send(shard(h, ch, core), shard(h, ch, core), sem(h, ch, core), peer, there)

    def across(step, up):
        if not square:
            return
        h = z - step if up else z + step
        there = z >= step if up else z + step < nh
        h = jnp.where(there, h, z)
        half = spd // 2
        ch = 3 - chip

        @pl.when(there)
        def _():
            for side in range(2):
                piece = full.at[h, pl.ds((ch * 2 + core) * spd + side * half, half)]
                arrived(piece, sem(h, ch, core, side))

        copies.send(shard(h, ch, core), shard(h, ch, core), sem(h, ch, core), peer, there)

    visits = [(0, True)] + [(step, up) for step in range(1, nh) for up in (True, False)]
    lag = 3
    for i in range(len(visits) + 2 * lag):
        if 0 < i < len(visits):
            column(*visits[i])
        if i == len(visits) - 1:
            for device in columns:
                copies.send(conv, conv_o.at[z], extra.at[3 + z], device)
            for k in range(1, ndp):
                copies.send(ints, ints_o.at[dp], isem.at[dp], ((dp + k) % ndp, z))

            @pl.when(swap)
            def _():
                for k, (src, dst) in enumerate(((frames, frames_o), (ograd, ograd_o))):
                    pltpu.make_async_remote_copy(
                        src_ref=src, dst_ref=dst, send_sem=local.at[3 + k], recv_sem=extra.at[1 + k],
                        device_id=me.swap_peer(), device_id_type=MESH,
                    ).start()

        if 0 <= i - lag < len(visits):
            beside(*visits[i - lag])
        if i >= 2 * lag:
            across(*visits[i - 2 * lag])
    for i in range(nh):
        h = (z + nh - i) % nh
        for k in range(nchip):
            ch = (chip + k) % nchip
            arrived(shard(h, ch, 1 - core), sem(h, ch, 1 - core))
    for k in range(1, ndp):
        arrived(ints_o.at[(dp + k) % ndp], isem.at[(dp + k) % ndp])
    for i in range(1, nh):
        h = (z + nh - i) % nh
        arrived(conv_o.at[h], extra.at[3 + h])

    @pl.when(swap)
    def _():
        arrived(frames_o, extra.at[1])
        arrived(ograd_o, extra.at[2])

    for i, ref in enumerate((frames, ograd)):
        arrived(ref, local.at[3 + i])
    for copy in keep:
        copy.wait()
    copies.finish()


def gather(ndp, nh, own, frames, ograd, bucket, batch, utts, conv):
    spd = own.shape[0]
    nchip = ndp // 2
    plane = 2 if nchip == 4 else nchip - 1
    visits = 2 * nh - 1
    halves = 2 * visits if nchip == 4 else 0
    count = 2 * visits + visits * (plane + 1) + visits * (nchip - 1) + halves + (ndp - 1) + (nh - 1)
    shapes = [
        jax.ShapeDtypeStruct((big(nh, ndp * spd), ndp * spd, BLOCKW, D), BF16),
        jax.ShapeDtypeStruct(frames.shape, BF16),
        jax.ShapeDtypeStruct(ograd.shape, BF16),
        jax.ShapeDtypeStruct((ndp, 8, 128), jnp.int32),
        jax.ShapeDtypeStruct((nh,) + conv.shape, F32),
    ]
    dma = pltpu.SemaphoreType.DMA
    return pl.pallas_call(
        functools.partial(gather_kernel, ndp, nh, spd),
        out_shape=shapes,
        in_specs=[ANY, HBM, HBM, VM, VM, VM, ANY],
        out_specs=[HBM] * 3 + [ANY] * 2,
        scratch_shapes=[
            pltpu.VMEM((8, 128), jnp.int32),
            dma((count,)),
            dma((nh * ndp, 2)),
            dma((3 + nh,)),
            dma((ndp,)),
            dma((5,)),
        ],
        compiler_params=params(52, 1),
        cost_estimate=cost(60),
        name="gather",
    )(own, frames, ograd, bucket, batch, utts, conv)


def totals_step(me, small, first, second, copies, sem1, sem2, local):
    ndp, nh = me.ndp, me.nh

    def one():
        for i in range(1, ndp):
            copies.send(small, first.at[me.dp], sem1.at[me.dp], ((me.dp + i) % ndp, me.z))
        first[me.dp] = small[...]

    def two():
        for i in range(1, ndp):
            src = (me.dp + i) % ndp
            arrived(first.at[src], sem1.at[src])
        total = first[0]
        for i in range(1, ndp):
            total = total + first[i]
        second[me.z] = total
        for i in range(1, nh):
            copies.send(second.at[me.z], second.at[me.z], sem2.at[me.z], (me.dp, (me.z + i) % nh))

    def three():
        for i in range(1, nh):
            src = (me.z + i) % nh
            arrived(second.at[src], sem2.at[src])
        total = second[0]
        for i in range(1, nh):
            total = total + second[i]
        return total

    return one, two, three


def halved_steps(me, small, pair, plane, column, final, copies, psem, asem, zsem, fsem):
    nchip, nh = me.nchip, me.nh
    core, chip, z = me.core, me.chip, me.z
    half = small.shape[0] // 2
    mine = pl.ds(pl.multiple_of(core * half, 8), half)
    yours = pl.ds(pl.multiple_of((1 - core) * half, 8), half)

    def zero():
        copies.send(small, pair.at[core], psem.at[core], me.core_peer())
        pair[core] = small[...]

    def one():
        arrived(pair.at[1 - core], psem.at[1 - core])
        plane[chip] = pair[0, mine, :] + pair[1, mine, :]
        for i in range(1, nchip):
            copies.send(plane.at[chip], plane.at[chip], asem.at[chip], ((chip + i) % nchip * 2 + core, z))

    def two():
        for i in range(1, nchip):
            src = (chip + i) % nchip
            arrived(plane.at[src], asem.at[src])
        total = plane[0]
        for i in range(1, nchip):
            total = total + plane[i]
        column[z] = total
        for i in range(1, nh):
            copies.send(column.at[z], column.at[z], zsem.at[z], (me.dp, (z + i) % nh))

    def three():
        for i in range(1, nh):
            src = (z + i) % nh
            arrived(column.at[src], zsem.at[src])
        total = column[0]
        for i in range(1, nh):
            total = total + column[i]
        final[mine, :] = total
        copies.send(final.at[mine], final.at[mine], fsem.at[core], me.core_peer())

    def four():
        arrived(final.at[yours], fsem.at[1 - core])
        return final[...]

    return zero, one, two, three, four


def totals_peers(me):
    return [((me.dp + i) % me.ndp, me.z) for i in range(1, me.ndp)] + [
        (me.dp, (me.z + i) % me.nh) for i in range(1, me.nh)
    ]


def totals_kernel(ndp, nh, halos, *refs):
    me = Place(ndp, nh)
    small = refs[0]
    edges = refs[1 : 1 + halos]
    out = refs[1 + halos]
    edges_o = refs[2 + halos : 2 + 2 * halos]
    first, second, sends, sem1, sem2, hsem = refs[2 + 2 * halos :]
    greet(totals_peers(me))
    copies = Copies(sends)
    one, two, three = totals_step(me, small, first, second, copies, sem1, sem2, None)
    one()
    for i in range(halos):
        send_edges(me, edges[i], edges_o[i], copies, hsem.at[2 * i], hsem.at[2 * i + 1])
    two()
    out[...] = three()
    for i in range(halos):
        arrived(edges_o[i].at[pl.ds(0, HALO)], hsem.at[2 * i])
        arrived(edges_o[i].at[pl.ds(HALO, HALO)], hsem.at[2 * i + 1])
    copies.finish()


def window(me, rows):
    span = LONGEST // rows
    at = me.part % span
    return span, at, me.part - at


def send_edges(me, src, dst, copies, sem_before, sem_after):
    rows = src.shape[0]
    span, at, base = window(me, rows)
    after = me.of_part(base + (at + 1) % span)
    before = me.of_part(base + (at + span - 1) % span)
    copies.send(src.at[pl.ds(rows - HALO, HALO)], dst.at[pl.ds(0, HALO)], sem_before, after)
    copies.send(src.at[pl.ds(0, HALO)], dst.at[pl.ds(HALO, HALO)], sem_after, before)


def totals(ndp, nh, collective_id, small, edges=()):
    dma = pltpu.SemaphoreType.DMA
    n = len(edges)
    halo = [jax.ShapeDtypeStruct((2 * HALO, D), e.dtype) for e in edges]
    return pl.pallas_call(
        functools.partial(totals_kernel, ndp, nh, n),
        out_shape=[jax.ShapeDtypeStruct(small.shape, F32)] + halo,
        in_specs=[VM] + [ANY] * n,
        out_specs=[VM] + [ANY] * n,
        scratch_shapes=[
            pltpu.VMEM((ndp,) + small.shape, F32),
            pltpu.VMEM((nh,) + small.shape, F32),
            dma((ndp + nh - 2 + 2 * n,)),
            dma((ndp,)),
            dma((nh,)),
            dma((2 * n + 1,)),
        ],
        compiler_params=params(16, collective_id),
        cost_estimate=cost(8),
        name=f"totals_{collective_id}",
    )(small, *edges)


def keys_kernel(ndp, nh, kv, q, x1, kv_o, q_o, x1_o, sends, recvs, local):
    me = Place(ndp, nh)
    rows = kv.shape[0]
    span, at, base = window(me, rows)
    peers = [me.of_part(base + (at + i) % span) for i in range(1, span)]
    greet(peers)
    copies = Copies(sends)
    place = kv_o.at[pl.ds(at * rows, rows)]
    for device in peers:
        copies.send(kv, place, recvs.at[at], device)
    own = pltpu.make_async_copy(kv, place, local.at[0])
    own.start()
    for i, (src, dst) in enumerate(((q, q_o), (x1, x1_o))):
        send_edges(me, src, dst, copies, recvs.at[span + 2 * i], recvs.at[span + 2 * i + 1])
    for i in range(1, span):
        other = (at + i) % span
        arrived(kv_o.at[pl.ds(other * rows, rows)], recvs.at[other])
    for i, dst in enumerate((q_o, x1_o)):
        arrived(dst.at[pl.ds(0, HALO)], recvs.at[span + 2 * i])
        arrived(dst.at[pl.ds(HALO, HALO)], recvs.at[span + 2 * i + 1])
    own.wait()
    copies.finish()


def keys(ndp, nh, kv, q, x1):
    span = LONGEST // kv.shape[0]
    dma = pltpu.SemaphoreType.DMA
    return pl.pallas_call(
        functools.partial(keys_kernel, ndp, nh),
        out_shape=[
            jax.ShapeDtypeStruct((LONGEST, 2 * D), BF16),
            jax.ShapeDtypeStruct((2 * HALO, D), BF16),
            jax.ShapeDtypeStruct((2 * HALO, D), F32),
        ],
        in_specs=[ANY] * 3,
        out_specs=[ANY] * 3,
        scratch_shapes=[dma((span + 3,)), dma((span + 4,)), dma((1,))],
        compiler_params=params(8, 2),
        cost_estimate=cost(3),
        name="keys",
    )(kv, q, x1)


def key_grads_kernel(ndp, nh, part, out, sends, recvs):
    me = Place(ndp, nh)
    rows = out.shape[1]
    span, at, base = window(me, rows)
    greet([me.of_part(base + (at + i) % span) for i in range(1, span)])
    copies = Copies(sends)
    for i in range(1, span):
        other = (at + i) % span
        copies.send(part.at[pl.ds(other * rows, rows)], out.at[i - 1], recvs.at[i - 1], me.of_part(base + other))
    for i in range(1, span):
        arrived(out.at[i - 1], recvs.at[i - 1])
    copies.finish()


def key_grads(ndp, nh, part, rows):
    span = LONGEST // rows
    dma = pltpu.SemaphoreType.DMA
    return pl.pallas_call(
        functools.partial(key_grads_kernel, ndp, nh),
        out_shape=jax.ShapeDtypeStruct((span - 1, rows, 2 * D), BF16),
        in_specs=[ANY],
        out_specs=ANY,
        scratch_shapes=[dma((span - 1,)), dma((span - 1,))],
        compiler_params=params(8, 5),
        cost_estimate=cost(3),
        name="key_grads",
    )(part)


def far_first(z, nh):
    orders = [sorted(range(nh), key=lambda h: (-abs(h - at), h)) for at in range(nh)]
    return [sum((orders[at][i] * (z == at).astype(jnp.int32) for at in range(nh)), 0) for i in range(nh)]


def scatter_kernel(ndp, nh, spd, grads, small, out_v, fgrad_v, owned, small_o, out_o, fgrad_o, part, cores, side_x, side_y, half_x, half_y, zrecv, pair, plane, column, final, sends, csem, psem, xsem, zsem, sem0, sem1, sem2, sem3, esem, local):
    me = Place(ndp, nh)
    dp, z, core, chip, nchip = me.dp, me.z, me.core, me.chip, me.nchip
    square = nchip == 4
    peer = me.core_peer()
    swap = me.core != me.z % 2
    half = spd // 2
    barrier = pltpu.get_barrier_semaphore()
    near = totals_peers(me)
    for device in near:
        pl.semaphore_signal(barrier, inc=1, device_id=device, device_id_type=MESH)

    @pl.when(swap)
    def _():
        pl.semaphore_signal(barrier, inc=1, device_id=me.swap_peer(), device_id_type=MESH)

    pl.semaphore_wait(barrier, len(near) + (core + z) % 2)
    copies = Copies(sends)
    order = far_first(z, nh)
    if square:
        chips = [3 - chip, me.x_chip(), me.y_chip(), chip]
    else:
        chips = [(chip + i + 1) % nchip for i in range(nchip)]
    loads = {}

    def begin(i):
        for k, ch in enumerate(chips):
            copies.send(grads.at[order[i], pl.ds((ch * 2 + 1 - core) * spd, spd)], cores.at[i, k], csem.at[i, k], peer)
            load = pltpu.make_async_copy(
                grads.at[order[i], pl.ds((ch * 2 + core) * spd, spd)], part.at[i, k], psem.at[i, k]
            )
            load.start()
            loads[i, k] = load

    begin(0)
    zero, one, two, three, four = halved_steps(
        me, small, pair, plane, column, final, copies, sem0, sem1, sem2, sem3
    )
    zero()

    @pl.when(swap)
    def _():
        for i, (src, dst) in enumerate(((out_v, out_o), (fgrad_v, fgrad_o))):
            pltpu.make_async_remote_copy(
                src_ref=src, dst_ref=dst, send_sem=local.at[i], recv_sem=esem.at[i],
                device_id=me.swap_peer(), device_id_type=MESH,
            ).start()

    @pl.when(jnp.logical_not(swap))
    def _():
        for i, (src, dst) in enumerate(((out_v, out_o), (fgrad_v, fgrad_o))):
            pltpu.make_async_copy(src, dst, local.at[i]).start()

    def add(i, k, others, lo=0, n=spd):
        @pl.loop(0, n, unroll=True)
        def _(s):
            total = part[i, k, lo + s].astype(F32)
            for other in others:
                total = total + other(s).astype(F32)
            part[i, k, lo + s] = total.astype(BF16)

    def meet(i, k):
        loads[i, k].wait()
        arrived(cores.at[i, k], csem.at[i, k])

    planes = [(me.x_chip() * 2 + core, z), (me.y_chip() * 2 + core, z)]

    def stage_a(i):
        if square:
            meet(i, 0)
            add(i, 0, [lambda s: cores[i, 0, s]])
            copies.send(part.at[i, 0, pl.ds(0, half)], half_x.at[i], xsem.at[i, 0], planes[0])
            copies.send(part.at[i, 0, pl.ds(half, half)], half_y.at[i], xsem.at[i, 1], planes[1])
        else:
            for k in range(nchip - 1):
                meet(i, k)
                add(i, k, [lambda s: cores[i, k, s]])
                copies.send(part.at[i, k], side_x.at[i, k], xsem.at[i, k], (chips[k] * 2 + core, z))

    def stage_b(i):
        if not square:
            return
        meet(i, 1)
        add(i, 1, [lambda s: cores[i, 1, s]], 0, half)
        arrived(half_y.at[i], xsem.at[i, 1])
        add(i, 1, [lambda s: cores[i, 1, half + s], lambda s: half_y[i, s]], half, half)
        copies.send(part.at[i, 1], side_x.at[i, 0], xsem.at[i, 2], planes[0])
        meet(i, 2)
        add(i, 2, [lambda s: cores[i, 2, half + s]], half, half)
        arrived(half_x.at[i], xsem.at[i, 0])
        add(i, 2, [lambda s: cores[i, 2, s], lambda s: half_x[i, s]], 0, half)
        copies.send(part.at[i, 2], side_y.at[i], xsem.at[i, 3], planes[1])

    last = nchip - 1

    def stage_c(i):
        meet(i, last)
        if square:
            arrived(side_x.at[i, 0], xsem.at[i, 2])
            arrived(side_y.at[i], xsem.at[i, 3])
            others = [lambda s: cores[i, last, s], lambda s: side_x[i, 0, s], lambda s: side_y[i, s]]
        else:
            others = [lambda s: cores[i, last, s]]
            for k in range(nchip - 1):
                arrived(side_x.at[i, k], xsem.at[i, k])
                others.append(lambda s, k=k: side_x[i, k, s])
        add(i, last, others)
        if i < nh - 1:
            copies.send(part.at[i, last], zrecv.at[z], zsem.at[z], (dp, order[i]))

    for i in range(nh + 2):
        if i + 1 < nh:
            begin(i + 1)
        if i < nh:
            stage_a(i)
        if 0 <= i - 1 < nh:
            stage_b(i - 1)
        if i < 4:
            (one, two, three, lambda: None)[min(i, 3)]()
        if i >= 2:
            stage_c(i - 2)
    small_o[...] = four()
    sources = [(z + i) % nh for i in range(1, nh)]
    for src in sources:
        arrived(zrecv.at[src], zsem.at[src])

    @pl.loop(0, spd)
    def _(s):
        total = part[nh - 1, last, s].astype(F32)
        for src in sources:
            total = total + zrecv[src, s].astype(F32)
        owned[s] = total

    @pl.when(swap)
    def _():
        arrived(out_o, esem.at[0])
        arrived(fgrad_o, esem.at[1])

    arrived(out_v, local.at[0])
    arrived(fgrad_v, local.at[1])
    copies.finish()


def scatter(ndp, nh, grads, small, out_v, fgrad_v):
    spd = grads.shape[1] // ndp
    nchip = ndp // 2
    square = nchip == 4
    dma = pltpu.SemaphoreType.DMA
    block = (spd, BLOCKW, D)
    halfb = (max(spd // 2, 1), BLOCKW, D)
    sides = 1 if square else nchip - 1
    halves = (small.shape[0] // 2, D)
    sent = nh * nchip + 2 + (nchip - 1) + (nh - 1) + (nh * 4 if square else nh * (nchip - 1)) + (nh - 1)
    return pl.pallas_call(
        functools.partial(scatter_kernel, ndp, nh, spd),
        out_shape=[
            jax.ShapeDtypeStruct(block, F32),
            jax.ShapeDtypeStruct(small.shape, F32),
            jax.ShapeDtypeStruct(out_v.shape, out_v.dtype),
            jax.ShapeDtypeStruct(fgrad_v.shape, fgrad_v.dtype),
        ],
        in_specs=[HBM, VM, HBM, HBM],
        out_specs=[VM, VM, HBM, HBM],
        scratch_shapes=[
            pltpu.VMEM((nh, nchip) + block, BF16),
            pltpu.VMEM((nh, nchip) + block, BF16),
            pltpu.VMEM((nh, sides) + block, BF16),
            pltpu.VMEM((nh,) + block, BF16),
            pltpu.VMEM((nh,) + halfb, BF16),
            pltpu.VMEM((nh,) + halfb, BF16),
            pltpu.VMEM((nh,) + block, BF16),
            pltpu.VMEM((2,) + small.shape, F32),
            pltpu.VMEM((nchip,) + halves, F32),
            pltpu.VMEM((nh,) + halves, F32),
            pltpu.VMEM(small.shape, F32),
            dma((sent,)),
            dma((nh, nchip)),
            dma((nh, nchip)),
            dma((nh, max(4, nchip))),
            dma((nh,)),
            dma((2,)),
            dma((nchip,)),
            dma((nh,)),
            dma((2,)),
            dma((2,)),
            dma((2,)),
        ],
        compiler_params=params(28, 6),
        cost_estimate=cost(65),
        name="scatter",
    )(grads, small, out_v, fgrad_v)


def nn(a, b):
    return jnp.dot(a, b, preferred_element_type=F32)


def nt(a, b):
    return lax.dot_general(a, b, (((1,), (1,)), ((), ())), preferred_element_type=F32)


def tn(a, b):
    return lax.dot_general(a, b, (((0,), (0,)), ((), ())), preferred_element_type=F32)


def sigmoid(v):
    return 0.5 * jnp.tanh(0.5 * v) + 0.5


def slope_of(v, sig):
    return sig * (1.0 + v * (1.0 - sig))


class Blocks:
    def __init__(self, nh):
        self.nh = nh
        ff, ch = FF // nh // BLOCKW, D // nh // BLOCKW
        self.ff, self.ch = ff, ch
        self.in_one, self.in_two = 0, ff
        self.query = 2 * ff
        self.key = self.query + ch
        self.value = self.key + ch
        self.conv_value = self.value + ch
        self.conv_gate = self.conv_value + ch
        rows = self.conv_gate + ch
        self.out_one, self.out_two = rows, rows + ff
        self.attn = rows + 2 * ff
        self.point = self.attn + ch
        self.total = self.point + ch


def fetch(full, inv, dst, sem, base, count, part, row):
    for j in range(count):
        pltpu.make_async_copy(
            full.at[part, inv[base + j]], dst.at[pl.ds(row + j * BLOCKW, BLOCKW)], sem
        ).start()


def fetch_all(full, inv, dst, sem, base, count, nh, row=0):
    for part in range(nh):
        fetch(full, inv, dst, sem, base, count, part, row + part * count * BLOCKW)


def landed(dst, sem):
    pltpu.make_async_copy(dst, dst, sem).wait()


def put(grads, inv, src, sem, base, count, part, row):
    for j in range(count):
        pltpu.make_async_copy(
            src.at[pl.ds(row + j * BLOCKW, BLOCKW)], grads.at[part, inv[base + j]], sem
        ).start()


def put_all(grads, inv, src, sem, base, count, nh, row=0):
    for part in range(nh):
        put(grads, inv, src, sem, base, count, part, row + part * count * BLOCKW)


def tables(meta, frame):
    length, batch = meta[0], meta[1]
    utterance = jnp.zeros_like(frame)
    for i in range(1, 8):
        utterance = utterance + (frame >= i * length).astype(jnp.int32)
    within = frame - utterance * length
    own = jnp.zeros_like(frame)
    for i in range(8):
        own = jnp.where(utterance == i, meta[2 + i], own)
    live = (utterance < batch) & (within < own)
    return utterance, within, live


def live_rows(meta, start, count):
    frame = start + lax.broadcasted_iota(jnp.int32, (count, 1), 0)
    return tables(meta, frame)[2].astype(F32)


def hat(x):
    center = jnp.mean(x, axis=1, keepdims=True)
    offset = x - center
    spread = lax.rsqrt(jnp.mean(offset * offset, axis=1, keepdims=True) + norm_eps)
    return offset * spread, spread


def norm(x, norms, i):
    return hat(x)[0] * norms[i : i + 1, :] + norms[i + 5 : i + 6, :]


def norm_back(x, grad, gain):
    return hat_back(*hat(x), grad, gain)


def hat_back(xhat, spread, grad, gain):
    scaled = grad * gain
    inner = scaled - jnp.mean(scaled, axis=1, keepdims=True) - xhat * jnp.mean(scaled * xhat, axis=1, keepdims=True)
    return spread * inner, jnp.sum(grad * xhat, axis=0, keepdims=True), jnp.sum(grad, axis=0, keepdims=True)


BAND = 64


def bands(rows, body, init=()):
    return lax.fori_loop(0, rows // BAND, lambda i, c: body(pl.ds(pl.multiple_of(i * BAND, BAND), BAND), i, c), init, unroll=True)


def partner(x):
    lane = lax.broadcasted_iota(jnp.int32, x.shape, 1) % HD
    return jnp.where(lane < HD // 2, pltpu.roll(x, 128 - HD // 2, 1), pltpu.roll(x, HD // 2, 1))


def turn(x, table, sign):
    first = lax.broadcasted_iota(jnp.int32, table.shape, 1) % HD < HD // 2
    cos = jnp.where(first, table, pltpu.roll(table, HD // 2, 1))
    sin = jnp.where(first, -pltpu.roll(table, 128 - HD // 2, 1), table)
    parts = []
    for i in range(D // 128):
        piece = x[:, i * 128 : (i + 1) * 128]
        parts.append(piece * cos + partner(piece) * (sign * sin))
    return jnp.concatenate(parts, axis=1)


def rope_table():
    freq = np.exp(np.arange(HD // 2, dtype=np.float32) * np.float32(-math.log(10000.0) / (HD // 2)))
    angle = np.arange(LONGEST, dtype=np.float32)[:, None] * freq[None, :].astype(np.float32)
    return np.tile(np.concatenate([np.cos(angle), np.sin(angle)], axis=1), (1, 2)).astype(np.float32)


def place_of(meta, i):
    return pl.multiple_of(lax.rem(meta[10] + i * BAND, meta[0]), BAND)


def feed(n_ref, w_in, w_out, acc_ref, sem, sem2, nh):
    unit = FF // nh
    for part in range(nh):
        rows = pl.ds(part * unit, unit)
        landed(w_in.at[rows], sem.at[part])
        pre = nt(n_ref[...], w_in[rows, :])
        act = (pre * sigmoid(pre)).astype(BF16)
        landed(w_out.at[rows], sem2.at[part])
        if part == 0:
            acc_ref[...] = nn(act, w_out[rows, :])
        else:
            acc_ref[...] += nn(act, w_out[rows, :])


def feed_back(n_ref, gb_ref, w_in, w_out, acc_ref, g_in, g_out, grads, inv, base_in, base_out, sem_in, sem_out, count, nh):
    unit = FF // nh

    def body(part, carry):
        rows = pl.ds(pl.multiple_of(part * unit, unit), unit)
        n, gb, win, wout = n_ref[...], gb_ref[...], w_in[rows, :], w_out[rows, :]
        pre = nt(win, n)
        sig = sigmoid(pre)
        act = (pre * sig).astype(BF16)
        dpre = (nt(wout, gb) * slope_of(pre, sig)).astype(BF16)
        g_out[rows, :] = nn(act, gb).astype(BF16)
        g_in[rows, :] = nn(dpre, n).astype(BF16)
        acc_ref[...] += tn(dpre, win)
        put(grads, inv, g_out, sem_out, base_out, count, part, part * unit)
        put(grads, inv, g_in, sem_in, base_in, count, part, part * unit)
        return carry

    acc_ref[...] = jnp.zeros_like(acc_ref)
    lax.fori_loop(0, nh, body, 0, unroll=True)


def front_kernel(ndp, nh, owner, place, ints, conv, frames, norms, table, full, x1, q, kv, meta, inv, taps, w_in, w_out, w_qkv, n_ref, acc, groups, sem, sem2, sem3):
    b = Blocks(nh)
    known = pltpu.make_async_copy(ints, groups, sem3.at[1])
    known.start()

    def slot(i, c):
        inv[owner[i]] = i
        return c

    lax.fori_loop(0, owner.shape[0], slot, 0)
    rows = frames.shape[0]
    unit = FF // nh
    for part in range(nh):
        fetch(full, inv, w_in, sem.at[part], b.in_one, b.ff, part, part * unit)
        fetch(full, inv, w_out, sem2.at[part], b.out_one, b.ff, part, part * unit)
    for i, base in enumerate((b.query, b.key, b.value)):
        fetch_all(full, inv, w_qkv, sem3.at[0], base, b.ch, nh, i * D)

    def first(at, i, c):
        n_ref[at, :] = norm(frames[at, :].astype(F32), norms, 0).astype(BF16)
        return c

    bands(rows, first)
    known.wait()
    for i in range(16):
        meta[i] = groups[place[0], 0, i]
    meta[10] = place[1] * rows

    def count(d, total):
        for u in range(8):
            total += jnp.where(u < groups[d, 0, 1], jnp.minimum(groups[d, 0, 2 + u], groups[d, 0, 0]), 0)
        return total

    meta[11] = lax.fori_loop(0, ndp, count, 0)
    taps[...] = jnp.zeros_like(taps)
    width = conv.shape[2]
    for h in range(nh):
        taps[0 : KERNEL + 2, h * width : (h + 1) * width] = conv[h]
    feed(n_ref, w_in, w_out, acc, sem, sem2, nh)

    def second(at, i, c):
        x = frames[at, :].astype(F32) + 0.5 * acc[at, :]
        x1[at, :] = x
        n_ref[at, :] = norm(x, norms, 1).astype(BF16)
        return c

    bands(rows, second)
    landed(w_qkv, sem3.at[0])
    for j, (dst, lo) in enumerate(((q, 0), (kv, 0), (kv, D))):
        acc[...] = nt(n_ref[...], w_qkv[j * D : (j + 1) * D, :])

        def third(at, i, c):
            x = acc[at, :]
            if j < 2:
                p = pl.ds(place_of(meta, i), BAND)
                x = turn(x, table[p, :], 1.0)
            dst[at, lo : lo + D] = x.astype(BF16)
            return c

        bands(rows, third)


def front(ndp, nh, owner, place, ints, conv, frames, norms, table, full):
    rows = frames.shape[0]
    dma = pltpu.SemaphoreType.DMA
    return pl.pallas_call(
        functools.partial(front_kernel, ndp, nh),
        out_shape=[
            jax.ShapeDtypeStruct((rows, D), F32),
            jax.ShapeDtypeStruct((rows, D), BF16),
            jax.ShapeDtypeStruct((rows, 2 * D), BF16),
            jax.ShapeDtypeStruct((16,), jnp.int32),
            jax.ShapeDtypeStruct(owner.shape, jnp.int32),
            jax.ShapeDtypeStruct((40, D), F32),
        ],
        in_specs=[SM, SM, ANY, VM, VM, VM, VM, HBM],
        out_specs=[VM, VM, VM, SM, SM, VM],
        scratch_shapes=[
            pltpu.VMEM((FF, D), BF16),
            pltpu.VMEM((FF, D), BF16),
            pltpu.VMEM((3 * D, D), BF16),
            pltpu.VMEM((rows, D), BF16),
            pltpu.VMEM((rows, D), F32),
            pltpu.SMEM((ndp, 8, 128), jnp.int32),
            dma((nh,)),
            dma((nh,)),
            dma((2,)),
        ],
        compiler_params=params(18),
        cost_estimate=cost(7),
        name="front",
    )(owner, place, ints, conv, frames, norms, table, full)


def fill_chunk(meta, src, chunk, k, start):
    lead = lax.rem(start + k * 256, meta[0]) != 0
    trail = lax.rem(start + (k + 1) * 256, meta[0]) != 0
    chunk[0:HALO, :] = jnp.where(lead, src[k * 256 : k * 256 + HALO, :], 0.0)
    chunk[HALO : HALO + 256, :] = src[k * 256 + HALO : k * 256 + HALO + 256, :]
    chunk[HALO + 256 :, :] = jnp.where(trail, src[k * 256 + HALO + 256 : k * 256 + 2 * HALO + 256, :], 0.0)


def shift_rows(chunk, moved):
    rows = chunk.shape[0]
    moved[0] = chunk[...]
    for b in range(1, 8):
        moved[b, 0 : rows - 8, :] = chunk[b : b + rows - 8, :]


def attend_kernel(nh, meta, inv, q, kvw, x1, qh, x1h, norms, taps, full, o_o, lse_o, x2_o, gated_o, h_o, sums_o, n_ref, val, sig, w_attn, w_glu, q_ext, o_ext, x_ext, bias, chunk, moved, lse_s, sem):
    b = Blocks(nh)
    rows = q.shape[0]
    ext = rows + 2 * HALO
    start = meta[10]
    fetch_all(full, inv, w_attn, sem.at[0], b.attn, b.ch, nh)
    for i, base in enumerate((b.conv_value, b.conv_gate)):
        fetch_all(full, inv, w_glu, sem.at[1], base, b.ch, nh, i * D)
    q_ext[0:HALO, :] = qh[0:HALO, :]
    q_ext[HALO : HALO + rows, :] = q[...]
    q_ext[HALO + rows :, :] = qh[HALO:, :]
    x_ext[0:HALO, :] = x1h[0:HALO, :]
    x_ext[HALO : HALO + rows, :] = x1[...]
    x_ext[HALO + rows :, :] = x1h[HALO:, :]
    base = start - lax.rem(start, LONGEST)
    key_frame = base + lax.broadcasted_iota(jnp.int32, (1, LONGEST), 1)
    ukey, _, lkey = tables(meta, key_frame)
    ukey = jnp.where(lkey, ukey, -1)
    query_frame = start - HALO + lax.broadcasted_iota(jnp.int32, (ext, 1), 0)
    uquery, _, lquery = tables(meta, query_frame)
    live = lquery.astype(F32)
    bias[...] = jnp.where(ukey == uquery, 0.0, masked_score)
    half = ext // 2
    head_lane = lax.broadcasted_iota(jnp.int32, (half, 128), 1)

    for pair in range(D // 128):
        lanes = slice(pair * 128, (pair + 1) * 128)
        kp = kvw[:, lanes]
        vp = kvw[:, D + pair * 128 : D + (pair + 1) * 128]
        for blk in range(2):
            at = slice(blk * half, (blk + 1) * half)
            qp = q_ext[at, lanes] * 0.125
            outs = []
            for hh in range(2):
                mine = head_lane < HD if hh == 0 else head_lane >= HD
                qm = jnp.where(mine, qp, jnp.zeros_like(qp))
                s = nt(qm, kp) + bias[at, :]
                top = jnp.max(s, axis=1, keepdims=True)
                e = jnp.exp(s - top)
                total = jnp.sum(e, axis=1, keepdims=True)
                outs.append(nn(e.astype(BF16), vp) * (1.0 / total))
                lse_s[at, pair * 2 + hh : pair * 2 + hh + 1] = top + jnp.log(total)
            o = jnp.where(head_lane < HD, outs[0], outs[1]) * live[at, :]
            o_ext[at, lanes] = o.astype(BF16)
    o_o[...] = o_ext[HALO : HALO + rows, :]
    lse_o[...] = jnp.transpose(lse_s[HALO : HALO + rows, :])[0:8, :]
    landed(w_attn, sem.at[0])
    x_ext[...] += nn(o_ext[...], w_attn[...])
    x2_o[...] = x_ext[HALO : HALO + rows, :]

    def third(i, c):
        at = pl.ds(pl.multiple_of(i * 32, 32), 32)
        n_ref[at, :] = norm(x_ext[at, :], norms, 2).astype(BF16)
        return c

    lax.fori_loop(0, ext // 32, third, 0, unroll=True)
    landed(w_glu, sem.at[1])
    val[...] = nt(n_ref[...], w_glu[0:D, :])
    sig[...] = sigmoid(nt(n_ref[...], w_glu[D:, :]))
    gated_o[...] = val[...] * sig[...] * live
    sums = [[0.0] * (D // 128) for _ in range(2)]
    for k in range(rows // 256):
        fill_chunk(meta, gated_o, chunk, k, start)
        alive = live[HALO + k * 256 : HALO + (k + 1) * 256, :]
        shift_rows(chunk, moved)
        for lc in range(D // 128):
            lanes = slice(lc * 128, (lc + 1) * 128)
            acc = moved[0, 0:256, lanes] * taps[0:1, lanes]
            for j in range(1, KERNEL):
                lo = j - j % 8
                acc = acc + moved[j % 8, lo : lo + 256, lanes] * taps[j : j + 1, lanes]
            h_o[k * 256 : (k + 1) * 256, lanes] = acc
            weighted = acc * alive
            sums[0][lc] += jnp.sum(weighted, axis=0, keepdims=True)
            sums[1][lc] += jnp.sum(weighted * acc, axis=0, keepdims=True)
    sums_o[...] = jnp.concatenate(sums[0] + sums[1], axis=0)


def attend(nh, meta, inv, q, kvw, x1, qh, x1h, norms, taps, full):
    rows = q.shape[0]
    ext = rows + 2 * HALO
    dma = pltpu.SemaphoreType.DMA
    f = jax.ShapeDtypeStruct
    return pl.pallas_call(
        functools.partial(attend_kernel, nh),
        out_shape=[
            f((rows, D), BF16),
            f((8, rows), F32),
            f((rows, D), F32),
            f((ext, D), F32),
            f((rows, D), F32),
            f((2 * D // 128, 128), F32),
            f((ext, D), BF16),
            f((ext, D), F32),
            f((ext, D), F32),
        ],
        in_specs=[SM, SM] + [VM] * 7 + [HBM],
        out_specs=[VM] * 9,
        scratch_shapes=[
            pltpu.VMEM((D, D), BF16),
            pltpu.VMEM((2 * D, D), BF16),
            pltpu.VMEM((ext, D), BF16),
            pltpu.VMEM((ext, D), BF16),
            pltpu.VMEM((ext, D), F32),
            pltpu.VMEM((ext, LONGEST), F32),
            pltpu.VMEM((256 + 2 * HALO, D), F32),
            pltpu.VMEM((8, 256 + 2 * HALO, D), F32),
            pltpu.VMEM((ext, 128), F32),
            dma((2,)),
        ],
        compiler_params=params(34),
        cost_estimate=cost(13),
        name="attend",
    )(meta, inv, q, kvw, x1, qh, x1h, norms, taps, full)


def compact(rows_of):
    pieces = [r[:, i * 128 : (i + 1) * 128] for r in rows_of for i in range(D // 128)]
    return jnp.concatenate(pieces, axis=0)


def spread(packed, row):
    n = D // 128
    return jnp.concatenate([packed[row * n + i : row * n + i + 1, :] for i in range(n)], axis=1)


def bn_terms(meta, packed):
    count = jnp.full((1, 1), meta[11], jnp.int32).astype(F32)
    stats = [spread(packed, 0), spread(packed, 1)]
    center = stats[0] / count
    inv_std = lax.rsqrt(stats[1] / count - center * center + norm_eps)
    return count, center, inv_std


def middle_kernel(nh, meta, inv, x2, h, stats, ograd, norms, taps, full, out_o, g3_o, gz_o, sums_o, ng_o, grads, w_in, w_out, w_pt, n_ref, gb, y3, x3, x4, acc, g_in, g_out, g_pt, sem, sem2, sem3, gsem):
    b = Blocks(nh)
    rows = x2.shape[0]
    unit = FF // nh
    fetch_all(full, inv, w_pt, sem3.at[0], b.point, b.ch, nh)
    for part in range(nh):
        fetch(full, inv, w_in, sem.at[part], b.in_two, b.ff, part, part * unit)
        fetch(full, inv, w_out, sem2.at[part], b.out_two, b.ff, part, part * unit)
    count, center, inv_std = bn_terms(meta, stats)
    gain, shift = taps[KERNEL : KERNEL + 1, :], taps[KERNEL + 1 : KERNEL + 2, :]

    def z_of(at):
        return (h[at, :] - center) * inv_std * gain + shift

    def first(at, i, c):
        z = z_of(at)
        y3[at, :] = (z * sigmoid(z)).astype(BF16)
        return c

    bands(rows, first)
    landed(w_pt, sem3.at[0])
    x3[...] = x2[...] + nn(y3[...], w_pt[...])

    def second(at, i, c):
        n_ref[at, :] = norm(x3[at, :], norms, 3).astype(BF16)
        return c

    bands(rows, second)
    feed(n_ref, w_in, w_out, acc, sem, sem2, nh)
    zero = jnp.zeros((1, D), F32)

    def last(at, i, c):
        x = x3[at, :] + 0.5 * acc[at, :]
        xhat, spread = hat(x)
        out_o[at, :] = (xhat * norms[4:5, :] + norms[9:10, :]).astype(BF16)
        dx, dg, db = hat_back(xhat, spread, ograd[at, :].astype(F32), norms[4:5, :])
        x4[at, :] = dx
        gb[at, :] = (0.5 * dx).astype(BF16)
        return c[0] + dg, c[1] + db

    gain4, shift4 = bands(rows, last, (zero, zero))
    feed_back(n_ref, gb, w_in, w_out, acc, g_in, g_out, grads, inv, b.in_two, b.out_two, gsem.at[0], gsem.at[1], b.ff, nh)

    def back(at, i, c):
        dx, dg, db = norm_back(x3[at, :], acc[at, :], norms[3:4, :])
        g3 = x4[at, :] + dx
        g3_o[at, :] = g3
        gb[at, :] = g3.astype(BF16)
        return c[0] + dg, c[1] + db

    gain3, shift3 = bands(rows, back, (zero, zero))
    ng_o[...] = jnp.zeros_like(ng_o)
    ng_o[3:4, :] = gain3
    ng_o[4:5, :] = gain4
    ng_o[8:9, :] = shift3
    ng_o[9:10, :] = shift4
    acc[...] = nt(gb[...], w_pt[...])
    g_pt[...] = tn(y3[...], gb[...]).astype(BF16)
    put_all(grads, inv, g_pt, gsem.at[2], b.point, b.ch, nh)

    def gz_part(at, i, c):
        white = (h[at, :] - center) * inv_std
        z = white * gain + shift
        gz = acc[at, :] * slope_of(z, sigmoid(z))
        gz_o[at, :] = gz
        return c[0] + jnp.sum(gz, axis=0, keepdims=True), c[1] + jnp.sum(gz * white, axis=0, keepdims=True)

    sg, sx = bands(rows, gz_part, (zero, zero))
    sums_o[...] = compact([sg, sx])
    y3[0:BLOCKW, :] = jnp.zeros((BLOCKW, D), BF16)
    empty = [(i, part) for i in range(b.total, grads.shape[1]) for part in range(nh)]
    for k, (i, part) in enumerate(empty):
        put(grads, inv, y3, gsem.at[3 + k], i, 1, part, 0)
    landed(g_in, gsem.at[0])
    landed(g_out, gsem.at[1])
    landed(g_pt, gsem.at[2])
    for k in range(len(empty)):
        landed(y3.at[pl.ds(0, BLOCKW)], gsem.at[3 + k])


def middle(nh, meta, inv, x2, h, stats, ograd, norms, taps, full):
    rows = x2.shape[0]
    slots = full.shape[1]
    zeros = (slots - Blocks(nh).total) * nh
    dma = pltpu.SemaphoreType.DMA
    f = jax.ShapeDtypeStruct
    v = pltpu.VMEM
    return pl.pallas_call(
        functools.partial(middle_kernel, nh),
        out_shape=[
            f((rows, D), BF16),
            f((rows, D), F32),
            f((rows, D), F32),
            f((2 * D // 128, 128), F32),
            f((16, D), F32),
            f((big(nh, slots), slots, BLOCKW, D), BF16),
        ],
        in_specs=[SM, SM] + [VM] * 6 + [HBM],
        out_specs=[VM] * 5 + [HBM],
        scratch_shapes=[
            v((FF, D), BF16),
            v((FF, D), BF16),
            v((D, D), BF16),
            v((rows, D), BF16),
            v((rows, D), BF16),
            v((rows, D), BF16),
            v((rows, D), F32),
            v((rows, D), F32),
            v((rows, D), F32),
            v((FF, D), BF16),
            v((FF, D), BF16),
            v((D, D), BF16),
            dma((nh,)),
            dma((nh,)),
            dma((1,)),
            dma((3 + zeros,)),
        ],
        compiler_params=params(26),
        cost_estimate=cost(17),
        name="middle",
    )(meta, inv, x2, h, stats, ograd, norms, taps, full)


def conv_back_kernel(nh, meta, inv, gz, gzh, h, hh, stats, bsums, gated, n3, val, sig, x2, g3, o, norms, taps, full, ng_in, grads_in, g2_o, do_o, taps_o, ng_o, grads, w_attn, w_glu, gb, dh, dgated, res, dglu, g_attn, g_glu, chunk, moved, tsum, sem, gsem):
    del grads_in
    b = Blocks(nh)
    rows = gz.shape[0]
    ext = rows + 2 * HALO
    start = meta[10]
    fetch_all(full, inv, w_attn, sem.at[0], b.attn, b.ch, nh)
    for i, base in enumerate((b.conv_value, b.conv_gate)):
        fetch_all(full, inv, w_glu, sem.at[1], base, b.ch, nh, i * D)
    count, center, inv_std = bn_terms(meta, stats)
    gain = taps[KERNEL : KERNEL + 1, :]
    sg, sx = spread(bsums, 0), spread(bsums, 1)

    def dh_of(gz_rows, h_rows, first):
        alive = live_rows(meta, first, gz_rows.shape[0])
        white = (h_rows - center) * inv_std
        return gain * inv_std * (gz_rows - alive / count * (sg + white * sx))

    def one(at, i, c):
        dh[pl.ds(pl.multiple_of(i * BAND + HALO, HALO), BAND), :] = dh_of(gz[at, :], h[at, :], start + i * BAND)
        return c

    bands(rows, one)
    dh[0:HALO, :] = dh_of(gzh[0:HALO, :], hh[0:HALO, :], start - HALO)
    dh[HALO + rows :, :] = dh_of(gzh[HALO:, :], hh[HALO:, :], start + rows)
    tsum[...] = jnp.zeros_like(tsum)
    for k in range(rows // 256):
        fill_chunk(meta, dh, chunk, k, start)
        shift_rows(chunk, moved)

        for i in range(4 * D // 128):
            lanes = slice(i // 4 * 128, i // 4 * 128 + 128)
            row = i % 4 * 64
            own = gated[row + HALO + k * 256 : row + HALO + k * 256 + 64, lanes]
            acc = jnp.zeros((64, 128), F32)
            for j in range(KERNEL):
                off = KERNEL - j
                there = moved[off % 8, row + off - off % 8 : row + off - off % 8 + 64, lanes]
                acc = acc + there * taps[j : j + 1, lanes]
                tsum[j, :, lanes] += jnp.sum((there * own).reshape(8, 8, 128), axis=0)
            dgated[row + k * 256 : row + k * 256 + 64, lanes] = acc
    taps_o[...] = jnp.sum(tsum[...], axis=1)

    def two(at, i, c):
        own = pl.ds(pl.multiple_of(i * BAND + HALO, HALO), BAND)
        s = sig[own, :]
        d = dgated[at, :] * live_rows(meta, start + i * BAND, BAND)
        dglu[at, 0:D] = (d * s).astype(BF16)
        dglu[at, D:] = (d * val[own, :] * s * (1.0 - s)).astype(BF16)
        return c

    bands(rows, two)
    g_glu[...] = tn(dglu[...], n3[HALO : HALO + rows, :]).astype(BF16)
    landed(w_glu, sem.at[1])
    for i, base in enumerate((b.conv_value, b.conv_gate)):
        put_all(grads, inv, g_glu, gsem.at[0], base, b.ch, nh, i * D)
    res[...] = nn(dglu[...], w_glu[...])
    zero = jnp.zeros((1, D), F32)

    def three(at, i, c):
        dx, dg, db = norm_back(x2[at, :], res[at, :], norms[2:3, :])
        g2 = g3[at, :] + dx
        g2_o[at, :] = g2
        gb[at, :] = g2.astype(BF16)
        return c[0] + dg, c[1] + db

    dgain, dshift = bands(rows, three, (zero, zero))
    ng_o[...] = ng_in[...]
    ng_o[2:3, :] = dgain
    ng_o[7:8, :] = dshift
    landed(w_attn, sem.at[0])
    res[...] = nt(gb[...], w_attn[...])
    g_attn[...] = tn(o[...], gb[...]).astype(BF16)
    put_all(grads, inv, g_attn, gsem.at[1], b.attn, b.ch, nh)

    def four(at, i, c):
        do_o[at, :] = (res[at, :] * live_rows(meta, start + i * BAND, BAND)).astype(BF16)
        return c

    bands(rows, four)
    landed(g_glu, gsem.at[0])
    landed(g_attn, gsem.at[1])


def conv_back(nh, meta, inv, gz, gzh, h, hh, stats, bsums, gated, n3, val, sig, x2, g3, o, norms, taps, full, ng, grads):
    rows = gz.shape[0]
    ext = rows + 2 * HALO
    dma = pltpu.SemaphoreType.DMA
    f = jax.ShapeDtypeStruct
    v = pltpu.VMEM
    return pl.pallas_call(
        functools.partial(conv_back_kernel, nh),
        out_shape=[
            f((rows, D), F32),
            f((rows, D), BF16),
            f((KERNEL, D), F32),
            f((16, D), F32),
            f(grads.shape, BF16),
        ],
        in_specs=[SM, SM] + [VM] * 15 + [HBM, VM, HBM],
        out_specs=[VM] * 4 + [HBM],
        input_output_aliases={19: 4},
        scratch_shapes=[
            v((D, D), BF16),
            v((2 * D, D), BF16),
            v((rows, D), BF16),
            v((ext, D), F32),
            v((rows, D), F32),
            v((rows, D), F32),
            v((rows, 2 * D), BF16),
            v((D, D), BF16),
            v((2 * D, D), BF16),
            v((256 + 2 * HALO, D), F32),
            v((8, 256 + 2 * HALO, D), F32),
            v((KERNEL, 8, D), F32),
            dma((2,)),
            dma((2,)),
        ],
        compiler_params=params(28),
        cost_estimate=cost(13),
        name="conv_back",
    )(meta, inv, gz, gzh, h, hh, stats, bsums, gated, n3, val, sig, x2, g3, o, norms, taps, full, ng, grads)


def attend_back_kernel(meta, q, kvw, do, lse, dq_o, dkv_o, send_o, bias, dkp, dvp):
    rows = q.shape[0]
    start = meta[10]
    base = start - lax.rem(start, LONGEST)
    offset = pl.multiple_of(lax.rem(start, LONGEST), rows)
    ukey, _, lkey = tables(meta, base + lax.broadcasted_iota(jnp.int32, (LONGEST, 1), 0))
    ukey = jnp.where(lkey, ukey, -1)
    uquery, _, _ = tables(meta, start + lax.broadcasted_iota(jnp.int32, (1, rows), 1))
    bias[...] = jnp.where(ukey == uquery, 0.0, masked_score)
    lane_q = lax.broadcasted_iota(jnp.int32, (rows, 128), 1)
    lane_k = lax.broadcasted_iota(jnp.int32, (LONGEST, 128), 1)
    for pair in range(D // 128):
        lanes = slice(pair * 128, (pair + 1) * 128)
        kp = kvw[:, lanes]
        vp = kvw[:, D + pair * 128 : D + (pair + 1) * 128]
        kms = [jnp.where(lane_k < HD, kp, jnp.zeros_like(kp)), jnp.where(lane_k >= HD, kp, jnp.zeros_like(kp))]
        qp = q[:, lanes] * 0.125
        dop = do[:, lanes]
        for hh in range(2):
            mine = lane_q < HD if hh == 0 else lane_q >= HD
            qm = jnp.where(mine, qp, jnp.zeros_like(qp))
            dom = jnp.where(mine, dop, jnp.zeros_like(dop))
            s = nt(kp, qm) + bias[...]
            p = jnp.exp(s - lse[pair * 2 + hh : pair * 2 + hh + 1, :])
            dp = nt(vp, dom)
            inner = jnp.sum(p * dp, axis=0, keepdims=True)
            ds = (p * (dp - inner)).astype(BF16)
            dv, dk, dq = nn(p.astype(BF16), dom), nn(ds, qm), tn(ds, kms[hh]) * 0.125
            if hh == 0:
                dvp[...], dkp[...], dq_o[:, lanes] = dv, dk, dq
            else:
                dvp[...] += dv
                dkp[...] += dk
                dq_o[:, lanes] += dq
        dkv_o[:, lanes] = dkp[pl.ds(offset, rows), :]
        dkv_o[:, D + pair * 128 : D + (pair + 1) * 128] = dvp[pl.ds(offset, rows), :]
        send_o[:, lanes] = dkp[...].astype(BF16)
        send_o[:, D + pair * 128 : D + (pair + 1) * 128] = dvp[...].astype(BF16)


def attend_back(meta, q, kvw, do, lse):
    rows = q.shape[0]
    f = jax.ShapeDtypeStruct
    v = pltpu.VMEM
    return pl.pallas_call(
        attend_back_kernel,
        out_shape=[f((rows, D), F32), f((rows, 2 * D), F32), f((LONGEST, 2 * D), BF16)],
        in_specs=[SM] + [VM] * 4,
        out_specs=[VM] * 3,
        scratch_shapes=[v((LONGEST, rows), F32), v((LONGEST, 128), F32), v((LONGEST, 128), F32)],
        compiler_params=params(26),
        cost_estimate=cost(14),
        name="attend_back",
    )(meta, q, kvw, do, lse)


def rear_kernel(nh, meta, inv, dq, dkv, recv, x1, frames, g2, norms, table, full, ng_in, grads_in, fg_o, ng_o, grads, w_in, w_out, w_qkv, n_ref, gb, dproj, x_ref, acc, g_in, g_out, g_qkv, sem, gsem):
    del grads_in
    b = Blocks(nh)
    rows = dq.shape[0]
    for i, base in enumerate((b.query, b.key, b.value)):
        fetch_all(full, inv, w_qkv, sem.at[0], base, b.ch, nh, i * D)
    fetch_all(full, inv, w_in, sem.at[1], b.in_one, b.ff, nh)
    fetch_all(full, inv, w_out, sem.at[2], b.out_one, b.ff, nh)
    spans = recv.shape[0]

    def one(at, i, c):
        p = pl.ds(place_of(meta, i), BAND)
        dproj[at, 0:D] = turn(dq[at, :], table[p, :], -1.0).astype(BF16)
        dk, dv = dkv[at, 0:D], dkv[at, D:]
        for s in range(spans):
            dk = dk + recv[s, at, 0:D].astype(F32)
            dv = dv + recv[s, at, D:].astype(F32)
        dproj[at, D : 2 * D] = turn(dk, table[p, :], -1.0).astype(BF16)
        dproj[at, 2 * D :] = dv.astype(BF16)
        n_ref[at, :] = norm(x1[at, :], norms, 1).astype(BF16)
        return c

    bands(rows, one)
    landed(w_qkv, sem.at[0])
    acc[...] = nn(dproj[...], w_qkv[...])
    for i in range(3):
        g_qkv[i * D : (i + 1) * D, :] = tn(dproj[:, i * D : (i + 1) * D], n_ref[...]).astype(BF16)
    for i, base in enumerate((b.query, b.key, b.value)):
        put_all(grads, inv, g_qkv, gsem.at[0], base, b.ch, nh, i * D)
    zero = jnp.zeros((1, D), F32)

    def two(at, i, c):
        dx, dg, db = norm_back(x1[at, :], acc[at, :], norms[1:2, :])
        g1 = g2[at, :] + dx
        x_ref[at, :] = g1
        gb[at, :] = (0.5 * g1).astype(BF16)
        n_ref[at, :] = norm(frames[at, :].astype(F32), norms, 0).astype(BF16)
        return c[0] + dg, c[1] + db

    gain1, shift1 = bands(rows, two, (zero, zero))
    landed(w_in, sem.at[1])
    landed(w_out, sem.at[2])
    feed_back(n_ref, gb, w_in, w_out, acc, g_in, g_out, grads, inv, b.in_one, b.out_one, gsem.at[1], gsem.at[2], b.ff, nh)

    def three(at, i, c):
        dx, dg, db = norm_back(frames[at, :].astype(F32), acc[at, :], norms[0:1, :])
        fg_o[at, :] = x_ref[at, :] + dx
        return c[0] + dg, c[1] + db

    gain0, shift0 = bands(rows, three, (zero, zero))
    ng_o[...] = ng_in[...]
    ng_o[0:1, :] = gain0
    ng_o[1:2, :] = gain1
    ng_o[5:6, :] = shift0
    ng_o[6:7, :] = shift1
    landed(g_qkv, gsem.at[0])
    landed(g_in, gsem.at[1])
    landed(g_out, gsem.at[2])


def rear(nh, meta, inv, dq, dkv, recv, x1, frames, g2, norms, table, full, ng, grads):
    rows = dq.shape[0]
    dma = pltpu.SemaphoreType.DMA
    f = jax.ShapeDtypeStruct
    v = pltpu.VMEM
    return pl.pallas_call(
        functools.partial(rear_kernel, nh),
        out_shape=[f((rows, D), F32), f((16, D), F32), f(grads.shape, BF16)],
        in_specs=[SM, SM] + [VM] * 8 + [HBM, VM, HBM],
        out_specs=[VM, VM, HBM],
        input_output_aliases={12: 2},
        scratch_shapes=[
            v((FF, D), BF16),
            v((FF, D), BF16),
            v((3 * D, D), BF16),
            v((rows, D), BF16),
            v((rows, D), BF16),
            v((rows, 3 * D), BF16),
            v((rows, D), F32),
            v((rows, D), F32),
            v((FF, D), BF16),
            v((FF, D), BF16),
            v((3 * D, D), BF16),
            dma((3,)),
            dma((3,)),
        ],
        compiler_params=params(28),
        cost_estimate=cost(13),
        name="rear",
    )(meta, inv, dq, dkv, recv, x1, frames, g2, norms, table, full, ng, grads)


def split(x):
    high = x.astype(BF16)
    return high, (x - high.astype(F32)).astype(BF16)


def three_products(dot, a, b):
    (ah, al), (bh, bl) = a, b
    return dot(ah, bh) + (dot(ah, bl) + dot(al, bh))


def wide_product(dot, a, b):
    rows = a.shape[0]
    ah, al = split(a)
    stacked = dot(jnp.concatenate([ah, al], axis=0), b[0])
    return stacked[0:rows] + (stacked[rows:] + dot(ah, b[1]))


def adam_step(weight, gradient, moment_one, moment_two, factor):
    one_new = beta_one * moment_one + (1.0 - beta_one) * gradient
    two_new = beta_two * moment_two + (1.0 - beta_two) * gradient * gradient
    return (weight - factor * one_new / (jnp.sqrt(two_new) + adam_eps), one_new, two_new)


def update_kernel(nh, head, grad, masters, first, second, left, right, small, bsums, norms, norm1, norm2, conv, conv1, conv2, out_v, fgrad_v, masters_o, first_o, second_o, ng_o, norms_o, norm1_o, norm2_o, conv_o, conv1_o, conv2_o, out_o, fgrad_o, sem):
    moves = [
        pltpu.make_async_copy(out_v, out_o, sem.at[0]),
        pltpu.make_async_copy(fgrad_v, fgrad_o, sem.at[1]),
    ]
    step = pl.program_id(0)

    @pl.when(step == 0)
    def _():
        for move in moves:
            move.start()
        grads = small[0:10, :]
        ng_o[...] = grads
        norms_o[...], norm1_o[...], norm2_o[...] = adam_step(norms[...], grads, norm1[...], norm2[...], 10.0 * FACTOR)
        width = conv.shape[1]
        rows = jnp.concatenate([small[16 : 16 + KERNEL, :], spread(bsums, 1), spread(bsums, 0)], axis=0)
        mine = rows[:, 0:width]
        for h in range(1, nh):
            mine = jnp.where(head[0] == h, rows[:, h * width : (h + 1) * width], mine)
        conv_o[...], conv1_o[...], conv2_o[...] = adam_step(conv[...], mine, conv1[...], conv2[...], 4.0 * FACTOR)

    for i in range(grad.shape[0]):
        g = grad[i]
        m1 = beta_one * first[i] + (1.0 - beta_one) * g
        first_o[i] = m1
        lefts, rights = split(left[i]), split(right[i])
        both = wide_product(nn, jnp.concatenate([g, m1], axis=0), lefts)
        rot = three_products(tn, rights, split(both[0:BLOCKW]))
        rot1 = three_products(tn, rights, split(both[BLOCKW:]))
        m2 = beta_two * second[i] + (1.0 - beta_two) * rot * rot
        second_o[i] = m2
        scaled = rot1 / (jnp.sqrt(m2) + adam_eps)
        back = wide_product(nt, three_products(nn, rights, split(scaled)), lefts)
        w = masters[i]
        masters_o[i] = w - FACTOR * back - step_rate * weight_decay * w

    @pl.when(step == pl.num_programs(0) - 1)
    def _():
        for move in moves:
            move.wait()


def update(nh, head, grad, masters, first, second, left, right, small, bsums, norms, norm1, norm2, conv, conv1, conv2, out_v, fgrad_v):
    spd = grad.shape[0]
    n = 2 if spd % 2 == 0 else 1
    block = pl.BlockSpec((n, BLOCKW, D), lambda i: (i, 0, 0))

    def whole(a):
        return pl.BlockSpec(a.shape, lambda i: (0, 0))

    f = jax.ShapeDtypeStruct
    return pl.pallas_call(
        functools.partial(update_kernel, nh),
        grid=(spd // n,),
        out_shape=[f(grad.shape, F32)] * 3
        + [f(norms.shape, F32)] * 4
        + [f(conv.shape, F32)] * 3
        + [f(out_v.shape, out_v.dtype), f(fgrad_v.shape, F32)],
        in_specs=[SM]
        + [block] * 4
        + [pl.BlockSpec((n, D, D), lambda i: (i, 0, 0)), pl.BlockSpec((n, BLOCKW, BLOCKW), lambda i: (i, 0, 0))]
        + [whole(a) for a in (small, bsums, norms, norm1, norm2, conv, conv1, conv2)]
        + [HBM, HBM],
        out_specs=[block] * 3 + [whole(norms)] * 4 + [whole(conv)] * 3 + [HBM, HBM],
        scratch_shapes=[pltpu.SemaphoreType.DMA((2,))],
        compiler_params=params(20),
        cost_estimate=cost(9),
        name="update",
    )(head, grad, masters, first, second, left, right, small, bsums, norms, norm1, norm2, conv, conv1, conv2, out_v, fgrad_v)


def per_device(
    ndp,
    nh,
    frames,
    out_grad,
    bucket_len,
    batch_count,
    utt_lengths,
    owner_slots,
    masters,
    first_moment,
    second_moment,
    left_basis,
    right_basis,
    norm_params,
    norm_first,
    norm_second,
    conv_params,
    conv_first,
    conv_second,
):
    rows = frames.shape[0]

    def flip(a):
        return jnp.transpose(a[0], (0, 2, 1))

    masters_t = flip(masters)
    z = lax.axis_index("head")
    dp = lax.axis_index("dp")
    place = jnp.stack([dp - dp % 2 + z % 2, 2 * (z // 2) + dp % 2])
    full, frames_v, ograd_v, ints, conv_all = gather(
        ndp,
        nh,
        masters_t.astype(BF16),
        frames,
        out_grad,
        bucket_len[None],
        batch_count[None],
        utt_lengths,
        conv_params.T,
    )
    table = jnp.asarray(rope_table())
    x1, q, kv, meta, inv, taps = front(
        ndp, nh, owner_slots, place, ints, conv_all, frames_v, norm_params, table, full
    )
    kvw, qh, x1h = keys(ndp, nh, kv, q, x1)
    o, lse, x2, gated, h, sums, n3, val, sig = attend(nh, meta, inv, q, kvw, x1, qh, x1h, norm_params, taps, full)
    (stats,) = totals(ndp, nh, 3, sums)
    out_v, g3, gz, bpart, ng, grads = middle(nh, meta, inv, x2, h, stats, ograd_v, norm_params, taps, full)
    bsums, gzh, hh = totals(ndp, nh, 4, bpart, (gz, h))
    g2, do, dtaps, ng, grads = conv_back(
        nh, meta, inv, gz, gzh, h, hh, stats, bsums, gated, n3, val, sig, x2, g3, o, norm_params, taps, full, ng, grads
    )
    dq, dkv, dkv_send = attend_back(meta, q, kvw, do, lse)
    recv = key_grads(ndp, nh, dkv_send, rows)
    fg_v, ng, grads = rear(
        nh, meta, inv, dq, dkv, recv, x1, frames_v, g2, norm_params, table, full, ng, grads
    )
    small = jnp.concatenate([ng, dtaps], axis=0)
    owned, small, out_w, fg_w = scatter(ndp, nh, grads, small, out_v, fg_v)
    (
        new_m,
        new_f,
        new_s,
        norm_grads,
        new_norms,
        norm_first_new,
        norm_second_new,
        new_conv,
        conv_first_new,
        conv_second_new,
        layer_out,
        frames_grad,
    ) = update(
        nh,
        jnp.reshape(z, (1,)),
        owned,
        masters_t,
        flip(first_moment),
        flip(second_moment),
        left_basis[0],
        right_basis[0],
        small,
        bsums,
        norm_params,
        norm_first,
        norm_second,
        conv_params.T,
        conv_first.T,
        conv_second.T,
        out_w,
        fg_w,
    )

    def unflip(a):
        return jnp.transpose(a, (0, 2, 1))[None]

    return (
        layer_out,
        frames_grad,
        unflip(new_m),
        unflip(new_f),
        unflip(new_s),
        norm_grads,
        new_norms,
        norm_first_new,
        norm_second_new,
        new_conv.T,
        conv_first_new.T,
        conv_second_new.T,
    )


def solution(mesh):
    both, blocks, chan = P(("dp", "head"), None), P("head", "dp", None, None), P("head", None)
    placed = (both, both, P("dp"), P("dp"), P("dp", None), P()) + (blocks,) * 5 + (P(),) * 3 + (chan,) * 3
    return jax.shard_map(
        functools.partial(per_device, mesh.shape["dp"], mesh.shape["head"]),
        mesh=mesh,
        in_specs=placed,
        out_specs=(both, both) + (blocks,) * 3 + (P(),) * 4 + (chan,) * 3,
        check_vma=False,
    )
```
